32 devices in a mesh: parts: 2 (over y), map: 16 (over z, x, core).
Axes of the slice: x: 2, y: 2, z: 4, core: 2. Of those that a mesh axis runs over, the one named last changes fastest.
Arguments:
- crust_velocity: float32 [6, 128, 32, 32], P('parts', 'map'), parts along dimension 0, may hold values from -6 to 6
- crust_stress: float32 [12, 128, 32, 32], P('parts', 'map'), parts along dimension 0, may hold values from -6 to 6
- ocean_state: float32 [8, 32, 32, 128], P('parts', 'map'), parts along dimension 0, may hold values from -6 to 6
- zones: int32 [128, 64, 32], P('map', 'parts'), parts along dimension 1, may hold values from 0 to 7
- materials: float32 [3, 8], replicated, may hold values from 0.4 to 1.2
- slip_rate: float32 [128, 64], P('map', 'parts'), parts along dimension 1, may hold values from -6 to 6
- bathymetry: int32 [32, 256], P('map', 'parts'), parts along dimension 1, may hold values from 1 to 32
Outputs:
- new_velocity: float32 [6, 128, 32, 32], P('parts', 'map'), parts along dimension 0
- new_stress: float32 [12, 128, 32, 32], P('parts', 'map'), parts along dimension 0
- new_ocean: float32 [8, 32, 32, 128], P('parts', 'map'), parts along dimension 0
The draws below stay inside these ranges and needn't reach their ends.
There are 2 independent parts, one for each index of `parts`. The reference program is written for one: setup_inputs(seed, part) draws one part's arguments, and reference() takes and returns one part's arrays. A program takes and returns all parts, laid end to end along the dimension named above; an argument that names none is the same for every part. Nothing has to cross between parts.
All inputs are finite; a program needn't handle non-finite values.
Results may differ from the reference program's by a relative error of at most 0.0001.
Values sent between devices are 32-bit elements; how exact they have to be, the bound alone decides.
No kernel may reach another device: no remote copies, remote signals or barrier semaphores. Data moves between devices by JAX's collectives and lax.ppermute only.
A program may use at most 64 MiB of HBM per device.

```python
import jax
import jax.numpy as jnp
from jax import lax

NZC = 32
OZ = 32
STEPS = 4
ZONES = 8
NX = 128
NY = 32


def with_ends(drawn, rng, least, top_value):
    longest = drawn.shape.index(max(drawn.shape))
    spots = []
    for shift in (0, 1):
        where = [jax.random.randint(jax.random.fold_in(rng, axis), (), 0, length) for axis, length in enumerate(drawn.shape)]
        where[longest] = (where[longest] + shift) % drawn.shape[longest]
        spots.append(tuple(where))
    return drawn.at[spots[0]].set(least).at[spots[1]].set(top_value)


def steps_of(own_key, dims, pieces, smallest, top_value):
    loudness = 1.0
    for axis_at, blocks in pieces:
        heights = jax.random.uniform(jax.random.fold_in(jax.random.fold_in(own_key, 6), axis_at), (blocks,), jnp.float32, smallest / len(pieces), top_value / len(pieces))
        loudness = loudness * jnp.repeat(jnp.exp(heights), dims[axis_at] // blocks).reshape((-1,) + (1,) * (len(dims) - 1 - axis_at))
    return loudness


def normal_values(own_key, extent, width, bound, pieces=(), kind=jnp.bfloat16):
    level = steps_of(own_key, extent, pieces, -0.22, 0.18) if pieces else 1.0
    array = jax.random.normal(own_key, extent, jnp.float32) * width * level
    return jnp.minimum(jnp.maximum(array, -bound), bound).astype(kind)


def setup_inputs(seed: int = 0, part: int = 0) -> dict:
    keys = jax.random.split(jax.random.key(seed), 8)
    part_splits = jax.random.split(jax.random.fold_in(keys[7], part), 8)
    return {
        "crust_velocity": normal_values(part_splits[0], (3, NX, NZC, NY), 1.0, 6.0, ((1, 16),), jnp.float32),
        "crust_stress": normal_values(part_splits[1], (6, NX, NZC, NY), 1.0, 6.0, ((1, 16),), jnp.float32),
        "ocean_state": normal_values(part_splits[2], (4, NY, OZ, NX), 1.0, 6.0, ((1, 16),), jnp.float32),
        "zones": with_ends(jax.random.randint(part_splits[3], (NX, NZC, NY), 0, ZONES), jax.random.fold_in(part_splits[3], 1), 0, ZONES - 1).astype(jnp.int32),
        "materials": jnp.clip(jax.random.uniform(keys[4], (3, ZONES), jnp.float32, 0.4, 1.2), 0.4, 1.2),
        "slip_rate": normal_values(part_splits[5], (NX, NY), 1.0, 6.0, ((0, 16),), jnp.float32),
        "bathymetry": with_ends(jax.random.randint(part_splits[6], (NY, NX), 1, OZ + 1), jax.random.fold_in(part_splits[6], 1), 1, OZ).astype(jnp.int32),
    }


DT = 0.25
KBULK = 2.25
GRAV = 0.1


def central(field, axis):
    count = field.shape[axis]
    widths = [(0, 0)] * field.ndim
    widths[axis] = (1, 1)
    padded = jnp.pad(field, widths)
    return (lax.slice_in_dim(padded, 2, count + 2, axis=axis) - lax.slice_in_dim(padded, 0, count, axis=axis)) * 0.5


def depth_diff(field, top):
    above = jnp.concatenate([top[:, None, :], field[:, :-1, :]], axis=1)
    below = jnp.concatenate([field[:, 1:, :], jnp.zeros_like(field[:, :1, :])], axis=1)
    return (below - above) * 0.5


def crust_step(velocity, stress, mats, fault, load, xdiff):
    buoy, lamb, shear = mats[0], mats[1], mats[2]
    sxx, syy, szz, sxy, sxz, syz = stress[0], stress[1], stress[2], stress[3], stress[4], stress[5]
    zero = jnp.zeros_like(load)
    grads = xdiff(jnp.stack([sxx, sxy, sxz]))
    acc_x = grads[0] + central(sxy, 2) + depth_diff(sxz, zero)
    acc_y = grads[1] + central(syy, 2) + depth_diff(syz, zero)
    acc_z = grads[2] + central(syz, 2) + depth_diff(szz, -load)
    vel_x = velocity[0] + DT * buoy * acc_x
    vel_y = velocity[1] + DT * buoy * acc_y
    vel_z = velocity[2] + DT * buoy * acc_z
    slopes = xdiff(jnp.stack([vel_x, vel_y, vel_z]))
    exx = slopes[0]
    eyy = central(vel_y, 2)
    ezz = depth_diff(vel_z, vel_z[:, 0, :])
    exy = 0.5 * (central(vel_x, 2) + slopes[1])
    exz = 0.5 * (depth_diff(vel_x, vel_x[:, 0, :]) + slopes[2])
    eyz = 0.5 * (depth_diff(vel_y, vel_y[:, 0, :]) + central(vel_z, 2))
    trace = exx + eyy + ezz
    new_stress = jnp.stack([
        sxx + DT * (lamb * trace + 2.0 * shear * exx),
        syy + DT * (lamb * trace + 2.0 * shear * eyy),
        szz + DT * (lamb * trace + 2.0 * shear * ezz),
        sxy + DT * 2.0 * shear * exy,
        sxz + DT * 2.0 * shear * exz + DT * fault,
        syz + DT * 2.0 * shear * eyz])
    return jnp.stack([vel_x, vel_y, vel_z]), new_stress


def next_layer(field):
    return jnp.concatenate([field[:, 1:, :], jnp.zeros_like(field[:, :1, :])], axis=1)


def ocean_step(fields, water, bottom, floor, xdiff, ydiff):
    press, flow_x, flow_y, flow_w = fields
    p_up = jnp.concatenate([-press[:, :1, :], press[:, :-1, :]], axis=1)
    p_down = next_layer(press) + bottom * press
    flow_x = water * (flow_x - DT * xdiff(press))
    flow_y = water * (flow_y - DT * ydiff(press))
    flow_w = water * (flow_w - DT * ((p_down - p_up) * 0.5 + GRAV * press))
    w_up = jnp.concatenate([flow_w[:, :1, :], flow_w[:, :-1, :]], axis=1)
    w_down = next_layer(flow_w) + bottom * floor[:, None, :]
    diverge = xdiff(flow_x) + ydiff(flow_y) + (w_down - w_up) * 0.5
    press = water * (press - DT * KBULK * diverge)
    return press, flow_x, flow_y, flow_w


def reference(crust_velocity, crust_stress, ocean_state, zones, materials, slip_rate, bathymetry):
    onehot = (zones[None] == jnp.arange(ZONES, dtype=jnp.int32)[:, None, None, None]).astype(jnp.float32)
    mats = jnp.einsum('cz,zabk->cabk', materials, onehot, precision=lax.Precision.HIGHEST)
    layer = (jnp.arange(NZC, dtype=jnp.int32) == NZC // 2).astype(jnp.float32)
    fault = slip_rate[:, None, :] * layer[None, :, None]
    depth_idx = jnp.arange(OZ, dtype=jnp.int32)
    water = (depth_idx[None, :, None] < bathymetry[:, None, :]).astype(jnp.float32)
    bottom = water - next_layer(water)
    fields = tuple(water * ocean_state[i] for i in range(4))
    velocity, stress = crust_velocity, crust_stress
    for step in range(STEPS):
        floor = velocity[2][:, 0, :].T
        fields = ocean_step(fields, water, bottom, floor, lambda f: central(f, 2), lambda f: central(f, 0))
        load = jnp.sum(bottom * fields[0], axis=1).T
        velocity, stress = crust_step(velocity, stress, mats, fault, load, lambda f: central(f, 1))
    return velocity, stress, jnp.stack(fields)
```

```python
import functools

import jax
import jax.numpy as jnp
from jax import lax
from jax.experimental import pallas as pl
from jax.experimental.pallas import tpu as pltpu
from jax.sharding import PartitionSpec as P

STEPS = 4
ZONES = 8
DT = 0.25
KBULK = 2.25
GRAV = 0.1
HALO = 2 * STEPS
LANES = 128
F32 = jnp.float32


class Plan:
    def __init__(self, devices, cells, depth, ny, strips):
        self.n = devices
        self.cells = cells
        self.depth = depth
        self.ny = ny
        self.strips = strips
        self.chunks = max(1, LANES // ny)
        self.sub = depth // self.chunks
        self.lanes = self.chunks * ny
        self.width = cells + 2 * HALO
        self.own_groups = cells // self.chunks
        self.halo_groups = HALO // self.chunks
        self.groups = self.width // self.chunks
        self.lead = self.chunks * strips
        self.rows = self.lead * (self.groups + 1)
        self.back_rows = self.lead * self.own_groups
        self.nx = devices * cells
        self.unrolled = self.sub * self.lanes <= 1024


BATHY_LANE = 64


def place(pieces, wanted, block):
    out = None
    for i, piece in enumerate(pieces):
        shift = (i - wanted[i]) * block % piece.shape[-1]
        moved = pltpu.roll(piece, shift, piece.ndim - 1) if shift else piece
        if out is None:
            out = moved
        else:
            lane = lax.broadcasted_iota(jnp.int32, moved.shape, moved.ndim - 1)
            out = jnp.where(lane >= i * block, moved, out)
    return out


def pack_kernel(
    plan, vel, stress, zones, slip, ocean, bathy, crust, message, turned, grouped, extra
):
    cells, sub, chunks, ny, n = plan.cells, plan.sub, plan.chunks, plan.ny, plan.n
    strips = plan.strips
    block = 4 * sub
    grouped[...] = jnp.zeros_like(grouped)
    for yl in range(strips):
        stacked = jnp.concatenate(
            [ocean[f, yl, kc * sub : (kc + 1) * sub, :] for kc in range(chunks) for f in range(4)],
            axis=0,
        )
        turned[yl] = stacked.T
        by_x = [turned[yl, pl.ds(i, plan.nx // chunks, stride=chunks), :] for i in range(chunks)]
        for kc in range(chunks):
            grouped[kc * strips + yl, pl.ds(plan.halo_groups, plan.nx // chunks), :] = place(
                by_x, [kc] * chunks, block
            )
    count = n - 2
    lane = lax.broadcasted_iota(jnp.int32, (n, LANES), 1)
    row = lax.broadcasted_iota(jnp.int32, (n, LANES), 0)
    for yl in range(strips):
        depths = bathy[yl : yl + 1, :].astype(F32)
        wide = lax.broadcasted_iota(jnp.int32, depths.shape, 1)
        for d in range(n):
            first = d * cells - HALO - 1
            moved = pltpu.roll(depths, (BATHY_LANE - first) % plan.nx, 1)
            at = wide - BATHY_LANE + first
            moved = jnp.where((at >= 0) & (at < plan.nx), moved, 0.0)
            extra[yl, d : d + 1, :] = moved[:, :LANES]
        left = jnp.zeros((n, LANES), F32)
        edges_low = turned[yl, pl.ds(2 * cells - HALO - 1, count, stride=cells), :]
        edges_high = turned[yl, pl.ds(cells + HALO, count, stride=cells), :]
        low = jnp.concatenate([jnp.zeros((2, LANES), F32), edges_low], axis=0)
        high = jnp.concatenate([edges_high, jnp.zeros((2, LANES), F32)], axis=0)
        for kc in range(chunks):
            low_moved = pltpu.roll(low, (-kc * block) % LANES, 1) if kc else low
            high_moved = pltpu.roll(high, (sub - kc * block) % LANES, 1)
            rest = jnp.where(lane < sub, low_moved, extra[yl])
            rest = jnp.where((lane >= sub) & (lane < 2 * sub), high_moved, rest)
            at = (kc * strips + yl) * (plan.groups + 1) + plan.groups
            message[pl.ds(at, n, stride=plan.rows), :] = rest
    for d in range(n):
        for q in range(plan.lead):
            start = d * plan.rows + q * (plan.groups + 1)
            message[start : start + plan.groups, :] = grouped[
                q, d * plan.own_groups : d * plan.own_groups + plan.groups, :
            ]
    def packed(ref, f, x):
        parts = [ref[f, x, kc * sub : (kc + 1) * sub, :] for kc in range(chunks)]
        return jnp.concatenate(parts, axis=-1) if chunks > 1 else parts[0]

    for f in range(3):
        for x in range(cells):
            crust[f * cells + x] = packed(vel, f, x)
    for f in range(6):
        for x in range(cells):
            crust[(3 + f) * cells + x] = packed(stress, f, x)
    for x in range(cells):
        parts = [zones[x, kc * sub : (kc + 1) * sub, :] for kc in range(chunks)]
        plane = jnp.concatenate(parts, axis=-1) if chunks > 1 else parts[0]
        crust[9 * cells + x] = (plane + 1).astype(F32)
    fault_chunk = (plan.depth // 2) // sub
    pieces = [
        slip[...] if kc == fault_chunk else jnp.zeros((cells, ny), F32) for kc in range(chunks)
    ]
    fault = jnp.concatenate(pieces, axis=-1) if chunks > 1 else pieces[0]
    if sub > cells:
        fault = jnp.concatenate([fault, jnp.zeros((sub - cells, plan.lanes), F32)], axis=0)
    crust[10 * cells] = fault


class Shifts:
    def __init__(self, plan):
        self.plan = plan
        shape = (plan.sub, plan.lanes)
        self.row = lax.broadcasted_iota(jnp.int32, shape, 0)
        self.lane = lax.broadcasted_iota(jnp.int32, shape, 1)
        self.y = lax.rem(self.lane, plan.ny)
        self.first_row = self.row == 0
        self.last_row = self.row == plan.sub - 1
        self.top = self.first_row & (self.lane < plan.ny)
        self.floor_cell = self.last_row & (self.lane >= plan.lanes - plan.ny)
        self.not_low_y = jnp.where(self.y == 0, 0.0, 1.0).astype(F32)
        self.not_high_y = jnp.where(self.y == plan.ny - 1, 0.0, 1.0).astype(F32)
        self.depth = (
            lax.div(self.lane, plan.ny) * plan.sub + self.row
        ).astype(F32)

    def dy(self, f):
        lanes = self.plan.lanes
        return pltpu.roll(f, lanes - 1, 1) * self.not_high_y - pltpu.roll(f, 1, 1) * self.not_low_y

    def below(self, f):
        plan = self.plan
        moved = pltpu.roll(f, plan.sub - 1, 0)
        if plan.chunks > 1:
            moved = jnp.where(self.last_row, pltpu.roll(moved, plan.lanes - plan.ny, 1), moved)
        return jnp.where(self.floor_cell, 0.0, moved)

    def above(self, f, top):
        plan = self.plan
        moved = pltpu.roll(f, 1, 0)
        if plan.chunks > 1:
            moved = jnp.where(self.first_row, pltpu.roll(moved, plan.ny, 1), moved)
        return jnp.where(self.top, top, moved)

    def over_chunks(self, f):
        shift = self.plan.ny
        while shift < self.plan.lanes:
            f = f + pltpu.roll(f, shift, 1)
            shift *= 2
        return f


def steps_kernel(
    plan, mats, own, low, high, arrived, vel_out, stress_out, message,
    crust, oc, water, bottom, buoy, lamb, shear, gather, depths,
):
    cells, sub, chunks, n, strips = plan.cells, plan.sub, plan.chunks, plan.n, plan.strips
    width = plan.width
    sh = Shifts(plan)
    half = 0.5 * DT

    def planes(start, stop, body):
        if plan.unrolled:
            for j in range(start, stop):
                body(j)
        else:
            def run(j, carry):
                body(j)
                return carry

            lax.fori_loop(start, stop, run, 0)

    def turn(group):
        for kc in range(chunks):
            for yl in range(strips):
                at = (kc * strips + yl) * (plan.groups + 1) + group
                gather[pl.ds(kc * plan.ny + yl, n, stride=strips), :] = arrived[
                    pl.ds(at, n, stride=plan.rows), :
                ]
        return gather[...].T

    rest = turn(plan.groups)
    oc[0, 0] = rest[:sub]
    oc[0, width + 1] = rest[sub : 2 * sub]
    depths[...] = rest[BATHY_LANE : BATHY_LANE + depths.shape[0]]
    for group in range(plan.groups):
        turned = turn(group)
        for i in range(chunks):
            for f in range(4):
                at = (i * 4 + f) * sub
                oc[f, 1 + group * chunks + i] = turned[at : at + sub]

    def mask(j):
        deep = jnp.broadcast_to(depths[pl.ds(j, 1), :], (sub, plan.lanes))
        wet = jnp.where(sh.depth < deep, 1.0, 0.0).astype(F32)
        water[j] = wet
        bottom[j] = jnp.where(sh.depth == deep - 1.0, 1.0, 0.0).astype(F32)
        oc[0, j] = oc[0, j] * wet

    def mask_flow(j):
        for f in range(1, 4):
            oc[f, j] = oc[f, j] * water[j]

    planes(0, width + 2, mask)
    planes(1, width + 1, mask_flow)

    for part, ref in enumerate((low, own, high)):
        def bring(x, part=part, ref=ref):
            j = part * cells + x
            for f in range(9):
                crust[f, j] = ref[f * cells + x]
            zone = ref[9 * cells + x]
            values = [jnp.zeros_like(zone) for _ in range(3)]
            for z in range(ZONES):
                here = zone == float(z + 1)
                values = [jnp.where(here, mats[c, z], values[c]) for c in range(3)]
            buoy[j] = values[0] * half
            lamb[j] = values[1] * half
            shear[j] = values[2] * half
            slip = jnp.broadcast_to(ref[10 * cells, pl.ds(x, 1), :], (sub, plan.lanes))
            crust[9, j] = jnp.where(sh.row == (plan.depth // 2) % sub, DT * slip, 0.0)

        planes(0, cells, bring)

    VX, VY, VZ, SXX, SYY, SZZ, SXY, SXZ, SYZ, FAULT = range(10)

    for t in range(STEPS):
        def flow(j):
            p = oc[0, j + 1]
            wet = water[j + 1]
            oc[1, j + 1] = wet * (oc[1, j + 1] - half * (oc[0, j + 2] - oc[0, j]))
            oc[2, j + 1] = wet * (oc[2, j + 1] - half * sh.dy(p))
            rise = sh.below(p) + bottom[j + 1] * p - sh.above(p, -p)
            oc[3, j + 1] = wet * (oc[3, j + 1] - (half * rise + (DT * GRAV) * p))

        def press(j):
            w = oc[3, j + 1]
            floor = jnp.where(sh.top, crust[VZ, j], 0.0)[0:1]
            floor = jnp.broadcast_to(sh.over_chunks(floor), (sub, plan.lanes))
            rise = sh.below(w) + bottom[j + 1] * floor - sh.above(w, w)
            spread = oc[1, j + 2] - oc[1, j] + sh.dy(oc[2, j + 1]) + rise
            oc[0, j + 1] = water[j + 1] * (oc[0, j + 1] - (half * KBULK) * spread)

        def move(j):
            load = jnp.sum(bottom[j + 1] * oc[0, j + 1], axis=0, keepdims=True)
            load = jnp.broadcast_to(sh.over_chunks(load), (sub, plan.lanes))
            b = buoy[j]
            syz, szz = crust[SYZ, j], crust[SZZ, j]
            sxy, sxz = crust[SXY, j], crust[SXZ, j]
            ax = crust[SXX, j + 1] - crust[SXX, j - 1] + sh.dy(sxy) + sh.below(sxz) - sh.above(sxz, 0.0)
            ay = crust[SXY, j + 1] - crust[SXY, j - 1] + sh.dy(crust[SYY, j]) + sh.below(syz) - sh.above(syz, 0.0)
            az = crust[SXZ, j + 1] - crust[SXZ, j - 1] + sh.dy(syz) + sh.below(szz) - sh.above(szz, -load)
            crust[VX, j] = crust[VX, j] + b * ax
            crust[VY, j] = crust[VY, j] + b * ay
            crust[VZ, j] = crust[VZ, j] + b * az

        def strain(j):
            vx, vy, vz = crust[VX, j], crust[VY, j], crust[VZ, j]
            exx = crust[VX, j + 1] - crust[VX, j - 1]
            eyy = sh.dy(vy)
            ezz = sh.below(vz) - sh.above(vz, vz)
            mu = shear[j]
            mu2 = mu + mu
            common = lamb[j] * (exx + eyy + ezz)
            crust[SXX, j] = crust[SXX, j] + (common + mu2 * exx)
            crust[SYY, j] = crust[SYY, j] + (common + mu2 * eyy)
            crust[SZZ, j] = crust[SZZ, j] + (common + mu2 * ezz)
            exy = sh.dy(vx) + crust[VY, j + 1] - crust[VY, j - 1]
            exz = sh.below(vx) - sh.above(vx, vx) + crust[VZ, j + 1] - crust[VZ, j - 1]
            eyz = sh.below(vy) - sh.above(vy, vy) + sh.dy(vz)
            crust[SXY, j] = crust[SXY, j] + mu * exy
            crust[SXZ, j] = crust[SXZ, j] + (mu * exz + crust[FAULT, j])
            crust[SYZ, j] = crust[SYZ, j] + mu * eyz

        planes(2 * t, width - 2 * t, flow)
        planes(2 * t + 1, width - 2 * t - 1, press)
        planes(2 * t + 1, width - 2 * t - 1, move)
        planes(2 * t + 2, width - 2 * t - 2, strain)

    def put(x):
        j = HALO + x
        for f in range(9):
            plane = crust[f, j]
            out, at = (vel_out, f) if f < 3 else (stress_out, f - 3)
            for kc in range(chunks):
                out[at, x, kc * sub : (kc + 1) * sub, :] = plane[:, kc * plan.ny : (kc + 1) * plan.ny]

    planes(0, cells, put)
    for group in range(plan.own_groups):
        stacked = jnp.concatenate(
            [
                oc[f, 1 + HALO + group * chunks + i]
                for i in range(chunks)
                for f in range(4)
            ],
            axis=0,
        )
        gather[...] = stacked.T
        for kc in range(chunks):
            for yl in range(strips):
                at = group * plan.lead + kc * strips + yl
                message[pl.ds(at, n, stride=plan.back_rows), :] = gather[
                    pl.ds(kc * plan.ny + yl, n, stride=strips), :
                ]


def unpack_kernel(plan, arrived, ocean, turned):
    sub, chunks = plan.sub, plan.chunks
    block = 4 * sub
    for yl in range(plan.strips):
        by_chunk = [
            arrived[pl.ds(kc * plan.strips + yl, plan.nx // chunks, stride=plan.lead), :]
            for kc in range(chunks)
        ]
        for i in range(chunks):
            turned[pl.ds(i, plan.nx // chunks, stride=chunks), :] = place(
                by_chunk, [i] * chunks, block
            )
        whole = turned[...].T
        for kc in range(chunks):
            for f in range(4):
                at = (kc * 4 + f) * sub
                ocean[f, yl, kc * sub : (kc + 1) * sub, :] = whole[at : at + sub]


def on_device(plan, velocity, stress, ocean, zones, materials, slip, bathy):
    n, cells, sub, lanes = plan.n, plan.cells, plan.sub, plan.lanes
    width = plan.width
    vmem = pl.BlockSpec(memory_space=pltpu.VMEM)
    smem = pl.BlockSpec(memory_space=pltpu.SMEM)
    params = pltpu.CompilerParams(vmem_limit_bytes=56 * 1024 * 1024)
    count = 10 * cells + 1
    crust, message = pl.pallas_call(
        functools.partial(pack_kernel, plan),
        out_shape=(
            jax.ShapeDtypeStruct((count, sub, lanes), F32),
            jax.ShapeDtypeStruct((n * plan.rows, LANES), F32),
        ),
        in_specs=[vmem] * 6,
        out_specs=(vmem, vmem),
        scratch_shapes=[
            pltpu.VMEM((plan.strips, plan.nx, LANES), F32),
            pltpu.VMEM(
                (plan.lead, plan.nx // plan.chunks + 2 * plan.halo_groups, LANES), F32
            ),
            pltpu.VMEM((plan.strips, n, LANES), F32),
        ],
        compiler_params=params,
        name="pack",
    )(velocity, stress, zones, slip, ocean, bathy)
    arrived = lax.all_to_all(
        message.reshape(n, plan.rows, LANES), "map", split_axis=0, concat_axis=0, tiled=True
    ).reshape(n * plan.rows, LANES)
    low = lax.ppermute(crust, "map", [(i, i + 1) for i in range(n - 1)])
    high = lax.ppermute(crust, "map", [(i + 1, i) for i in range(n - 1)])
    out = pl.pallas_call(
        functools.partial(steps_kernel, plan),
        out_shape=(
            jax.ShapeDtypeStruct(velocity.shape, F32),
            jax.ShapeDtypeStruct(stress.shape, F32),
            jax.ShapeDtypeStruct((n * plan.back_rows, LANES), F32),
        ),
        in_specs=[smem] + [vmem] * 4,
        out_specs=(vmem, vmem, vmem),
        scratch_shapes=[
            pltpu.VMEM((10, width, sub, lanes), F32),
            pltpu.VMEM((4, width + 2, sub, lanes), F32),
            pltpu.VMEM((width + 2, sub, lanes), F32),
            pltpu.VMEM((width + 2, sub, lanes), F32),
            pltpu.VMEM((width, sub, lanes), F32),
            pltpu.VMEM((width, sub, lanes), F32),
            pltpu.VMEM((width, sub, lanes), F32),
            pltpu.VMEM((lanes, LANES), F32),
            pltpu.VMEM((32, lanes), F32),
        ],
        compiler_params=params,
        name="substeps",
    )(materials, crust, low, high, arrived)
    new_velocity, new_stress, back = out
    returned = lax.all_to_all(
        back.reshape(n, plan.back_rows, LANES), "map", split_axis=0, concat_axis=0, tiled=True
    ).reshape(n * plan.back_rows, LANES)
    new_ocean = pl.pallas_call(
        functools.partial(unpack_kernel, plan),
        out_shape=jax.ShapeDtypeStruct(ocean.shape, F32),
        in_specs=[vmem],
        out_specs=vmem,
        scratch_shapes=[pltpu.VMEM((plan.nx, LANES), F32)],
        compiler_params=params,
        name="unpack",
    )(returned)
    return new_velocity, new_stress, new_ocean


def solution(mesh):
    n = mesh.shape["map"]

    def body(velocity, stress, ocean, zones, materials, slip, bathy):
        _, cells, depth, ny = velocity.shape
        plan = Plan(n, cells, depth, ny, ocean.shape[1])
        return on_device(plan, velocity, stress, ocean, zones, materials, slip, bathy)

    return jax.shard_map(
        body,
        mesh=mesh,
        in_specs=(
            P("parts", "map", None, None),
            P("parts", "map", None, None),
            P("parts", "map", None, None),
            P("map", "parts", None),
            P(),
            P("map", "parts"),
            P("map", "parts"),
        ),
        out_specs=(
            P("parts", "map", None, None),
            P("parts", "map", None, None),
            P("parts", "map", None, None),
        ),
        check_vma=False,
    )
```

```python
import functools

import jax
import jax.numpy as jnp
from jax import lax
from jax.experimental import pallas as pl
from jax.experimental.pallas import tpu as pltpu
from jax.sharding import PartitionSpec as P

STEPS = 4
ZONES = 8
DT = 0.25
KBULK = 2.25
GRAV = 0.1
HALO = 2 * STEPS
LANES = 128
F32 = jnp.float32


class Plan:
    def __init__(self, devices, cells, depth, ny, strips):
        self.n = devices
        self.cells = cells
        self.depth = depth
        self.ny = ny
        self.strips = strips
        self.chunks = max(1, LANES // ny)
        self.sub = depth // self.chunks
        self.lanes = self.chunks * ny
        self.width = cells + 2 * HALO
        self.own_groups = cells // self.chunks
        self.halo_groups = HALO // self.chunks
        self.groups = self.width // self.chunks
        self.lead = self.chunks * strips
        self.rows = self.lead * (self.groups + 1)
        self.back_rows = self.lead * self.own_groups
        self.nx = devices * cells
        self.unrolled = self.sub * self.lanes <= 1024


BATHY_LANE = 64


def place(pieces, wanted, block):
    out = None
    for i, piece in enumerate(pieces):
        shift = (i - wanted[i]) * block % piece.shape[-1]
        moved = pltpu.roll(piece, shift, piece.ndim - 1) if shift else piece
        if out is None:
            out = moved
        else:
            lane = lax.broadcasted_iota(jnp.int32, moved.shape, moved.ndim - 1)
            out = jnp.where(lane >= i * block, moved, out)
    return out


def pack_kernel(
    plan, vel, stress, zones, slip, ocean, bathy, crust, message, turned, grouped, extra
):
    cells, sub, chunks, ny, n = plan.cells, plan.sub, plan.chunks, plan.ny, plan.n
    strips = plan.strips
    block = 4 * sub
    grouped[...] = jnp.zeros_like(grouped)
    for yl in range(strips):
        stacked = jnp.concatenate(
            [ocean[f, yl, kc * sub : (kc + 1) * sub, :] for kc in range(chunks) for f in range(4)],
            axis=0,
        )
        turned[yl] = stacked.T
        by_x = [turned[yl, pl.ds(i, plan.nx // chunks, stride=chunks), :] for i in range(chunks)]
        for kc in range(chunks):
            grouped[kc * strips + yl, pl.ds(plan.halo_groups, plan.nx // chunks), :] = place(
                by_x, [kc] * chunks, block
            )
    count = n - 2
    lane = lax.broadcasted_iota(jnp.int32, (n, LANES), 1)
    row = lax.broadcasted_iota(jnp.int32, (n, LANES), 0)
    for yl in range(strips):
        depths = bathy[yl : yl + 1, :].astype(F32)
        wide = lax.broadcasted_iota(jnp.int32, depths.shape, 1)
        for d in range(n):
            first = d * cells - HALO - 1
            moved = pltpu.roll(depths, (BATHY_LANE - first) % plan.nx, 1)
            at = wide - BATHY_LANE + first
            moved = jnp.where((at >= 0) & (at < plan.nx), moved, 0.0)
            extra[yl, d : d + 1, :] = moved[:, :LANES]
        edges_low = turned[yl, pl.ds(2 * cells - HALO - 1, count, stride=cells), :]
        edges_high = turned[yl, pl.ds(cells + HALO, count, stride=cells), :]
        low = jnp.concatenate([jnp.zeros((2, LANES), F32), edges_low], axis=0)
        high = jnp.concatenate([edges_high, jnp.zeros((2, LANES), F32)], axis=0)
        for kc in range(chunks):
            low_moved = pltpu.roll(low, (-kc * block) % LANES, 1) if kc else low
            high_moved = pltpu.roll(high, (sub - kc * block) % LANES, 1)
            rest = jnp.where(lane < sub, low_moved, extra[yl])
            rest = jnp.where((lane >= sub) & (lane < 2 * sub), high_moved, rest)
            at = (kc * strips + yl) * (plan.groups + 1) + plan.groups
            message[pl.ds(at, n, stride=plan.rows), :] = rest
    for d in range(n):
        for q in range(plan.lead):
            start = d * plan.rows + q * (plan.groups + 1)
            message[start : start + plan.groups, :] = grouped[
                q, d * plan.own_groups : d * plan.own_groups + plan.groups, :
            ]
    def packed(ref, f, x):
        parts = [ref[f, x, kc * sub : (kc + 1) * sub, :] for kc in range(chunks)]
        return jnp.concatenate(parts, axis=-1) if chunks > 1 else parts[0]

    for f in range(3):
        for x in range(cells):
            crust[f * cells + x] = packed(vel, f, x)
    for f in range(6):
        for x in range(cells):
            crust[(3 + f) * cells + x] = packed(stress, f, x)
    for x in range(cells):
        parts = [zones[x, kc * sub : (kc + 1) * sub, :] for kc in range(chunks)]
        plane = jnp.concatenate(parts, axis=-1) if chunks > 1 else parts[0]
        crust[9 * cells + x] = (plane + 1).astype(F32)
    fault_chunk = (plan.depth // 2) // sub
    pieces = [
        slip[...] if kc == fault_chunk else jnp.zeros((cells, ny), F32) for kc in range(chunks)
    ]
    fault = jnp.concatenate(pieces, axis=-1) if chunks > 1 else pieces[0]
    if sub > cells:
        fault = jnp.concatenate([fault, jnp.zeros((sub - cells, plan.lanes), F32)], axis=0)
    crust[10 * cells] = fault


class Shifts:
    def __init__(self, plan):
        self.plan = plan
        shape = (plan.sub, plan.lanes)
        self.row = lax.broadcasted_iota(jnp.int32, shape, 0)
        self.lane = lax.broadcasted_iota(jnp.int32, shape, 1)
        self.y = lax.rem(self.lane, plan.ny)
        self.first_row = self.row == 0
        self.last_row = self.row == plan.sub - 1
        self.top = self.first_row & (self.lane < plan.ny)
        self.floor_cell = self.last_row & (self.lane >= plan.lanes - plan.ny)
        self.not_low_y = jnp.where(self.y == 0, 0.0, 1.0).astype(F32)
        self.not_high_y = jnp.where(self.y == plan.ny - 1, 0.0, 1.0).astype(F32)
        self.depth = (
            lax.div(self.lane, plan.ny) * plan.sub + self.row
        ).astype(F32)

    def dy(self, f):
        lanes = self.plan.lanes
        return pltpu.roll(f, lanes - 1, 1) * self.not_high_y - pltpu.roll(f, 1, 1) * self.not_low_y

    def below(self, f):
        plan = self.plan
        moved = pltpu.roll(f, plan.sub - 1, 0)
        if plan.chunks > 1:
            moved = jnp.where(self.last_row, pltpu.roll(moved, plan.lanes - plan.ny, 1), moved)
        return jnp.where(self.floor_cell, 0.0, moved)

    def above(self, f, top):
        plan = self.plan
        moved = pltpu.roll(f, 1, 0)
        if plan.chunks > 1:
            moved = jnp.where(self.first_row, pltpu.roll(moved, plan.ny, 1), moved)
        return jnp.where(self.top, top, moved)

    def over_chunks(self, f):
        shift = self.plan.ny
        while shift < self.plan.lanes:
            f = f + pltpu.roll(f, shift, 1)
            shift *= 2
        return f


def steps_kernel(
    plan, mats, own, low, high, arrived, vel_out, stress_out, message,
    crust, oc, water, bottom, buoy, lamb, shear, gather, depths,
):
    cells, sub, chunks, n, strips = plan.cells, plan.sub, plan.chunks, plan.n, plan.strips
    width = plan.width
    sh = Shifts(plan)
    half = 0.5 * DT

    def planes(start, stop, body):
        if plan.unrolled:
            for j in range(start, stop):
                body(j)
        else:
            def run(j, carry):
                body(j)
                return carry

            lax.fori_loop(start, stop, run, 0)

    def turn(group):
        for kc in range(chunks):
            for yl in range(strips):
                at = (kc * strips + yl) * (plan.groups + 1) + group
                gather[pl.ds(kc * plan.ny + yl, n, stride=strips), :] = arrived[
                    pl.ds(at, n, stride=plan.rows), :
                ]
        return gather[...].T

    rest = turn(plan.groups)
    oc[0, 0] = rest[:sub]
    oc[0, width + 1] = rest[sub : 2 * sub]
    depths[...] = rest[BATHY_LANE : BATHY_LANE + depths.shape[0]]
    for group in range(plan.groups):
        turned = turn(group)
        for i in range(chunks):
            for f in range(4):
                at = (i * 4 + f) * sub
                oc[f, 1 + group * chunks + i] = turned[at : at + sub]

    def mask(j):
        deep = jnp.broadcast_to(depths[pl.ds(j, 1), :], (sub, plan.lanes))
        wet = jnp.where(sh.depth < deep, 1.0, 0.0).astype(F32)
        water[j] = wet
        bottom[j] = jnp.where(sh.depth == deep - 1.0, 1.0, 0.0).astype(F32)
        oc[0, j] = oc[0, j] * wet

    def mask_flow(j):
        for f in range(1, 4):
            oc[f, j] = oc[f, j] * water[j]

    planes(0, width + 2, mask)
    planes(1, width + 1, mask_flow)

    for part, ref in enumerate((low, own, high)):
        def bring(x, part=part, ref=ref):
            j = part * cells + x
            for f in range(9):
                crust[f, j] = ref[f * cells + x]
            zone = ref[9 * cells + x]
            values = [jnp.zeros_like(zone) for _ in range(3)]
            for z in range(ZONES):
                here = zone == float(z + 1)
                values = [jnp.where(here, mats[c, z], values[c]) for c in range(3)]
            buoy[j] = values[0] * half
            lamb[j] = values[1] * half
            shear[j] = values[2] * half
            slip = jnp.broadcast_to(ref[10 * cells, pl.ds(x, 1), :], (sub, plan.lanes))
            crust[9, j] = jnp.where(sh.row == (plan.depth // 2) % sub, DT * slip, 0.0)

        planes(0, cells, bring)

    VX, VY, VZ, SXX, SYY, SZZ, SXY, SXZ, SYZ, FAULT = range(10)

    for t in range(STEPS):
        def flow(j):
            p = oc[0, j + 1]
            wet = water[j + 1]
            oc[1, j + 1] = wet * (oc[1, j + 1] - half * (oc[0, j + 2] - oc[0, j]))
            oc[2, j + 1] = wet * (oc[2, j + 1] - half * sh.dy(p))
            rise = sh.below(p) + bottom[j + 1] * p - sh.above(p, -p)
            oc[3, j + 1] = wet * (oc[3, j + 1] - (half * rise + (DT * GRAV) * p))

        def press(j):
            w = oc[3, j + 1]
            floor = jnp.where(sh.top, crust[VZ, j], 0.0)[0:1]
            floor = jnp.broadcast_to(sh.over_chunks(floor), (sub, plan.lanes))
            rise = sh.below(w) + bottom[j + 1] * floor - sh.above(w, w)
            spread = oc[1, j + 2] - oc[1, j] + sh.dy(oc[2, j + 1]) + rise
            oc[0, j + 1] = water[j + 1] * (oc[0, j + 1] - (half * KBULK) * spread)

        def move(j):
            load = jnp.sum(bottom[j + 1] * oc[0, j + 1], axis=0, keepdims=True)
            load = jnp.broadcast_to(sh.over_chunks(load), (sub, plan.lanes))
            b = buoy[j]
            syz, szz = crust[SYZ, j], crust[SZZ, j]
            sxy, sxz = crust[SXY, j], crust[SXZ, j]
            ax = crust[SXX, j + 1] - crust[SXX, j - 1] + sh.dy(sxy) + sh.below(sxz) - sh.above(sxz, 0.0)
            ay = crust[SXY, j + 1] - crust[SXY, j - 1] + sh.dy(crust[SYY, j]) + sh.below(syz) - sh.above(syz, 0.0)
            az = crust[SXZ, j + 1] - crust[SXZ, j - 1] + sh.dy(syz) + sh.below(szz) - sh.above(szz, -load)
            crust[VX, j] = crust[VX, j] + b * ax
            crust[VY, j] = crust[VY, j] + b * ay
            crust[VZ, j] = crust[VZ, j] + b * az

        def strain(j):
            vx, vy, vz = crust[VX, j], crust[VY, j], crust[VZ, j]
            exx = crust[VX, j + 1] - crust[VX, j - 1]
            eyy = sh.dy(vy)
            ezz = sh.below(vz) - sh.above(vz, vz)
            mu = shear[j]
            mu2 = mu + mu
            common = lamb[j] * (exx + eyy + ezz)
            crust[SXX, j] = crust[SXX, j] + (common + mu2 * exx)
            crust[SYY, j] = crust[SYY, j] + (common + mu2 * eyy)
            crust[SZZ, j] = crust[SZZ, j] + (common + mu2 * ezz)
            exy = sh.dy(vx) + crust[VY, j + 1] - crust[VY, j - 1]
            exz = sh.below(vx) - sh.above(vx, vx) + crust[VZ, j + 1] - crust[VZ, j - 1]
            eyz = sh.below(vy) - sh.above(vy, vy) + sh.dy(vz)
            crust[SXY, j] = crust[SXY, j] + mu * exy
            crust[SXZ, j] = crust[SXZ, j] + (mu * exz + crust[FAULT, j])
            crust[SYZ, j] = crust[SYZ, j] + mu * eyz

        planes(2 * t, width - 2 * t, flow)
        planes(2 * t + 1, width - 2 * t - 1, press)
        planes(2 * t + 1, width - 2 * t - 1, move)
        planes(2 * t + 2, width - 2 * t - 2, strain)

    def put(x):
        j = HALO + x
        for f in range(9):
            plane = crust[f, j]
            out, at = (vel_out, f) if f < 3 else (stress_out, f - 3)
            for kc in range(chunks):
                out[at, x, kc * sub : (kc + 1) * sub, :] = plane[:, kc * plan.ny : (kc + 1) * plan.ny]

    planes(0, cells, put)
    for group in range(plan.own_groups):
        stacked = jnp.concatenate(
            [
                oc[f, 1 + HALO + group * chunks + i]
                for i in range(chunks)
                for f in range(4)
            ],
            axis=0,
        )
        gather[...] = stacked.T
        for kc in range(chunks):
            for yl in range(strips):
                at = group * plan.lead + kc * strips + yl
                message[pl.ds(at, n, stride=plan.back_rows), :] = gather[
                    pl.ds(kc * plan.ny + yl, n, stride=strips), :
                ]


def unpack_kernel(plan, arrived, ocean, turned):
    sub, chunks = plan.sub, plan.chunks
    block = 4 * sub
    for yl in range(plan.strips):
        by_chunk = [
            arrived[pl.ds(kc * plan.strips + yl, plan.nx // chunks, stride=plan.lead), :]
            for kc in range(chunks)
        ]
        for i in range(chunks):
            turned[pl.ds(i, plan.nx // chunks, stride=chunks), :] = place(
                by_chunk, [i] * chunks, block
            )
        whole = turned[...].T
        for kc in range(chunks):
            for f in range(4):
                at = (kc * 4 + f) * sub
                ocean[f, yl, kc * sub : (kc + 1) * sub, :] = whole[at : at + sub]


def on_device(plan, velocity, stress, ocean, zones, materials, slip, bathy):
    n, cells, sub, lanes = plan.n, plan.cells, plan.sub, plan.lanes
    width = plan.width
    vmem = pl.BlockSpec(memory_space=pltpu.VMEM)
    smem = pl.BlockSpec(memory_space=pltpu.SMEM)
    params = pltpu.CompilerParams(vmem_limit_bytes=(16 if plan.unrolled else 56) * 1024 * 1024)
    count = 10 * cells + 1
    crust, message = pl.pallas_call(
        functools.partial(pack_kernel, plan),
        out_shape=(
            jax.ShapeDtypeStruct((count, sub, lanes), F32),
            jax.ShapeDtypeStruct((n * plan.rows, LANES), F32),
        ),
        in_specs=[vmem] * 6,
        out_specs=(vmem, vmem),
        scratch_shapes=[
            pltpu.VMEM((plan.strips, plan.nx, LANES), F32),
            pltpu.VMEM(
                (plan.lead, plan.nx // plan.chunks + 2 * plan.halo_groups, LANES), F32
            ),
            pltpu.VMEM((plan.strips, n, LANES), F32),
        ],
        compiler_params=params,
        name="pack",
    )(velocity, stress, zones, slip, ocean, bathy)
    arrived = lax.all_to_all(
        message.reshape(n, plan.rows, LANES), "map", split_axis=0, concat_axis=0, tiled=True
    ).reshape(n * plan.rows, LANES)
    low = lax.ppermute(crust, "map", [(i, i + 1) for i in range(n - 1)])
    high = lax.ppermute(crust, "map", [(i + 1, i) for i in range(n - 1)])
    out = pl.pallas_call(
        functools.partial(steps_kernel, plan),
        out_shape=(
            jax.ShapeDtypeStruct(velocity.shape, F32),
            jax.ShapeDtypeStruct(stress.shape, F32),
            jax.ShapeDtypeStruct((n * plan.back_rows, LANES), F32),
        ),
        in_specs=[smem] + [vmem] * 4,
        out_specs=(vmem, vmem, vmem),
        scratch_shapes=[
            pltpu.VMEM((10, width, sub, lanes), F32),
            pltpu.VMEM((4, width + 2, sub, lanes), F32),
            pltpu.VMEM((width + 2, sub, lanes), F32),
            pltpu.VMEM((width + 2, sub, lanes), F32),
            pltpu.VMEM((width, sub, lanes), F32),
            pltpu.VMEM((width, sub, lanes), F32),
            pltpu.VMEM((width, sub, lanes), F32),
            pltpu.VMEM((lanes, LANES), F32),
            pltpu.VMEM((32, lanes), F32),
        ],
        compiler_params=params,
        name="substeps",
    )(materials, crust, low, high, arrived)
    new_velocity, new_stress, back = out
    returned = lax.all_to_all(
        back.reshape(n, plan.back_rows, LANES), "map", split_axis=0, concat_axis=0, tiled=True
    ).reshape(n * plan.back_rows, LANES)
    new_ocean = pl.pallas_call(
        functools.partial(unpack_kernel, plan),
        out_shape=jax.ShapeDtypeStruct(ocean.shape, F32),
        in_specs=[vmem],
        out_specs=vmem,
        scratch_shapes=[pltpu.VMEM((plan.nx, LANES), F32)],
        compiler_params=params,
        name="unpack",
    )(returned)
    return new_velocity, new_stress, new_ocean


def solution(mesh):
    n = mesh.shape["map"]

    def body(velocity, stress, ocean, zones, materials, slip, bathy):
        _, cells, depth, ny = velocity.shape
        plan = Plan(n, cells, depth, ny, ocean.shape[1])
        return on_device(plan, velocity, stress, ocean, zones, materials, slip, bathy)

    return jax.shard_map(
        body,
        mesh=mesh,
        in_specs=(
            P("parts", "map", None, None),
            P("parts", "map", None, None),
            P("parts", "map", None, None),
            P("map", "parts", None),
            P(),
            P("map", "parts"),
            P("map", "parts"),
        ),
        out_specs=(
            P("parts", "map", None, None),
            P("parts", "map", None, None),
            P("parts", "map", None, None),
        ),
        check_vma=False,
    )
```

```python
import functools

import jax
import jax.numpy as jnp
from jax import lax
from jax.experimental import pallas as pl
from jax.experimental.pallas import tpu as pltpu
from jax.sharding import PartitionSpec as P

STEPS = 4
ZONES = 8
DT = 0.25
HALF = 0.5 * DT
KBULK = 2.25
GRAV = 0.1
HALO = 2 * STEPS
LANES = 128
F32 = jnp.float32
VX, VY, VZ = range(3)
SXX, SYY, SZZ, SXY, SXZ, SYZ = range(6)
BUOY, LAMB, SHEAR, FAULT, FLOOR = range(5)


class Plan:
    def __init__(self, devices, cells, depth, ny, strips):
        self.n = devices
        self.cells = cells
        self.depth = depth
        self.ny = ny
        self.strips = strips
        self.chunks = max(1, LANES // ny)
        self.sub = depth // self.chunks
        self.lanes = self.chunks * ny
        self.width = cells + 2 * HALO
        self.own_groups = cells // self.chunks
        self.halo_groups = HALO // self.chunks
        self.sent_groups = self.own_groups + self.halo_groups
        self.lead = self.chunks * strips
        self.rows = self.lead * self.sent_groups
        self.back_rows = self.lead * self.own_groups
        self.nx = devices * cells
        self.block = 4 * self.sub
        self.unrolled = self.sub * self.lanes <= 1024
        assert devices % 2 == 0 and cells == HALO and self.block * self.chunks == LANES

    def planes(self, start, stop, body):
        if self.unrolled:
            for j in range(start, stop):
                body(j)
        else:
            def run(j, carry):
                body(j)
                return carry

            lax.fori_loop(start, stop, run, 0)


def odd_device():
    return lax.rem(lax.axis_index("map"), 2)


def place(pieces, wanted, block):
    out = None
    for i, piece in enumerate(pieces):
        shift = (i - wanted[i]) * block % piece.shape[-1]
        moved = pltpu.roll(piece, shift, piece.ndim - 1) if shift else piece
        if out is None:
            out = moved
        else:
            lane = lax.broadcasted_iota(jnp.int32, moved.shape, moved.ndim - 1)
            out = jnp.where(lane >= i * block, moved, out)
    return out


def ocean_kernel(plan, ocean_ref, bathy_ref, message, ocean, bathy, turned, grouped, extra, sems):
    cells, sub, chunks, n, strips = plan.cells, plan.sub, plan.chunks, plan.n, plan.strips
    block, sent, rows = plan.block, plan.sent_groups, plan.rows
    copies = [
        pltpu.make_async_copy(ocean_ref, ocean, sems.at[0]),
        pltpu.make_async_copy(bathy_ref, bathy, sems.at[1]),
    ]
    for copy in copies:
        copy.start()
    for copy in copies:
        copy.wait()
    border = jnp.zeros((plan.lead, plan.halo_groups, LANES), F32)
    count = plan.nx // chunks
    grouped[:, : plan.halo_groups, :] = border
    grouped[:, plan.halo_groups + count :, :] = border
    for yl in range(strips):
        stacked = jnp.concatenate(
            [ocean[f, yl, kc * sub : (kc + 1) * sub, :] for kc in range(chunks) for f in range(4)],
            axis=0,
        )
        turned[yl] = stacked.T
        by_x = [turned[yl, pl.ds(i, count, stride=chunks), :] for i in range(chunks)]
        for kc in range(chunks):
            grouped[kc * strips + yl, pl.ds(plan.halo_groups, count), :] = place(
                by_x, [kc] * chunks, block
            )
    for d in range(n):
        start = d * plan.own_groups + (d % 2) * plan.halo_groups
        for q in range(plan.lead):
            message[d * rows + q * sent : d * rows + (q + 1) * sent, :] = grouped[
                q, start : start + sent, :
            ]
    depths = bathy[...].astype(F32)
    wide = lax.broadcasted_iota(jnp.int32, depths.shape, 1)
    for d in range(n):
        first = d * cells - HALO - 1
        moved = pltpu.roll(depths, -first % plan.nx, 1)
        moved = jnp.where((wide + first >= 0) & (wide + first < plan.nx), moved, 0.0)
        extra[d * strips : (d + 1) * strips, :] = moved[:, :LANES]
    pairs = n // 2
    lane = lax.broadcasted_iota(jnp.int32, (pairs, LANES), 1)
    blank = jnp.zeros((1, LANES), F32)
    for odd in range(2):
        slot = (odd * (chunks - 1) * 4 + 2) * sub
        group = odd * (sent - 1)
        for yl in range(strips):
            if odd:
                column = turned[yl, pl.ds(2 * cells + HALO, pairs - 1, stride=2 * cells), :]
                column = jnp.concatenate([column, blank], axis=0)
            else:
                column = turned[yl, pl.ds(2 * cells - HALO - 1, pairs - 1, stride=2 * cells), :]
                column = jnp.concatenate([blank, column], axis=0)
            deep = extra[pl.ds(odd * strips + yl, pairs, stride=2 * strips), :]
            for kc in range(chunks):
                at = odd * rows + (kc * strips + yl) * sent + group
                old = message[pl.ds(at, pairs, stride=2 * rows), :]
                edge = pltpu.roll(column, (slot - kc * block) % LANES, 1)
                floor = pltpu.roll(deep, (slot + sub - kc * sub) % LANES, 1)
                new = jnp.where((lane >= slot) & (lane < slot + sub), edge, old)
                new = jnp.where((lane >= slot + sub) & (lane < slot + 2 * sub), floor, new)
                message[pl.ds(at, pairs, stride=2 * rows), :] = new


def crust_kernel(
    plan, vel_ref, stress_ref, zones_ref, slip_ref, _, crust, vel, stress, zones, slip, sems
):
    cells, sub, chunks, ny = plan.cells, plan.sub, plan.chunks, plan.ny
    copies = [
        pltpu.make_async_copy(source, target, sems.at[i])
        for i, (source, target) in enumerate(
            ((vel_ref, vel), (stress_ref, stress), (zones_ref, zones), (slip_ref, slip))
        )
    ]
    for copy in copies:
        copy.start()

    def joined(ref, *at):
        parts = [ref[(*at, pl.ds(kc * sub, sub), slice(None))] for kc in range(chunks)]
        return jnp.concatenate(parts, axis=-1) if chunks > 1 else parts[0]

    copies[0].wait()
    for f in range(3):
        for x in range(cells):
            crust[f * cells + x] = joined(vel, f, x)
    copies[1].wait()
    for f in range(6):
        for x in range(cells):
            crust[(3 + f) * cells + x] = joined(stress, f, x)
    copies[2].wait()
    for x in range(cells):
        crust[9 * cells + x] = (joined(zones, x) + 1).astype(F32)
    copies[3].wait()
    fault_chunk = (plan.depth // 2) // sub
    pieces = [
        slip[...] if kc == fault_chunk else jnp.zeros((cells, ny), F32) for kc in range(chunks)
    ]
    fault = jnp.concatenate(pieces, axis=-1) if chunks > 1 else pieces[0]
    if sub > cells:
        fault = jnp.concatenate([fault, jnp.zeros((sub - cells, plan.lanes), F32)], axis=0)
    crust[10 * cells] = fault


class Shifts:
    def __init__(self, plan):
        self.plan = plan
        shape = (plan.sub, plan.lanes)
        self.row = lax.broadcasted_iota(jnp.int32, shape, 0)
        self.lane = lax.broadcasted_iota(jnp.int32, shape, 1)
        self.y = lax.rem(self.lane, plan.ny)
        self.first_row = self.row == 0
        self.last_row = self.row == plan.sub - 1
        self.top = self.first_row & (self.lane < plan.ny)
        self.floor_cell = self.last_row & (self.lane >= plan.lanes - plan.ny)
        self.not_low_y = jnp.where(self.y == 0, 0.0, 1.0).astype(F32)
        self.not_high_y = jnp.where(self.y == plan.ny - 1, 0.0, 1.0).astype(F32)
        self.depth = (
            lax.div(self.lane, plan.ny) * plan.sub + self.row
        ).astype(F32)

    def dy(self, f):
        lanes = self.plan.lanes
        return pltpu.roll(f, lanes - 1, 1) * self.not_high_y - pltpu.roll(f, 1, 1) * self.not_low_y

    def below(self, f):
        plan = self.plan
        moved = pltpu.roll(f, plan.sub - 1, 0)
        if plan.chunks > 1:
            moved = jnp.where(self.last_row, pltpu.roll(moved, plan.lanes - plan.ny, 1), moved)
        return jnp.where(self.floor_cell, 0.0, moved)

    def above(self, f, top):
        plan = self.plan
        moved = pltpu.roll(f, 1, 0)
        if plan.chunks > 1:
            moved = jnp.where(self.first_row, pltpu.roll(moved, plan.ny, 1), moved)
        return jnp.where(self.top, top, moved)

    def seafloor(self, vz):
        row = self.over_chunks(jnp.where(self.top, vz, 0.0)[0:1])
        return jnp.broadcast_to(row, vz.shape)

    def over_chunks(self, f):
        shift = self.plan.ny
        while shift < self.plan.lanes:
            f = f + pltpu.roll(f, shift, 1)
            shift *= 2
        return f


def acceleration(sh, stress, j):
    sxy, sxz = stress[SXY, j], stress[SXZ, j]
    syz, szz = stress[SYZ, j], stress[SZZ, j]
    ax = stress[SXX, j + 1] - stress[SXX, j - 1] + sh.dy(sxy) + sh.below(sxz) - sh.above(sxz, 0.0)
    ay = stress[SXY, j + 1] - stress[SXY, j - 1] + sh.dy(stress[SYY, j])
    ay = ay + sh.below(syz) - sh.above(syz, 0.0)
    az = stress[SXZ, j + 1] - stress[SXZ, j - 1] + sh.dy(syz) + sh.below(szz) - sh.above(szz, 0.0)
    return ax, ay, az


def strained(sh, vel, stress, mats, j):
    vx, vy, vz = vel[VX, j], vel[VY, j], vel[VZ, j]
    exx = vel[VX, j + 1] - vel[VX, j - 1]
    eyy = sh.dy(vy)
    ezz = sh.below(vz) - sh.above(vz, vz)
    mu = mats[SHEAR, j]
    mu2 = mu + mu
    common = mats[LAMB, j] * (exx + eyy + ezz)
    exy = sh.dy(vx) + vel[VY, j + 1] - vel[VY, j - 1]
    exz = sh.below(vx) - sh.above(vx, vx) + vel[VZ, j + 1] - vel[VZ, j - 1]
    eyz = sh.below(vy) - sh.above(vy, vy) + sh.dy(vz)
    return (
        stress[SXX, j] + (common + mu2 * exx),
        stress[SYY, j] + (common + mu2 * eyy),
        stress[SZZ, j] + (common + mu2 * ezz),
        stress[SXY, j] + mu * exy,
        stress[SXZ, j] + (mu * exz + mats[FAULT, j]),
        stress[SYZ, j] + mu * eyz,
    )


def begin_kernel(plan, table, own, mate, other, vel, stress, mats):
    cells, sub = plan.cells, plan.sub
    sh = Shifts(plan)
    odd = odd_device()
    starts = (HALO, (HALO + cells) * (1 - odd), (HALO + cells) * odd)
    for start, ref in zip(starts, (own, mate, other)):
        def bring(x, start=start, ref=ref):
            j = start + x
            for f in range(3):
                vel[f, j] = ref[f * cells + x]
            for f in range(6):
                stress[f, j] = ref[(3 + f) * cells + x]
            zone = ref[9 * cells + x]
            values = [jnp.zeros_like(zone) for _ in range(3)]
            for z in range(ZONES):
                here = zone == float(z + 1)
                values = [jnp.where(here, table[c, z], values[c]) for c in range(3)]
            for c in range(3):
                mats[c, j] = values[c] * HALF
            slip = jnp.broadcast_to(ref[10 * cells, pl.ds(x, 1), :], (sub, plan.lanes))
            mats[FAULT, j] = jnp.where(sh.row == (plan.depth // 2) % sub, DT * slip, 0.0)
            mats[FLOOR, j] = sh.seafloor(ref[VZ * cells + x])

        plan.planes(0, cells, bring)

    def move(j):
        b = mats[BUOY, j]
        for f, a in enumerate(acceleration(sh, stress, j)):
            vel[f, j] = vel[f, j] + b * a

    plan.planes(1, plan.width - 1, move)


def middle_kernel(
    plan, arrived, swapped, vel_in, stress_in, mats, vel, stress, loads, message,
    oc, water, bottom, gather, depths,
):
    sub, chunks, n, strips = plan.sub, plan.chunks, plan.n, plan.strips
    width, sent = plan.width, plan.sent_groups
    sh = Shifts(plan)
    odd = odd_device()

    def turn(ref, group):
        for kc in range(chunks):
            for yl in range(strips):
                at = (kc * strips + yl) * sent + group
                gather[pl.ds(kc * plan.ny + yl, n, stride=strips), :] = ref[
                    pl.ds(at, n, stride=plan.rows), :
                ]
        return gather[...].T

    def spread(turned, group):
        for i in range(chunks):
            for f in range(4):
                at = (i * 4 + f) * sub
                oc[f, 1 + group * chunks + i] = turned[at : at + sub]

    ends = []
    for group in range(sent):
        turned = turn(arrived, group)
        spread(turned, group + plan.halo_groups * odd)
        if group == 0:
            ends.append((turned[2 * sub : 3 * sub], turned[3 * sub : 4 * sub]))
        if group == sent - 1:
            ends.append((turned[LANES - 2 * sub : LANES - sub], turned[LANES - sub :]))
    for group in range(plan.halo_groups):
        spread(turn(swapped, group + plan.own_groups * odd), group + sent * (1 - odd))
    turned = turn(swapped, plan.own_groups - odd)
    is_odd = odd == 1
    oc[0, (width + 1) * odd] = jnp.where(is_odd, ends[1][0], ends[0][0])
    oc[0, (width + 1) * (1 - odd)] = jnp.where(
        is_odd, turned[LANES - 4 * sub : LANES - 3 * sub], turned[:sub]
    )
    deep = jnp.where(is_odd, ends[1][1], ends[0][1])
    for kc in range(chunks):
        mine = (sh.lane >= kc * plan.ny) & (sh.lane < (kc + 1) * plan.ny)
        depths[kc * sub : (kc + 1) * sub, :] = sh.over_chunks(jnp.where(mine, deep, 0.0))

    def mask(j):
        low = jnp.broadcast_to(depths[pl.ds(j, 1), :], (sub, plan.lanes))
        wet = jnp.where(sh.depth < low, 1.0, 0.0).astype(F32)
        water[j] = wet
        bottom[j] = jnp.where(sh.depth == low - 1.0, 1.0, 0.0).astype(F32)
        oc[0, j] = oc[0, j] * wet

    def mask_x(j):
        oc[1, j] = oc[1, j] * water[j]

    def mask_yw(j):
        oc[2, j] = oc[2, j] * water[j]
        oc[3, j] = oc[3, j] * water[j]

    plan.planes(0, width + 2, mask)
    plan.planes(1, width + 1, mask_x)
    plan.planes(2, width, mask_yw)

    for t in range(STEPS):
        first, last = 2 * t, width - 2 * t
        before = t == 0

        def flow_x(j):
            oc[1, j + 1] = water[j + 1] * (oc[1, j + 1] - HALF * (oc[0, j + 2] - oc[0, j]))

        def flow(j):
            p = oc[0, j + 1]
            wet = water[j + 1]
            oc[2, j + 1] = wet * (oc[2, j + 1] - HALF * sh.dy(p))
            rise = sh.below(p) + bottom[j + 1] * p - sh.above(p, -p)
            oc[3, j + 1] = wet * (oc[3, j + 1] - (HALF * rise + (DT * GRAV) * p))

        def press(j):
            w = oc[3, j + 1]
            floor = mats[FLOOR, j] if before else sh.seafloor(vel[VZ, j])
            rise = sh.below(w) + bottom[j + 1] * floor - sh.above(w, w)
            total = oc[1, j + 2] - oc[1, j] + sh.dy(oc[2, j + 1]) + rise
            oc[0, j + 1] = water[j + 1] * (oc[0, j + 1] - (HALF * KBULK) * total)

        def load(j):
            column = jnp.sum(bottom[j + 1] * oc[0, j + 1], axis=0, keepdims=True)
            column = jnp.broadcast_to(sh.over_chunks(column), (sub, plan.lanes))
            return jnp.where(sh.top, column, 0.0)

        plan.planes(first, last, flow_x)
        plan.planes(first + 1, last - 1, flow)
        plan.planes(first + 1, last - 1, press)
        if before:
            def add_load(j):
                for f in (VX, VY):
                    vel[f, j] = vel_in[f, j]
                vel[VZ, j] = vel_in[VZ, j] + mats[BUOY, j] * load(j)

            plan.planes(first + 1, last - 1, add_load)
        elif t < STEPS - 1:
            def move(j):
                ax, ay, az = acceleration(sh, stress, j)
                b = mats[BUOY, j]
                vel[VX, j] = vel[VX, j] + b * ax
                vel[VY, j] = vel[VY, j] + b * ay
                vel[VZ, j] = vel[VZ, j] + b * (az + load(j))

            plan.planes(first + 1, last - 1, move)
        else:
            def keep(j):
                loads[j] = load(j)

            plan.planes(first + 1, last - 1, keep)
        if t < STEPS - 2:
            def strain(j):
                source = stress_in if before else stress
                for f, value in enumerate(strained(sh, vel, source, mats, j)):
                    stress[f, j] = value

            plan.planes(first + 2, last - 2, strain)

    for group in range(plan.own_groups):
        stacked = jnp.concatenate(
            [
                oc[f, 1 + HALO + group * chunks + i]
                for i in range(chunks)
                for f in range(4)
            ],
            axis=0,
        )
        gather[...] = stacked.T
        for kc in range(chunks):
            for yl in range(strips):
                at = group * plan.lead + kc * strips + yl
                message[pl.ds(at, n, stride=plan.back_rows), :] = gather[
                    pl.ds(kc * plan.ny + yl, n, stride=strips), :
                ]


def end_kernel(plan, vel_in, stress_in, mats, loads, vel_out, stress_out, vel, stress):
    cells, sub, chunks, ny = plan.cells, plan.sub, plan.chunks, plan.ny
    sh = Shifts(plan)
    first, last = 2 * (STEPS - 1), plan.width - 2 * (STEPS - 1)

    def put(out, f, x, plane):
        for kc in range(chunks):
            out[f, x, kc * sub : (kc + 1) * sub, :] = plane[:, kc * ny : (kc + 1) * ny]

    def strain(j):
        for f, value in enumerate(strained(sh, vel_in, stress_in, mats, j)):
            stress[f, j] = value

    def move(j):
        ax, ay, az = acceleration(sh, stress, j)
        b = mats[BUOY, j]
        for f, a in enumerate((ax, ay, az + loads[j])):
            vel[f, j] = vel_in[f, j] + b * a

    def finish(x):
        for f in range(3):
            put(vel_out, f, x, vel[f, x + HALO])
        for f, value in enumerate(strained(sh, vel, stress, mats, x + HALO)):
            put(stress_out, f, x, value)

    plan.planes(first, last, strain)
    plan.planes(first + 1, last - 1, move)
    plan.planes(0, cells, finish)


def unpack_kernel(plan, arrived, ocean, turned):
    sub, chunks = plan.sub, plan.chunks
    block = 4 * sub
    for yl in range(plan.strips):
        by_chunk = [
            arrived[pl.ds(kc * plan.strips + yl, plan.nx // chunks, stride=plan.lead), :]
            for kc in range(chunks)
        ]
        for i in range(chunks):
            turned[pl.ds(i, plan.nx // chunks, stride=chunks), :] = place(
                by_chunk, [i] * chunks, block
            )
        whole = turned[...].T
        for kc in range(chunks):
            for f in range(4):
                at = (kc * 4 + f) * sub
                ocean[f, yl, kc * sub : (kc + 1) * sub, :] = whole[at : at + sub]


def on_device(plan, velocity, stress, ocean, zones, materials, slip, bathy):
    n, cells, sub, lanes, width = plan.n, plan.cells, plan.sub, plan.lanes, plan.width
    vmem = pl.BlockSpec(memory_space=pltpu.VMEM)
    smem = pl.BlockSpec(memory_space=pltpu.SMEM)
    hbm = pl.BlockSpec(memory_space=pltpu.HBM)

    def shape(*dims):
        return jax.ShapeDtypeStruct(dims, F32)

    def like(array):
        return pltpu.VMEM(array.shape, array.dtype)

    def call(kernel, name, out, ins, scratch, room=16, **rest):
        room = room if plan.unrolled else 56
        return pl.pallas_call(
            functools.partial(kernel, plan),
            out_shape=out,
            in_specs=ins,
            out_specs=jax.tree.map(lambda _: vmem, out),
            scratch_shapes=scratch,
            compiler_params=pltpu.CompilerParams(vmem_limit_bytes=room * 1024 * 1024),
            name=name,
            **rest,
        )

    def exchange(rows, count):
        whole = rows.reshape(n, count, LANES)
        moved = lax.all_to_all(whole, "map", split_axis=0, concat_axis=0, tiled=True)
        return moved.reshape(n * count, LANES)

    message = call(
        ocean_kernel,
        "ocean_rows",
        shape(n * plan.rows, LANES),
        [hbm] * 2,
        [
            like(ocean),
            like(bathy),
            pltpu.VMEM((plan.strips, plan.nx, LANES), F32),
            pltpu.VMEM(
                (plan.lead, plan.nx // plan.chunks + 2 * plan.halo_groups, LANES), F32
            ),
            pltpu.VMEM((n * plan.strips, LANES), F32),
            pltpu.SemaphoreType.DMA((2,)),
        ],
        room=56,
    )(ocean, bathy)
    arrived = exchange(message, plan.rows)
    crust = call(
        crust_kernel,
        "crust_planes",
        shape(10 * cells + 1, sub, lanes),
        [hbm] * 4 + [pl.BlockSpec(memory_space=pl.ANY)],
        [like(velocity), like(stress), like(zones), like(slip), pltpu.SemaphoreType.DMA((4,))],
        room=56,
    )(velocity, stress, zones, slip, message)
    mates = [(i, i ^ 1) for i in range(n)]
    others = [(i, i + 1) for i in range(1, n - 1, 2)]
    others += [(target, source) for source, target in others]
    other = lax.ppermute(crust, "map", others)
    mate = lax.ppermute(crust, "map", mates)
    vel, strs, mats = call(
        begin_kernel,
        "first_velocity",
        (shape(3, width, sub, lanes), shape(6, width, sub, lanes), shape(5, width, sub, lanes)),
        [smem] + [vmem] * 3,
        [],
    )(materials, crust, mate, other)
    swapped = lax.ppermute(arrived, "map", mates)
    vel, strs, loads, back = call(
        middle_kernel,
        "substeps",
        (
            shape(3, width, sub, lanes),
            shape(6, width, sub, lanes),
            shape(width, sub, lanes),
            shape(n * plan.back_rows, LANES),
        ),
        [vmem] * 5,
        [
            pltpu.VMEM((4, width + 2, sub, lanes), F32),
            pltpu.VMEM((width + 2, sub, lanes), F32),
            pltpu.VMEM((width + 2, sub, lanes), F32),
            pltpu.VMEM((lanes, LANES), F32),
            pltpu.VMEM((plan.depth, lanes), F32),
        ],
        input_output_aliases={2: 0, 3: 1},
    )(arrived, swapped, vel, strs, mats)
    returned = exchange(back, plan.back_rows)
    new_velocity, new_stress = call(
        end_kernel,
        "last_updates",
        (shape(*velocity.shape), shape(*stress.shape)),
        [vmem] * 4,
        [
            pltpu.VMEM((3, width, sub, lanes), F32),
            pltpu.VMEM((6, width, sub, lanes), F32),
        ],
    )(vel, strs, mats, loads)
    new_ocean = call(
        unpack_kernel,
        "ocean_strips",
        shape(*ocean.shape),
        [vmem],
        [pltpu.VMEM((plan.nx, LANES), F32)],
    )(returned)
    return new_velocity, new_stress, new_ocean


def solution(mesh):
    n = mesh.shape["map"]

    def body(velocity, stress, ocean, zones, materials, slip, bathy):
        _, cells, depth, ny = velocity.shape
        plan = Plan(n, cells, depth, ny, ocean.shape[1])
        return on_device(plan, velocity, stress, ocean, zones, materials, slip, bathy)

    return jax.shard_map(
        body,
        mesh=mesh,
        in_specs=(
            P("parts", "map", None, None),
            P("parts", "map", None, None),
            P("parts", "map", None, None),
            P("map", "parts", None),
            P(),
            P("map", "parts"),
            P("map", "parts"),
        ),
        out_specs=(
            P("parts", "map", None, None),
            P("parts", "map", None, None),
            P("parts", "map", None, None),
        ),
        check_vma=False,
    )
```

```python
import functools

import jax
import jax.numpy as jnp
from jax import lax
from jax.experimental import pallas as pl
from jax.experimental.pallas import tpu as pltpu
from jax.sharding import PartitionSpec as P

STEPS = 4
ZONES = 8
DT = 0.25
HALF = 0.5 * DT
KBULK = 2.25
GRAV = 0.1
HALO = 2 * STEPS
LANES = 128
F32 = jnp.float32
VX, VY, VZ = range(3)
SXX, SYY, SZZ, SXY, SXZ, SYZ = range(6)
BUOY, LAMB, SHEAR, FAULT, FLOOR = range(5)


class Plan:
    def __init__(self, devices, cells, depth, ny, strips):
        self.n = devices
        self.cells = cells
        self.depth = depth
        self.ny = ny
        self.strips = strips
        self.chunks = max(1, LANES // ny)
        self.sub = depth // self.chunks
        self.lanes = self.chunks * ny
        self.width = cells + 2 * HALO
        self.own_groups = cells // self.chunks
        self.halo_groups = HALO // self.chunks
        self.sent_groups = self.own_groups + self.halo_groups
        self.lead = self.chunks * strips
        self.rows = self.lead * self.sent_groups
        self.back_rows = self.lead * self.own_groups
        self.nx = devices * cells
        self.block = 4 * self.sub
        self.unrolled = self.sub * self.lanes <= 1024
        assert devices % 2 == 0 and cells == HALO and self.block * self.chunks == LANES

    def planes(self, start, stop, body):
        if self.unrolled:
            for j in range(start, stop):
                body(j)
        else:
            def run(j, carry):
                body(j)
                return carry

            lax.fori_loop(start, stop, run, 0)


def odd_device():
    return lax.rem(lax.axis_index("map"), 2)


def place(pieces, wanted, block):
    out = None
    for i, piece in enumerate(pieces):
        shift = (i - wanted[i]) * block % piece.shape[-1]
        moved = pltpu.roll(piece, shift, piece.ndim - 1) if shift else piece
        if out is None:
            out = moved
        else:
            lane = lax.broadcasted_iota(jnp.int32, moved.shape, moved.ndim - 1)
            out = jnp.where(lane >= i * block, moved, out)
    return out


def ocean_kernel(plan, ocean, bathy, message, turned, grouped, extra):
    cells, sub, chunks, n, strips = plan.cells, plan.sub, plan.chunks, plan.n, plan.strips
    block, sent, rows = plan.block, plan.sent_groups, plan.rows
    border = jnp.zeros((plan.lead, plan.halo_groups, LANES), F32)
    count = plan.nx // chunks
    grouped[:, : plan.halo_groups, :] = border
    grouped[:, plan.halo_groups + count :, :] = border
    for yl in range(strips):
        stacked = jnp.concatenate(
            [ocean[f, yl, kc * sub : (kc + 1) * sub, :] for kc in range(chunks) for f in range(4)],
            axis=0,
        )
        turned[yl] = stacked.T
        by_x = [turned[yl, pl.ds(i, count, stride=chunks), :] for i in range(chunks)]
        for kc in range(chunks):
            grouped[kc * strips + yl, pl.ds(plan.halo_groups, count), :] = place(
                by_x, [kc] * chunks, block
            )
    for d in range(n):
        start = d * plan.own_groups + (d % 2) * plan.halo_groups
        for q in range(plan.lead):
            message[d * rows + q * sent : d * rows + (q + 1) * sent, :] = grouped[
                q, start : start + sent, :
            ]
    depths = bathy[...].astype(F32)
    wide = lax.broadcasted_iota(jnp.int32, depths.shape, 1)
    for d in range(n):
        first = d * cells - HALO - 1
        moved = pltpu.roll(depths, -first % plan.nx, 1)
        moved = jnp.where((wide + first >= 0) & (wide + first < plan.nx), moved, 0.0)
        extra[d * strips : (d + 1) * strips, :] = moved[:, :LANES]
    pairs = n // 2
    lane = lax.broadcasted_iota(jnp.int32, (pairs, LANES), 1)
    blank = jnp.zeros((1, LANES), F32)
    for odd in range(2):
        slot = (odd * (chunks - 1) * 4 + 2) * sub
        group = odd * (sent - 1)
        for yl in range(strips):
            if odd:
                column = turned[yl, pl.ds(2 * cells + HALO, pairs - 1, stride=2 * cells), :]
                column = jnp.concatenate([column, blank], axis=0)
            else:
                column = turned[yl, pl.ds(2 * cells - HALO - 1, pairs - 1, stride=2 * cells), :]
                column = jnp.concatenate([blank, column], axis=0)
            deep = extra[pl.ds(odd * strips + yl, pairs, stride=2 * strips), :]
            for kc in range(chunks):
                at = odd * rows + (kc * strips + yl) * sent + group
                old = message[pl.ds(at, pairs, stride=2 * rows), :]
                edge = pltpu.roll(column, (slot - kc * block) % LANES, 1)
                floor = pltpu.roll(deep, (slot + sub - kc * sub) % LANES, 1)
                new = jnp.where((lane >= slot) & (lane < slot + sub), edge, old)
                new = jnp.where((lane >= slot + sub) & (lane < slot + 2 * sub), floor, new)
                message[pl.ds(at, pairs, stride=2 * rows), :] = new


def crust_kernel(
    plan, vel_ref, stress_ref, zones_ref, slip_ref, ocean_ref, bathy_ref,
    crust, ocean, bathy, vel, stress, zones, slip, sems,
):
    cells, sub, chunks, ny = plan.cells, plan.sub, plan.chunks, plan.ny
    pairs = (
        (vel_ref, vel),
        (stress_ref, stress),
        (zones_ref, zones),
        (slip_ref, slip),
        (ocean_ref, ocean),
        (bathy_ref, bathy),
    )
    copies = [
        pltpu.make_async_copy(source, target, sems.at[i])
        for i, (source, target) in enumerate(pairs)
    ]
    for copy in copies:
        copy.start()

    def joined(ref, *at):
        parts = [ref[(*at, pl.ds(kc * sub, sub), slice(None))] for kc in range(chunks)]
        return jnp.concatenate(parts, axis=-1) if chunks > 1 else parts[0]

    copies[0].wait()
    for f in range(3):
        for x in range(cells):
            crust[f * cells + x] = joined(vel, f, x)
    copies[1].wait()
    for f in range(6):
        for x in range(cells):
            crust[(3 + f) * cells + x] = joined(stress, f, x)
    copies[2].wait()
    for x in range(cells):
        crust[9 * cells + x] = (joined(zones, x) + 1).astype(F32)
    copies[3].wait()
    fault_chunk = (plan.depth // 2) // sub
    pieces = [
        slip[...] if kc == fault_chunk else jnp.zeros((cells, ny), F32) for kc in range(chunks)
    ]
    fault = jnp.concatenate(pieces, axis=-1) if chunks > 1 else pieces[0]
    if sub > cells:
        fault = jnp.concatenate([fault, jnp.zeros((sub - cells, plan.lanes), F32)], axis=0)
    crust[10 * cells] = fault
    copies[4].wait()
    copies[5].wait()


class Shifts:
    def __init__(self, plan):
        self.plan = plan
        shape = (plan.sub, plan.lanes)
        self.row = lax.broadcasted_iota(jnp.int32, shape, 0)
        self.lane = lax.broadcasted_iota(jnp.int32, shape, 1)
        self.y = lax.rem(self.lane, plan.ny)
        self.first_row = self.row == 0
        self.last_row = self.row == plan.sub - 1
        self.top = self.first_row & (self.lane < plan.ny)
        self.floor_cell = self.last_row & (self.lane >= plan.lanes - plan.ny)
        self.not_low_y = jnp.where(self.y == 0, 0.0, 1.0).astype(F32)
        self.not_high_y = jnp.where(self.y == plan.ny - 1, 0.0, 1.0).astype(F32)
        self.depth = (
            lax.div(self.lane, plan.ny) * plan.sub + self.row
        ).astype(F32)

    def dy(self, f):
        lanes = self.plan.lanes
        return pltpu.roll(f, lanes - 1, 1) * self.not_high_y - pltpu.roll(f, 1, 1) * self.not_low_y

    def below(self, f):
        plan = self.plan
        moved = pltpu.roll(f, plan.sub - 1, 0)
        if plan.chunks > 1:
            moved = jnp.where(self.last_row, pltpu.roll(moved, plan.lanes - plan.ny, 1), moved)
        return jnp.where(self.floor_cell, 0.0, moved)

    def above(self, f, top):
        plan = self.plan
        moved = pltpu.roll(f, 1, 0)
        if plan.chunks > 1:
            moved = jnp.where(self.first_row, pltpu.roll(moved, plan.ny, 1), moved)
        return jnp.where(self.top, top, moved)

    def seafloor(self, vz):
        row = self.over_chunks(jnp.where(self.top, vz, 0.0)[0:1])
        return jnp.broadcast_to(row, vz.shape)

    def over_chunks(self, f):
        shift = self.plan.ny
        while shift < self.plan.lanes:
            f = f + pltpu.roll(f, shift, 1)
            shift *= 2
        return f


def acceleration(sh, stress, j):
    sxy, sxz = stress[SXY, j], stress[SXZ, j]
    syz, szz = stress[SYZ, j], stress[SZZ, j]
    ax = stress[SXX, j + 1] - stress[SXX, j - 1] + sh.dy(sxy) + sh.below(sxz) - sh.above(sxz, 0.0)
    ay = stress[SXY, j + 1] - stress[SXY, j - 1] + sh.dy(stress[SYY, j])
    ay = ay + sh.below(syz) - sh.above(syz, 0.0)
    az = stress[SXZ, j + 1] - stress[SXZ, j - 1] + sh.dy(syz) + sh.below(szz) - sh.above(szz, 0.0)
    return ax, ay, az


def strained(sh, vel, stress, mats, j):
    vx, vy, vz = vel[VX, j], vel[VY, j], vel[VZ, j]
    exx = vel[VX, j + 1] - vel[VX, j - 1]
    eyy = sh.dy(vy)
    ezz = sh.below(vz) - sh.above(vz, vz)
    mu = mats[SHEAR, j]
    mu2 = mu + mu
    common = mats[LAMB, j] * (exx + eyy + ezz)
    exy = sh.dy(vx) + vel[VY, j + 1] - vel[VY, j - 1]
    exz = sh.below(vx) - sh.above(vx, vx) + vel[VZ, j + 1] - vel[VZ, j - 1]
    eyz = sh.below(vy) - sh.above(vy, vy) + sh.dy(vz)
    return (
        stress[SXX, j] + (common + mu2 * exx),
        stress[SYY, j] + (common + mu2 * eyy),
        stress[SZZ, j] + (common + mu2 * ezz),
        stress[SXY, j] + mu * exy,
        stress[SXZ, j] + (mu * exz + mats[FAULT, j]),
        stress[SYZ, j] + mu * eyz,
    )


def begin_kernel(plan, table, own, mate, other, vel, stress, mats):
    cells, sub = plan.cells, plan.sub
    sh = Shifts(plan)
    odd = odd_device()
    starts = (HALO, (HALO + cells) * (1 - odd), (HALO + cells) * odd)
    for start, ref in zip(starts, (own, mate, other)):
        def bring(x, start=start, ref=ref):
            j = start + x
            for f in range(3):
                vel[f, j] = ref[f * cells + x]
            for f in range(6):
                stress[f, j] = ref[(3 + f) * cells + x]
            zone = ref[9 * cells + x]
            values = [jnp.zeros_like(zone) for _ in range(3)]
            for z in range(ZONES):
                here = zone == float(z + 1)
                values = [jnp.where(here, table[c, z], values[c]) for c in range(3)]
            for c in range(3):
                mats[c, j] = values[c] * HALF
            slip = jnp.broadcast_to(ref[10 * cells, pl.ds(x, 1), :], (sub, plan.lanes))
            mats[FAULT, j] = jnp.where(sh.row == (plan.depth // 2) % sub, DT * slip, 0.0)
            mats[FLOOR, j] = sh.seafloor(ref[VZ * cells + x])

        plan.planes(0, cells, bring)

    def move(j):
        b = mats[BUOY, j]
        for f, a in enumerate(acceleration(sh, stress, j)):
            vel[f, j] = vel[f, j] + b * a

    plan.planes(1, plan.width - 1, move)


def middle_kernel(
    plan, arrived, swapped, vel_in, stress_in, mats, vel, stress, loads, message,
    oc, water, bottom, gather, depths,
):
    sub, chunks, n, strips = plan.sub, plan.chunks, plan.n, plan.strips
    width, sent = plan.width, plan.sent_groups
    sh = Shifts(plan)
    odd = odd_device()

    half = n // 2
    mate = 1 - odd

    def turn(owner, group):
        for core, ref in ((odd, arrived), (mate, swapped)):
            for kc in range(chunks):
                for yl in range(strips):
                    at = owner * plan.rows + (kc * strips + yl) * sent + group
                    to = kc * plan.ny + core * strips + yl
                    gather[pl.ds(to, half, stride=2 * strips), :] = ref[
                        pl.ds(at, half, stride=2 * plan.rows), :
                    ]
        return gather[...].T

    def spread(turned, group):
        for i in range(chunks):
            for f in range(4):
                at = (i * 4 + f) * sub
                oc[f, 1 + group * chunks + i] = turned[at : at + sub]

    ends = []
    for group in range(sent):
        turned = turn(odd, group)
        spread(turned, group + plan.halo_groups * odd)
        if group == 0:
            ends.append((turned[2 * sub : 3 * sub], turned[3 * sub : 4 * sub]))
        if group == sent - 1:
            ends.append((turned[LANES - 2 * sub : LANES - sub], turned[LANES - sub :]))
    for group in range(plan.halo_groups):
        spread(turn(mate, group + plan.own_groups * odd), group + sent * mate)
    turned = turn(mate, plan.own_groups - odd)
    is_odd = odd == 1
    oc[0, (width + 1) * odd] = jnp.where(is_odd, ends[1][0], ends[0][0])
    oc[0, (width + 1) * mate] = jnp.where(
        is_odd, turned[LANES - 4 * sub : LANES - 3 * sub], turned[:sub]
    )
    deep = jnp.where(is_odd, ends[1][1], ends[0][1])
    for kc in range(chunks):
        mine = (sh.lane >= kc * plan.ny) & (sh.lane < (kc + 1) * plan.ny)
        depths[kc * sub : (kc + 1) * sub, :] = sh.over_chunks(jnp.where(mine, deep, 0.0))

    def mask(j):
        low = jnp.broadcast_to(depths[pl.ds(j, 1), :], (sub, plan.lanes))
        wet = jnp.where(sh.depth < low, 1.0, 0.0).astype(F32)
        water[j] = wet
        bottom[j] = jnp.where(sh.depth == low - 1.0, 1.0, 0.0).astype(F32)
        oc[0, j] = oc[0, j] * wet

    def mask_x(j):
        oc[1, j] = oc[1, j] * water[j]

    def mask_yw(j):
        oc[2, j] = oc[2, j] * water[j]
        oc[3, j] = oc[3, j] * water[j]

    plan.planes(0, width + 2, mask)
    plan.planes(1, width + 1, mask_x)
    plan.planes(2, width, mask_yw)

    for t in range(STEPS):
        first, last = 2 * t, width - 2 * t
        before = t == 0

        def flow_x(j):
            oc[1, j + 1] = water[j + 1] * (oc[1, j + 1] - HALF * (oc[0, j + 2] - oc[0, j]))

        def flow(j):
            p = oc[0, j + 1]
            wet = water[j + 1]
            oc[2, j + 1] = wet * (oc[2, j + 1] - HALF * sh.dy(p))
            rise = sh.below(p) + bottom[j + 1] * p - sh.above(p, -p)
            oc[3, j + 1] = wet * (oc[3, j + 1] - (HALF * rise + (DT * GRAV) * p))

        def press(j):
            w = oc[3, j + 1]
            floor = mats[FLOOR, j] if before else sh.seafloor(vel[VZ, j])
            rise = sh.below(w) + bottom[j + 1] * floor - sh.above(w, w)
            total = oc[1, j + 2] - oc[1, j] + sh.dy(oc[2, j + 1]) + rise
            oc[0, j + 1] = water[j + 1] * (oc[0, j + 1] - (HALF * KBULK) * total)

        def load(j):
            column = jnp.sum(bottom[j + 1] * oc[0, j + 1], axis=0, keepdims=True)
            column = jnp.broadcast_to(sh.over_chunks(column), (sub, plan.lanes))
            return jnp.where(sh.top, column, 0.0)

        plan.planes(first, last, flow_x)
        plan.planes(first + 1, last - 1, flow)
        plan.planes(first + 1, last - 1, press)
        if before:
            def add_load(j):
                for f in (VX, VY):
                    vel[f, j] = vel_in[f, j]
                vel[VZ, j] = vel_in[VZ, j] + mats[BUOY, j] * load(j)

            plan.planes(first + 1, last - 1, add_load)
        elif t < STEPS - 1:
            def move(j):
                ax, ay, az = acceleration(sh, stress, j)
                b = mats[BUOY, j]
                vel[VX, j] = vel[VX, j] + b * ax
                vel[VY, j] = vel[VY, j] + b * ay
                vel[VZ, j] = vel[VZ, j] + b * (az + load(j))

            plan.planes(first + 1, last - 1, move)
        else:
            def keep(j):
                loads[j] = load(j)

            plan.planes(first + 1, last - 1, keep)
        if t < STEPS - 2:
            def strain(j):
                source = stress_in if before else stress
                for f, value in enumerate(strained(sh, vel, source, mats, j)):
                    stress[f, j] = value

            plan.planes(first + 2, last - 2, strain)

    for group in range(plan.own_groups):
        stacked = jnp.concatenate(
            [
                oc[f, 1 + HALO + group * chunks + i]
                for i in range(chunks)
                for f in range(4)
            ],
            axis=0,
        )
        gather[...] = stacked.T
        for kc in range(chunks):
            for yl in range(strips):
                at = group * plan.lead + kc * strips + yl
                message[pl.ds(at, n, stride=plan.back_rows), :] = gather[
                    pl.ds(kc * plan.ny + yl, n, stride=strips), :
                ]


def end_kernel(plan, vel_in, stress_in, mats, loads, vel_out, stress_out, vel, stress):
    cells, sub, chunks, ny = plan.cells, plan.sub, plan.chunks, plan.ny
    sh = Shifts(plan)
    first, last = 2 * (STEPS - 1), plan.width - 2 * (STEPS - 1)

    def put(out, f, x, plane):
        for kc in range(chunks):
            out[f, x, kc * sub : (kc + 1) * sub, :] = plane[:, kc * ny : (kc + 1) * ny]

    def strain(j):
        for f, value in enumerate(strained(sh, vel_in, stress_in, mats, j)):
            stress[f, j] = value

    def move(j):
        ax, ay, az = acceleration(sh, stress, j)
        b = mats[BUOY, j]
        for f, a in enumerate((ax, ay, az + loads[j])):
            vel[f, j] = vel_in[f, j] + b * a

    def finish(x):
        for f in range(3):
            put(vel_out, f, x, vel[f, x + HALO])
        for f, value in enumerate(strained(sh, vel, stress, mats, x + HALO)):
            put(stress_out, f, x, value)

    plan.planes(first, last, strain)
    plan.planes(first + 1, last - 1, move)
    plan.planes(0, cells, finish)


def unpack_kernel(plan, arrived, ocean, turned):
    sub, chunks = plan.sub, plan.chunks
    block = 4 * sub
    for yl in range(plan.strips):
        by_chunk = [
            arrived[pl.ds(kc * plan.strips + yl, plan.nx // chunks, stride=plan.lead), :]
            for kc in range(chunks)
        ]
        for i in range(chunks):
            turned[pl.ds(i, plan.nx // chunks, stride=chunks), :] = place(
                by_chunk, [i] * chunks, block
            )
        whole = turned[...].T
        for kc in range(chunks):
            for f in range(4):
                at = (kc * 4 + f) * sub
                ocean[f, yl, kc * sub : (kc + 1) * sub, :] = whole[at : at + sub]


def on_device(plan, velocity, stress, ocean, zones, materials, slip, bathy):
    n, cells, sub, lanes, width = plan.n, plan.cells, plan.sub, plan.lanes, plan.width
    vmem = pl.BlockSpec(memory_space=pltpu.VMEM)
    smem = pl.BlockSpec(memory_space=pltpu.SMEM)
    hbm = pl.BlockSpec(memory_space=pltpu.HBM)

    def shape(*dims):
        return jax.ShapeDtypeStruct(dims, F32)

    def like(array):
        return jax.ShapeDtypeStruct(array.shape, array.dtype)

    def held(array):
        return pltpu.VMEM(array.shape, array.dtype)

    def call(kernel, name, out, ins, scratch, room=16, **rest):
        room = room if plan.unrolled else 56
        return pl.pallas_call(
            functools.partial(kernel, plan),
            out_shape=out,
            in_specs=ins,
            out_specs=jax.tree.map(lambda _: vmem, out),
            scratch_shapes=scratch,
            compiler_params=pltpu.CompilerParams(vmem_limit_bytes=room * 1024 * 1024),
            name=name,
            **rest,
        )

    def pinned(array):
        return pltpu.with_memory_space_constraint(array, pltpu.HBM)

    mates = [(i, i ^ 1) for i in range(n)]
    others = [(i, i + 1) for i in range(1, n - 1, 2)]
    others += [(target, source) for source, target in others]
    crust, ocean_near, bathy_near = call(
        crust_kernel,
        "crust_planes",
        (shape(10 * cells + 1, sub, lanes), like(ocean), like(bathy)),
        [hbm] * 6,
        [held(velocity), held(stress), held(zones), held(slip), pltpu.SemaphoreType.DMA((6,))],
    )(*(pinned(a) for a in (velocity, stress, zones, slip, ocean, bathy)))
    other = lax.ppermute(crust, "map", others)
    message = call(
        ocean_kernel,
        "ocean_rows",
        shape(n * plan.rows, LANES),
        [vmem] * 2,
        [
            pltpu.VMEM((plan.strips, plan.nx, LANES), F32),
            pltpu.VMEM(
                (plan.lead, plan.nx // plan.chunks + 2 * plan.halo_groups, LANES), F32
            ),
            pltpu.VMEM((n * plan.strips, LANES), F32),
        ],
    )(ocean_near, bathy_near)
    arrived = lax.all_to_all(
        message.reshape(n // 2, 2 * plan.rows, LANES),
        "map",
        split_axis=0,
        concat_axis=0,
        axis_index_groups=[list(range(core, n, 2)) for core in range(2)],
        tiled=True,
    ).reshape(n * plan.rows, LANES)
    mate = lax.ppermute(crust, "map", mates)
    vel, strs, mats = call(
        begin_kernel,
        "first_velocity",
        (shape(3, width, sub, lanes), shape(6, width, sub, lanes), shape(5, width, sub, lanes)),
        [smem] + [vmem] * 3,
        [],
        cost_estimate=pl.CostEstimate(flops=0, bytes_accessed=20_000_000, transcendentals=0),
    )(materials, crust, mate, other)
    swapped = lax.ppermute(arrived, "map", mates)
    vel, strs, loads, back = call(
        middle_kernel,
        "substeps",
        (
            shape(3, width, sub, lanes),
            shape(6, width, sub, lanes),
            shape(width, sub, lanes),
            shape(n * plan.back_rows, LANES),
        ),
        [vmem] * 5,
        [
            pltpu.VMEM((4, width + 2, sub, lanes), F32),
            pltpu.VMEM((width + 2, sub, lanes), F32),
            pltpu.VMEM((width + 2, sub, lanes), F32),
            pltpu.VMEM((lanes, LANES), F32),
            pltpu.VMEM((plan.depth, lanes), F32),
        ],
        input_output_aliases={2: 0, 3: 1},
    )(arrived, swapped, vel, strs, mats)
    returned = lax.all_to_all(
        back.reshape(n, plan.back_rows, LANES), "map", split_axis=0, concat_axis=0, tiled=True
    ).reshape(n * plan.back_rows, LANES)
    new_velocity, new_stress = call(
        end_kernel,
        "last_updates",
        (shape(*velocity.shape), shape(*stress.shape)),
        [vmem] * 4,
        [
            pltpu.VMEM((3, width, sub, lanes), F32),
            pltpu.VMEM((6, width, sub, lanes), F32),
        ],
    )(vel, strs, mats, loads)
    new_ocean = call(
        unpack_kernel,
        "ocean_strips",
        shape(*ocean.shape),
        [vmem],
        [pltpu.VMEM((plan.nx, LANES), F32)],
    )(returned)
    return new_velocity, new_stress, new_ocean


def solution(mesh):
    n = mesh.shape["map"]

    def body(velocity, stress, ocean, zones, materials, slip, bathy):
        _, cells, depth, ny = velocity.shape
        plan = Plan(n, cells, depth, ny, ocean.shape[1])
        return on_device(plan, velocity, stress, ocean, zones, materials, slip, bathy)

    return jax.shard_map(
        body,
        mesh=mesh,
        in_specs=(
            P("parts", "map", None, None),
            P("parts", "map", None, None),
            P("parts", "map", None, None),
            P("map", "parts", None),
            P(),
            P("map", "parts"),
            P("map", "parts"),
        ),
        out_specs=(
            P("parts", "map", None, None),
            P("parts", "map", None, None),
            P("parts", "map", None, None),
        ),
        check_vma=False,
    )
```

```python
import functools

import jax
import jax.numpy as jnp
from jax import lax
from jax.experimental import pallas as pl
from jax.experimental.pallas import tpu as pltpu
from jax.sharding import PartitionSpec as P

STEPS = 4
ZONES = 8
DT = 0.25
HALF = 0.5 * DT
KBULK = 2.25
GRAV = 0.1
HALO = 2 * STEPS
LANES = 128
F32 = jnp.float32
VX, VY, VZ = range(3)
SXX, SYY, SZZ, SXY, SXZ, SYZ = range(6)
BUOY, LAMB, SHEAR, FAULT, FLOOR = range(5)


class Plan:
    def __init__(self, devices, cells, depth, ny, strips):
        self.n = devices
        self.cells = cells
        self.depth = depth
        self.ny = ny
        self.strips = strips
        self.chunks = max(1, LANES // ny)
        self.sub = depth // self.chunks
        self.lanes = self.chunks * ny
        self.width = cells + 2 * HALO
        self.own_groups = cells // self.chunks
        self.halo_groups = HALO // self.chunks
        self.sent_groups = self.own_groups + self.halo_groups
        self.lead = self.chunks * strips
        self.rows = self.lead * self.sent_groups
        self.back_rows = self.lead * self.own_groups
        self.nx = devices * cells
        self.block = 4 * self.sub
        self.unrolled = self.sub * self.lanes <= 1024
        assert devices % 2 == 0 and cells == HALO and self.block * self.chunks == LANES

    def planes(self, start, stop, body):
        if self.unrolled:
            for j in range(start, stop):
                body(j)
        else:
            def run(j, carry):
                body(j)
                return carry

            lax.fori_loop(start, stop, run, 0)


def odd_device():
    return lax.rem(lax.axis_index("map"), 2)


def place(pieces, wanted, block):
    out = None
    for i, piece in enumerate(pieces):
        shift = (i - wanted[i]) * block % piece.shape[-1]
        moved = pltpu.roll(piece, shift, piece.ndim - 1) if shift else piece
        if out is None:
            out = moved
        else:
            lane = lax.broadcasted_iota(jnp.int32, moved.shape, moved.ndim - 1)
            out = jnp.where(lane >= i * block, moved, out)
    return out


def ocean_kernel(plan, ocean, bathy, message, turned, grouped, extra):
    cells, sub, chunks, n, strips = plan.cells, plan.sub, plan.chunks, plan.n, plan.strips
    block, sent, rows = plan.block, plan.sent_groups, plan.rows
    border = jnp.zeros((plan.lead, plan.halo_groups, LANES), F32)
    count = plan.nx // chunks
    grouped[:, : plan.halo_groups, :] = border
    grouped[:, plan.halo_groups + count :, :] = border
    for yl in range(strips):
        stacked = jnp.concatenate(
            [ocean[f, yl, kc * sub : (kc + 1) * sub, :] for kc in range(chunks) for f in range(4)],
            axis=0,
        )
        turned[yl] = stacked.T
        by_x = [turned[yl, pl.ds(i, count, stride=chunks), :] for i in range(chunks)]
        for kc in range(chunks):
            grouped[kc * strips + yl, pl.ds(plan.halo_groups, count), :] = place(
                by_x, [kc] * chunks, block
            )
    for d in range(n):
        start = d * plan.own_groups + (d % 2) * plan.halo_groups
        for q in range(plan.lead):
            message[d * rows + q * sent : d * rows + (q + 1) * sent, :] = grouped[
                q, start : start + sent, :
            ]
    depths = bathy[...].astype(F32)
    wide = lax.broadcasted_iota(jnp.int32, depths.shape, 1)
    for d in range(n):
        first = d * cells - HALO - 1
        moved = pltpu.roll(depths, -first % plan.nx, 1)
        moved = jnp.where((wide + first >= 0) & (wide + first < plan.nx), moved, 0.0)
        extra[d * strips : (d + 1) * strips, :] = moved[:, :LANES]
    pairs = n // 2
    lane = lax.broadcasted_iota(jnp.int32, (pairs, LANES), 1)
    blank = jnp.zeros((1, LANES), F32)
    for odd in range(2):
        slot = (odd * (chunks - 1) * 4 + 2) * sub
        group = odd * (sent - 1)
        for yl in range(strips):
            if odd:
                column = turned[yl, pl.ds(2 * cells + HALO, pairs - 1, stride=2 * cells), :]
                column = jnp.concatenate([column, blank], axis=0)
            else:
                column = turned[yl, pl.ds(2 * cells - HALO - 1, pairs - 1, stride=2 * cells), :]
                column = jnp.concatenate([blank, column], axis=0)
            deep = extra[pl.ds(odd * strips + yl, pairs, stride=2 * strips), :]
            for kc in range(chunks):
                at = odd * rows + (kc * strips + yl) * sent + group
                old = message[pl.ds(at, pairs, stride=2 * rows), :]
                edge = pltpu.roll(column, (slot - kc * block) % LANES, 1)
                floor = pltpu.roll(deep, (slot + sub - kc * sub) % LANES, 1)
                new = jnp.where((lane >= slot) & (lane < slot + sub), edge, old)
                new = jnp.where((lane >= slot + sub) & (lane < slot + 2 * sub), floor, new)
                message[pl.ds(at, pairs, stride=2 * rows), :] = new


def crust_kernel(
    plan, vel_ref, stress_ref, zones_ref, slip_ref, ocean_ref, bathy_ref,
    crust, ocean, bathy, vel, stress, zones, slip, sems,
):
    cells, sub, chunks, ny = plan.cells, plan.sub, plan.chunks, plan.ny
    pairs = (
        (vel_ref, vel),
        (stress_ref, stress),
        (zones_ref, zones),
        (slip_ref, slip),
        (ocean_ref, ocean),
        (bathy_ref, bathy),
    )
    copies = [
        pltpu.make_async_copy(source, target, sems.at[i])
        for i, (source, target) in enumerate(pairs)
    ]
    for copy in copies:
        copy.start()

    def joined(ref, *at):
        parts = [ref[(*at, pl.ds(kc * sub, sub), slice(None))] for kc in range(chunks)]
        return jnp.concatenate(parts, axis=-1) if chunks > 1 else parts[0]

    copies[0].wait()
    for f in range(3):
        for x in range(cells):
            crust[f * cells + x] = joined(vel, f, x)
    copies[1].wait()
    for f in range(6):
        for x in range(cells):
            crust[(3 + f) * cells + x] = joined(stress, f, x)
    copies[2].wait()
    for x in range(cells):
        crust[9 * cells + x] = (joined(zones, x) + 1).astype(F32)
    copies[3].wait()
    fault_chunk = (plan.depth // 2) // sub
    pieces = [
        slip[...] if kc == fault_chunk else jnp.zeros((cells, ny), F32) for kc in range(chunks)
    ]
    fault = jnp.concatenate(pieces, axis=-1) if chunks > 1 else pieces[0]
    if sub > cells:
        fault = jnp.concatenate([fault, jnp.zeros((sub - cells, plan.lanes), F32)], axis=0)
    crust[10 * cells] = fault
    copies[4].wait()
    copies[5].wait()


class Shifts:
    def __init__(self, plan):
        self.plan = plan
        shape = (plan.sub, plan.lanes)
        self.row = lax.broadcasted_iota(jnp.int32, shape, 0)
        self.lane = lax.broadcasted_iota(jnp.int32, shape, 1)
        self.y = lax.rem(self.lane, plan.ny)
        self.first_row = self.row == 0
        self.last_row = self.row == plan.sub - 1
        self.top = self.first_row & (self.lane < plan.ny)
        self.floor_cell = self.last_row & (self.lane >= plan.lanes - plan.ny)
        self.not_low_y = jnp.where(self.y == 0, 0.0, 1.0).astype(F32)
        self.not_high_y = jnp.where(self.y == plan.ny - 1, 0.0, 1.0).astype(F32)
        self.depth = (
            lax.div(self.lane, plan.ny) * plan.sub + self.row
        ).astype(F32)

    def dy(self, f):
        lanes = self.plan.lanes
        return pltpu.roll(f, lanes - 1, 1) * self.not_high_y - pltpu.roll(f, 1, 1) * self.not_low_y

    def below(self, f):
        plan = self.plan
        moved = pltpu.roll(f, plan.sub - 1, 0)
        if plan.chunks > 1:
            moved = jnp.where(self.last_row, pltpu.roll(moved, plan.lanes - plan.ny, 1), moved)
        return jnp.where(self.floor_cell, 0.0, moved)

    def above(self, f, top):
        plan = self.plan
        moved = pltpu.roll(f, 1, 0)
        if plan.chunks > 1:
            moved = jnp.where(self.first_row, pltpu.roll(moved, plan.ny, 1), moved)
        return jnp.where(self.top, top, moved)

    def seafloor(self, vz):
        row = self.over_chunks(jnp.where(self.top, vz, 0.0)[0:1])
        return jnp.broadcast_to(row, vz.shape)

    def over_chunks(self, f):
        shift = self.plan.ny
        while shift < self.plan.lanes:
            f = f + pltpu.roll(f, shift, 1)
            shift *= 2
        return f


def acceleration(sh, stress, j):
    sxy, sxz = stress[SXY, j], stress[SXZ, j]
    syz, szz = stress[SYZ, j], stress[SZZ, j]
    ax = stress[SXX, j + 1] - stress[SXX, j - 1] + sh.dy(sxy) + sh.below(sxz) - sh.above(sxz, 0.0)
    ay = stress[SXY, j + 1] - stress[SXY, j - 1] + sh.dy(stress[SYY, j])
    ay = ay + sh.below(syz) - sh.above(syz, 0.0)
    az = stress[SXZ, j + 1] - stress[SXZ, j - 1] + sh.dy(syz) + sh.below(szz) - sh.above(szz, 0.0)
    return ax, ay, az


def strained(sh, vel, stress, mats, j):
    vx, vy, vz = vel[VX, j], vel[VY, j], vel[VZ, j]
    exx = vel[VX, j + 1] - vel[VX, j - 1]
    eyy = sh.dy(vy)
    ezz = sh.below(vz) - sh.above(vz, vz)
    mu = mats[SHEAR, j]
    mu2 = mu + mu
    common = mats[LAMB, j] * (exx + eyy + ezz)
    exy = sh.dy(vx) + vel[VY, j + 1] - vel[VY, j - 1]
    exz = sh.below(vx) - sh.above(vx, vx) + vel[VZ, j + 1] - vel[VZ, j - 1]
    eyz = sh.below(vy) - sh.above(vy, vy) + sh.dy(vz)
    return (
        stress[SXX, j] + (common + mu2 * exx),
        stress[SYY, j] + (common + mu2 * eyy),
        stress[SZZ, j] + (common + mu2 * ezz),
        stress[SXY, j] + mu * exy,
        stress[SXZ, j] + (mu * exz + mats[FAULT, j]),
        stress[SYZ, j] + mu * eyz,
    )


def begin_kernel(plan, table, own, mate, other, vel, stress, mats):
    cells, sub = plan.cells, plan.sub
    sh = Shifts(plan)
    odd = odd_device()
    starts = (HALO, (HALO + cells) * (1 - odd), (HALO + cells) * odd)
    for start, ref in zip(starts, (own, mate, other)):
        def bring(x, start=start, ref=ref):
            j = start + x
            for f in range(3):
                vel[f, j] = ref[f * cells + x]
            for f in range(6):
                stress[f, j] = ref[(3 + f) * cells + x]
            zone = ref[9 * cells + x]
            values = [jnp.zeros_like(zone) for _ in range(3)]
            for z in range(ZONES):
                here = zone == float(z + 1)
                values = [jnp.where(here, table[c, z], values[c]) for c in range(3)]
            for c in range(3):
                mats[c, j] = values[c] * HALF
            slip = jnp.broadcast_to(ref[10 * cells, pl.ds(x, 1), :], (sub, plan.lanes))
            mats[FAULT, j] = jnp.where(sh.row == (plan.depth // 2) % sub, DT * slip, 0.0)
            mats[FLOOR, j] = sh.seafloor(ref[VZ * cells + x])

        plan.planes(0, cells, bring)

    def move(j):
        b = mats[BUOY, j]
        for f, a in enumerate(acceleration(sh, stress, j)):
            vel[f, j] = vel[f, j] + b * a

    plan.planes(1, plan.width - 1, move)


def middle_kernel(
    plan, arrived, swapped, vel_in, stress_in, mats, vel, stress, loads, message,
    oc, water, bottom, gather, depths,
):
    sub, chunks, n, strips = plan.sub, plan.chunks, plan.n, plan.strips
    width, sent = plan.width, plan.sent_groups
    sh = Shifts(plan)
    odd = odd_device()

    half = n // 2
    mate = 1 - odd

    def turn(owner, group):
        for core, ref in ((odd, arrived), (mate, swapped)):
            for kc in range(chunks):
                for yl in range(strips):
                    at = owner * plan.rows + (kc * strips + yl) * sent + group
                    to = kc * plan.ny + core * strips + yl
                    gather[pl.ds(to, half, stride=2 * strips), :] = ref[
                        pl.ds(at, half, stride=2 * plan.rows), :
                    ]
        return gather[...].T

    def spread(turned, group):
        for i in range(chunks):
            for f in range(4):
                at = (i * 4 + f) * sub
                oc[f, 1 + group * chunks + i] = turned[at : at + sub]

    ends = []
    for group in range(sent):
        turned = turn(odd, group)
        spread(turned, group + plan.halo_groups * odd)
        if group == 0:
            ends.append((turned[2 * sub : 3 * sub], turned[3 * sub : 4 * sub]))
        if group == sent - 1:
            ends.append((turned[LANES - 2 * sub : LANES - sub], turned[LANES - sub :]))
    for group in range(plan.halo_groups):
        spread(turn(mate, group + plan.own_groups * odd), group + sent * mate)
    turned = turn(mate, plan.own_groups - odd)
    is_odd = odd == 1
    oc[0, (width + 1) * odd] = jnp.where(is_odd, ends[1][0], ends[0][0])
    oc[0, (width + 1) * mate] = jnp.where(
        is_odd, turned[LANES - 4 * sub : LANES - 3 * sub], turned[:sub]
    )
    deep = jnp.where(is_odd, ends[1][1], ends[0][1])
    for kc in range(chunks):
        mine = (sh.lane >= kc * plan.ny) & (sh.lane < (kc + 1) * plan.ny)
        depths[kc * sub : (kc + 1) * sub, :] = sh.over_chunks(jnp.where(mine, deep, 0.0))

    def mask(j):
        low = jnp.broadcast_to(depths[pl.ds(j, 1), :], (sub, plan.lanes))
        wet = jnp.where(sh.depth < low, 1.0, 0.0).astype(F32)
        water[j] = wet
        bottom[j] = jnp.where(sh.depth == low - 1.0, 1.0, 0.0).astype(F32)
        oc[0, j] = oc[0, j] * wet

    def mask_x(j):
        oc[1, j] = oc[1, j] * water[j]

    def mask_yw(j):
        oc[2, j] = oc[2, j] * water[j]
        oc[3, j] = oc[3, j] * water[j]

    plan.planes(0, width + 2, mask)
    plan.planes(1, width + 1, mask_x)
    plan.planes(2, width, mask_yw)

    for t in range(STEPS):
        first, last = 2 * t, width - 2 * t
        before = t == 0

        def flow_x(j):
            oc[1, j + 1] = water[j + 1] * (oc[1, j + 1] - HALF * (oc[0, j + 2] - oc[0, j]))

        def flow(j):
            p = oc[0, j + 1]
            wet = water[j + 1]
            oc[2, j + 1] = wet * (oc[2, j + 1] - HALF * sh.dy(p))
            rise = sh.below(p) + bottom[j + 1] * p - sh.above(p, -p)
            oc[3, j + 1] = wet * (oc[3, j + 1] - (HALF * rise + (DT * GRAV) * p))

        def press(j):
            w = oc[3, j + 1]
            floor = mats[FLOOR, j] if before else sh.seafloor(vel[VZ, j])
            rise = sh.below(w) + bottom[j + 1] * floor - sh.above(w, w)
            total = oc[1, j + 2] - oc[1, j] + sh.dy(oc[2, j + 1]) + rise
            oc[0, j + 1] = water[j + 1] * (oc[0, j + 1] - (HALF * KBULK) * total)

        def load(j):
            column = jnp.sum(bottom[j + 1] * oc[0, j + 1], axis=0, keepdims=True)
            column = jnp.broadcast_to(sh.over_chunks(column), (sub, plan.lanes))
            return jnp.where(sh.top, column, 0.0)

        plan.planes(first, last, flow_x)
        plan.planes(first + 1, last - 1, flow)
        plan.planes(first + 1, last - 1, press)
        if before:
            def add_load(j):
                for f in (VX, VY):
                    vel[f, j] = vel_in[f, j]
                vel[VZ, j] = vel_in[VZ, j] + mats[BUOY, j] * load(j)

            plan.planes(first + 1, last - 1, add_load)
        elif t < STEPS - 1:
            def move(j):
                ax, ay, az = acceleration(sh, stress, j)
                b = mats[BUOY, j]
                vel[VX, j] = vel[VX, j] + b * ax
                vel[VY, j] = vel[VY, j] + b * ay
                vel[VZ, j] = vel[VZ, j] + b * (az + load(j))

            plan.planes(first + 1, last - 1, move)
        else:
            def keep(j):
                loads[j] = load(j)

            plan.planes(first + 1, last - 1, keep)
        if t < STEPS - 2:
            def strain(j):
                source = stress_in if before else stress
                for f, value in enumerate(strained(sh, vel, source, mats, j)):
                    stress[f, j] = value

            plan.planes(first + 2, last - 2, strain)

    for group in range(plan.own_groups):
        stacked = jnp.concatenate(
            [
                oc[f, 1 + HALO + group * chunks + i]
                for i in range(chunks)
                for f in range(4)
            ],
            axis=0,
        )
        gather[...] = stacked.T
        for kc in range(chunks):
            for yl in range(strips):
                at = group * plan.lead + kc * strips + yl
                message[pl.ds(at, n, stride=plan.back_rows), :] = gather[
                    pl.ds(kc * plan.ny + yl, n, stride=strips), :
                ]


def end_kernel(plan, vel_in, stress_in, mats, loads, vel_out, stress_out, vel, stress):
    cells, sub, chunks, ny = plan.cells, plan.sub, plan.chunks, plan.ny
    sh = Shifts(plan)
    first, last = 2 * (STEPS - 1), plan.width - 2 * (STEPS - 1)

    def put(out, f, x, plane):
        for kc in range(chunks):
            out[f, x, kc * sub : (kc + 1) * sub, :] = plane[:, kc * ny : (kc + 1) * ny]

    def strain(j):
        for f, value in enumerate(strained(sh, vel_in, stress_in, mats, j)):
            stress[f, j] = value

    def move(j):
        ax, ay, az = acceleration(sh, stress, j)
        b = mats[BUOY, j]
        for f, a in enumerate((ax, ay, az + loads[j])):
            vel[f, j] = vel_in[f, j] + b * a

    def finish(x):
        for f in range(3):
            put(vel_out, f, x, vel[f, x + HALO])
        for f, value in enumerate(strained(sh, vel, stress, mats, x + HALO)):
            put(stress_out, f, x, value)

    plan.planes(first, last, strain)
    plan.planes(first + 1, last - 1, move)
    plan.planes(0, cells, finish)


def unpack_kernel(plan, arrived, ocean, turned):
    sub, chunks = plan.sub, plan.chunks
    block = 4 * sub
    for yl in range(plan.strips):
        by_chunk = [
            arrived[pl.ds(kc * plan.strips + yl, plan.nx // chunks, stride=plan.lead), :]
            for kc in range(chunks)
        ]
        for i in range(chunks):
            turned[pl.ds(i, plan.nx // chunks, stride=chunks), :] = place(
                by_chunk, [i] * chunks, block
            )
        whole = turned[...].T
        for kc in range(chunks):
            for f in range(4):
                at = (kc * 4 + f) * sub
                ocean[f, yl, kc * sub : (kc + 1) * sub, :] = whole[at : at + sub]


def on_device(plan, velocity, stress, ocean, zones, materials, slip, bathy):
    n, cells, sub, lanes, width = plan.n, plan.cells, plan.sub, plan.lanes, plan.width
    vmem = pl.BlockSpec(memory_space=pltpu.VMEM)
    smem = pl.BlockSpec(memory_space=pltpu.SMEM)
    hbm = pl.BlockSpec(memory_space=pltpu.HBM)

    def shape(*dims):
        return jax.ShapeDtypeStruct(dims, F32)

    def like(array):
        return jax.ShapeDtypeStruct(array.shape, array.dtype)

    def held(array):
        return pltpu.VMEM(array.shape, array.dtype)

    def call(kernel, name, out, ins, scratch, room=16, **rest):
        room = room if plan.unrolled else 56
        return pl.pallas_call(
            functools.partial(kernel, plan),
            out_shape=out,
            in_specs=ins,
            out_specs=jax.tree.map(lambda _: vmem, out),
            scratch_shapes=scratch,
            compiler_params=pltpu.CompilerParams(vmem_limit_bytes=room * 1024 * 1024),
            name=name,
            **rest,
        )

    def pinned(array):
        return pltpu.with_memory_space_constraint(array, pltpu.HBM)

    mates = [(i, i ^ 1) for i in range(n)]
    others = [(i, i + 1) for i in range(1, n - 1, 2)]
    others += [(target, source) for source, target in others]
    crust, ocean_near, bathy_near = call(
        crust_kernel,
        "crust_planes",
        (shape(10 * cells + 1, sub, lanes), like(ocean), like(bathy)),
        [hbm] * 6,
        [held(velocity), held(stress), held(zones), held(slip), pltpu.SemaphoreType.DMA((6,))],
    )(*(pinned(a) for a in (velocity, stress, zones, slip, ocean, bathy)))
    other = lax.ppermute(crust, "map", others)
    message = call(
        ocean_kernel,
        "ocean_rows",
        shape(n * plan.rows, LANES),
        [vmem] * 2,
        [
            pltpu.VMEM((plan.strips, plan.nx, LANES), F32),
            pltpu.VMEM(
                (plan.lead, plan.nx // plan.chunks + 2 * plan.halo_groups, LANES), F32
            ),
            pltpu.VMEM((n * plan.strips, LANES), F32),
        ],
    )(ocean_near, bathy_near)
    arrived = lax.all_to_all(
        message.reshape(n // 2, 2 * plan.rows, LANES),
        "map",
        split_axis=0,
        concat_axis=0,
        axis_index_groups=[list(range(core, n, 2)) for core in range(2)],
        tiled=True,
    ).reshape(n * plan.rows, LANES)
    mate = lax.ppermute(crust, "map", mates)
    vel, strs, mats = call(
        begin_kernel,
        "first_velocity",
        (shape(3, width, sub, lanes), shape(6, width, sub, lanes), shape(5, width, sub, lanes)),
        [smem] + [vmem] * 3,
        [],
        cost_estimate=pl.CostEstimate(flops=0, bytes_accessed=20_000_000, transcendentals=0),
    )(materials, crust, mate, other)
    arrived, vel = lax.optimization_barrier((arrived, vel))
    swapped = lax.ppermute(arrived, "map", mates)
    vel, strs, loads, back = call(
        middle_kernel,
        "substeps",
        (
            shape(3, width, sub, lanes),
            shape(6, width, sub, lanes),
            shape(width, sub, lanes),
            shape(n * plan.back_rows, LANES),
        ),
        [vmem] * 5,
        [
            pltpu.VMEM((4, width + 2, sub, lanes), F32),
            pltpu.VMEM((width + 2, sub, lanes), F32),
            pltpu.VMEM((width + 2, sub, lanes), F32),
            pltpu.VMEM((lanes, LANES), F32),
            pltpu.VMEM((plan.depth, lanes), F32),
        ],
        input_output_aliases={2: 0, 3: 1},
    )(arrived, swapped, vel, strs, mats)
    returned = lax.all_to_all(
        back.reshape(n, plan.back_rows, LANES), "map", split_axis=0, concat_axis=0, tiled=True
    ).reshape(n * plan.back_rows, LANES)
    new_velocity, new_stress = call(
        end_kernel,
        "last_updates",
        (shape(*velocity.shape), shape(*stress.shape)),
        [vmem] * 4,
        [
            pltpu.VMEM((3, width, sub, lanes), F32),
            pltpu.VMEM((6, width, sub, lanes), F32),
        ],
    )(vel, strs, mats, loads)
    new_ocean = call(
        unpack_kernel,
        "ocean_strips",
        shape(*ocean.shape),
        [vmem],
        [pltpu.VMEM((plan.nx, LANES), F32)],
    )(returned)
    return new_velocity, new_stress, new_ocean


def solution(mesh):
    n = mesh.shape["map"]

    def body(velocity, stress, ocean, zones, materials, slip, bathy):
        _, cells, depth, ny = velocity.shape
        plan = Plan(n, cells, depth, ny, ocean.shape[1])
        return on_device(plan, velocity, stress, ocean, zones, materials, slip, bathy)

    return jax.shard_map(
        body,
        mesh=mesh,
        in_specs=(
            P("parts", "map", None, None),
            P("parts", "map", None, None),
            P("parts", "map", None, None),
            P("map", "parts", None),
            P(),
            P("map", "parts"),
            P("map", "parts"),
        ),
        out_specs=(
            P("parts", "map", None, None),
            P("parts", "map", None, None),
            P("parts", "map", None, None),
        ),
        check_vma=False,
    )
```

```python
import functools

import jax
import jax.numpy as jnp
from jax import lax
from jax.experimental import pallas as pl
from jax.experimental.pallas import tpu as pltpu
from jax.sharding import PartitionSpec as P

STEPS = 4
ZONES = 8
DT = 0.25
HALF = 0.5 * DT
KBULK = 2.25
GRAV = 0.1
HALO = 2 * STEPS
LANES = 128
F32 = jnp.float32
VX, VY, VZ = range(3)
SXX, SYY, SZZ, SXY, SXZ, SYZ = range(6)
BUOY, LAMB, SHEAR, FAULT, FLOOR = range(5)


class Plan:
    def __init__(self, devices, cells, depth, ny, strips):
        self.n = devices
        self.cells = cells
        self.depth = depth
        self.ny = ny
        self.strips = strips
        self.chunks = max(1, LANES // ny)
        self.sub = depth // self.chunks
        self.lanes = self.chunks * ny
        self.width = cells + 2 * HALO
        self.own_groups = cells // self.chunks
        self.halo_groups = HALO // self.chunks
        self.sent_groups = self.own_groups + self.halo_groups
        self.lead = self.chunks * strips
        self.rows = self.lead * self.sent_groups
        self.back_rows = self.lead * self.own_groups
        self.nx = devices * cells
        self.block = 4 * self.sub
        self.unrolled = self.sub * self.lanes <= 1024
        assert devices % 2 == 0 and cells == HALO and self.block * self.chunks == LANES

    def planes(self, start, stop, body):
        if self.unrolled:
            for j in range(start, stop):
                body(j)
        else:
            def run(j, carry):
                body(j)
                return carry

            lax.fori_loop(start, stop, run, 0)


def odd_device():
    return lax.rem(lax.axis_index("map"), 2)


def place(pieces, wanted, block):
    out = None
    for i, piece in enumerate(pieces):
        shift = (i - wanted[i]) * block % piece.shape[-1]
        moved = pltpu.roll(piece, shift, piece.ndim - 1) if shift else piece
        if out is None:
            out = moved
        else:
            lane = lax.broadcasted_iota(jnp.int32, moved.shape, moved.ndim - 1)
            out = jnp.where(lane >= i * block, moved, out)
    return out


def ocean_kernel(plan, ocean, bathy, message, turned, grouped, extra):
    cells, sub, chunks, n, strips = plan.cells, plan.sub, plan.chunks, plan.n, plan.strips
    block, sent, rows = plan.block, plan.sent_groups, plan.rows
    border = jnp.zeros((plan.lead, plan.halo_groups, LANES), F32)
    count = plan.nx // chunks
    grouped[:, : plan.halo_groups, :] = border
    grouped[:, plan.halo_groups + count :, :] = border
    for yl in range(strips):
        stacked = jnp.concatenate(
            [ocean[f, yl, kc * sub : (kc + 1) * sub, :] for kc in range(chunks) for f in range(4)],
            axis=0,
        )
        turned[yl] = stacked.T
        by_x = [turned[yl, pl.ds(i, count, stride=chunks), :] for i in range(chunks)]
        for kc in range(chunks):
            grouped[kc * strips + yl, pl.ds(plan.halo_groups, count), :] = place(
                by_x, [kc] * chunks, block
            )
    for d in range(n):
        start = d * plan.own_groups + (d % 2) * plan.halo_groups
        for q in range(plan.lead):
            message[d * rows + q * sent : d * rows + (q + 1) * sent, :] = grouped[
                q, start : start + sent, :
            ]
    depths = bathy[...].astype(F32)
    wide = lax.broadcasted_iota(jnp.int32, depths.shape, 1)
    for d in range(n):
        first = d * cells - HALO - 1
        moved = pltpu.roll(depths, -first % plan.nx, 1)
        moved = jnp.where((wide + first >= 0) & (wide + first < plan.nx), moved, 0.0)
        extra[d * strips : (d + 1) * strips, :] = moved[:, :LANES]
    pairs = n // 2
    lane = lax.broadcasted_iota(jnp.int32, (pairs, LANES), 1)
    blank = jnp.zeros((1, LANES), F32)
    for odd in range(2):
        slot = (odd * (chunks - 1) * 4 + 2) * sub
        group = odd * (sent - 1)
        for yl in range(strips):
            if odd:
                column = turned[yl, pl.ds(2 * cells + HALO, pairs - 1, stride=2 * cells), :]
                column = jnp.concatenate([column, blank], axis=0)
            else:
                column = turned[yl, pl.ds(2 * cells - HALO - 1, pairs - 1, stride=2 * cells), :]
                column = jnp.concatenate([blank, column], axis=0)
            deep = extra[pl.ds(odd * strips + yl, pairs, stride=2 * strips), :]
            for kc in range(chunks):
                at = odd * rows + (kc * strips + yl) * sent + group
                old = message[pl.ds(at, pairs, stride=2 * rows), :]
                edge = pltpu.roll(column, (slot - kc * block) % LANES, 1)
                floor = pltpu.roll(deep, (slot + sub - kc * sub) % LANES, 1)
                new = jnp.where((lane >= slot) & (lane < slot + sub), edge, old)
                new = jnp.where((lane >= slot + sub) & (lane < slot + 2 * sub), floor, new)
                message[pl.ds(at, pairs, stride=2 * rows), :] = new


def crust_kernel(
    plan, vel_ref, stress_ref, zones_ref, slip_ref, ocean_ref, bathy_ref,
    crust, ocean, bathy, vel, stress, zones, slip, sems,
):
    cells, sub, chunks, ny = plan.cells, plan.sub, plan.chunks, plan.ny
    pairs = (
        (vel_ref, vel),
        (stress_ref, stress),
        (zones_ref, zones),
        (slip_ref, slip),
        (ocean_ref, ocean),
        (bathy_ref, bathy),
    )
    copies = [
        pltpu.make_async_copy(source, target, sems.at[i])
        for i, (source, target) in enumerate(pairs)
    ]
    for copy in copies:
        copy.start()

    def joined(ref, *at):
        parts = [ref[(*at, pl.ds(kc * sub, sub), slice(None))] for kc in range(chunks)]
        return jnp.concatenate(parts, axis=-1) if chunks > 1 else parts[0]

    copies[0].wait()
    for f in range(3):
        for x in range(cells):
            crust[f * cells + x] = joined(vel, f, x)
    copies[1].wait()
    for f in range(6):
        for x in range(cells):
            crust[(3 + f) * cells + x] = joined(stress, f, x)
    copies[2].wait()
    for x in range(cells):
        crust[9 * cells + x] = (joined(zones, x) + 1).astype(F32)
    copies[3].wait()
    fault_chunk = (plan.depth // 2) // sub
    pieces = [
        slip[...] if kc == fault_chunk else jnp.zeros((cells, ny), F32) for kc in range(chunks)
    ]
    fault = jnp.concatenate(pieces, axis=-1) if chunks > 1 else pieces[0]
    if sub > cells:
        fault = jnp.concatenate([fault, jnp.zeros((sub - cells, plan.lanes), F32)], axis=0)
    crust[10 * cells] = fault
    copies[4].wait()
    copies[5].wait()


class Shifts:
    def __init__(self, plan):
        self.plan = plan
        shape = (plan.sub, plan.lanes)
        self.row = lax.broadcasted_iota(jnp.int32, shape, 0)
        self.lane = lax.broadcasted_iota(jnp.int32, shape, 1)
        self.y = lax.rem(self.lane, plan.ny)
        self.first_row = self.row == 0
        self.last_row = self.row == plan.sub - 1
        self.top = self.first_row & (self.lane < plan.ny)
        self.floor_cell = self.last_row & (self.lane >= plan.lanes - plan.ny)
        self.not_low_y = jnp.where(self.y == 0, 0.0, 1.0).astype(F32)
        self.not_high_y = jnp.where(self.y == plan.ny - 1, 0.0, 1.0).astype(F32)
        self.depth = (
            lax.div(self.lane, plan.ny) * plan.sub + self.row
        ).astype(F32)

    def dy(self, f):
        lanes = self.plan.lanes
        return pltpu.roll(f, lanes - 1, 1) * self.not_high_y - pltpu.roll(f, 1, 1) * self.not_low_y

    def below(self, f):
        plan = self.plan
        moved = pltpu.roll(f, plan.sub - 1, 0)
        if plan.chunks > 1:
            moved = jnp.where(self.last_row, pltpu.roll(moved, plan.lanes - plan.ny, 1), moved)
        return jnp.where(self.floor_cell, 0.0, moved)

    def above(self, f, top):
        plan = self.plan
        moved = pltpu.roll(f, 1, 0)
        if plan.chunks > 1:
            moved = jnp.where(self.first_row, pltpu.roll(moved, plan.ny, 1), moved)
        return jnp.where(self.top, top, moved)

    def seafloor(self, vz):
        row = self.over_chunks(jnp.where(self.top, vz, 0.0)[0:1])
        return jnp.broadcast_to(row, vz.shape)

    def over_chunks(self, f):
        shift = self.plan.ny
        while shift < self.plan.lanes:
            f = f + pltpu.roll(f, shift, 1)
            shift *= 2
        return f


def acceleration(sh, stress, j):
    sxy, sxz = stress[SXY, j], stress[SXZ, j]
    syz, szz = stress[SYZ, j], stress[SZZ, j]
    ax = stress[SXX, j + 1] - stress[SXX, j - 1] + sh.dy(sxy) + sh.below(sxz) - sh.above(sxz, 0.0)
    ay = stress[SXY, j + 1] - stress[SXY, j - 1] + sh.dy(stress[SYY, j])
    ay = ay + sh.below(syz) - sh.above(syz, 0.0)
    az = stress[SXZ, j + 1] - stress[SXZ, j - 1] + sh.dy(syz) + sh.below(szz) - sh.above(szz, 0.0)
    return ax, ay, az


def strained(sh, vel, stress, mats, j):
    vx, vy, vz = vel[VX, j], vel[VY, j], vel[VZ, j]
    exx = vel[VX, j + 1] - vel[VX, j - 1]
    eyy = sh.dy(vy)
    ezz = sh.below(vz) - sh.above(vz, vz)
    mu = mats[SHEAR, j]
    mu2 = mu + mu
    common = mats[LAMB, j] * (exx + eyy + ezz)
    exy = sh.dy(vx) + vel[VY, j + 1] - vel[VY, j - 1]
    exz = sh.below(vx) - sh.above(vx, vx) + vel[VZ, j + 1] - vel[VZ, j - 1]
    eyz = sh.below(vy) - sh.above(vy, vy) + sh.dy(vz)
    return (
        stress[SXX, j] + (common + mu2 * exx),
        stress[SYY, j] + (common + mu2 * eyy),
        stress[SZZ, j] + (common + mu2 * ezz),
        stress[SXY, j] + mu * exy,
        stress[SXZ, j] + (mu * exz + mats[FAULT, j]),
        stress[SYZ, j] + mu * eyz,
    )


def begin_kernel(plan, table, own, mate, other, vel, stress, mats):
    cells, sub = plan.cells, plan.sub
    sh = Shifts(plan)
    odd = odd_device()
    starts = (HALO, (HALO + cells) * (1 - odd), (HALO + cells) * odd)
    for start, ref in zip(starts, (own, mate, other)):
        def bring(x, start=start, ref=ref):
            j = start + x
            for f in range(3):
                vel[f, j] = ref[f * cells + x]
            for f in range(6):
                stress[f, j] = ref[(3 + f) * cells + x]
            zone = ref[9 * cells + x]
            values = [jnp.zeros_like(zone) for _ in range(3)]
            for z in range(ZONES):
                here = zone == float(z + 1)
                values = [jnp.where(here, table[c, z], values[c]) for c in range(3)]
            for c in range(3):
                mats[c, j] = values[c] * HALF
            slip = jnp.broadcast_to(ref[10 * cells, pl.ds(x, 1), :], (sub, plan.lanes))
            mats[FAULT, j] = jnp.where(sh.row == (plan.depth // 2) % sub, DT * slip, 0.0)
            mats[FLOOR, j] = sh.seafloor(ref[VZ * cells + x])

        plan.planes(0, cells, bring)

    def move(j):
        b = mats[BUOY, j]
        for f, a in enumerate(acceleration(sh, stress, j)):
            vel[f, j] = vel[f, j] + b * a

    plan.planes(1, plan.width - 1, move)


def middle_kernel(
    plan, arrived, swapped, vel_in, stress_in, mats, vel, stress, loads, message,
    oc, water, bottom, gather, depths,
):
    sub, chunks, n, strips = plan.sub, plan.chunks, plan.n, plan.strips
    width, sent = plan.width, plan.sent_groups
    sh = Shifts(plan)
    odd = odd_device()

    half = n // 2
    mate = 1 - odd

    def turn(owner, group):
        for core, ref in ((odd, arrived), (mate, swapped)):
            for kc in range(chunks):
                for yl in range(strips):
                    at = owner * plan.rows + (kc * strips + yl) * sent + group
                    to = kc * plan.ny + core * strips + yl
                    gather[pl.ds(to, half, stride=2 * strips), :] = ref[
                        pl.ds(at, half, stride=2 * plan.rows), :
                    ]
        return gather[...].T

    def spread(turned, group):
        for i in range(chunks):
            for f in range(4):
                at = (i * 4 + f) * sub
                oc[f, 1 + group * chunks + i] = turned[at : at + sub]

    ends = []
    for group in range(sent):
        turned = turn(odd, group)
        spread(turned, group + plan.halo_groups * odd)
        if group == 0:
            ends.append((turned[2 * sub : 3 * sub], turned[3 * sub : 4 * sub]))
        if group == sent - 1:
            ends.append((turned[LANES - 2 * sub : LANES - sub], turned[LANES - sub :]))
    for group in range(plan.halo_groups):
        spread(turn(mate, group + plan.own_groups * odd), group + sent * mate)
    turned = turn(mate, plan.own_groups - odd)
    is_odd = odd == 1
    oc[0, (width + 1) * odd] = jnp.where(is_odd, ends[1][0], ends[0][0])
    oc[0, (width + 1) * mate] = jnp.where(
        is_odd, turned[LANES - 4 * sub : LANES - 3 * sub], turned[:sub]
    )
    deep = jnp.where(is_odd, ends[1][1], ends[0][1])
    for kc in range(chunks):
        mine = (sh.lane >= kc * plan.ny) & (sh.lane < (kc + 1) * plan.ny)
        depths[kc * sub : (kc + 1) * sub, :] = sh.over_chunks(jnp.where(mine, deep, 0.0))

    def mask(j):
        low = jnp.broadcast_to(depths[pl.ds(j, 1), :], (sub, plan.lanes))
        wet = jnp.where(sh.depth < low, 1.0, 0.0).astype(F32)
        water[j] = wet
        bottom[j] = jnp.where(sh.depth == low - 1.0, 1.0, 0.0).astype(F32)
        oc[0, j] = oc[0, j] * wet

    def mask_x(j):
        oc[1, j] = oc[1, j] * water[j]

    def mask_yw(j):
        oc[2, j] = oc[2, j] * water[j]
        oc[3, j] = oc[3, j] * water[j]

    plan.planes(0, width + 2, mask)
    plan.planes(1, width + 1, mask_x)
    plan.planes(2, width, mask_yw)

    for t in range(STEPS):
        first, last = 2 * t, width - 2 * t
        before = t == 0

        def flow_x(j):
            oc[1, j + 1] = water[j + 1] * (oc[1, j + 1] - HALF * (oc[0, j + 2] - oc[0, j]))

        def flow(j):
            p = oc[0, j + 1]
            wet = water[j + 1]
            oc[2, j + 1] = wet * (oc[2, j + 1] - HALF * sh.dy(p))
            rise = sh.below(p) + bottom[j + 1] * p - sh.above(p, -p)
            oc[3, j + 1] = wet * (oc[3, j + 1] - (HALF * rise + (DT * GRAV) * p))

        def press(j):
            w = oc[3, j + 1]
            floor = mats[FLOOR, j] if before else sh.seafloor(vel[VZ, j])
            rise = sh.below(w) + bottom[j + 1] * floor - sh.above(w, w)
            total = oc[1, j + 2] - oc[1, j] + sh.dy(oc[2, j + 1]) + rise
            oc[0, j + 1] = water[j + 1] * (oc[0, j + 1] - (HALF * KBULK) * total)

        def load(j):
            column = jnp.sum(bottom[j + 1] * oc[0, j + 1], axis=0, keepdims=True)
            column = jnp.broadcast_to(sh.over_chunks(column), (sub, plan.lanes))
            return jnp.where(sh.top, column, 0.0)

        plan.planes(first, last, flow_x)
        plan.planes(first + 1, last - 1, flow)
        plan.planes(first + 1, last - 1, press)
        if before:
            def add_load(j):
                for f in (VX, VY):
                    vel[f, j] = vel_in[f, j]
                vel[VZ, j] = vel_in[VZ, j] + mats[BUOY, j] * load(j)

            plan.planes(first + 1, last - 1, add_load)
        elif t < STEPS - 1:
            def move(j):
                ax, ay, az = acceleration(sh, stress, j)
                b = mats[BUOY, j]
                vel[VX, j] = vel[VX, j] + b * ax
                vel[VY, j] = vel[VY, j] + b * ay
                vel[VZ, j] = vel[VZ, j] + b * (az + load(j))

            plan.planes(first + 1, last - 1, move)
        else:
            def keep(j):
                loads[j] = load(j)

            plan.planes(first + 1, last - 1, keep)
        if t < STEPS - 2:
            def strain(j):
                source = stress_in if before else stress
                for f, value in enumerate(strained(sh, vel, source, mats, j)):
                    stress[f, j] = value

            plan.planes(first + 2, last - 2, strain)

    for group in range(plan.own_groups):
        stacked = jnp.concatenate(
            [
                oc[f, 1 + HALO + group * chunks + i]
                for i in range(chunks)
                for f in range(4)
            ],
            axis=0,
        )
        gather[...] = stacked.T
        for kc in range(chunks):
            for yl in range(strips):
                at = group * plan.lead + kc * strips + yl
                message[pl.ds(at, n, stride=plan.back_rows), :] = gather[
                    pl.ds(kc * plan.ny + yl, n, stride=strips), :
                ]


def end_kernel(plan, vel_in, stress_in, mats, loads, vel_out, stress_out, vel, stress):
    cells, sub, chunks, ny = plan.cells, plan.sub, plan.chunks, plan.ny
    sh = Shifts(plan)
    first, last = 2 * (STEPS - 1), plan.width - 2 * (STEPS - 1)

    def put(out, f, x, plane):
        for kc in range(chunks):
            out[f, x, kc * sub : (kc + 1) * sub, :] = plane[:, kc * ny : (kc + 1) * ny]

    def strain(j):
        for f, value in enumerate(strained(sh, vel_in, stress_in, mats, j)):
            stress[f, j] = value

    def move(j):
        ax, ay, az = acceleration(sh, stress, j)
        b = mats[BUOY, j]
        for f, a in enumerate((ax, ay, az + loads[j])):
            vel[f, j] = vel_in[f, j] + b * a

    def finish(x):
        for f in range(3):
            put(vel_out, f, x, vel[f, x + HALO])
        for f, value in enumerate(strained(sh, vel, stress, mats, x + HALO)):
            put(stress_out, f, x, value)

    plan.planes(first, last, strain)
    plan.planes(first + 1, last - 1, move)
    plan.planes(0, cells, finish)


def unpack_kernel(plan, arrived, ocean, turned):
    sub, chunks = plan.sub, plan.chunks
    block = 4 * sub
    for yl in range(plan.strips):
        by_chunk = [
            arrived[pl.ds(kc * plan.strips + yl, plan.nx // chunks, stride=plan.lead), :]
            for kc in range(chunks)
        ]
        for i in range(chunks):
            turned[pl.ds(i, plan.nx // chunks, stride=chunks), :] = place(
                by_chunk, [i] * chunks, block
            )
        whole = turned[...].T
        for kc in range(chunks):
            for f in range(4):
                at = (kc * 4 + f) * sub
                ocean[f, yl, kc * sub : (kc + 1) * sub, :] = whole[at : at + sub]


def on_device(plan, velocity, stress, ocean, zones, materials, slip, bathy):
    n, cells, sub, lanes, width = plan.n, plan.cells, plan.sub, plan.lanes, plan.width
    vmem = pl.BlockSpec(memory_space=pltpu.VMEM)
    smem = pl.BlockSpec(memory_space=pltpu.SMEM)
    hbm = pl.BlockSpec(memory_space=pltpu.HBM)

    def shape(*dims):
        return jax.ShapeDtypeStruct(dims, F32)

    def like(array):
        return jax.ShapeDtypeStruct(array.shape, array.dtype)

    def held(array):
        return pltpu.VMEM(array.shape, array.dtype)

    def call(kernel, name, out, ins, scratch, room=16, **rest):
        room = room if plan.unrolled else 56
        return pl.pallas_call(
            functools.partial(kernel, plan),
            out_shape=out,
            in_specs=ins,
            out_specs=jax.tree.map(lambda _: vmem, out),
            scratch_shapes=scratch,
            compiler_params=pltpu.CompilerParams(vmem_limit_bytes=room * 1024 * 1024),
            name=name,
            **rest,
        )

    def pinned(array):
        return pltpu.with_memory_space_constraint(array, pltpu.HBM)

    mates = [(i, i ^ 1) for i in range(n)]
    others = [(i, i + 1) for i in range(1, n - 1, 2)]
    others += [(target, source) for source, target in others]
    crust, ocean_near, bathy_near = call(
        crust_kernel,
        "crust_planes",
        (shape(10 * cells + 1, sub, lanes), like(ocean), like(bathy)),
        [hbm] * 6,
        [held(velocity), held(stress), held(zones), held(slip), pltpu.SemaphoreType.DMA((6,))],
    )(*(pinned(a) for a in (velocity, stress, zones, slip, ocean, bathy)))
    other = lax.ppermute(crust, "map", others)
    message = call(
        ocean_kernel,
        "ocean_rows",
        shape(n * plan.rows, LANES),
        [vmem] * 2,
        [
            pltpu.VMEM((plan.strips, plan.nx, LANES), F32),
            pltpu.VMEM(
                (plan.lead, plan.nx // plan.chunks + 2 * plan.halo_groups, LANES), F32
            ),
            pltpu.VMEM((n * plan.strips, LANES), F32),
        ],
    )(ocean_near, bathy_near)
    arrived = lax.all_to_all(
        message.reshape(n // 2, 2 * plan.rows, LANES),
        "map",
        split_axis=0,
        concat_axis=0,
        axis_index_groups=[list(range(core, n, 2)) for core in range(2)],
        tiled=True,
    ).reshape(n * plan.rows, LANES)
    mate = lax.ppermute(crust, "map", mates)
    vel, strs, mats = call(
        begin_kernel,
        "first_velocity",
        (shape(3, width, sub, lanes), shape(6, width, sub, lanes), shape(5, width, sub, lanes)),
        [smem] + [vmem] * 3,
        [],
        cost_estimate=pl.CostEstimate(
            flops=10**12, bytes_accessed=2 * 10**9, transcendentals=0
        ),
    )(materials, crust, mate, other)
    arrived, vel = lax.optimization_barrier((arrived, vel))
    swapped = lax.ppermute(arrived, "map", mates)
    vel, strs, loads, back = call(
        middle_kernel,
        "substeps",
        (
            shape(3, width, sub, lanes),
            shape(6, width, sub, lanes),
            shape(width, sub, lanes),
            shape(n * plan.back_rows, LANES),
        ),
        [vmem] * 5,
        [
            pltpu.VMEM((4, width + 2, sub, lanes), F32),
            pltpu.VMEM((width + 2, sub, lanes), F32),
            pltpu.VMEM((width + 2, sub, lanes), F32),
            pltpu.VMEM((lanes, LANES), F32),
            pltpu.VMEM((plan.depth, lanes), F32),
        ],
        input_output_aliases={2: 0, 3: 1},
    )(arrived, swapped, vel, strs, mats)
    returned = lax.all_to_all(
        back.reshape(n, plan.back_rows, LANES), "map", split_axis=0, concat_axis=0, tiled=True
    ).reshape(n * plan.back_rows, LANES)
    new_velocity, new_stress = call(
        end_kernel,
        "last_updates",
        (shape(*velocity.shape), shape(*stress.shape)),
        [vmem] * 4,
        [
            pltpu.VMEM((3, width, sub, lanes), F32),
            pltpu.VMEM((6, width, sub, lanes), F32),
        ],
    )(vel, strs, mats, loads)
    new_ocean = call(
        unpack_kernel,
        "ocean_strips",
        shape(*ocean.shape),
        [vmem],
        [pltpu.VMEM((plan.nx, LANES), F32)],
    )(returned)
    return new_velocity, new_stress, new_ocean


def solution(mesh):
    n = mesh.shape["map"]

    def body(velocity, stress, ocean, zones, materials, slip, bathy):
        _, cells, depth, ny = velocity.shape
        plan = Plan(n, cells, depth, ny, ocean.shape[1])
        return on_device(plan, velocity, stress, ocean, zones, materials, slip, bathy)

    return jax.shard_map(
        body,
        mesh=mesh,
        in_specs=(
            P("parts", "map", None, None),
            P("parts", "map", None, None),
            P("parts", "map", None, None),
            P("map", "parts", None),
            P(),
            P("map", "parts"),
            P("map", "parts"),
        ),
        out_specs=(
            P("parts", "map", None, None),
            P("parts", "map", None, None),
            P("parts", "map", None, None),
        ),
        check_vma=False,
    )
```

```python
import functools

import jax
import jax.numpy as jnp
from jax import lax
from jax.experimental import pallas as pl
from jax.experimental.pallas import tpu as pltpu
from jax.sharding import PartitionSpec as P

STEPS = 4
ZONES = 8
DT = 0.25
HALF = 0.5 * DT
KBULK = 2.25
GRAV = 0.1
HALO = 2 * STEPS
LANES = 128
F32 = jnp.float32
VX, VY, VZ = range(3)
SXX, SYY, SZZ, SXY, SXZ, SYZ = range(6)
BUOY, LAMB, SHEAR, FAULT, FLOOR = range(5)


class Plan:
    def __init__(self, devices, cells, depth, ny, strips):
        self.n = devices
        self.cells = cells
        self.depth = depth
        self.ny = ny
        self.strips = strips
        self.chunks = max(1, LANES // ny)
        self.sub = depth // self.chunks
        self.lanes = self.chunks * ny
        self.width = cells + 2 * HALO
        self.own_groups = cells // self.chunks
        self.halo_groups = HALO // self.chunks
        self.sent_groups = self.own_groups + self.halo_groups
        self.lead = self.chunks * strips
        self.rows = self.lead * self.sent_groups
        self.back_rows = self.lead * self.own_groups
        self.nx = devices * cells
        self.block = 4 * self.sub
        self.unrolled = self.sub * self.lanes <= 1024
        assert devices % 2 == 0 and cells == HALO and self.block * self.chunks == LANES

    def planes(self, start, stop, body):
        if self.unrolled:
            for j in range(start, stop):
                body(j)
        else:
            def run(j, carry):
                body(j)
                return carry

            lax.fori_loop(start, stop, run, 0)


def odd_device():
    return lax.rem(lax.axis_index("map"), 2)


def place(pieces, wanted, block):
    out = None
    for i, piece in enumerate(pieces):
        shift = (i - wanted[i]) * block % piece.shape[-1]
        moved = pltpu.roll(piece, shift, piece.ndim - 1) if shift else piece
        if out is None:
            out = moved
        else:
            lane = lax.broadcasted_iota(jnp.int32, moved.shape, moved.ndim - 1)
            out = jnp.where(lane >= i * block, moved, out)
    return out


def ocean_kernel(plan, ocean, bathy, message, turned, grouped, extra):
    cells, sub, chunks, n, strips = plan.cells, plan.sub, plan.chunks, plan.n, plan.strips
    block, sent, rows = plan.block, plan.sent_groups, plan.rows
    border = jnp.zeros((plan.lead, plan.halo_groups, LANES), F32)
    count = plan.nx // chunks
    grouped[:, : plan.halo_groups, :] = border
    grouped[:, plan.halo_groups + count :, :] = border
    for yl in range(strips):
        stacked = jnp.concatenate(
            [ocean[f, yl, kc * sub : (kc + 1) * sub, :] for kc in range(chunks) for f in range(4)],
            axis=0,
        )
        turned[yl] = stacked.T
        by_x = [turned[yl, pl.ds(i, count, stride=chunks), :] for i in range(chunks)]
        for kc in range(chunks):
            grouped[kc * strips + yl, pl.ds(plan.halo_groups, count), :] = place(
                by_x, [kc] * chunks, block
            )
    for d in range(n):
        start = d * plan.own_groups + (d % 2) * plan.halo_groups
        for q in range(plan.lead):
            message[d * rows + q * sent : d * rows + (q + 1) * sent, :] = grouped[
                q, start : start + sent, :
            ]
    depths = bathy[...].astype(F32)
    wide = lax.broadcasted_iota(jnp.int32, depths.shape, 1)
    for d in range(n):
        first = d * cells - HALO - 1
        moved = pltpu.roll(depths, -first % plan.nx, 1)
        moved = jnp.where((wide + first >= 0) & (wide + first < plan.nx), moved, 0.0)
        extra[d * strips : (d + 1) * strips, :] = moved[:, :LANES]
    pairs = n // 2
    lane = lax.broadcasted_iota(jnp.int32, (pairs, LANES), 1)
    blank = jnp.zeros((1, LANES), F32)
    for odd in range(2):
        slot = (odd * (chunks - 1) * 4 + 2) * sub
        group = odd * (sent - 1)
        for yl in range(strips):
            if odd:
                column = turned[yl, pl.ds(2 * cells + HALO, pairs - 1, stride=2 * cells), :]
                column = jnp.concatenate([column, blank], axis=0)
            else:
                column = turned[yl, pl.ds(2 * cells - HALO - 1, pairs - 1, stride=2 * cells), :]
                column = jnp.concatenate([blank, column], axis=0)
            deep = extra[pl.ds(odd * strips + yl, pairs, stride=2 * strips), :]
            for kc in range(chunks):
                at = odd * rows + (kc * strips + yl) * sent + group
                old = message[pl.ds(at, pairs, stride=2 * rows), :]
                edge = pltpu.roll(column, (slot - kc * block) % LANES, 1)
                floor = pltpu.roll(deep, (slot + sub - kc * sub) % LANES, 1)
                new = jnp.where((lane >= slot) & (lane < slot + sub), edge, old)
                new = jnp.where((lane >= slot + sub) & (lane < slot + 2 * sub), floor, new)
                message[pl.ds(at, pairs, stride=2 * rows), :] = new


def crust_kernel(
    plan, vel_ref, stress_ref, zones_ref, slip_ref, ocean_ref, bathy_ref,
    crust, ocean, bathy, vel, stress, zones, slip, sems,
):
    cells, sub, chunks, ny = plan.cells, plan.sub, plan.chunks, plan.ny
    pairs = (
        (vel_ref, vel),
        (stress_ref, stress),
        (zones_ref, zones),
        (slip_ref, slip),
        (ocean_ref, ocean),
        (bathy_ref, bathy),
    )
    copies = [
        pltpu.make_async_copy(source, target, sems.at[i])
        for i, (source, target) in enumerate(pairs)
    ]
    for copy in copies:
        copy.start()

    def joined(ref, *at):
        parts = [ref[(*at, pl.ds(kc * sub, sub), slice(None))] for kc in range(chunks)]
        return jnp.concatenate(parts, axis=-1) if chunks > 1 else parts[0]

    copies[0].wait()
    for f in range(3):
        for x in range(cells):
            crust[f * cells + x] = joined(vel, f, x)
    copies[1].wait()
    for f in range(6):
        for x in range(cells):
            crust[(3 + f) * cells + x] = joined(stress, f, x)
    copies[2].wait()
    for x in range(cells):
        crust[9 * cells + x] = (joined(zones, x) + 1).astype(F32)
    copies[3].wait()
    fault_chunk = (plan.depth // 2) // sub
    pieces = [
        slip[...] if kc == fault_chunk else jnp.zeros((cells, ny), F32) for kc in range(chunks)
    ]
    fault = jnp.concatenate(pieces, axis=-1) if chunks > 1 else pieces[0]
    if sub > cells:
        fault = jnp.concatenate([fault, jnp.zeros((sub - cells, plan.lanes), F32)], axis=0)
    crust[10 * cells] = fault
    copies[4].wait()
    copies[5].wait()


class Shifts:
    def __init__(self, plan):
        self.plan = plan
        shape = (plan.sub, plan.lanes)
        self.row = lax.broadcasted_iota(jnp.int32, shape, 0)
        self.lane = lax.broadcasted_iota(jnp.int32, shape, 1)
        self.y = lax.rem(self.lane, plan.ny)
        self.first_row = self.row == 0
        self.last_row = self.row == plan.sub - 1
        self.top = self.first_row & (self.lane < plan.ny)
        self.floor_cell = self.last_row & (self.lane >= plan.lanes - plan.ny)
        self.not_low_y = jnp.where(self.y == 0, 0.0, 1.0).astype(F32)
        self.not_high_y = jnp.where(self.y == plan.ny - 1, 0.0, 1.0).astype(F32)
        self.depth = (
            lax.div(self.lane, plan.ny) * plan.sub + self.row
        ).astype(F32)

    def dy(self, f):
        lanes = self.plan.lanes
        return pltpu.roll(f, lanes - 1, 1) * self.not_high_y - pltpu.roll(f, 1, 1) * self.not_low_y

    def below(self, f):
        plan = self.plan
        moved = pltpu.roll(f, plan.sub - 1, 0)
        if plan.chunks > 1:
            moved = jnp.where(self.last_row, pltpu.roll(moved, plan.lanes - plan.ny, 1), moved)
        return jnp.where(self.floor_cell, 0.0, moved)

    def above(self, f, top):
        plan = self.plan
        moved = pltpu.roll(f, 1, 0)
        if plan.chunks > 1:
            moved = jnp.where(self.first_row, pltpu.roll(moved, plan.ny, 1), moved)
        return jnp.where(self.top, top, moved)

    def seafloor(self, vz):
        row = self.over_chunks(jnp.where(self.top, vz, 0.0)[0:1])
        return jnp.broadcast_to(row, vz.shape)

    def over_chunks(self, f):
        shift = self.plan.ny
        while shift < self.plan.lanes:
            f = f + pltpu.roll(f, shift, 1)
            shift *= 2
        return f


def acceleration(sh, stress, j):
    sxy, sxz = stress[SXY, j], stress[SXZ, j]
    syz, szz = stress[SYZ, j], stress[SZZ, j]
    ax = stress[SXX, j + 1] - stress[SXX, j - 1] + sh.dy(sxy) + sh.below(sxz) - sh.above(sxz, 0.0)
    ay = stress[SXY, j + 1] - stress[SXY, j - 1] + sh.dy(stress[SYY, j])
    ay = ay + sh.below(syz) - sh.above(syz, 0.0)
    az = stress[SXZ, j + 1] - stress[SXZ, j - 1] + sh.dy(syz) + sh.below(szz) - sh.above(szz, 0.0)
    return ax, ay, az


def strained(sh, vel, stress, mats, j):
    vx, vy, vz = vel[VX, j], vel[VY, j], vel[VZ, j]
    exx = vel[VX, j + 1] - vel[VX, j - 1]
    eyy = sh.dy(vy)
    ezz = sh.below(vz) - sh.above(vz, vz)
    mu = mats[SHEAR, j]
    mu2 = mu + mu
    common = mats[LAMB, j] * (exx + eyy + ezz)
    exy = sh.dy(vx) + vel[VY, j + 1] - vel[VY, j - 1]
    exz = sh.below(vx) - sh.above(vx, vx) + vel[VZ, j + 1] - vel[VZ, j - 1]
    eyz = sh.below(vy) - sh.above(vy, vy) + sh.dy(vz)
    return (
        stress[SXX, j] + (common + mu2 * exx),
        stress[SYY, j] + (common + mu2 * eyy),
        stress[SZZ, j] + (common + mu2 * ezz),
        stress[SXY, j] + mu * exy,
        stress[SXZ, j] + (mu * exz + mats[FAULT, j]),
        stress[SYZ, j] + mu * eyz,
    )


def begin_kernel(plan, table, own, mate, both, vel, stress, mats):
    cells, sub = plan.cells, plan.sub
    sh = Shifts(plan)
    odd = odd_device()
    here = lax.axis_index("map")
    inner = (here > 0) & (here < plan.n - 1)
    starts = (HALO, (HALO + cells) * (1 - odd), (HALO + cells) * odd)
    reads = (
        lambda i: own[i],
        lambda i: mate[i],
        lambda i: jnp.where(inner, both[odd, i], 0.0),
    )
    for start, read in zip(starts, reads):
        def bring(x, start=start, read=read):
            j = start + x
            for f in range(3):
                vel[f, j] = read(f * cells + x)
            for f in range(6):
                stress[f, j] = read((3 + f) * cells + x)
            zone = read(9 * cells + x)
            values = [jnp.zeros_like(zone) for _ in range(3)]
            for z in range(ZONES):
                here = zone == float(z + 1)
                values = [jnp.where(here, table[c, z], values[c]) for c in range(3)]
            for c in range(3):
                mats[c, j] = values[c] * HALF
            slips = read(10 * cells)
            slip = jnp.sum(jnp.where(sh.row == x, slips, 0.0), axis=0, keepdims=True)
            slip = jnp.broadcast_to(slip, (sub, plan.lanes))
            mats[FAULT, j] = jnp.where(sh.row == (plan.depth // 2) % sub, DT * slip, 0.0)
            mats[FLOOR, j] = sh.seafloor(vel[VZ, j])

        plan.planes(0, cells, bring)

    def move(j):
        b = mats[BUOY, j]
        for f, a in enumerate(acceleration(sh, stress, j)):
            vel[f, j] = vel[f, j] + b * a

    plan.planes(1, plan.width - 1, move)


def middle_kernel(
    plan, arrived, swapped, vel_in, stress_in, mats, vel, stress, loads, message,
    oc, water, bottom, gather, depths,
):
    sub, chunks, n, strips = plan.sub, plan.chunks, plan.n, plan.strips
    width, sent = plan.width, plan.sent_groups
    sh = Shifts(plan)
    odd = odd_device()

    half = n // 2
    mate = 1 - odd

    def turn(owner, group):
        for core, ref in ((odd, arrived), (mate, swapped)):
            for kc in range(chunks):
                for yl in range(strips):
                    at = owner * plan.rows + (kc * strips + yl) * sent + group
                    to = kc * plan.ny + core * strips + yl
                    gather[pl.ds(to, half, stride=2 * strips), :] = ref[
                        pl.ds(at, half, stride=2 * plan.rows), :
                    ]
        return gather[...].T

    def spread(turned, group):
        for i in range(chunks):
            for f in range(4):
                at = (i * 4 + f) * sub
                oc[f, 1 + group * chunks + i] = turned[at : at + sub]

    ends = []
    for group in range(sent):
        turned = turn(odd, group)
        spread(turned, group + plan.halo_groups * odd)
        if group == 0:
            ends.append((turned[2 * sub : 3 * sub], turned[3 * sub : 4 * sub]))
        if group == sent - 1:
            ends.append((turned[LANES - 2 * sub : LANES - sub], turned[LANES - sub :]))
    for group in range(plan.halo_groups):
        spread(turn(mate, group + plan.own_groups * odd), group + sent * mate)
    turned = turn(mate, plan.own_groups - odd)
    is_odd = odd == 1
    oc[0, (width + 1) * odd] = jnp.where(is_odd, ends[1][0], ends[0][0])
    oc[0, (width + 1) * mate] = jnp.where(
        is_odd, turned[LANES - 4 * sub : LANES - 3 * sub], turned[:sub]
    )
    deep = jnp.where(is_odd, ends[1][1], ends[0][1])
    for kc in range(chunks):
        mine = (sh.lane >= kc * plan.ny) & (sh.lane < (kc + 1) * plan.ny)
        depths[kc * sub : (kc + 1) * sub, :] = sh.over_chunks(jnp.where(mine, deep, 0.0))

    def mask(j):
        low = jnp.broadcast_to(depths[pl.ds(j, 1), :], (sub, plan.lanes))
        wet = jnp.where(sh.depth < low, 1.0, 0.0).astype(F32)
        water[j] = wet
        bottom[j] = jnp.where(sh.depth == low - 1.0, 1.0, 0.0).astype(F32)
        oc[0, j] = oc[0, j] * wet

    def mask_x(j):
        oc[1, j] = oc[1, j] * water[j]

    def mask_yw(j):
        oc[2, j] = oc[2, j] * water[j]
        oc[3, j] = oc[3, j] * water[j]

    plan.planes(0, width + 2, mask)
    plan.planes(1, width + 1, mask_x)
    plan.planes(2, width, mask_yw)

    for t in range(STEPS):
        first, last = 2 * t, width - 2 * t
        before = t == 0

        def flow_x(j):
            oc[1, j + 1] = water[j + 1] * (oc[1, j + 1] - HALF * (oc[0, j + 2] - oc[0, j]))

        def flow(j):
            p = oc[0, j + 1]
            wet = water[j + 1]
            oc[2, j + 1] = wet * (oc[2, j + 1] - HALF * sh.dy(p))
            rise = sh.below(p) + bottom[j + 1] * p - sh.above(p, -p)
            oc[3, j + 1] = wet * (oc[3, j + 1] - (HALF * rise + (DT * GRAV) * p))

        def press(j):
            w = oc[3, j + 1]
            floor = mats[FLOOR, j] if before else sh.seafloor(vel[VZ, j])
            rise = sh.below(w) + bottom[j + 1] * floor - sh.above(w, w)
            total = oc[1, j + 2] - oc[1, j] + sh.dy(oc[2, j + 1]) + rise
            oc[0, j + 1] = water[j + 1] * (oc[0, j + 1] - (HALF * KBULK) * total)

        def load(j):
            column = jnp.sum(bottom[j + 1] * oc[0, j + 1], axis=0, keepdims=True)
            column = jnp.broadcast_to(sh.over_chunks(column), (sub, plan.lanes))
            return jnp.where(sh.top, column, 0.0)

        plan.planes(first, last, flow_x)
        plan.planes(first + 1, last - 1, flow)
        plan.planes(first + 1, last - 1, press)
        if before:
            def add_load(j):
                for f in (VX, VY):
                    vel[f, j] = vel_in[f, j]
                vel[VZ, j] = vel_in[VZ, j] + mats[BUOY, j] * load(j)

            plan.planes(first + 1, last - 1, add_load)
        elif t < STEPS - 1:
            def move(j):
                ax, ay, az = acceleration(sh, stress, j)
                b = mats[BUOY, j]
                vel[VX, j] = vel[VX, j] + b * ax
                vel[VY, j] = vel[VY, j] + b * ay
                vel[VZ, j] = vel[VZ, j] + b * (az + load(j))

            plan.planes(first + 1, last - 1, move)
        else:
            def keep(j):
                loads[j] = load(j)

            plan.planes(first + 1, last - 1, keep)
        if t < STEPS - 2:
            def strain(j):
                source = stress_in if before else stress
                for f, value in enumerate(strained(sh, vel, source, mats, j)):
                    stress[f, j] = value

            plan.planes(first + 2, last - 2, strain)

    for group in range(plan.own_groups):
        stacked = jnp.concatenate(
            [
                oc[f, 1 + HALO + group * chunks + i]
                for i in range(chunks)
                for f in range(4)
            ],
            axis=0,
        )
        gather[...] = stacked.T
        for kc in range(chunks):
            for yl in range(strips):
                at = group * plan.lead + kc * strips + yl
                message[pl.ds(at, n, stride=plan.back_rows), :] = gather[
                    pl.ds(kc * plan.ny + yl, n, stride=strips), :
                ]


def end_kernel(plan, vel_in, stress_in, mats, loads, vel_out, stress_out, vel, stress):
    cells, sub, chunks, ny = plan.cells, plan.sub, plan.chunks, plan.ny
    sh = Shifts(plan)
    first, last = 2 * (STEPS - 1), plan.width - 2 * (STEPS - 1)

    def put(out, f, x, plane):
        for kc in range(chunks):
            out[f, x, kc * sub : (kc + 1) * sub, :] = plane[:, kc * ny : (kc + 1) * ny]

    def strain(j):
        for f, value in enumerate(strained(sh, vel_in, stress_in, mats, j)):
            stress[f, j] = value

    def move(j):
        ax, ay, az = acceleration(sh, stress, j)
        b = mats[BUOY, j]
        for f, a in enumerate((ax, ay, az + loads[j])):
            vel[f, j] = vel_in[f, j] + b * a

    def finish(x):
        for f in range(3):
            put(vel_out, f, x, vel[f, x + HALO])
        for f, value in enumerate(strained(sh, vel, stress, mats, x + HALO)):
            put(stress_out, f, x, value)

    plan.planes(first, last, strain)
    plan.planes(first + 1, last - 1, move)
    plan.planes(0, cells, finish)


def unpack_kernel(plan, arrived, ocean, turned):
    sub, chunks = plan.sub, plan.chunks
    block = 4 * sub
    for yl in range(plan.strips):
        by_chunk = [
            arrived[pl.ds(kc * plan.strips + yl, plan.nx // chunks, stride=plan.lead), :]
            for kc in range(chunks)
        ]
        for i in range(chunks):
            turned[pl.ds(i, plan.nx // chunks, stride=chunks), :] = place(
                by_chunk, [i] * chunks, block
            )
        whole = turned[...].T
        for kc in range(chunks):
            for f in range(4):
                at = (kc * 4 + f) * sub
                ocean[f, yl, kc * sub : (kc + 1) * sub, :] = whole[at : at + sub]


def on_device(plan, velocity, stress, ocean, zones, materials, slip, bathy):
    n, cells, sub, lanes, width = plan.n, plan.cells, plan.sub, plan.lanes, plan.width
    vmem = pl.BlockSpec(memory_space=pltpu.VMEM)
    smem = pl.BlockSpec(memory_space=pltpu.SMEM)
    hbm = pl.BlockSpec(memory_space=pltpu.HBM)

    def shape(*dims):
        return jax.ShapeDtypeStruct(dims, F32)

    def like(array):
        return jax.ShapeDtypeStruct(array.shape, array.dtype)

    def held(array):
        return pltpu.VMEM(array.shape, array.dtype)

    def call(kernel, name, out, ins, scratch, room=16, **rest):
        room = room if plan.unrolled else 56
        return pl.pallas_call(
            functools.partial(kernel, plan),
            out_shape=out,
            in_specs=ins,
            out_specs=jax.tree.map(lambda _: vmem, out),
            scratch_shapes=scratch,
            compiler_params=pltpu.CompilerParams(vmem_limit_bytes=room * 1024 * 1024),
            name=name,
            **rest,
        )

    def pinned(array):
        return pltpu.with_memory_space_constraint(array, pltpu.HBM)

    def near(array):
        return pltpu.with_memory_space_constraint(array, pltpu.VMEM) if plan.unrolled else array

    mates = [(i, i ^ 1) for i in range(n)]
    pairs = [[0, n - 1]] + [[i, i + 1] for i in range(1, n - 1, 2)]
    crust, ocean_near, bathy_near = call(
        crust_kernel,
        "crust_planes",
        (shape(10 * cells + 1, sub, lanes), like(ocean), like(bathy)),
        [hbm] * 6,
        [held(velocity), held(stress), held(zones), held(slip), pltpu.SemaphoreType.DMA((6,))],
    )(*(pinned(a) for a in (velocity, stress, zones, slip, ocean, bathy)))
    both = lax.all_gather(crust, "map", axis_index_groups=pairs)
    message = call(
        ocean_kernel,
        "ocean_rows",
        shape(n * plan.rows, LANES),
        [vmem] * 2,
        [
            pltpu.VMEM((plan.strips, plan.nx, LANES), F32),
            pltpu.VMEM(
                (plan.lead, plan.nx // plan.chunks + 2 * plan.halo_groups, LANES), F32
            ),
            pltpu.VMEM((n * plan.strips, LANES), F32),
        ],
    )(ocean_near, bathy_near)
    message, crust = lax.optimization_barrier((message, crust))
    arrived = lax.all_to_all(
        message.reshape(n // 2, 2 * plan.rows, LANES),
        "map",
        split_axis=0,
        concat_axis=0,
        axis_index_groups=[list(range(core, n, 2)) for core in range(2)],
        tiled=True,
    ).reshape(n * plan.rows, LANES)
    mate = lax.ppermute(crust, "map", mates)
    vel, strs, mats = call(
        begin_kernel,
        "first_velocity",
        (shape(3, width, sub, lanes), shape(6, width, sub, lanes), shape(5, width, sub, lanes)),
        [smem] + [vmem] * 3,
        [],
        cost_estimate=pl.CostEstimate(
            flops=10**11, bytes_accessed=200 * 10**6, transcendentals=0
        ),
    )(materials, crust, mate, both)
    arrived, vel = lax.optimization_barrier((arrived, vel))
    swapped = lax.ppermute(arrived, "map", mates)
    vel, strs, loads, back = call(
        middle_kernel,
        "substeps",
        (
            shape(3, width, sub, lanes),
            shape(6, width, sub, lanes),
            shape(width, sub, lanes),
            shape(n * plan.back_rows, LANES),
        ),
        [vmem] * 5,
        [
            pltpu.VMEM((4, width + 2, sub, lanes), F32),
            pltpu.VMEM((width + 2, sub, lanes), F32),
            pltpu.VMEM((width + 2, sub, lanes), F32),
            pltpu.VMEM((lanes, LANES), F32),
            pltpu.VMEM((plan.depth, lanes), F32),
        ],
        input_output_aliases={2: 0, 3: 1},
    )(*(near(a) for a in (arrived, swapped, vel, strs, mats)))
    returned = lax.all_to_all(
        back.reshape(n, plan.back_rows, LANES), "map", split_axis=0, concat_axis=0, tiled=True
    ).reshape(n * plan.back_rows, LANES)
    new_velocity, new_stress = call(
        end_kernel,
        "last_updates",
        (shape(*velocity.shape), shape(*stress.shape)),
        [vmem] * 4,
        [
            pltpu.VMEM((3, width, sub, lanes), F32),
            pltpu.VMEM((6, width, sub, lanes), F32),
        ],
    )(vel, strs, mats, loads)
    new_ocean = call(
        unpack_kernel,
        "ocean_strips",
        shape(*ocean.shape),
        [vmem],
        [pltpu.VMEM((plan.nx, LANES), F32)],
    )(returned)
    return new_velocity, new_stress, new_ocean


def solution(mesh):
    n = mesh.shape["map"]

    def body(velocity, stress, ocean, zones, materials, slip, bathy):
        _, cells, depth, ny = velocity.shape
        plan = Plan(n, cells, depth, ny, ocean.shape[1])
        return on_device(plan, velocity, stress, ocean, zones, materials, slip, bathy)

    return jax.shard_map(
        body,
        mesh=mesh,
        in_specs=(
            P("parts", "map", None, None),
            P("parts", "map", None, None),
            P("parts", "map", None, None),
            P("map", "parts", None),
            P(),
            P("map", "parts"),
            P("map", "parts"),
        ),
        out_specs=(
            P("parts", "map", None, None),
            P("parts", "map", None, None),
            P("parts", "map", None, None),
        ),
        check_vma=False,
    )
```

```python
import functools

import jax
import jax.numpy as jnp
from jax import lax
from jax.experimental import pallas as pl
from jax.experimental.pallas import tpu as pltpu
from jax.sharding import PartitionSpec as P

STEPS = 4
ZONES = 8
DT = 0.25
HALF = 0.5 * DT
KBULK = 2.25
GRAV = 0.1
HALO = 2 * STEPS
LANES = 128
F32 = jnp.float32
VX, VY, VZ = range(3)
SXX, SYY, SZZ, SXY, SXZ, SYZ = range(6)
BUOY, LAMB, SHEAR, FAULT, FLOOR = range(5)


class Plan:
    def __init__(self, devices, cells, depth, ny, strips):
        self.n = devices
        self.cells = cells
        self.depth = depth
        self.ny = ny
        self.strips = strips
        self.chunks = max(1, LANES // ny)
        self.sub = depth // self.chunks
        self.lanes = self.chunks * ny
        self.width = cells + 2 * HALO
        self.own_groups = cells // self.chunks
        self.halo_groups = HALO // self.chunks
        self.sent_groups = self.own_groups + self.halo_groups
        self.lead = self.chunks * strips
        self.rows = self.lead * self.sent_groups
        self.back_rows = self.lead * self.own_groups
        self.nx = devices * cells
        self.block = 4 * self.sub
        self.unrolled = self.sub * self.lanes <= 1024
        assert devices % 2 == 0 and cells == HALO and self.block * self.chunks == LANES

    def planes(self, start, stop, body):
        if self.unrolled:
            for j in range(start, stop):
                body(j)
        else:
            def run(j, carry):
                body(j)
                return carry

            lax.fori_loop(start, stop, run, 0)


def odd_device():
    return lax.rem(lax.axis_index("map"), 2)


def place(pieces, wanted, block):
    out = None
    for i, piece in enumerate(pieces):
        shift = (i - wanted[i]) * block % piece.shape[-1]
        moved = pltpu.roll(piece, shift, piece.ndim - 1) if shift else piece
        if out is None:
            out = moved
        else:
            lane = lax.broadcasted_iota(jnp.int32, moved.shape, moved.ndim - 1)
            out = jnp.where(lane >= i * block, moved, out)
    return out


def pack_kernel(
    plan, vel_ref, stress_ref, zones_ref, slip_ref, ocean_ref, bathy_ref, crust, message,
    vel, stress, zones, slip, ocean, bathy, turned, grouped, extra, sems,
):
    cells, sub, chunks, ny = plan.cells, plan.sub, plan.chunks, plan.ny
    n, strips, block, sent, rows = plan.n, plan.strips, plan.block, plan.sent_groups, plan.rows
    pairs = (
        (ocean_ref, ocean),
        (bathy_ref, bathy),
        (vel_ref, vel),
        (stress_ref, stress),
        (zones_ref, zones),
        (slip_ref, slip),
    )
    copies = [
        pltpu.make_async_copy(source, target, sems.at[i])
        for i, (source, target) in enumerate(pairs)
    ]
    for copy in copies:
        copy.start()
    copies[0].wait()
    copies[1].wait()
    border = jnp.zeros((plan.lead, plan.halo_groups, LANES), F32)
    count = plan.nx // chunks
    grouped[:, : plan.halo_groups, :] = border
    grouped[:, plan.halo_groups + count :, :] = border
    for yl in range(strips):
        stacked = jnp.concatenate(
            [ocean[f, yl, kc * sub : (kc + 1) * sub, :] for kc in range(chunks) for f in range(4)],
            axis=0,
        )
        turned[yl] = stacked.T
        by_x = [turned[yl, pl.ds(i, count, stride=chunks), :] for i in range(chunks)]
        for kc in range(chunks):
            grouped[kc * strips + yl, pl.ds(plan.halo_groups, count), :] = place(
                by_x, [kc] * chunks, block
            )
    for d in range(n):
        start = d * plan.own_groups + (d % 2) * plan.halo_groups
        for q in range(plan.lead):
            message[d * rows + q * sent : d * rows + (q + 1) * sent, :] = grouped[
                q, start : start + sent, :
            ]
    depths = bathy[...].astype(F32)
    wide = lax.broadcasted_iota(jnp.int32, depths.shape, 1)
    for d in range(n):
        first = d * cells - HALO - 1
        moved = pltpu.roll(depths, -first % plan.nx, 1)
        moved = jnp.where((wide + first >= 0) & (wide + first < plan.nx), moved, 0.0)
        extra[d * strips : (d + 1) * strips, :] = moved[:, :LANES]
    pairs = n // 2
    lane = lax.broadcasted_iota(jnp.int32, (pairs, LANES), 1)
    blank = jnp.zeros((1, LANES), F32)
    for odd in range(2):
        slot = (odd * (chunks - 1) * 4 + 2) * sub
        group = odd * (sent - 1)
        for yl in range(strips):
            if odd:
                column = turned[yl, pl.ds(2 * cells + HALO, pairs - 1, stride=2 * cells), :]
                column = jnp.concatenate([column, blank], axis=0)
            else:
                column = turned[yl, pl.ds(2 * cells - HALO - 1, pairs - 1, stride=2 * cells), :]
                column = jnp.concatenate([blank, column], axis=0)
            deep = extra[pl.ds(odd * strips + yl, pairs, stride=2 * strips), :]
            for kc in range(chunks):
                at = odd * rows + (kc * strips + yl) * sent + group
                old = message[pl.ds(at, pairs, stride=2 * rows), :]
                edge = pltpu.roll(column, (slot - kc * block) % LANES, 1)
                floor = pltpu.roll(deep, (slot + sub - kc * sub) % LANES, 1)
                new = jnp.where((lane >= slot) & (lane < slot + sub), edge, old)
                new = jnp.where((lane >= slot + sub) & (lane < slot + 2 * sub), floor, new)
                message[pl.ds(at, pairs, stride=2 * rows), :] = new

    def joined(ref, *at):
        parts = [ref[(*at, pl.ds(kc * sub, sub), slice(None))] for kc in range(chunks)]
        return jnp.concatenate(parts, axis=-1) if chunks > 1 else parts[0]

    copies[2].wait()
    for f in range(3):
        for x in range(cells):
            crust[f * cells + x] = joined(vel, f, x)
    copies[3].wait()
    for f in range(6):
        for x in range(cells):
            crust[(3 + f) * cells + x] = joined(stress, f, x)
    copies[4].wait()
    for x in range(cells):
        crust[9 * cells + x] = (joined(zones, x) + 1).astype(F32)
    copies[5].wait()
    fault_chunk = (plan.depth // 2) // sub
    pieces = [
        slip[...] if kc == fault_chunk else jnp.zeros((cells, ny), F32) for kc in range(chunks)
    ]
    fault = jnp.concatenate(pieces, axis=-1) if chunks > 1 else pieces[0]
    if sub > cells:
        fault = jnp.concatenate([fault, jnp.zeros((sub - cells, plan.lanes), F32)], axis=0)
    crust[10 * cells] = fault


class Shifts:
    def __init__(self, plan):
        self.plan = plan
        shape = (plan.sub, plan.lanes)
        self.row = lax.broadcasted_iota(jnp.int32, shape, 0)
        self.lane = lax.broadcasted_iota(jnp.int32, shape, 1)
        self.y = lax.rem(self.lane, plan.ny)
        self.first_row = self.row == 0
        self.last_row = self.row == plan.sub - 1
        self.top = self.first_row & (self.lane < plan.ny)
        self.floor_cell = self.last_row & (self.lane >= plan.lanes - plan.ny)
        self.not_low_y = jnp.where(self.y == 0, 0.0, 1.0).astype(F32)
        self.not_high_y = jnp.where(self.y == plan.ny - 1, 0.0, 1.0).astype(F32)
        self.depth = (
            lax.div(self.lane, plan.ny) * plan.sub + self.row
        ).astype(F32)

    def dy(self, f):
        lanes = self.plan.lanes
        return pltpu.roll(f, lanes - 1, 1) * self.not_high_y - pltpu.roll(f, 1, 1) * self.not_low_y

    def below(self, f):
        plan = self.plan
        moved = pltpu.roll(f, plan.sub - 1, 0)
        if plan.chunks > 1:
            moved = jnp.where(self.last_row, pltpu.roll(moved, plan.lanes - plan.ny, 1), moved)
        return jnp.where(self.floor_cell, 0.0, moved)

    def above(self, f, top):
        plan = self.plan
        moved = pltpu.roll(f, 1, 0)
        if plan.chunks > 1:
            moved = jnp.where(self.first_row, pltpu.roll(moved, plan.ny, 1), moved)
        return jnp.where(self.top, top, moved)

    def seafloor(self, vz):
        row = self.over_chunks(jnp.where(self.top, vz, 0.0)[0:1])
        return jnp.broadcast_to(row, vz.shape)

    def over_chunks(self, f):
        shift = self.plan.ny
        while shift < self.plan.lanes:
            f = f + pltpu.roll(f, shift, 1)
            shift *= 2
        return f


def acceleration(sh, stress, j):
    sxy, sxz = stress[SXY, j], stress[SXZ, j]
    syz, szz = stress[SYZ, j], stress[SZZ, j]
    ax = stress[SXX, j + 1] - stress[SXX, j - 1] + sh.dy(sxy) + sh.below(sxz) - sh.above(sxz, 0.0)
    ay = stress[SXY, j + 1] - stress[SXY, j - 1] + sh.dy(stress[SYY, j])
    ay = ay + sh.below(syz) - sh.above(syz, 0.0)
    az = stress[SXZ, j + 1] - stress[SXZ, j - 1] + sh.dy(syz) + sh.below(szz) - sh.above(szz, 0.0)
    return ax, ay, az


def strained(sh, vel, stress, mats, j):
    vx, vy, vz = vel[VX, j], vel[VY, j], vel[VZ, j]
    exx = vel[VX, j + 1] - vel[VX, j - 1]
    eyy = sh.dy(vy)
    ezz = sh.below(vz) - sh.above(vz, vz)
    mu = mats[SHEAR, j]
    mu2 = mu + mu
    common = mats[LAMB, j] * (exx + eyy + ezz)
    exy = sh.dy(vx) + vel[VY, j + 1] - vel[VY, j - 1]
    exz = sh.below(vx) - sh.above(vx, vx) + vel[VZ, j + 1] - vel[VZ, j - 1]
    eyz = sh.below(vy) - sh.above(vy, vy) + sh.dy(vz)
    return (
        stress[SXX, j] + (common + mu2 * exx),
        stress[SYY, j] + (common + mu2 * eyy),
        stress[SZZ, j] + (common + mu2 * ezz),
        stress[SXY, j] + mu * exy,
        stress[SXZ, j] + (mu * exz + mats[FAULT, j]),
        stress[SYZ, j] + mu * eyz,
    )


def begin_kernel(plan, table, own, mate, other, vel, stress, mats):
    cells, sub = plan.cells, plan.sub
    sh = Shifts(plan)
    odd = odd_device()
    starts = (HALO, (HALO + cells) * (1 - odd), (HALO + cells) * odd)
    for start, ref in zip(starts, (own, mate, other)):
        def bring(x, start=start, ref=ref):
            j = start + x
            for f in range(3):
                vel[f, j] = ref[f * cells + x]
            for f in range(6):
                stress[f, j] = ref[(3 + f) * cells + x]
            zone = ref[9 * cells + x]
            values = [jnp.zeros_like(zone) for _ in range(3)]
            for z in range(ZONES):
                here = zone == float(z + 1)
                values = [jnp.where(here, table[c, z], values[c]) for c in range(3)]
            for c in range(3):
                mats[c, j] = values[c] * HALF
            slip = jnp.broadcast_to(ref[10 * cells, pl.ds(x, 1), :], (sub, plan.lanes))
            mats[FAULT, j] = jnp.where(sh.row == (plan.depth // 2) % sub, DT * slip, 0.0)
            mats[FLOOR, j] = sh.seafloor(ref[VZ * cells + x])

        plan.planes(0, cells, bring)

    def move(j):
        b = mats[BUOY, j]
        for f, a in enumerate(acceleration(sh, stress, j)):
            vel[f, j] = vel[f, j] + b * a

    plan.planes(1, plan.width - 1, move)


def middle_kernel(
    plan, arrived, swapped, vel_in, stress_in, mats, vel, stress, loads, message,
    oc, water, bottom, floors, gather, depths,
):
    sub, chunks, n, strips = plan.sub, plan.chunks, plan.n, plan.strips
    width, sent = plan.width, plan.sent_groups
    sh = Shifts(plan)
    odd = odd_device()
    mate = 1 - odd
    half = n // 2

    def turn(slot, owner, group):
        for core, ref in ((odd, arrived), (mate, swapped)):
            for kc in range(chunks):
                for yl in range(strips):
                    at = owner * plan.rows + (kc * strips + yl) * sent + group
                    to = kc * plan.ny + core * strips + yl
                    gather[slot, pl.ds(to, half, stride=2 * strips), :] = ref[
                        pl.ds(at, half, stride=2 * plan.rows), :
                    ]
        return gather[slot].T

    def spread(turned, group):
        for i in range(chunks):
            for f in range(4):
                at = (i * 4 + f) * sub
                oc[f, 1 + group * chunks + i] = turned[at : at + sub]

    ends = []
    for group in range(sent):
        turned = turn(group, odd, group)
        spread(turned, group + plan.halo_groups * odd)
        if group == 0:
            ends.append((turned[2 * sub : 3 * sub], turned[3 * sub : 4 * sub]))
        if group == sent - 1:
            ends.append((turned[LANES - 2 * sub : LANES - sub], turned[LANES - sub :]))
    for group in range(plan.halo_groups):
        spread(
            turn(sent + group, mate, group + plan.own_groups * odd), group + sent * mate
        )
    turned = turn(sent + plan.halo_groups, mate, plan.own_groups - odd)
    is_odd = odd == 1
    oc[0, (width + 1) * odd] = jnp.where(is_odd, ends[1][0], ends[0][0])
    oc[0, (width + 1) * mate] = jnp.where(
        is_odd, turned[LANES - 4 * sub : LANES - 3 * sub], turned[:sub]
    )
    deep = jnp.where(is_odd, ends[1][1], ends[0][1])
    for kc in range(chunks):
        mine = (sh.lane >= kc * plan.ny) & (sh.lane < (kc + 1) * plan.ny)
        depths[kc * sub : (kc + 1) * sub, :] = sh.over_chunks(jnp.where(mine, deep, 0.0))

    def mask(j):
        low = jnp.broadcast_to(depths[pl.ds(j, 1), :], (sub, plan.lanes))
        wet = jnp.where(sh.depth < low, 1.0, 0.0).astype(F32)
        water[j] = wet
        bottom[j] = jnp.where(sh.depth == low - 1.0, 1.0, 0.0).astype(F32)
        oc[0, j] = oc[0, j] * wet

    def mask_x(j):
        oc[1, j] = oc[1, j] * water[j]

    def mask_yw(j):
        oc[2, j] = oc[2, j] * water[j]
        oc[3, j] = oc[3, j] * water[j]

    plan.planes(0, width + 2, mask)
    plan.planes(1, width + 1, mask_x)
    plan.planes(2, width, mask_yw)

    def flow_x(j):
        oc[1, j + 1] = water[j + 1] * (oc[1, j + 1] - HALF * (oc[0, j + 2] - oc[0, j]))

    def flow(j):
        p = oc[0, j + 1]
        wet = water[j + 1]
        oc[2, j + 1] = wet * (oc[2, j + 1] - HALF * sh.dy(p))
        rise = sh.below(p) + bottom[j + 1] * p - sh.above(p, -p)
        oc[3, j + 1] = wet * (oc[3, j + 1] - (HALF * rise + (DT * GRAV) * p))

    def press(j, floor):
        w = oc[3, j + 1]
        rise = sh.below(w) + bottom[j + 1] * floor - sh.above(w, w)
        total = oc[1, j + 2] - oc[1, j] + sh.dy(oc[2, j + 1]) + rise
        p = water[j + 1] * (oc[0, j + 1] - (HALF * KBULK) * total)
        oc[0, j + 1] = p
        column = jnp.sum(bottom[j + 1] * p, axis=0, keepdims=True)
        column = jnp.broadcast_to(sh.over_chunks(column), (sub, plan.lanes))
        loads[j] = jnp.where(sh.top, column, 0.0)

    def first_load(j):
        for f in (VX, VY):
            vel[f, j] = vel_in[f, j]
        vz = vel_in[VZ, j] + mats[BUOY, j] * loads[j]
        vel[VZ, j] = vz
        floors[j] = sh.seafloor(vz)

    def move(j):
        ax, ay, az = acceleration(sh, stress, j)
        b = mats[BUOY, j]
        vel[VX, j] = vel[VX, j] + b * ax
        vel[VY, j] = vel[VY, j] + b * ay
        vz = vel[VZ, j] + b * (az + loads[j])
        vel[VZ, j] = vz
        floors[j] = sh.seafloor(vz)

    def strain(j, source):
        for f, value in enumerate(strained(sh, vel, source, mats, j)):
            stress[f, j] = value

    plan.planes(0, width, flow_x)
    plan.planes(1, width - 1, flow)
    plan.planes(1, width - 1, lambda j: press(j, mats[FLOOR, j]))
    for t in range(STEPS - 1):
        first, last = 2 * t, width - 2 * t

        def velocity_and_flow(j, t=t, first=first, last=last):
            if t == 0:
                first_load(j)
            else:
                move(j)
            if plan.unrolled and first + 2 <= j < last - 2:
                flow_x(j)
                if first + 3 <= j < last - 3:
                    flow(j)

        def stress_and_press(j, t=t, first=first, last=last):
            if t < STEPS - 2:
                strain(j, stress_in if t == 0 else stress)
            if plan.unrolled and first + 3 <= j < last - 3:
                press(j, floors[j])

        plan.planes(first + 1, last - 1, velocity_and_flow)
        if not plan.unrolled:
            plan.planes(first + 2, last - 2, flow_x)
            plan.planes(first + 3, last - 3, flow)
        plan.planes(first + 2, last - 2, stress_and_press)
        if not plan.unrolled:
            plan.planes(first + 3, last - 3, lambda j: press(j, floors[j]))

    for group in range(plan.own_groups):
        stacked = jnp.concatenate(
            [
                oc[f, 1 + HALO + group * chunks + i]
                for i in range(chunks)
                for f in range(4)
            ],
            axis=0,
        )
        gather[group] = stacked.T
        for kc in range(chunks):
            for yl in range(strips):
                at = group * plan.lead + kc * strips + yl
                message[pl.ds(at, n, stride=plan.back_rows), :] = gather[
                    group, pl.ds(kc * plan.ny + yl, n, stride=strips), :
                ]


def end_kernel(plan, vel_in, stress_in, mats, loads, vel_out, stress_out, vel, stress):
    cells, sub, chunks, ny = plan.cells, plan.sub, plan.chunks, plan.ny
    sh = Shifts(plan)
    first, last = 2 * (STEPS - 1), plan.width - 2 * (STEPS - 1)

    def put(out, f, x, plane):
        for kc in range(chunks):
            out[f, x, kc * sub : (kc + 1) * sub, :] = plane[:, kc * ny : (kc + 1) * ny]

    def strain(j):
        for f, value in enumerate(strained(sh, vel_in, stress_in, mats, j)):
            stress[f, j] = value

    def move(j):
        ax, ay, az = acceleration(sh, stress, j)
        b = mats[BUOY, j]
        for f, a in enumerate((ax, ay, az + loads[j])):
            vel[f, j] = vel_in[f, j] + b * a

    def finish(x):
        for f in range(3):
            put(vel_out, f, x, vel[f, x + HALO])
        for f, value in enumerate(strained(sh, vel, stress, mats, x + HALO)):
            put(stress_out, f, x, value)

    plan.planes(first, last, strain)
    plan.planes(first + 1, last - 1, move)
    plan.planes(0, cells, finish)


def unpack_kernel(plan, arrived, ocean, turned):
    sub, chunks = plan.sub, plan.chunks
    block = 4 * sub
    for yl in range(plan.strips):
        by_chunk = [
            arrived[pl.ds(kc * plan.strips + yl, plan.nx // chunks, stride=plan.lead), :]
            for kc in range(chunks)
        ]
        for i in range(chunks):
            turned[pl.ds(i, plan.nx // chunks, stride=chunks), :] = place(
                by_chunk, [i] * chunks, block
            )
        whole = turned[...].T
        for kc in range(chunks):
            for f in range(4):
                at = (kc * 4 + f) * sub
                ocean[f, yl, kc * sub : (kc + 1) * sub, :] = whole[at : at + sub]


def on_device(plan, velocity, stress, ocean, zones, materials, slip, bathy):
    n, cells, sub, lanes, width = plan.n, plan.cells, plan.sub, plan.lanes, plan.width
    vmem = pl.BlockSpec(memory_space=pltpu.VMEM)
    smem = pl.BlockSpec(memory_space=pltpu.SMEM)
    hbm = pl.BlockSpec(memory_space=pltpu.HBM)

    def shape(*dims):
        return jax.ShapeDtypeStruct(dims, F32)

    def like(array):
        return jax.ShapeDtypeStruct(array.shape, array.dtype)

    def held(array):
        return pltpu.VMEM(array.shape, array.dtype)

    def call(kernel, name, out, ins, scratch, room=16, **rest):
        room = room if plan.unrolled else 56
        return pl.pallas_call(
            functools.partial(kernel, plan),
            out_shape=out,
            in_specs=ins,
            out_specs=jax.tree.map(lambda _: vmem, out),
            scratch_shapes=scratch,
            compiler_params=pltpu.CompilerParams(vmem_limit_bytes=room * 1024 * 1024),
            name=name,
            **rest,
        )

    def pinned(array):
        return pltpu.with_memory_space_constraint(array, pltpu.HBM)

    def near(array):
        return pltpu.with_memory_space_constraint(array, pltpu.VMEM) if plan.unrolled else array

    mates = [(i, i ^ 1) for i in range(n)]
    others = [(i, i + 1) for i in range(1, n - 1, 2)]
    others += [(target, source) for source, target in others]
    crust, message = call(
        pack_kernel,
        "pack",
        (shape(10 * cells + 1, sub, lanes), shape(n * plan.rows, LANES)),
        [hbm] * 6,
        [held(a) for a in (velocity, stress, zones, slip, ocean, bathy)]
        + [
            pltpu.VMEM((plan.strips, plan.nx, LANES), F32),
            pltpu.VMEM(
                (plan.lead, plan.nx // plan.chunks + 2 * plan.halo_groups, LANES), F32
            ),
            pltpu.VMEM((n * plan.strips, LANES), F32),
            pltpu.SemaphoreType.DMA((6,)),
        ],
    )(*(pinned(a) for a in (velocity, stress, zones, slip, ocean, bathy)))
    other = lax.ppermute(crust, "map", others)
    arrived = lax.all_to_all(
        message.reshape(n // 2, 2 * plan.rows, LANES),
        "map",
        split_axis=0,
        concat_axis=0,
        axis_index_groups=[list(range(core, n, 2)) for core in range(2)],
        tiled=True,
    ).reshape(n * plan.rows, LANES)
    mate = lax.ppermute(crust, "map", mates)
    vel, strs, mats = call(
        begin_kernel,
        "first_velocity",
        (shape(3, width, sub, lanes), shape(6, width, sub, lanes), shape(5, width, sub, lanes)),
        [smem] + [vmem] * 3,
        [],
        cost_estimate=pl.CostEstimate(
            flops=10**11, bytes_accessed=200 * 10**6, transcendentals=0
        ),
    )(materials, crust, mate, other)
    arrived, vel = lax.optimization_barrier((arrived, vel))
    swapped = lax.ppermute(arrived, "map", mates)
    vel, strs, loads, back = call(
        middle_kernel,
        "substeps",
        (
            shape(3, width, sub, lanes),
            shape(6, width, sub, lanes),
            shape(width, sub, lanes),
            shape(n * plan.back_rows, LANES),
        ),
        [vmem] * 5,
        [
            pltpu.VMEM((4, width + 2, sub, lanes), F32),
            pltpu.VMEM((width + 2, sub, lanes), F32),
            pltpu.VMEM((width + 2, sub, lanes), F32),
            pltpu.VMEM((width, sub, lanes), F32),
            pltpu.VMEM((plan.sent_groups + plan.halo_groups + 1, lanes, LANES), F32),
            pltpu.VMEM((plan.depth, lanes), F32),
        ],
        input_output_aliases={2: 0, 3: 1},
    )(*(near(a) for a in (arrived, swapped, vel, strs, mats)))
    returned = lax.all_to_all(
        back.reshape(n, plan.back_rows, LANES), "map", split_axis=0, concat_axis=0, tiled=True
    ).reshape(n * plan.back_rows, LANES)
    new_velocity, new_stress = call(
        end_kernel,
        "last_updates",
        (shape(*velocity.shape), shape(*stress.shape)),
        [vmem] * 4,
        [
            pltpu.VMEM((3, width, sub, lanes), F32),
            pltpu.VMEM((6, width, sub, lanes), F32),
        ],
    )(vel, strs, mats, loads)
    new_ocean = call(
        unpack_kernel,
        "ocean_strips",
        shape(*ocean.shape),
        [vmem],
        [pltpu.VMEM((plan.nx, LANES), F32)],
    )(returned)
    return new_velocity, new_stress, new_ocean


def solution(mesh):
    n = mesh.shape["map"]

    def body(velocity, stress, ocean, zones, materials, slip, bathy):
        _, cells, depth, ny = velocity.shape
        plan = Plan(n, cells, depth, ny, ocean.shape[1])
        return on_device(plan, velocity, stress, ocean, zones, materials, slip, bathy)

    return jax.shard_map(
        body,
        mesh=mesh,
        in_specs=(
            P("parts", "map", None, None),
            P("parts", "map", None, None),
            P("parts", "map", None, None),
            P("map", "parts", None),
            P(),
            P("map", "parts"),
            P("map", "parts"),
        ),
        out_specs=(
            P("parts", "map", None, None),
            P("parts", "map", None, None),
            P("parts", "map", None, None),
        ),
        check_vma=False,
    )
```

```python
import functools

import jax
import jax.numpy as jnp
from jax import lax
from jax.experimental import pallas as pl
from jax.experimental.pallas import tpu as pltpu
from jax.sharding import PartitionSpec as P

STEPS = 4
ZONES = 8
DT = 0.25
HALF = 0.5 * DT
KBULK = 2.25
GRAV = 0.1
HALO = 2 * STEPS
LANES = 128
F32 = jnp.float32
VX, VY, VZ = range(3)
SXX, SYY, SZZ, SXY, SXZ, SYZ = range(6)
BUOY, LAMB, SHEAR, FAULT, FLOOR = range(5)


class Plan:
    def __init__(self, devices, cells, depth, ny, strips):
        self.n = devices
        self.cells = cells
        self.depth = depth
        self.ny = ny
        self.strips = strips
        self.chunks = max(1, LANES // ny)
        self.sub = depth // self.chunks
        self.lanes = self.chunks * ny
        self.width = cells + 2 * HALO
        self.own_groups = cells // self.chunks
        self.halo_groups = HALO // self.chunks
        self.sent_groups = self.own_groups + self.halo_groups
        self.lead = self.chunks * strips
        self.rows = self.lead * self.sent_groups
        self.back_rows = self.lead * self.own_groups
        self.nx = devices * cells
        self.block = 4 * self.sub
        self.unrolled = self.sub * self.lanes <= 1024
        assert devices % 2 == 0 and cells == HALO and self.block * self.chunks == LANES

    def planes(self, start, stop, body):
        if self.unrolled:
            for j in range(start, stop):
                body(j)
        else:
            def run(j, carry):
                body(j)
                return carry

            lax.fori_loop(start, stop, run, 0)


def odd_device():
    return lax.rem(lax.axis_index("map"), 2)


def place(pieces, wanted, block):
    out = None
    for i, piece in enumerate(pieces):
        shift = (i - wanted[i]) * block % piece.shape[-1]
        moved = pltpu.roll(piece, shift, piece.ndim - 1) if shift else piece
        if out is None:
            out = moved
        else:
            lane = lax.broadcasted_iota(jnp.int32, moved.shape, moved.ndim - 1)
            out = jnp.where(lane >= i * block, moved, out)
    return out


def pack_kernel(
    plan, vel_ref, stress_ref, zones_ref, slip_ref, ocean_ref, bathy_ref, crust, message_out,
    vel, stress, zones, slip, ocean, bathy, turned, grouped, extra, message, sems,
):
    cells, sub, chunks, ny = plan.cells, plan.sub, plan.chunks, plan.ny
    n, strips, block, sent, rows = plan.n, plan.strips, plan.block, plan.sent_groups, plan.rows
    pairs = (
        (ocean_ref, ocean),
        (bathy_ref, bathy),
        (vel_ref, vel),
        (stress_ref, stress),
        (zones_ref, zones),
        (slip_ref, slip),
    )
    copies = [
        pltpu.make_async_copy(source, target, sems.at[i])
        for i, (source, target) in enumerate(pairs)
    ]
    for copy in copies:
        copy.start()
    copies[0].wait()
    copies[1].wait()
    border = jnp.zeros((plan.lead, plan.halo_groups, LANES), F32)
    count = plan.nx // chunks
    grouped[:, : plan.halo_groups, :] = border
    grouped[:, plan.halo_groups + count :, :] = border
    for yl in range(strips):
        stacked = jnp.concatenate(
            [ocean[f, yl, kc * sub : (kc + 1) * sub, :] for kc in range(chunks) for f in range(4)],
            axis=0,
        )
        turned[yl] = stacked.T
        by_x = [turned[yl, pl.ds(i, count, stride=chunks), :] for i in range(chunks)]
        for kc in range(chunks):
            grouped[kc * strips + yl, pl.ds(plan.halo_groups, count), :] = place(
                by_x, [kc] * chunks, block
            )
    for d in range(n):
        start = d * plan.own_groups + (d % 2) * plan.halo_groups
        for q in range(plan.lead):
            message[d * rows + q * sent : d * rows + (q + 1) * sent, :] = grouped[
                q, start : start + sent, :
            ]
    depths = bathy[...].astype(F32)
    wide = lax.broadcasted_iota(jnp.int32, depths.shape, 1)
    for d in range(n):
        first = d * cells - HALO - 1
        moved = pltpu.roll(depths, -first % plan.nx, 1)
        moved = jnp.where((wide + first >= 0) & (wide + first < plan.nx), moved, 0.0)
        extra[d * strips : (d + 1) * strips, :] = moved[:, :LANES]
    pairs = n // 2
    lane = lax.broadcasted_iota(jnp.int32, (pairs, LANES), 1)
    blank = jnp.zeros((1, LANES), F32)
    for odd in range(2):
        slot = (odd * (chunks - 1) * 4 + 2) * sub
        group = odd * (sent - 1)
        for yl in range(strips):
            if odd:
                column = turned[yl, pl.ds(2 * cells + HALO, pairs - 1, stride=2 * cells), :]
                column = jnp.concatenate([column, blank], axis=0)
            else:
                column = turned[yl, pl.ds(2 * cells - HALO - 1, pairs - 1, stride=2 * cells), :]
                column = jnp.concatenate([blank, column], axis=0)
            deep = extra[pl.ds(odd * strips + yl, pairs, stride=2 * strips), :]
            for kc in range(chunks):
                at = odd * rows + (kc * strips + yl) * sent + group
                old = message[pl.ds(at, pairs, stride=2 * rows), :]
                edge = pltpu.roll(column, (slot - kc * block) % LANES, 1)
                floor = pltpu.roll(deep, (slot + sub - kc * sub) % LANES, 1)
                new = jnp.where((lane >= slot) & (lane < slot + sub), edge, old)
                new = jnp.where((lane >= slot + sub) & (lane < slot + 2 * sub), floor, new)
                message[pl.ds(at, pairs, stride=2 * rows), :] = new
    message_out[...] = message[...]

    def joined(ref, *at):
        parts = [ref[(*at, pl.ds(kc * sub, sub), slice(None))] for kc in range(chunks)]
        return jnp.concatenate(parts, axis=-1) if chunks > 1 else parts[0]

    copies[2].wait()
    for f in range(3):
        for x in range(cells):
            crust[f * cells + x] = joined(vel, f, x)
    copies[3].wait()
    for f in range(6):
        for x in range(cells):
            crust[(3 + f) * cells + x] = joined(stress, f, x)
    copies[4].wait()
    for x in range(cells):
        crust[9 * cells + x] = (joined(zones, x) + 1).astype(F32)
    copies[5].wait()
    fault_chunk = (plan.depth // 2) // sub
    pieces = [
        slip[...] if kc == fault_chunk else jnp.zeros((cells, ny), F32) for kc in range(chunks)
    ]
    fault = jnp.concatenate(pieces, axis=-1) if chunks > 1 else pieces[0]
    if sub > cells:
        fault = jnp.concatenate([fault, jnp.zeros((sub - cells, plan.lanes), F32)], axis=0)
    crust[10 * cells] = fault


class Shifts:
    def __init__(self, plan):
        self.plan = plan
        shape = (plan.sub, plan.lanes)
        self.row = lax.broadcasted_iota(jnp.int32, shape, 0)
        self.lane = lax.broadcasted_iota(jnp.int32, shape, 1)
        self.y = lax.rem(self.lane, plan.ny)
        self.first_row = self.row == 0
        self.last_row = self.row == plan.sub - 1
        self.top = self.first_row & (self.lane < plan.ny)
        self.floor_cell = self.last_row & (self.lane >= plan.lanes - plan.ny)
        self.not_low_y = jnp.where(self.y == 0, 0.0, 1.0).astype(F32)
        self.not_high_y = jnp.where(self.y == plan.ny - 1, 0.0, 1.0).astype(F32)
        self.depth = (
            lax.div(self.lane, plan.ny) * plan.sub + self.row
        ).astype(F32)

    def dy(self, f):
        lanes = self.plan.lanes
        return pltpu.roll(f, lanes - 1, 1) * self.not_high_y - pltpu.roll(f, 1, 1) * self.not_low_y

    def below(self, f):
        plan = self.plan
        moved = pltpu.roll(f, plan.sub - 1, 0)
        if plan.chunks > 1:
            moved = jnp.where(self.last_row, pltpu.roll(moved, plan.lanes - plan.ny, 1), moved)
        return jnp.where(self.floor_cell, 0.0, moved)

    def above(self, f, top):
        plan = self.plan
        moved = pltpu.roll(f, 1, 0)
        if plan.chunks > 1:
            moved = jnp.where(self.first_row, pltpu.roll(moved, plan.ny, 1), moved)
        return jnp.where(self.top, top, moved)

    def seafloor(self, vz):
        row = self.over_chunks(jnp.where(self.top, vz, 0.0)[0:1])
        return jnp.broadcast_to(row, vz.shape)

    def over_chunks(self, f):
        shift = self.plan.ny
        while shift < self.plan.lanes:
            f = f + pltpu.roll(f, shift, 1)
            shift *= 2
        return f


def acceleration(sh, stress, j):
    sxy, sxz = stress[SXY, j], stress[SXZ, j]
    syz, szz = stress[SYZ, j], stress[SZZ, j]
    ax = stress[SXX, j + 1] - stress[SXX, j - 1] + sh.dy(sxy) + sh.below(sxz) - sh.above(sxz, 0.0)
    ay = stress[SXY, j + 1] - stress[SXY, j - 1] + sh.dy(stress[SYY, j])
    ay = ay + sh.below(syz) - sh.above(syz, 0.0)
    az = stress[SXZ, j + 1] - stress[SXZ, j - 1] + sh.dy(syz) + sh.below(szz) - sh.above(szz, 0.0)
    return ax, ay, az


def strained(sh, vel, stress, mats, j):
    vx, vy, vz = vel[VX, j], vel[VY, j], vel[VZ, j]
    exx = vel[VX, j + 1] - vel[VX, j - 1]
    eyy = sh.dy(vy)
    ezz = sh.below(vz) - sh.above(vz, vz)
    mu = mats[SHEAR, j]
    mu2 = mu + mu
    common = mats[LAMB, j] * (exx + eyy + ezz)
    exy = sh.dy(vx) + vel[VY, j + 1] - vel[VY, j - 1]
    exz = sh.below(vx) - sh.above(vx, vx) + vel[VZ, j + 1] - vel[VZ, j - 1]
    eyz = sh.below(vy) - sh.above(vy, vy) + sh.dy(vz)
    return (
        stress[SXX, j] + (common + mu2 * exx),
        stress[SYY, j] + (common + mu2 * eyy),
        stress[SZZ, j] + (common + mu2 * ezz),
        stress[SXY, j] + mu * exy,
        stress[SXZ, j] + (mu * exz + mats[FAULT, j]),
        stress[SYZ, j] + mu * eyz,
    )


def begin_kernel(plan, table, own, mate, other, vel, stress, mats):
    cells, sub = plan.cells, plan.sub
    sh = Shifts(plan)
    odd = odd_device()
    starts = (HALO, (HALO + cells) * (1 - odd), (HALO + cells) * odd)
    for start, ref in zip(starts, (own, mate, other)):
        def bring(x, start=start, ref=ref):
            j = start + x
            for f in range(3):
                vel[f, j] = ref[f * cells + x]
            for f in range(6):
                stress[f, j] = ref[(3 + f) * cells + x]
            zone = ref[9 * cells + x]
            values = [jnp.zeros_like(zone) for _ in range(3)]
            for z in range(ZONES):
                here = zone == float(z + 1)
                values = [jnp.where(here, table[c, z], values[c]) for c in range(3)]
            for c in range(3):
                mats[c, j] = values[c] * HALF
            slip = jnp.broadcast_to(ref[10 * cells, pl.ds(x, 1), :], (sub, plan.lanes))
            mats[FAULT, j] = jnp.where(sh.row == (plan.depth // 2) % sub, DT * slip, 0.0)
            mats[FLOOR, j] = sh.seafloor(ref[VZ * cells + x])

        plan.planes(0, cells, bring)

    def move(j):
        b = mats[BUOY, j]
        for f, a in enumerate(acceleration(sh, stress, j)):
            vel[f, j] = vel[f, j] + b * a

    plan.planes(1, plan.width - 1, move)


def middle_kernel(
    plan, arrived, swapped, vel_in, stress_in, mats, vel_out, stress_out, loads_out, message,
    vel, stress, loads, oc, water, bottom, floors, gather, rows, depths,
):
    sub, chunks, n, strips = plan.sub, plan.chunks, plan.n, plan.strips
    width, sent = plan.width, plan.sent_groups
    sh = Shifts(plan)
    odd = odd_device()
    mate = 1 - odd
    half = n // 2

    def bring(j):
        for f in range(3):
            vel[f, j] = vel_in[f, j]
        for f in range(6):
            stress[f, j] = stress_in[f, j]

    plan.planes(0, width, bring)

    def turn(slot, owner, group):
        for core, ref in ((odd, arrived), (mate, swapped)):
            for kc in range(chunks):
                for yl in range(strips):
                    at = owner * plan.rows + (kc * strips + yl) * sent + group
                    to = kc * plan.ny + core * strips + yl
                    gather[slot, pl.ds(to, half, stride=2 * strips), :] = ref[
                        pl.ds(at, half, stride=2 * plan.rows), :
                    ]
        return gather[slot].T

    def spread(turned, group):
        for i in range(chunks):
            for f in range(4):
                at = (i * 4 + f) * sub
                oc[f, 1 + group * chunks + i] = turned[at : at + sub]

    ends = []
    for group in range(sent):
        turned = turn(group, odd, group)
        spread(turned, group + plan.halo_groups * odd)
        if group == 0:
            ends.append((turned[2 * sub : 3 * sub], turned[3 * sub : 4 * sub]))
        if group == sent - 1:
            ends.append((turned[LANES - 2 * sub : LANES - sub], turned[LANES - sub :]))
    for group in range(plan.halo_groups):
        spread(
            turn(sent + group, mate, group + plan.own_groups * odd), group + sent * mate
        )
    turned = turn(sent + plan.halo_groups, mate, plan.own_groups - odd)
    is_odd = odd == 1
    oc[0, (width + 1) * odd] = jnp.where(is_odd, ends[1][0], ends[0][0])
    oc[0, (width + 1) * mate] = jnp.where(
        is_odd, turned[LANES - 4 * sub : LANES - 3 * sub], turned[:sub]
    )
    deep = jnp.where(is_odd, ends[1][1], ends[0][1])
    for kc in range(chunks):
        mine = (sh.lane >= kc * plan.ny) & (sh.lane < (kc + 1) * plan.ny)
        depths[kc * sub : (kc + 1) * sub, :] = sh.over_chunks(jnp.where(mine, deep, 0.0))

    def mask(j):
        low = jnp.broadcast_to(depths[pl.ds(j, 1), :], (sub, plan.lanes))
        wet = jnp.where(sh.depth < low, 1.0, 0.0).astype(F32)
        water[j] = wet
        bottom[j] = jnp.where(sh.depth == low - 1.0, 1.0, 0.0).astype(F32)
        oc[0, j] = oc[0, j] * wet

    def mask_x(j):
        oc[1, j] = oc[1, j] * water[j]

    def mask_yw(j):
        oc[2, j] = oc[2, j] * water[j]
        oc[3, j] = oc[3, j] * water[j]

    plan.planes(0, width + 2, mask)
    plan.planes(1, width + 1, mask_x)
    plan.planes(2, width, mask_yw)

    def flow_x(j):
        oc[1, j + 1] = water[j + 1] * (oc[1, j + 1] - HALF * (oc[0, j + 2] - oc[0, j]))

    def flow(j):
        p = oc[0, j + 1]
        wet = water[j + 1]
        oc[2, j + 1] = wet * (oc[2, j + 1] - HALF * sh.dy(p))
        rise = sh.below(p) + bottom[j + 1] * p - sh.above(p, -p)
        oc[3, j + 1] = wet * (oc[3, j + 1] - (HALF * rise + (DT * GRAV) * p))

    def press(j, floor):
        w = oc[3, j + 1]
        rise = sh.below(w) + bottom[j + 1] * floor - sh.above(w, w)
        total = oc[1, j + 2] - oc[1, j] + sh.dy(oc[2, j + 1]) + rise
        p = water[j + 1] * (oc[0, j + 1] - (HALF * KBULK) * total)
        oc[0, j + 1] = p
        column = jnp.sum(bottom[j + 1] * p, axis=0, keepdims=True)
        column = jnp.broadcast_to(sh.over_chunks(column), (sub, plan.lanes))
        loads[j] = jnp.where(sh.top, column, 0.0)

    def first_load(j):
        vz = vel[VZ, j] + mats[BUOY, j] * loads[j]
        vel[VZ, j] = vz
        floors[j] = sh.seafloor(vz)

    def move(j):
        ax, ay, az = acceleration(sh, stress, j)
        b = mats[BUOY, j]
        vel[VX, j] = vel[VX, j] + b * ax
        vel[VY, j] = vel[VY, j] + b * ay
        vz = vel[VZ, j] + b * (az + loads[j])
        vel[VZ, j] = vz
        floors[j] = sh.seafloor(vz)

    def strain(j):
        for f, value in enumerate(strained(sh, vel, stress, mats, j)):
            stress[f, j] = value

    plan.planes(0, width, flow_x)
    plan.planes(1, width - 1, flow)
    plan.planes(1, width - 1, lambda j: press(j, mats[FLOOR, j]))
    for t in range(STEPS - 1):
        first, last = 2 * t, width - 2 * t

        def velocity_and_flow(j, t=t, first=first, last=last):
            if t == 0:
                first_load(j)
            else:
                move(j)
            if plan.unrolled and first + 2 <= j < last - 2:
                flow_x(j)
                if first + 3 <= j < last - 3:
                    flow(j)

        def stress_and_press(j, t=t, first=first, last=last):
            if t < STEPS - 2:
                strain(j)
            if plan.unrolled and first + 3 <= j < last - 3:
                press(j, floors[j])

        plan.planes(first + 1, last - 1, velocity_and_flow)
        if not plan.unrolled:
            plan.planes(first + 2, last - 2, flow_x)
            plan.planes(first + 3, last - 3, flow)
        plan.planes(first + 2, last - 2, stress_and_press)
        if not plan.unrolled:
            plan.planes(first + 3, last - 3, lambda j: press(j, floors[j]))

    for group in range(plan.own_groups):
        stacked = jnp.concatenate(
            [
                oc[f, 1 + HALO + group * chunks + i]
                for i in range(chunks)
                for f in range(4)
            ],
            axis=0,
        )
        gather[group] = stacked.T
        for kc in range(chunks):
            for yl in range(strips):
                at = group * plan.lead + kc * strips + yl
                rows[pl.ds(at, n, stride=plan.back_rows), :] = gather[
                    group, pl.ds(kc * plan.ny + yl, n, stride=strips), :
                ]
    message[...] = rows[...]

    def hand_on(j):
        for f in range(3):
            vel_out[f, j] = vel[f, j]
        for f in range(6):
            stress_out[f, j] = stress[f, j]
        loads_out[j] = loads[j]

    edge = 2 * STEPS - 3
    plan.planes(edge, width - edge, hand_on)


def end_kernel(plan, vel_in, stress_in, mats, loads, vel_out, stress_out, vel, stress):
    cells, sub, chunks, ny = plan.cells, plan.sub, plan.chunks, plan.ny
    sh = Shifts(plan)
    first, last = 2 * (STEPS - 1), plan.width - 2 * (STEPS - 1)

    def put(out, f, x, plane):
        for kc in range(chunks):
            out[f, x, kc * sub : (kc + 1) * sub, :] = plane[:, kc * ny : (kc + 1) * ny]

    def strain(j):
        for f, value in enumerate(strained(sh, vel_in, stress_in, mats, j)):
            stress[f, j] = value

    def move(j):
        ax, ay, az = acceleration(sh, stress, j)
        b = mats[BUOY, j]
        for f, a in enumerate((ax, ay, az + loads[j])):
            vel[f, j] = vel_in[f, j] + b * a

    def finish(x):
        for f in range(3):
            put(vel_out, f, x, vel[f, x + HALO])
        for f, value in enumerate(strained(sh, vel, stress, mats, x + HALO)):
            put(stress_out, f, x, value)

    plan.planes(first, last, strain)
    plan.planes(first + 1, last - 1, move)
    plan.planes(0, cells, finish)


def unpack_kernel(plan, arrived, ocean, turned):
    sub, chunks = plan.sub, plan.chunks
    block = 4 * sub
    for yl in range(plan.strips):
        by_chunk = [
            arrived[pl.ds(kc * plan.strips + yl, plan.nx // chunks, stride=plan.lead), :]
            for kc in range(chunks)
        ]
        for i in range(chunks):
            turned[pl.ds(i, plan.nx // chunks, stride=chunks), :] = place(
                by_chunk, [i] * chunks, block
            )
        whole = turned[...].T
        for kc in range(chunks):
            for f in range(4):
                at = (kc * 4 + f) * sub
                ocean[f, yl, kc * sub : (kc + 1) * sub, :] = whole[at : at + sub]


def on_device(plan, velocity, stress, ocean, zones, materials, slip, bathy):
    n, cells, sub, lanes, width = plan.n, plan.cells, plan.sub, plan.lanes, plan.width
    vmem = pl.BlockSpec(memory_space=pltpu.VMEM)
    smem = pl.BlockSpec(memory_space=pltpu.SMEM)
    hbm = pl.BlockSpec(memory_space=pltpu.HBM)

    def shape(*dims):
        return jax.ShapeDtypeStruct(dims, F32)

    def like(array):
        return jax.ShapeDtypeStruct(array.shape, array.dtype)

    def held(array):
        return pltpu.VMEM(array.shape, array.dtype)

    def call(kernel, name, out, ins, scratch, room=16, **rest):
        room = room if plan.unrolled else 56
        return pl.pallas_call(
            functools.partial(kernel, plan),
            out_shape=out,
            in_specs=ins,
            out_specs=jax.tree.map(lambda _: vmem, out),
            scratch_shapes=scratch,
            compiler_params=pltpu.CompilerParams(vmem_limit_bytes=room * 1024 * 1024),
            name=name,
            **rest,
        )

    def pinned(array):
        return pltpu.with_memory_space_constraint(array, pltpu.HBM)

    def near(array):
        return pltpu.with_memory_space_constraint(array, pltpu.VMEM) if plan.unrolled else array

    mates = [(i, i ^ 1) for i in range(n)]
    others = [(i, i + 1) for i in range(1, n - 1, 2)]
    others += [(target, source) for source, target in others]
    crust, message = call(
        pack_kernel,
        "pack",
        (shape(10 * cells + 1, sub, lanes), shape(n * plan.rows, LANES)),
        [hbm] * 6,
        [held(a) for a in (velocity, stress, zones, slip, ocean, bathy)]
        + [
            pltpu.VMEM((plan.strips, plan.nx, LANES), F32),
            pltpu.VMEM(
                (plan.lead, plan.nx // plan.chunks + 2 * plan.halo_groups, LANES), F32
            ),
            pltpu.VMEM((n * plan.strips, LANES), F32),
            pltpu.VMEM((n * plan.rows, LANES), F32),
            pltpu.SemaphoreType.DMA((6,)),
        ],
    )(*(pinned(a) for a in (velocity, stress, zones, slip, ocean, bathy)))
    other = lax.ppermute(crust, "map", others)
    arrived = lax.all_to_all(
        message.reshape(n // 2, 2 * plan.rows, LANES),
        "map",
        split_axis=0,
        concat_axis=0,
        axis_index_groups=[list(range(core, n, 2)) for core in range(2)],
        tiled=True,
    ).reshape(n * plan.rows, LANES)
    mate = lax.ppermute(crust, "map", mates)
    vel, strs, mats = call(
        begin_kernel,
        "first_velocity",
        (shape(3, width, sub, lanes), shape(6, width, sub, lanes), shape(5, width, sub, lanes)),
        [smem] + [vmem] * 3,
        [],
        cost_estimate=pl.CostEstimate(
            flops=10**11, bytes_accessed=200 * 10**6, transcendentals=0
        ),
    )(materials, crust, mate, other)
    arrived, vel = lax.optimization_barrier((arrived, vel))
    swapped = lax.ppermute(arrived, "map", mates)
    vel, strs, loads, back = call(
        middle_kernel,
        "substeps",
        (
            shape(3, width, sub, lanes),
            shape(6, width, sub, lanes),
            shape(width, sub, lanes),
            shape(n * plan.back_rows, LANES),
        ),
        [vmem] * 5,
        [
            pltpu.VMEM((3, width, sub, lanes), F32),
            pltpu.VMEM((6, width, sub, lanes), F32),
            pltpu.VMEM((width, sub, lanes), F32),
            pltpu.VMEM((4, width + 2, sub, lanes), F32),
            pltpu.VMEM((width + 2, sub, lanes), F32),
            pltpu.VMEM((width + 2, sub, lanes), F32),
            pltpu.VMEM((width, sub, lanes), F32),
            pltpu.VMEM((plan.sent_groups + plan.halo_groups + 1, lanes, LANES), F32),
            pltpu.VMEM((n * plan.back_rows, LANES), F32),
            pltpu.VMEM((plan.depth, lanes), F32),
        ],
    )(*(near(a) for a in (arrived, swapped, vel, strs, mats)))
    returned = lax.all_to_all(
        back.reshape(n, plan.back_rows, LANES), "map", split_axis=0, concat_axis=0, tiled=True
    ).reshape(n * plan.back_rows, LANES)
    new_velocity, new_stress = call(
        end_kernel,
        "last_updates",
        (shape(*velocity.shape), shape(*stress.shape)),
        [vmem] * 4,
        [
            pltpu.VMEM((3, width, sub, lanes), F32),
            pltpu.VMEM((6, width, sub, lanes), F32),
        ],
    )(vel, strs, mats, loads)
    new_ocean = call(
        unpack_kernel,
        "ocean_strips",
        shape(*ocean.shape),
        [vmem],
        [pltpu.VMEM((plan.nx, LANES), F32)],
    )(returned)
    return new_velocity, new_stress, new_ocean


def solution(mesh):
    n = mesh.shape["map"]

    def body(velocity, stress, ocean, zones, materials, slip, bathy):
        _, cells, depth, ny = velocity.shape
        plan = Plan(n, cells, depth, ny, ocean.shape[1])
        return on_device(plan, velocity, stress, ocean, zones, materials, slip, bathy)

    return jax.shard_map(
        body,
        mesh=mesh,
        in_specs=(
            P("parts", "map", None, None),
            P("parts", "map", None, None),
            P("parts", "map", None, None),
            P("map", "parts", None),
            P(),
            P("map", "parts"),
            P("map", "parts"),
        ),
        out_specs=(
            P("parts", "map", None, None),
            P("parts", "map", None, None),
            P("parts", "map", None, None),
        ),
        check_vma=False,
    )
```

```python
import functools

import jax
import jax.numpy as jnp
from jax import lax
from jax.experimental import pallas as pl
from jax.experimental.pallas import tpu as pltpu
from jax.sharding import PartitionSpec as P

STEPS = 4
ZONES = 8
DT = 0.25
HALF = 0.5 * DT
KBULK = 2.25
GRAV = 0.1
HALO = 2 * STEPS
LANES = 128
F32 = jnp.float32
VX, VY, VZ = range(3)
SXX, SYY, SZZ, SXY, SXZ, SYZ = range(6)
BUOY, LAMB, SHEAR, FAULT, FLOOR = range(5)


class Plan:
    def __init__(self, devices, cells, depth, ny, strips):
        self.n = devices
        self.cells = cells
        self.depth = depth
        self.ny = ny
        self.strips = strips
        self.chunks = max(1, LANES // ny)
        self.sub = depth // self.chunks
        self.lanes = self.chunks * ny
        self.width = cells + 2 * HALO
        self.own_groups = cells // self.chunks
        self.halo_groups = HALO // self.chunks
        self.sent_groups = self.own_groups + self.halo_groups
        self.lead = self.chunks * strips
        self.rows = self.lead * self.sent_groups
        self.back_rows = self.lead * self.own_groups
        self.nx = devices * cells
        self.block = 4 * self.sub
        self.unrolled = self.sub * self.lanes <= 1024
        assert devices % 2 == 0 and cells == HALO and self.block * self.chunks == LANES

    def planes(self, start, stop, body):
        if self.unrolled:
            for j in range(start, stop):
                body(j)
        else:
            def run(j, carry):
                body(j)
                return carry

            lax.fori_loop(start, stop, run, 0)


def odd_device():
    return lax.rem(lax.axis_index("map"), 2)


def place(pieces, wanted, block):
    out = None
    for i, piece in enumerate(pieces):
        shift = (i - wanted[i]) * block % piece.shape[-1]
        moved = pltpu.roll(piece, shift, piece.ndim - 1) if shift else piece
        if out is None:
            out = moved
        else:
            lane = lax.broadcasted_iota(jnp.int32, moved.shape, moved.ndim - 1)
            out = jnp.where(lane >= i * block, moved, out)
    return out


def pack_kernel(
    plan, vel_ref, stress_ref, zones_ref, slip_ref, ocean_ref, bathy_ref, crust, message_out,
    vel, stress, zones, slip, ocean, bathy, turned, grouped, extra, message, sems,
):
    cells, sub, chunks, ny = plan.cells, plan.sub, plan.chunks, plan.ny
    n, strips, block, sent, rows = plan.n, plan.strips, plan.block, plan.sent_groups, plan.rows
    pairs = (
        (ocean_ref, ocean),
        (bathy_ref, bathy),
        (vel_ref, vel),
        (stress_ref, stress),
        (zones_ref, zones),
        (slip_ref, slip),
    )
    copies = [
        pltpu.make_async_copy(source, target, sems.at[i])
        for i, (source, target) in enumerate(pairs)
    ]
    for copy in copies:
        copy.start()
    copies[0].wait()
    copies[1].wait()
    border = jnp.zeros((plan.lead, plan.halo_groups, LANES), F32)
    count = plan.nx // chunks
    grouped[:, : plan.halo_groups, :] = border
    grouped[:, plan.halo_groups + count :, :] = border
    for yl in range(strips):
        stacked = jnp.concatenate(
            [ocean[f, yl, kc * sub : (kc + 1) * sub, :] for kc in range(chunks) for f in range(4)],
            axis=0,
        )
        turned[yl] = stacked.T
        by_x = [turned[yl, pl.ds(i, count, stride=chunks), :] for i in range(chunks)]
        for kc in range(chunks):
            grouped[kc * strips + yl, pl.ds(plan.halo_groups, count), :] = place(
                by_x, [kc] * chunks, block
            )
    for d in range(n):
        start = d * plan.own_groups + (d % 2) * plan.halo_groups
        for q in range(plan.lead):
            message[d * rows + q * sent : d * rows + (q + 1) * sent, :] = grouped[
                q, start : start + sent, :
            ]
    depths = bathy[...].astype(F32)
    wide = lax.broadcasted_iota(jnp.int32, depths.shape, 1)
    for d in range(n):
        first = d * cells - HALO - 1
        moved = pltpu.roll(depths, -first % plan.nx, 1)
        moved = jnp.where((wide + first >= 0) & (wide + first < plan.nx), moved, 0.0)
        extra[d * strips : (d + 1) * strips, :] = moved[:, :LANES]
    pairs = n // 2
    lane = lax.broadcasted_iota(jnp.int32, (pairs, LANES), 1)
    blank = jnp.zeros((1, LANES), F32)
    for odd in range(2):
        slot = (odd * (chunks - 1) * 4 + 2) * sub
        group = odd * (sent - 1)
        for yl in range(strips):
            if odd:
                column = turned[yl, pl.ds(2 * cells + HALO, pairs - 1, stride=2 * cells), :]
                column = jnp.concatenate([column, blank], axis=0)
            else:
                column = turned[yl, pl.ds(2 * cells - HALO - 1, pairs - 1, stride=2 * cells), :]
                column = jnp.concatenate([blank, column], axis=0)
            deep = extra[pl.ds(odd * strips + yl, pairs, stride=2 * strips), :]
            for kc in range(chunks):
                at = odd * rows + (kc * strips + yl) * sent + group
                old = message[pl.ds(at, pairs, stride=2 * rows), :]
                edge = pltpu.roll(column, (slot - kc * block) % LANES, 1)
                floor = pltpu.roll(deep, (slot + sub - kc * sub) % LANES, 1)
                new = jnp.where((lane >= slot) & (lane < slot + sub), edge, old)
                new = jnp.where((lane >= slot + sub) & (lane < slot + 2 * sub), floor, new)
                message[pl.ds(at, pairs, stride=2 * rows), :] = new
    message_out[...] = message[...]

    def joined(ref, *at):
        parts = [ref[(*at, pl.ds(kc * sub, sub), slice(None))] for kc in range(chunks)]
        return jnp.concatenate(parts, axis=-1) if chunks > 1 else parts[0]

    copies[2].wait()
    for f in range(3):
        for x in range(cells):
            crust[f * cells + x] = joined(vel, f, x)
    copies[3].wait()
    for f in range(6):
        for x in range(cells):
            crust[(3 + f) * cells + x] = joined(stress, f, x)
    copies[4].wait()
    for x in range(cells):
        crust[9 * cells + x] = (joined(zones, x) + 1).astype(F32)
    copies[5].wait()
    fault_chunk = (plan.depth // 2) // sub
    pieces = [
        slip[...] if kc == fault_chunk else jnp.zeros((cells, ny), F32) for kc in range(chunks)
    ]
    fault = jnp.concatenate(pieces, axis=-1) if chunks > 1 else pieces[0]
    if sub > cells:
        fault = jnp.concatenate([fault, jnp.zeros((sub - cells, plan.lanes), F32)], axis=0)
    crust[10 * cells] = fault


class Shifts:
    def __init__(self, plan):
        self.plan = plan
        shape = (plan.sub, plan.lanes)
        self.row = lax.broadcasted_iota(jnp.int32, shape, 0)
        self.lane = lax.broadcasted_iota(jnp.int32, shape, 1)
        self.y = lax.rem(self.lane, plan.ny)
        self.first_row = self.row == 0
        self.last_row = self.row == plan.sub - 1
        self.top = self.first_row & (self.lane < plan.ny)
        self.floor_cell = self.last_row & (self.lane >= plan.lanes - plan.ny)
        self.not_low_y = jnp.where(self.y == 0, 0.0, 1.0).astype(F32)
        self.not_high_y = jnp.where(self.y == plan.ny - 1, 0.0, 1.0).astype(F32)
        self.depth = (
            lax.div(self.lane, plan.ny) * plan.sub + self.row
        ).astype(F32)

    def dy(self, f):
        lanes = self.plan.lanes
        return pltpu.roll(f, lanes - 1, 1) * self.not_high_y - pltpu.roll(f, 1, 1) * self.not_low_y

    def below(self, f):
        plan = self.plan
        moved = pltpu.roll(f, plan.sub - 1, 0)
        if plan.chunks > 1:
            moved = jnp.where(self.last_row, pltpu.roll(moved, plan.lanes - plan.ny, 1), moved)
        return jnp.where(self.floor_cell, 0.0, moved)

    def above(self, f, top):
        plan = self.plan
        moved = pltpu.roll(f, 1, 0)
        if plan.chunks > 1:
            moved = jnp.where(self.first_row, pltpu.roll(moved, plan.ny, 1), moved)
        return jnp.where(self.top, top, moved)

    def seafloor(self, vz):
        row = self.over_chunks(jnp.where(self.top, vz, 0.0)[0:1])
        return jnp.broadcast_to(row, vz.shape)

    def over_chunks(self, f):
        shift = self.plan.ny
        while shift < self.plan.lanes:
            f = f + pltpu.roll(f, shift, 1)
            shift *= 2
        return f


def acceleration(sh, stress, j):
    sxy, sxz = stress[SXY, j], stress[SXZ, j]
    syz, szz = stress[SYZ, j], stress[SZZ, j]
    ax = stress[SXX, j + 1] - stress[SXX, j - 1] + sh.dy(sxy) + sh.below(sxz) - sh.above(sxz, 0.0)
    ay = stress[SXY, j + 1] - stress[SXY, j - 1] + sh.dy(stress[SYY, j])
    ay = ay + sh.below(syz) - sh.above(syz, 0.0)
    az = stress[SXZ, j + 1] - stress[SXZ, j - 1] + sh.dy(syz) + sh.below(szz) - sh.above(szz, 0.0)
    return ax, ay, az


def strained(sh, vel, stress, mats, j):
    vx, vy, vz = vel[VX, j], vel[VY, j], vel[VZ, j]
    exx = vel[VX, j + 1] - vel[VX, j - 1]
    eyy = sh.dy(vy)
    ezz = sh.below(vz) - sh.above(vz, vz)
    mu = mats[SHEAR, j]
    mu2 = mu + mu
    common = mats[LAMB, j] * (exx + eyy + ezz)
    exy = sh.dy(vx) + vel[VY, j + 1] - vel[VY, j - 1]
    exz = sh.below(vx) - sh.above(vx, vx) + vel[VZ, j + 1] - vel[VZ, j - 1]
    eyz = sh.below(vy) - sh.above(vy, vy) + sh.dy(vz)
    return (
        stress[SXX, j] + (common + mu2 * exx),
        stress[SYY, j] + (common + mu2 * eyy),
        stress[SZZ, j] + (common + mu2 * ezz),
        stress[SXY, j] + mu * exy,
        stress[SXZ, j] + (mu * exz + mats[FAULT, j]),
        stress[SYZ, j] + mu * eyz,
    )


def begin_kernel(plan, table, own, mate, other, vel, stress, mats):
    cells, sub = plan.cells, plan.sub
    sh = Shifts(plan)
    odd = odd_device()
    starts = (HALO, (HALO + cells) * (1 - odd), (HALO + cells) * odd)
    for start, ref in zip(starts, (own, mate, other)):
        def bring(x, start=start, ref=ref):
            j = start + x
            for f in range(3):
                vel[f, j] = ref[f * cells + x]
            for f in range(6):
                stress[f, j] = ref[(3 + f) * cells + x]
            zone = ref[9 * cells + x]
            values = [jnp.zeros_like(zone) for _ in range(3)]
            for z in range(ZONES):
                here = zone == float(z + 1)
                values = [jnp.where(here, table[c, z], values[c]) for c in range(3)]
            for c in range(3):
                mats[c, j] = values[c] * HALF
            slip = jnp.broadcast_to(ref[10 * cells, pl.ds(x, 1), :], (sub, plan.lanes))
            mats[FAULT, j] = jnp.where(sh.row == (plan.depth // 2) % sub, DT * slip, 0.0)
            mats[FLOOR, j] = sh.seafloor(ref[VZ * cells + x])

        plan.planes(0, cells, bring)

    def move(j):
        b = mats[BUOY, j]
        for f, a in enumerate(acceleration(sh, stress, j)):
            vel[f, j] = vel[f, j] + b * a

    plan.planes(1, plan.width - 1, move)


def middle_kernel(
    plan, arrived, swapped, vel_in, stress_in, mats, vel, stress, loads, message,
    oc, water, bottom, gather, depths,
):
    sub, chunks, n, strips = plan.sub, plan.chunks, plan.n, plan.strips
    width, sent = plan.width, plan.sent_groups
    sh = Shifts(plan)
    odd = odd_device()

    half = n // 2
    mate = 1 - odd

    def turn(owner, group):
        for core, ref in ((odd, arrived), (mate, swapped)):
            for kc in range(chunks):
                for yl in range(strips):
                    at = owner * plan.rows + (kc * strips + yl) * sent + group
                    to = kc * plan.ny + core * strips + yl
                    gather[pl.ds(to, half, stride=2 * strips), :] = ref[
                        pl.ds(at, half, stride=2 * plan.rows), :
                    ]
        return gather[...].T

    def spread(turned, group):
        for i in range(chunks):
            for f in range(4):
                at = (i * 4 + f) * sub
                oc[f, 1 + group * chunks + i] = turned[at : at + sub]

    ends = []
    for group in range(sent):
        turned = turn(odd, group)
        spread(turned, group + plan.halo_groups * odd)
        if group == 0:
            ends.append((turned[2 * sub : 3 * sub], turned[3 * sub : 4 * sub]))
        if group == sent - 1:
            ends.append((turned[LANES - 2 * sub : LANES - sub], turned[LANES - sub :]))
    for group in range(plan.halo_groups):
        spread(turn(mate, group + plan.own_groups * odd), group + sent * mate)
    turned = turn(mate, plan.own_groups - odd)
    is_odd = odd == 1
    oc[0, (width + 1) * odd] = jnp.where(is_odd, ends[1][0], ends[0][0])
    oc[0, (width + 1) * mate] = jnp.where(
        is_odd, turned[LANES - 4 * sub : LANES - 3 * sub], turned[:sub]
    )
    deep = jnp.where(is_odd, ends[1][1], ends[0][1])
    for kc in range(chunks):
        mine = (sh.lane >= kc * plan.ny) & (sh.lane < (kc + 1) * plan.ny)
        depths[kc * sub : (kc + 1) * sub, :] = sh.over_chunks(jnp.where(mine, deep, 0.0))

    def mask(j):
        low = jnp.broadcast_to(depths[pl.ds(j, 1), :], (sub, plan.lanes))
        wet = jnp.where(sh.depth < low, 1.0, 0.0).astype(F32)
        water[j] = wet
        bottom[j] = jnp.where(sh.depth == low - 1.0, 1.0, 0.0).astype(F32)
        oc[0, j] = oc[0, j] * wet

    def mask_x(j):
        oc[1, j] = oc[1, j] * water[j]

    def mask_yw(j):
        oc[2, j] = oc[2, j] * water[j]
        oc[3, j] = oc[3, j] * water[j]

    plan.planes(0, width + 2, mask)
    plan.planes(1, width + 1, mask_x)
    plan.planes(2, width, mask_yw)

    for t in range(STEPS):
        first, last = 2 * t, width - 2 * t
        before = t == 0

        def flow_x(j):
            oc[1, j + 1] = water[j + 1] * (oc[1, j + 1] - HALF * (oc[0, j + 2] - oc[0, j]))

        def flow(j):
            p = oc[0, j + 1]
            wet = water[j + 1]
            oc[2, j + 1] = wet * (oc[2, j + 1] - HALF * sh.dy(p))
            rise = sh.below(p) + bottom[j + 1] * p - sh.above(p, -p)
            oc[3, j + 1] = wet * (oc[3, j + 1] - (HALF * rise + (DT * GRAV) * p))

        def press(j):
            w = oc[3, j + 1]
            floor = mats[FLOOR, j] if before else sh.seafloor(vel[VZ, j])
            rise = sh.below(w) + bottom[j + 1] * floor - sh.above(w, w)
            total = oc[1, j + 2] - oc[1, j] + sh.dy(oc[2, j + 1]) + rise
            oc[0, j + 1] = water[j + 1] * (oc[0, j + 1] - (HALF * KBULK) * total)

        def load(j):
            column = jnp.sum(bottom[j + 1] * oc[0, j + 1], axis=0, keepdims=True)
            column = jnp.broadcast_to(sh.over_chunks(column), (sub, plan.lanes))
            return jnp.where(sh.top, column, 0.0)

        plan.planes(first, last, flow_x)
        plan.planes(first + 1, last - 1, flow)
        plan.planes(first + 1, last - 1, press)
        if before:
            def add_load(j):
                for f in (VX, VY):
                    vel[f, j] = vel_in[f, j]
                vel[VZ, j] = vel_in[VZ, j] + mats[BUOY, j] * load(j)

            plan.planes(first + 1, last - 1, add_load)
        elif t < STEPS - 1:
            def move(j):
                ax, ay, az = acceleration(sh, stress, j)
                b = mats[BUOY, j]
                vel[VX, j] = vel[VX, j] + b * ax
                vel[VY, j] = vel[VY, j] + b * ay
                vel[VZ, j] = vel[VZ, j] + b * (az + load(j))

            plan.planes(first + 1, last - 1, move)
        else:
            def keep(j):
                loads[j] = load(j)

            plan.planes(first + 1, last - 1, keep)
        if t < STEPS - 2:
            def strain(j):
                source = stress_in if before else stress
                for f, value in enumerate(strained(sh, vel, source, mats, j)):
                    stress[f, j] = value

            plan.planes(first + 2, last - 2, strain)

    for group in range(plan.own_groups):
        stacked = jnp.concatenate(
            [
                oc[f, 1 + HALO + group * chunks + i]
                for i in range(chunks)
                for f in range(4)
            ],
            axis=0,
        )
        gather[...] = stacked.T
        for kc in range(chunks):
            for yl in range(strips):
                at = group * plan.lead + kc * strips + yl
                message[pl.ds(at, n, stride=plan.back_rows), :] = gather[
                    pl.ds(kc * plan.ny + yl, n, stride=strips), :
                ]


def end_kernel(plan, vel_in, stress_in, mats, loads, vel_out, stress_out, vel, stress):
    cells, sub, chunks, ny = plan.cells, plan.sub, plan.chunks, plan.ny
    sh = Shifts(plan)
    first, last = 2 * (STEPS - 1), plan.width - 2 * (STEPS - 1)

    def put(out, f, x, plane):
        for kc in range(chunks):
            out[f, x, kc * sub : (kc + 1) * sub, :] = plane[:, kc * ny : (kc + 1) * ny]

    def strain(j):
        for f, value in enumerate(strained(sh, vel_in, stress_in, mats, j)):
            stress[f, j] = value

    def move(j):
        ax, ay, az = acceleration(sh, stress, j)
        b = mats[BUOY, j]
        for f, a in enumerate((ax, ay, az + loads[j])):
            vel[f, j] = vel_in[f, j] + b * a

    def finish(x):
        for f in range(3):
            put(vel_out, f, x, vel[f, x + HALO])
        for f, value in enumerate(strained(sh, vel, stress, mats, x + HALO)):
            put(stress_out, f, x, value)

    plan.planes(first, last, strain)
    plan.planes(first + 1, last - 1, move)
    plan.planes(0, cells, finish)


def unpack_kernel(plan, arrived, ocean, turned):
    sub, chunks = plan.sub, plan.chunks
    block = 4 * sub
    for yl in range(plan.strips):
        by_chunk = [
            arrived[pl.ds(kc * plan.strips + yl, plan.nx // chunks, stride=plan.lead), :]
            for kc in range(chunks)
        ]
        for i in range(chunks):
            turned[pl.ds(i, plan.nx // chunks, stride=chunks), :] = place(
                by_chunk, [i] * chunks, block
            )
        whole = turned[...].T
        for kc in range(chunks):
            for f in range(4):
                at = (kc * 4 + f) * sub
                ocean[f, yl, kc * sub : (kc + 1) * sub, :] = whole[at : at + sub]


def on_device(plan, velocity, stress, ocean, zones, materials, slip, bathy):
    n, cells, sub, lanes, width = plan.n, plan.cells, plan.sub, plan.lanes, plan.width
    vmem = pl.BlockSpec(memory_space=pltpu.VMEM)
    smem = pl.BlockSpec(memory_space=pltpu.SMEM)
    hbm = pl.BlockSpec(memory_space=pltpu.HBM)

    def shape(*dims):
        return jax.ShapeDtypeStruct(dims, F32)

    def like(array):
        return jax.ShapeDtypeStruct(array.shape, array.dtype)

    def held(array):
        return pltpu.VMEM(array.shape, array.dtype)

    def call(kernel, name, out, ins, scratch, room=16, **rest):
        room = room if plan.unrolled else 56
        return pl.pallas_call(
            functools.partial(kernel, plan),
            out_shape=out,
            in_specs=ins,
            out_specs=jax.tree.map(lambda _: vmem, out),
            scratch_shapes=scratch,
            compiler_params=pltpu.CompilerParams(vmem_limit_bytes=room * 1024 * 1024),
            name=name,
            **rest,
        )

    def pinned(array):
        return pltpu.with_memory_space_constraint(array, pltpu.HBM)

    def near(array):
        return pltpu.with_memory_space_constraint(array, pltpu.VMEM) if plan.unrolled else array

    mates = [(i, i ^ 1) for i in range(n)]
    others = [(i, i + 1) for i in range(1, n - 1, 2)]
    others += [(target, source) for source, target in others]
    crust, message = call(
        pack_kernel,
        "pack",
        (shape(10 * cells + 1, sub, lanes), shape(n * plan.rows, LANES)),
        [hbm] * 6,
        [held(a) for a in (velocity, stress, zones, slip, ocean, bathy)]
        + [
            pltpu.VMEM((plan.strips, plan.nx, LANES), F32),
            pltpu.VMEM(
                (plan.lead, plan.nx // plan.chunks + 2 * plan.halo_groups, LANES), F32
            ),
            pltpu.VMEM((n * plan.strips, LANES), F32),
            pltpu.VMEM((n * plan.rows, LANES), F32),
            pltpu.SemaphoreType.DMA((6,)),
        ],
    )(*(pinned(a) for a in (velocity, stress, zones, slip, ocean, bathy)))
    other = lax.ppermute(crust, "map", others)
    arrived = lax.all_to_all(
        message.reshape(n // 2, 2 * plan.rows, LANES),
        "map",
        split_axis=0,
        concat_axis=0,
        axis_index_groups=[list(range(core, n, 2)) for core in range(2)],
        tiled=True,
    ).reshape(n * plan.rows, LANES)
    mate = lax.ppermute(crust, "map", mates)
    vel, strs, mats = call(
        begin_kernel,
        "first_velocity",
        (shape(3, width, sub, lanes), shape(6, width, sub, lanes), shape(5, width, sub, lanes)),
        [smem] + [vmem] * 3,
        [],
        cost_estimate=pl.CostEstimate(
            flops=10**11, bytes_accessed=200 * 10**6, transcendentals=0
        ),
    )(materials, crust, mate, other)
    arrived, vel = lax.optimization_barrier((arrived, vel))
    swapped = lax.ppermute(arrived, "map", mates)
    vel, strs, loads, back = call(
        middle_kernel,
        "substeps",
        (
            shape(3, width, sub, lanes),
            shape(6, width, sub, lanes),
            shape(width, sub, lanes),
            shape(n * plan.back_rows, LANES),
        ),
        [vmem] * 5,
        [
            pltpu.VMEM((4, width + 2, sub, lanes), F32),
            pltpu.VMEM((width + 2, sub, lanes), F32),
            pltpu.VMEM((width + 2, sub, lanes), F32),
            pltpu.VMEM((lanes, LANES), F32),
            pltpu.VMEM((plan.depth, lanes), F32),
        ],
        input_output_aliases={2: 0, 3: 1},
    )(*(near(a) for a in (arrived, swapped, vel, strs, mats)))
    returned = lax.all_to_all(
        back.reshape(n, plan.back_rows, LANES), "map", split_axis=0, concat_axis=0, tiled=True
    ).reshape(n * plan.back_rows, LANES)
    new_velocity, new_stress = call(
        end_kernel,
        "last_updates",
        (shape(*velocity.shape), shape(*stress.shape)),
        [vmem] * 4,
        [
            pltpu.VMEM((3, width, sub, lanes), F32),
            pltpu.VMEM((6, width, sub, lanes), F32),
        ],
    )(vel, strs, mats, loads)
    new_ocean = call(
        unpack_kernel,
        "ocean_strips",
        shape(*ocean.shape),
        [vmem],
        [pltpu.VMEM((plan.nx, LANES), F32)],
    )(returned)
    return new_velocity, new_stress, new_ocean


def solution(mesh):
    n = mesh.shape["map"]

    def body(velocity, stress, ocean, zones, materials, slip, bathy):
        _, cells, depth, ny = velocity.shape
        plan = Plan(n, cells, depth, ny, ocean.shape[1])
        return on_device(plan, velocity, stress, ocean, zones, materials, slip, bathy)

    return jax.shard_map(
        body,
        mesh=mesh,
        in_specs=(
            P("parts", "map", None, None),
            P("parts", "map", None, None),
            P("parts", "map", None, None),
            P("map", "parts", None),
            P(),
            P("map", "parts"),
            P("map", "parts"),
        ),
        out_specs=(
            P("parts", "map", None, None),
            P("parts", "map", None, None),
            P("parts", "map", None, None),
        ),
        check_vma=False,
    )
```

```python
import functools

import jax
import jax.numpy as jnp
from jax import lax
from jax.experimental import pallas as pl
from jax.experimental.pallas import tpu as pltpu
from jax.sharding import PartitionSpec as P

STEPS = 4
ZONES = 8
DT = 0.25
HALF = 0.5 * DT
KBULK = 2.25
GRAV = 0.1
HALO = 2 * STEPS
LANES = 128
F32 = jnp.float32
VX, VY, VZ = range(3)
SXX, SYY, SZZ, SXY, SXZ, SYZ = range(6)
BUOY, LAMB, SHEAR, FAULT, FLOOR = range(5)


class Plan:
    def __init__(self, devices, cells, depth, ny, strips):
        self.n = devices
        self.cells = cells
        self.depth = depth
        self.ny = ny
        self.strips = strips
        self.chunks = max(1, LANES // ny)
        self.sub = depth // self.chunks
        self.lanes = self.chunks * ny
        self.width = cells + 2 * HALO
        self.own_groups = cells // self.chunks
        self.halo_groups = HALO // self.chunks
        self.sent_groups = self.own_groups + self.halo_groups
        self.lead = self.chunks * strips
        self.rows = self.lead * self.sent_groups
        self.back_rows = self.lead * self.own_groups
        self.nx = devices * cells
        self.block = 4 * self.sub
        self.unrolled = self.sub * self.lanes <= 1024
        assert devices % 2 == 0 and cells == HALO and self.block * self.chunks == LANES

    def planes(self, start, stop, body):
        if self.unrolled:
            for j in range(start, stop):
                body(j)
        else:
            def run(j, carry):
                body(j)
                return carry

            lax.fori_loop(start, stop, run, 0)


def odd_device():
    return lax.rem(lax.axis_index("map"), 2)


def place(pieces, wanted, block):
    out = None
    for i, piece in enumerate(pieces):
        shift = (i - wanted[i]) * block % piece.shape[-1]
        moved = pltpu.roll(piece, shift, piece.ndim - 1) if shift else piece
        if out is None:
            out = moved
        else:
            lane = lax.broadcasted_iota(jnp.int32, moved.shape, moved.ndim - 1)
            out = jnp.where(lane >= i * block, moved, out)
    return out


def ocean_kernel(plan, ocean, bathy, message, turned, grouped, extra):
    cells, sub, chunks, n, strips = plan.cells, plan.sub, plan.chunks, plan.n, plan.strips
    block, sent, rows = plan.block, plan.sent_groups, plan.rows
    border = jnp.zeros((plan.lead, plan.halo_groups, LANES), F32)
    count = plan.nx // chunks
    grouped[:, : plan.halo_groups, :] = border
    grouped[:, plan.halo_groups + count :, :] = border
    for yl in range(strips):
        stacked = jnp.concatenate(
            [ocean[f, yl, kc * sub : (kc + 1) * sub, :] for kc in range(chunks) for f in range(4)],
            axis=0,
        )
        turned[yl] = stacked.T
        by_x = [turned[yl, pl.ds(i, count, stride=chunks), :] for i in range(chunks)]
        for kc in range(chunks):
            grouped[kc * strips + yl, pl.ds(plan.halo_groups, count), :] = place(
                by_x, [kc] * chunks, block
            )
    for d in range(n):
        start = d * plan.own_groups + (d % 2) * plan.halo_groups
        for q in range(plan.lead):
            message[d * rows + q * sent : d * rows + (q + 1) * sent, :] = grouped[
                q, start : start + sent, :
            ]
    depths = bathy[...].astype(F32)
    wide = lax.broadcasted_iota(jnp.int32, depths.shape, 1)
    for d in range(n):
        first = d * cells - HALO - 1
        moved = pltpu.roll(depths, -first % plan.nx, 1)
        moved = jnp.where((wide + first >= 0) & (wide + first < plan.nx), moved, 0.0)
        extra[d * strips : (d + 1) * strips, :] = moved[:, :LANES]
    pairs = n // 2
    lane = lax.broadcasted_iota(jnp.int32, (pairs, LANES), 1)
    blank = jnp.zeros((1, LANES), F32)
    for odd in range(2):
        slot = (odd * (chunks - 1) * 4 + 2) * sub
        group = odd * (sent - 1)
        for yl in range(strips):
            if odd:
                column = turned[yl, pl.ds(2 * cells + HALO, pairs - 1, stride=2 * cells), :]
                column = jnp.concatenate([column, blank], axis=0)
            else:
                column = turned[yl, pl.ds(2 * cells - HALO - 1, pairs - 1, stride=2 * cells), :]
                column = jnp.concatenate([blank, column], axis=0)
            deep = extra[pl.ds(odd * strips + yl, pairs, stride=2 * strips), :]
            for kc in range(chunks):
                at = odd * rows + (kc * strips + yl) * sent + group
                old = message[pl.ds(at, pairs, stride=2 * rows), :]
                edge = pltpu.roll(column, (slot - kc * block) % LANES, 1)
                floor = pltpu.roll(deep, (slot + sub - kc * sub) % LANES, 1)
                new = jnp.where((lane >= slot) & (lane < slot + sub), edge, old)
                new = jnp.where((lane >= slot + sub) & (lane < slot + 2 * sub), floor, new)
                message[pl.ds(at, pairs, stride=2 * rows), :] = new


def crust_kernel(
    plan, vel_ref, stress_ref, zones_ref, slip_ref, ocean_ref, bathy_ref,
    crust, border, ocean, bathy, vel, stress, zones, slip, sems,
):
    cells, sub, chunks, ny = plan.cells, plan.sub, plan.chunks, plan.ny
    pairs = (
        (vel_ref, vel),
        (stress_ref, stress),
        (zones_ref, zones),
        (slip_ref, slip),
        (ocean_ref, ocean),
        (bathy_ref, bathy),
    )
    copies = [
        pltpu.make_async_copy(source, target, sems.at[i])
        for i, (source, target) in enumerate(pairs)
    ]
    for copy in copies:
        copy.start()

    def joined(ref, *at):
        parts = [ref[(*at, pl.ds(kc * sub, sub), slice(None))] for kc in range(chunks)]
        return jnp.concatenate(parts, axis=-1) if chunks > 1 else parts[0]

    copies[0].wait()
    for f in range(3):
        for x in range(cells):
            crust[f * cells + x] = joined(vel, f, x)
    copies[1].wait()
    for f in range(6):
        for x in range(cells):
            crust[(3 + f) * cells + x] = joined(stress, f, x)
    copies[2].wait()
    for x in range(cells):
        crust[9 * cells + x] = (joined(zones, x) + 1).astype(F32)
    copies[3].wait()
    fault_chunk = (plan.depth // 2) // sub
    pieces = [
        slip[...] if kc == fault_chunk else jnp.zeros((cells, ny), F32) for kc in range(chunks)
    ]
    fault = jnp.concatenate(pieces, axis=-1) if chunks > 1 else pieces[0]
    if sub > cells:
        fault = jnp.concatenate([fault, jnp.zeros((sub - cells, plan.lanes), F32)], axis=0)
    crust[10 * cells] = fault
    odd = odd_device()
    near = cells - 1
    for f in range(10):
        for i in range(near):
            border[f * near + i] = crust[f * cells + i + odd]
    for i, f in enumerate((SXX, SXY, SXZ)):
        border[10 * near + i] = crust[(3 + f) * cells + near * (1 - odd)]
    border[10 * near + 3] = fault
    copies[4].wait()
    copies[5].wait()


class Shifts:
    def __init__(self, plan):
        self.plan = plan
        shape = (plan.sub, plan.lanes)
        self.row = lax.broadcasted_iota(jnp.int32, shape, 0)
        self.lane = lax.broadcasted_iota(jnp.int32, shape, 1)
        self.y = lax.rem(self.lane, plan.ny)
        self.first_row = self.row == 0
        self.last_row = self.row == plan.sub - 1
        self.top = self.first_row & (self.lane < plan.ny)
        self.floor_cell = self.last_row & (self.lane >= plan.lanes - plan.ny)
        self.not_low_y = jnp.where(self.y == 0, 0.0, 1.0).astype(F32)
        self.not_high_y = jnp.where(self.y == plan.ny - 1, 0.0, 1.0).astype(F32)
        self.depth = (
            lax.div(self.lane, plan.ny) * plan.sub + self.row
        ).astype(F32)

    def dy(self, f):
        lanes = self.plan.lanes
        return pltpu.roll(f, lanes - 1, 1) * self.not_high_y - pltpu.roll(f, 1, 1) * self.not_low_y

    def below(self, f):
        plan = self.plan
        moved = pltpu.roll(f, plan.sub - 1, 0)
        if plan.chunks > 1:
            moved = jnp.where(self.last_row, pltpu.roll(moved, plan.lanes - plan.ny, 1), moved)
        return jnp.where(self.floor_cell, 0.0, moved)

    def above(self, f, top):
        plan = self.plan
        moved = pltpu.roll(f, 1, 0)
        if plan.chunks > 1:
            moved = jnp.where(self.first_row, pltpu.roll(moved, plan.ny, 1), moved)
        return jnp.where(self.top, top, moved)

    def seafloor(self, vz):
        row = self.over_chunks(jnp.where(self.top, vz, 0.0)[0:1])
        return jnp.broadcast_to(row, vz.shape)

    def over_chunks(self, f):
        shift = self.plan.ny
        while shift < self.plan.lanes:
            f = f + pltpu.roll(f, shift, 1)
            shift *= 2
        return f


def acceleration(sh, stress, j):
    sxy, sxz = stress[SXY, j], stress[SXZ, j]
    syz, szz = stress[SYZ, j], stress[SZZ, j]
    ax = stress[SXX, j + 1] - stress[SXX, j - 1] + sh.dy(sxy) + sh.below(sxz) - sh.above(sxz, 0.0)
    ay = stress[SXY, j + 1] - stress[SXY, j - 1] + sh.dy(stress[SYY, j])
    ay = ay + sh.below(syz) - sh.above(syz, 0.0)
    az = stress[SXZ, j + 1] - stress[SXZ, j - 1] + sh.dy(syz) + sh.below(szz) - sh.above(szz, 0.0)
    return ax, ay, az


def strained(sh, vel, stress, mats, j):
    vx, vy, vz = vel[VX, j], vel[VY, j], vel[VZ, j]
    exx = vel[VX, j + 1] - vel[VX, j - 1]
    eyy = sh.dy(vy)
    ezz = sh.below(vz) - sh.above(vz, vz)
    mu = mats[SHEAR, j]
    mu2 = mu + mu
    common = mats[LAMB, j] * (exx + eyy + ezz)
    exy = sh.dy(vx) + vel[VY, j + 1] - vel[VY, j - 1]
    exz = sh.below(vx) - sh.above(vx, vx) + vel[VZ, j + 1] - vel[VZ, j - 1]
    eyz = sh.below(vy) - sh.above(vy, vy) + sh.dy(vz)
    return (
        stress[SXX, j] + (common + mu2 * exx),
        stress[SYY, j] + (common + mu2 * eyy),
        stress[SZZ, j] + (common + mu2 * ezz),
        stress[SXY, j] + mu * exy,
        stress[SXZ, j] + (mu * exz + mats[FAULT, j]),
        stress[SYZ, j] + mu * eyz,
    )


def begin_kernel(plan, table, own, mate, border, vel, stress, mats):
    cells, sub = plan.cells, plan.sub
    near = cells - 1
    sh = Shifts(plan)
    odd = odd_device()

    def bring(x, ref, count, start, first):
        j = start + x
        for f in range(3):
            vel[f, j] = ref[f * count + x]
        for f in range(6):
            stress[f, j] = ref[(3 + f) * count + x]
        zone = ref[9 * count + x]
        values = [jnp.zeros_like(zone) for _ in range(3)]
        for z in range(ZONES):
            here = zone == float(z + 1)
            values = [jnp.where(here, table[c, z], values[c]) for c in range(3)]
        for c in range(3):
            mats[c, j] = values[c] * HALF
        slips = ref[ref.shape[0] - 1, pl.ds(first + x, 1), :]
        slip = jnp.broadcast_to(slips, (sub, plan.lanes))
        mats[FAULT, j] = jnp.where(sh.row == (plan.depth // 2) % sub, DT * slip, 0.0)
        mats[FLOOR, j] = sh.seafloor(ref[VZ * count + x])

    plan.planes(0, cells, lambda x: bring(x, own, cells, HALO, 0))
    plan.planes(0, cells, lambda x: bring(x, mate, cells, (HALO + cells) * (1 - odd), 0))
    low = 1 + (HALO + cells - 1) * odd
    plan.planes(0, near, lambda x: bring(x, border, near, low, 1 - odd))
    for i, f in enumerate((SXX, SXY, SXZ)):
        stress[f, (plan.width - 1) * odd] = border[10 * near + i]

    def move(j):
        b = mats[BUOY, j]
        for f, a in enumerate(acceleration(sh, stress, j)):
            vel[f, j] = vel[f, j] + b * a

    plan.planes(1, plan.width - 1, move)


def middle_kernel(
    plan, arrived, swapped, vel_in, stress_in, mats, vel, stress, loads, message,
    oc, water, bottom, gather, depths,
):
    sub, chunks, n, strips = plan.sub, plan.chunks, plan.n, plan.strips
    width, sent = plan.width, plan.sent_groups
    sh = Shifts(plan)
    odd = odd_device()

    half = n // 2
    mate = 1 - odd

    def turn(owner, group):
        for core, ref in ((odd, arrived), (mate, swapped)):
            for kc in range(chunks):
                for yl in range(strips):
                    at = owner * plan.rows + (kc * strips + yl) * sent + group
                    to = kc * plan.ny + core * strips + yl
                    gather[pl.ds(to, half, stride=2 * strips), :] = ref[
                        pl.ds(at, half, stride=2 * plan.rows), :
                    ]
        return gather[...].T

    def spread(turned, group):
        for i in range(chunks):
            for f in range(4):
                at = (i * 4 + f) * sub
                oc[f, 1 + group * chunks + i] = turned[at : at + sub]

    ends = []
    for group in range(sent):
        turned = turn(odd, group)
        spread(turned, group + plan.halo_groups * odd)
        if group == 0:
            ends.append((turned[2 * sub : 3 * sub], turned[3 * sub : 4 * sub]))
        if group == sent - 1:
            ends.append((turned[LANES - 2 * sub : LANES - sub], turned[LANES - sub :]))
    for group in range(plan.halo_groups):
        spread(turn(mate, group + plan.own_groups * odd), group + sent * mate)
    turned = turn(mate, plan.own_groups - odd)
    is_odd = odd == 1
    oc[0, (width + 1) * odd] = jnp.where(is_odd, ends[1][0], ends[0][0])
    oc[0, (width + 1) * mate] = jnp.where(
        is_odd, turned[LANES - 4 * sub : LANES - 3 * sub], turned[:sub]
    )
    deep = jnp.where(is_odd, ends[1][1], ends[0][1])
    for kc in range(chunks):
        mine = (sh.lane >= kc * plan.ny) & (sh.lane < (kc + 1) * plan.ny)
        depths[kc * sub : (kc + 1) * sub, :] = sh.over_chunks(jnp.where(mine, deep, 0.0))

    def mask(j):
        low = jnp.broadcast_to(depths[pl.ds(j, 1), :], (sub, plan.lanes))
        wet = jnp.where(sh.depth < low, 1.0, 0.0).astype(F32)
        water[j] = wet
        bottom[j] = jnp.where(sh.depth == low - 1.0, 1.0, 0.0).astype(F32)
        oc[0, j] = oc[0, j] * wet

    def mask_x(j):
        oc[1, j] = oc[1, j] * water[j]

    def mask_yw(j):
        oc[2, j] = oc[2, j] * water[j]
        oc[3, j] = oc[3, j] * water[j]

    plan.planes(0, width + 2, mask)
    plan.planes(1, width + 1, mask_x)
    plan.planes(2, width, mask_yw)

    for t in range(STEPS):
        first, last = 2 * t, width - 2 * t
        before = t == 0

        def flow_x(j):
            oc[1, j + 1] = water[j + 1] * (oc[1, j + 1] - HALF * (oc[0, j + 2] - oc[0, j]))

        def flow(j):
            p = oc[0, j + 1]
            wet = water[j + 1]
            oc[2, j + 1] = wet * (oc[2, j + 1] - HALF * sh.dy(p))
            rise = sh.below(p) + bottom[j + 1] * p - sh.above(p, -p)
            oc[3, j + 1] = wet * (oc[3, j + 1] - (HALF * rise + (DT * GRAV) * p))

        def press(j):
            w = oc[3, j + 1]
            floor = mats[FLOOR, j] if before else sh.seafloor(vel[VZ, j])
            rise = sh.below(w) + bottom[j + 1] * floor - sh.above(w, w)
            total = oc[1, j + 2] - oc[1, j] + sh.dy(oc[2, j + 1]) + rise
            oc[0, j + 1] = water[j + 1] * (oc[0, j + 1] - (HALF * KBULK) * total)

        def load(j):
            column = jnp.sum(bottom[j + 1] * oc[0, j + 1], axis=0, keepdims=True)
            column = jnp.broadcast_to(sh.over_chunks(column), (sub, plan.lanes))
            return jnp.where(sh.top, column, 0.0)

        plan.planes(first, last, flow_x)
        plan.planes(first + 1, last - 1, flow)
        plan.planes(first + 1, last - 1, press)
        if before:
            def add_load(j):
                for f in (VX, VY):
                    vel[f, j] = vel_in[f, j]
                vel[VZ, j] = vel_in[VZ, j] + mats[BUOY, j] * load(j)

            plan.planes(first + 1, last - 1, add_load)
        elif t < STEPS - 1:
            def move(j):
                ax, ay, az = acceleration(sh, stress, j)
                b = mats[BUOY, j]
                vel[VX, j] = vel[VX, j] + b * ax
                vel[VY, j] = vel[VY, j] + b * ay
                vel[VZ, j] = vel[VZ, j] + b * (az + load(j))

            plan.planes(first + 1, last - 1, move)
        else:
            def keep(j):
                loads[j] = load(j)

            plan.planes(first + 1, last - 1, keep)
        if t < STEPS - 2:
            def strain(j):
                source = stress_in if before else stress
                for f, value in enumerate(strained(sh, vel, source, mats, j)):
                    stress[f, j] = value

            plan.planes(first + 2, last - 2, strain)

    for group in range(plan.own_groups):
        stacked = jnp.concatenate(
            [
                oc[f, 1 + HALO + group * chunks + i]
                for i in range(chunks)
                for f in range(4)
            ],
            axis=0,
        )
        gather[...] = stacked.T
        for kc in range(chunks):
            for yl in range(strips):
                at = group * plan.lead + kc * strips + yl
                message[pl.ds(at, n, stride=plan.back_rows), :] = gather[
                    pl.ds(kc * plan.ny + yl, n, stride=strips), :
                ]


def end_kernel(plan, vel_in, stress_in, mats, loads, vel_out, stress_out, vel, stress):
    cells, sub, chunks, ny = plan.cells, plan.sub, plan.chunks, plan.ny
    sh = Shifts(plan)
    first, last = 2 * (STEPS - 1), plan.width - 2 * (STEPS - 1)

    def put(out, f, x, plane):
        for kc in range(chunks):
            out[f, x, kc * sub : (kc + 1) * sub, :] = plane[:, kc * ny : (kc + 1) * ny]

    def strain(j):
        for f, value in enumerate(strained(sh, vel_in, stress_in, mats, j)):
            stress[f, j] = value

    def move(j):
        ax, ay, az = acceleration(sh, stress, j)
        b = mats[BUOY, j]
        for f, a in enumerate((ax, ay, az + loads[j])):
            vel[f, j] = vel_in[f, j] + b * a

    def finish(x):
        for f in range(3):
            put(vel_out, f, x, vel[f, x + HALO])
        for f, value in enumerate(strained(sh, vel, stress, mats, x + HALO)):
            put(stress_out, f, x, value)

    plan.planes(first, last, strain)
    plan.planes(first + 1, last - 1, move)
    plan.planes(0, cells, finish)


def unpack_kernel(plan, arrived, ocean, turned):
    sub, chunks = plan.sub, plan.chunks
    block = 4 * sub
    for yl in range(plan.strips):
        by_chunk = [
            arrived[pl.ds(kc * plan.strips + yl, plan.nx // chunks, stride=plan.lead), :]
            for kc in range(chunks)
        ]
        for i in range(chunks):
            turned[pl.ds(i, plan.nx // chunks, stride=chunks), :] = place(
                by_chunk, [i] * chunks, block
            )
        whole = turned[...].T
        for kc in range(chunks):
            for f in range(4):
                at = (kc * 4 + f) * sub
                ocean[f, yl, kc * sub : (kc + 1) * sub, :] = whole[at : at + sub]


def on_device(plan, velocity, stress, ocean, zones, materials, slip, bathy):
    n, cells, sub, lanes, width = plan.n, plan.cells, plan.sub, plan.lanes, plan.width
    vmem = pl.BlockSpec(memory_space=pltpu.VMEM)
    smem = pl.BlockSpec(memory_space=pltpu.SMEM)
    hbm = pl.BlockSpec(memory_space=pltpu.HBM)

    def shape(*dims):
        return jax.ShapeDtypeStruct(dims, F32)

    def like(array):
        return jax.ShapeDtypeStruct(array.shape, array.dtype)

    def held(array):
        return pltpu.VMEM(array.shape, array.dtype)

    def call(kernel, name, out, ins, scratch, room=16, **rest):
        room = room if plan.unrolled else 56
        return pl.pallas_call(
            functools.partial(kernel, plan),
            out_shape=out,
            in_specs=ins,
            out_specs=jax.tree.map(lambda _: vmem, out),
            scratch_shapes=scratch,
            compiler_params=pltpu.CompilerParams(vmem_limit_bytes=room * 1024 * 1024),
            name=name,
            **rest,
        )

    def pinned(array):
        return pltpu.with_memory_space_constraint(array, pltpu.HBM)

    def near(array):
        return pltpu.with_memory_space_constraint(array, pltpu.VMEM) if plan.unrolled else array

    mates = [(i, i ^ 1) for i in range(n)]
    others = [(i, i + 1) for i in range(1, n - 1, 2)]
    others += [(target, source) for source, target in others]
    crust, border, ocean_near, bathy_near = call(
        crust_kernel,
        "crust_planes",
        (
            shape(10 * cells + 1, sub, lanes),
            shape(10 * cells - 6, sub, lanes),
            like(ocean),
            like(bathy),
        ),
        [hbm] * 6,
        [held(a) for a in (velocity, stress, zones, slip)] + [pltpu.SemaphoreType.DMA((6,))],
    )(*(pinned(a) for a in (velocity, stress, zones, slip, ocean, bathy)))
    other = lax.ppermute(border, "map", others)
    message = call(
        ocean_kernel,
        "ocean_rows",
        shape(n * plan.rows, LANES),
        [vmem] * 2,
        [
            pltpu.VMEM((plan.strips, plan.nx, LANES), F32),
            pltpu.VMEM(
                (plan.lead, plan.nx // plan.chunks + 2 * plan.halo_groups, LANES), F32
            ),
            pltpu.VMEM((n * plan.strips, LANES), F32),
        ],
    )(ocean_near, bathy_near)
    message, crust = lax.optimization_barrier((message, crust))
    arrived = lax.all_to_all(
        message.reshape(n // 2, 2 * plan.rows, LANES),
        "map",
        split_axis=0,
        concat_axis=0,
        axis_index_groups=[list(range(core, n, 2)) for core in range(2)],
        tiled=True,
    ).reshape(n * plan.rows, LANES)
    mate = lax.ppermute(crust, "map", mates)
    vel, strs, mats = call(
        begin_kernel,
        "first_velocity",
        (shape(3, width, sub, lanes), shape(6, width, sub, lanes), shape(5, width, sub, lanes)),
        [smem] + [vmem] * 3,
        [],
        cost_estimate=pl.CostEstimate(
            flops=10**11, bytes_accessed=200 * 10**6, transcendentals=0
        ),
    )(materials, crust, mate, other)
    arrived, vel = lax.optimization_barrier((arrived, vel))
    swapped = lax.ppermute(arrived, "map", mates)
    vel, strs, loads, back = call(
        middle_kernel,
        "substeps",
        (
            shape(3, width, sub, lanes),
            shape(6, width, sub, lanes),
            shape(width, sub, lanes),
            shape(n * plan.back_rows, LANES),
        ),
        [vmem] * 5,
        [
            pltpu.VMEM((4, width + 2, sub, lanes), F32),
            pltpu.VMEM((width + 2, sub, lanes), F32),
            pltpu.VMEM((width + 2, sub, lanes), F32),
            pltpu.VMEM((lanes, LANES), F32),
            pltpu.VMEM((plan.depth, lanes), F32),
        ],
        input_output_aliases={2: 0, 3: 1},
    )(*(near(a) for a in (arrived, swapped, vel, strs, mats)))
    returned = lax.all_to_all(
        back.reshape(n, plan.back_rows, LANES), "map", split_axis=0, concat_axis=0, tiled=True
    ).reshape(n * plan.back_rows, LANES)
    new_velocity, new_stress = call(
        end_kernel,
        "last_updates",
        (shape(*velocity.shape), shape(*stress.shape)),
        [vmem] * 4,
        [
            pltpu.VMEM((3, width, sub, lanes), F32),
            pltpu.VMEM((6, width, sub, lanes), F32),
        ],
    )(vel, strs, mats, loads)
    new_ocean = call(
        unpack_kernel,
        "ocean_strips",
        shape(*ocean.shape),
        [vmem],
        [pltpu.VMEM((plan.nx, LANES), F32)],
    )(returned)
    return new_velocity, new_stress, new_ocean


def solution(mesh):
    n = mesh.shape["map"]

    def body(velocity, stress, ocean, zones, materials, slip, bathy):
        _, cells, depth, ny = velocity.shape
        plan = Plan(n, cells, depth, ny, ocean.shape[1])
        return on_device(plan, velocity, stress, ocean, zones, materials, slip, bathy)

    return jax.shard_map(
        body,
        mesh=mesh,
        in_specs=(
            P("parts", "map", None, None),
            P("parts", "map", None, None),
            P("parts", "map", None, None),
            P("map", "parts", None),
            P(),
            P("map", "parts"),
            P("map", "parts"),
        ),
        out_specs=(
            P("parts", "map", None, None),
            P("parts", "map", None, None),
            P("parts", "map", None, None),
        ),
        check_vma=False,
    )
```

```python
import functools

import jax
import jax.numpy as jnp
from jax import lax
from jax.experimental import pallas as pl
from jax.experimental.pallas import tpu as pltpu
from jax.sharding import PartitionSpec as P

STEPS = 4
ZONES = 8
DT = 0.25
HALF = 0.5 * DT
KBULK = 2.25
GRAV = 0.1
HALO = 2 * STEPS
LANES = 128
F32 = jnp.float32
VX, VY, VZ = range(3)
SXX, SYY, SZZ, SXY, SXZ, SYZ = range(6)
BUOY, LAMB, SHEAR, FAULT, FLOOR = range(5)


class Plan:
    def __init__(self, devices, cells, depth, ny, strips):
        self.n = devices
        self.cells = cells
        self.depth = depth
        self.ny = ny
        self.strips = strips
        self.chunks = max(1, LANES // ny)
        self.sub = depth // self.chunks
        self.lanes = self.chunks * ny
        self.width = cells + 2 * HALO
        self.own_groups = cells // self.chunks
        self.halo_groups = HALO // self.chunks
        self.sent_groups = self.own_groups + self.halo_groups
        self.lead = self.chunks * strips
        self.rows = self.lead * self.sent_groups
        self.back_rows = self.lead * self.own_groups
        self.nx = devices * cells
        self.block = 4 * self.sub
        self.unrolled = self.sub * self.lanes <= 1024
        assert devices % 2 == 0 and cells == HALO and self.block * self.chunks == LANES

    def planes(self, start, stop, body):
        if self.unrolled:
            for j in range(start, stop):
                body(j)
        else:
            def run(j, carry):
                body(j)
                return carry

            lax.fori_loop(start, stop, run, 0)


def odd_device():
    return lax.rem(lax.axis_index("map"), 2)


def place(pieces, wanted, block):
    out = None
    for i, piece in enumerate(pieces):
        shift = (i - wanted[i]) * block % piece.shape[-1]
        moved = pltpu.roll(piece, shift, piece.ndim - 1) if shift else piece
        if out is None:
            out = moved
        else:
            lane = lax.broadcasted_iota(jnp.int32, moved.shape, moved.ndim - 1)
            out = jnp.where(lane >= i * block, moved, out)
    return out


def pack_kernel(
    plan, vel_ref, stress_ref, zones_ref, slip_ref, ocean_ref, bathy_ref, crust, border, message_out,
    vel, stress, zones, slip, ocean, bathy, turned, grouped, extra, message, sems,
):
    cells, sub, chunks, ny = plan.cells, plan.sub, plan.chunks, plan.ny
    n, strips, block, sent, rows = plan.n, plan.strips, plan.block, plan.sent_groups, plan.rows
    pairs = (
        (ocean_ref, ocean),
        (bathy_ref, bathy),
        (vel_ref, vel),
        (stress_ref, stress),
        (zones_ref, zones),
        (slip_ref, slip),
    )
    copies = [
        pltpu.make_async_copy(source, target, sems.at[i])
        for i, (source, target) in enumerate(pairs)
    ]
    for copy in copies:
        copy.start()
    copies[0].wait()
    copies[1].wait()
    outside = jnp.zeros((plan.lead, plan.halo_groups, LANES), F32)
    count = plan.nx // chunks
    grouped[:, : plan.halo_groups, :] = outside
    grouped[:, plan.halo_groups + count :, :] = outside
    for yl in range(strips):
        stacked = jnp.concatenate(
            [ocean[f, yl, kc * sub : (kc + 1) * sub, :] for kc in range(chunks) for f in range(4)],
            axis=0,
        )
        turned[yl] = stacked.T
        by_x = [turned[yl, pl.ds(i, count, stride=chunks), :] for i in range(chunks)]
        for kc in range(chunks):
            grouped[kc * strips + yl, pl.ds(plan.halo_groups, count), :] = place(
                by_x, [kc] * chunks, block
            )
    for d in range(n):
        start = d * plan.own_groups + (d % 2) * plan.halo_groups
        for q in range(plan.lead):
            message[d * rows + q * sent : d * rows + (q + 1) * sent, :] = grouped[
                q, start : start + sent, :
            ]
    depths = bathy[...].astype(F32)
    wide = lax.broadcasted_iota(jnp.int32, depths.shape, 1)
    for d in range(n):
        first = d * cells - HALO - 1
        moved = pltpu.roll(depths, -first % plan.nx, 1)
        moved = jnp.where((wide + first >= 0) & (wide + first < plan.nx), moved, 0.0)
        extra[d * strips : (d + 1) * strips, :] = moved[:, :LANES]
    pairs = n // 2
    lane = lax.broadcasted_iota(jnp.int32, (pairs, LANES), 1)
    blank = jnp.zeros((1, LANES), F32)
    for odd in range(2):
        slot = (odd * (chunks - 1) * 4 + 2) * sub
        group = odd * (sent - 1)
        for yl in range(strips):
            if odd:
                column = turned[yl, pl.ds(2 * cells + HALO, pairs - 1, stride=2 * cells), :]
                column = jnp.concatenate([column, blank], axis=0)
            else:
                column = turned[yl, pl.ds(2 * cells - HALO - 1, pairs - 1, stride=2 * cells), :]
                column = jnp.concatenate([blank, column], axis=0)
            deep = extra[pl.ds(odd * strips + yl, pairs, stride=2 * strips), :]
            for kc in range(chunks):
                at = odd * rows + (kc * strips + yl) * sent + group
                old = message[pl.ds(at, pairs, stride=2 * rows), :]
                edge = pltpu.roll(column, (slot - kc * block) % LANES, 1)
                floor = pltpu.roll(deep, (slot + sub - kc * sub) % LANES, 1)
                new = jnp.where((lane >= slot) & (lane < slot + sub), edge, old)
                new = jnp.where((lane >= slot + sub) & (lane < slot + 2 * sub), floor, new)
                message[pl.ds(at, pairs, stride=2 * rows), :] = new
    message_out[...] = message[...]

    def joined(ref, *at):
        parts = [ref[(*at, pl.ds(kc * sub, sub), slice(None))] for kc in range(chunks)]
        return jnp.concatenate(parts, axis=-1) if chunks > 1 else parts[0]

    copies[2].wait()
    for f in range(3):
        for x in range(cells):
            crust[f * cells + x] = joined(vel, f, x)
    copies[3].wait()
    for f in range(6):
        for x in range(cells):
            crust[(3 + f) * cells + x] = joined(stress, f, x)
    copies[4].wait()
    for x in range(cells):
        crust[9 * cells + x] = (joined(zones, x) + 1).astype(F32)
    copies[5].wait()
    fault_chunk = (plan.depth // 2) // sub
    pieces = [
        slip[...] if kc == fault_chunk else jnp.zeros((cells, ny), F32) for kc in range(chunks)
    ]
    fault = jnp.concatenate(pieces, axis=-1) if chunks > 1 else pieces[0]
    if sub > cells:
        fault = jnp.concatenate([fault, jnp.zeros((sub - cells, plan.lanes), F32)], axis=0)
    crust[10 * cells] = fault
    odd = odd_device()
    near = cells - 1
    for f in range(10):
        for i in range(near):
            border[f * near + i] = crust[f * cells + i + odd]
    for i, f in enumerate((SXX, SXY, SXZ)):
        border[10 * near + i] = crust[(3 + f) * cells + near * (1 - odd)]
    border[10 * near + 3] = fault


class Shifts:
    def __init__(self, plan):
        self.plan = plan
        shape = (plan.sub, plan.lanes)
        self.row = lax.broadcasted_iota(jnp.int32, shape, 0)
        self.lane = lax.broadcasted_iota(jnp.int32, shape, 1)
        self.y = lax.rem(self.lane, plan.ny)
        self.first_row = self.row == 0
        self.last_row = self.row == plan.sub - 1
        self.top = self.first_row & (self.lane < plan.ny)
        self.floor_cell = self.last_row & (self.lane >= plan.lanes - plan.ny)
        self.not_low_y = jnp.where(self.y == 0, 0.0, 1.0).astype(F32)
        self.not_high_y = jnp.where(self.y == plan.ny - 1, 0.0, 1.0).astype(F32)
        self.depth = (
            lax.div(self.lane, plan.ny) * plan.sub + self.row
        ).astype(F32)

    def dy(self, f):
        lanes = self.plan.lanes
        return pltpu.roll(f, lanes - 1, 1) * self.not_high_y - pltpu.roll(f, 1, 1) * self.not_low_y

    def below(self, f):
        plan = self.plan
        moved = pltpu.roll(f, plan.sub - 1, 0)
        if plan.chunks > 1:
            moved = jnp.where(self.last_row, pltpu.roll(moved, plan.lanes - plan.ny, 1), moved)
        return jnp.where(self.floor_cell, 0.0, moved)

    def above(self, f, top):
        plan = self.plan
        moved = pltpu.roll(f, 1, 0)
        if plan.chunks > 1:
            moved = jnp.where(self.first_row, pltpu.roll(moved, plan.ny, 1), moved)
        return jnp.where(self.top, top, moved)

    def seafloor(self, vz):
        row = self.over_chunks(jnp.where(self.top, vz, 0.0)[0:1])
        return jnp.broadcast_to(row, vz.shape)

    def over_chunks(self, f):
        shift = self.plan.ny
        while shift < self.plan.lanes:
            f = f + pltpu.roll(f, shift, 1)
            shift *= 2
        return f


def acceleration(sh, stress, j):
    sxy, sxz = stress[SXY, j], stress[SXZ, j]
    syz, szz = stress[SYZ, j], stress[SZZ, j]
    ax = stress[SXX, j + 1] - stress[SXX, j - 1] + sh.dy(sxy) + sh.below(sxz) - sh.above(sxz, 0.0)
    ay = stress[SXY, j + 1] - stress[SXY, j - 1] + sh.dy(stress[SYY, j])
    ay = ay + sh.below(syz) - sh.above(syz, 0.0)
    az = stress[SXZ, j + 1] - stress[SXZ, j - 1] + sh.dy(syz) + sh.below(szz) - sh.above(szz, 0.0)
    return ax, ay, az


def strained(sh, vel, stress, mats, j):
    vx, vy, vz = vel[VX, j], vel[VY, j], vel[VZ, j]
    exx = vel[VX, j + 1] - vel[VX, j - 1]
    eyy = sh.dy(vy)
    ezz = sh.below(vz) - sh.above(vz, vz)
    mu = mats[SHEAR, j]
    mu2 = mu + mu
    common = mats[LAMB, j] * (exx + eyy + ezz)
    exy = sh.dy(vx) + vel[VY, j + 1] - vel[VY, j - 1]
    exz = sh.below(vx) - sh.above(vx, vx) + vel[VZ, j + 1] - vel[VZ, j - 1]
    eyz = sh.below(vy) - sh.above(vy, vy) + sh.dy(vz)
    return (
        stress[SXX, j] + (common + mu2 * exx),
        stress[SYY, j] + (common + mu2 * eyy),
        stress[SZZ, j] + (common + mu2 * ezz),
        stress[SXY, j] + mu * exy,
        stress[SXZ, j] + (mu * exz + mats[FAULT, j]),
        stress[SYZ, j] + mu * eyz,
    )


def bring(plan, sh, table, state, ref, count, x, column, first):
    vel, stress, mats = state
    for f in range(3):
        vel[f, column] = ref[f * count + x]
    for f in range(6):
        stress[f, column] = ref[(3 + f) * count + x]
    zone = ref[9 * count + x]
    values = [jnp.zeros_like(zone) for _ in range(3)]
    for z in range(ZONES):
        here = zone == float(z + 1)
        values = [jnp.where(here, table[c, z], values[c]) for c in range(3)]
    for c in range(3):
        mats[c, column] = values[c] * HALF
    slip = ref[ref.shape[0] - 1, pl.ds(first + x, 1), :]
    slip = jnp.broadcast_to(slip, zone.shape)
    mats[FAULT, column] = jnp.where(sh.row == (plan.depth // 2) % plan.sub, DT * slip, 0.0)
    mats[FLOOR, column] = sh.seafloor(ref[VZ * count + x])


def begin_kernel(plan, table, own, mate, vel, stress, mats):
    cells = plan.cells
    sh = Shifts(plan)
    odd = odd_device()
    state = (vel, stress, mats)
    starts = (HALO + cells * odd, HALO + cells * (1 - odd))
    for start, ref in zip(starts, (own, mate)):
        plan.planes(
            0,
            cells,
            lambda x, start=start, ref=ref: bring(
                plan, sh, table, state, ref, cells, x, start + x, 0
            ),
        )

    def move(j):
        b = mats[BUOY, j]
        for f, a in enumerate(acceleration(sh, stress, j)):
            vel[f, j] = vel[f, j] + b * a

    plan.planes(HALO + 1, HALO + 2 * cells - 1, move)


class Updates:
    def __init__(self, plan, sh, vel, stress, mats, oc, water, bottom, loads):
        self.plan, self.sh = plan, sh
        self.vel, self.stress, self.mats = vel, stress, mats
        self.oc, self.water, self.bottom, self.loads = oc, water, bottom, loads

    def flow_x(self, j):
        oc = self.oc
        oc[1, j + 1] = self.water[j + 1] * (oc[1, j + 1] - HALF * (oc[0, j + 2] - oc[0, j]))

    def flow(self, j):
        oc, sh = self.oc, self.sh
        p = oc[0, j + 1]
        wet = self.water[j + 1]
        oc[2, j + 1] = wet * (oc[2, j + 1] - HALF * sh.dy(p))
        rise = sh.below(p) + self.bottom[j + 1] * p - sh.above(p, -p)
        oc[3, j + 1] = wet * (oc[3, j + 1] - (HALF * rise + (DT * GRAV) * p))

    def press(self, j, start):
        oc, sh = self.oc, self.sh
        w = oc[3, j + 1]
        floor = self.mats[FLOOR, j] if start else sh.seafloor(self.vel[VZ, j])
        rise = sh.below(w) + self.bottom[j + 1] * floor - sh.above(w, w)
        total = oc[1, j + 2] - oc[1, j] + sh.dy(oc[2, j + 1]) + rise
        oc[0, j + 1] = self.water[j + 1] * (oc[0, j + 1] - (HALF * KBULK) * total)

    def load(self, j):
        sh, plan = self.sh, self.plan
        column = jnp.sum(self.bottom[j + 1] * self.oc[0, j + 1], axis=0, keepdims=True)
        column = jnp.broadcast_to(sh.over_chunks(column), (plan.sub, plan.lanes))
        return jnp.where(sh.top, column, 0.0)

    def keep(self, j):
        self.loads[j] = self.load(j)

    def add_load(self, j):
        self.vel[VZ, j] = self.vel[VZ, j] + self.mats[BUOY, j] * self.load(j)

    def move(self, j):
        vel = self.vel
        ax, ay, az = acceleration(self.sh, self.stress, j)
        b = self.mats[BUOY, j]
        vel[VX, j] = vel[VX, j] + b * ax
        vel[VY, j] = vel[VY, j] + b * ay
        vel[VZ, j] = vel[VZ, j] + b * (az + self.load(j))

    def strain(self, j):
        for f, value in enumerate(strained(self.sh, self.vel, self.stress, self.mats, j)):
            self.stress[f, j] = value

    def run(self, spans, moved):
        planes = self.plan.planes
        for t in range(STEPS):
            planes(*spans(t, 0), self.flow_x)
            planes(*spans(t, 1), self.flow)
            planes(*spans(t, 1), lambda j, t=t: self.press(j, t == 0))
            if t == STEPS - 1:
                planes(*spans(t, 1), self.keep)
            elif t == 0 and moved:
                planes(*spans(t, 1), self.add_load)
            else:
                planes(*spans(t, 1), self.move)
            if t < STEPS - 2:
                planes(*spans(t, 2), self.strain)


def inner_kernel(
    plan, arrived, swapped, mats, vel_in, stress_in, vel, stress, oc, water, bottom, loads,
    gather, depths,
):
    sub, chunks, n, strips = plan.sub, plan.chunks, plan.n, plan.strips
    cells, sent = plan.cells, plan.sent_groups
    sh = Shifts(plan)
    odd = odd_device()
    half = n // 2
    columns = 2 * cells + 2 * HALO

    def turn(owner, group):
        for core, ref in ((odd, arrived), (1 - odd, swapped)):
            for kc in range(chunks):
                for yl in range(strips):
                    at = owner * plan.rows + (kc * strips + yl) * sent + group
                    to = kc * plan.ny + core * strips + yl
                    gather[pl.ds(to, half, stride=2 * strips), :] = ref[
                        pl.ds(at, half, stride=2 * plan.rows), :
                    ]
        return gather[...].T

    deeps = []
    for owner in range(2):
        for group in range(sent):
            turned = turn(owner, group)
            for i in range(chunks):
                for f in range(4):
                    at = (i * 4 + f) * sub
                    column = 1 + owner * (cells + HALO) + group * chunks + i
                    oc[f, column] = turned[at : at + sub]
            if owner == 0 and group == 0:
                oc[0, 0] = turned[2 * sub : 3 * sub]
                deeps.append(turned[3 * sub : 4 * sub])
            if owner == 1 and group == sent - 1:
                oc[0, columns + 1] = turned[LANES - 2 * sub : LANES - sub]
                deeps.append(turned[LANES - sub :])
    for i, deep in enumerate(deeps):
        for kc in range(chunks):
            mine = (sh.lane >= kc * plan.ny) & (sh.lane < (kc + 1) * plan.ny)
            depths[i, kc * sub : (kc + 1) * sub, :] = sh.over_chunks(jnp.where(mine, deep, 0.0))

    def mask(owner, j):
        low = jnp.broadcast_to(depths[owner, pl.ds(j - owner * cells, 1), :], (sub, plan.lanes))
        wet = jnp.where(sh.depth < low, 1.0, 0.0).astype(F32)
        water[j] = wet
        bottom[j] = jnp.where(sh.depth == low - 1.0, 1.0, 0.0).astype(F32)
        oc[0, j] = oc[0, j] * wet

    def mask_x(j):
        oc[1, j] = oc[1, j] * water[j]

    def mask_yw(j):
        oc[2, j] = oc[2, j] * water[j]
        oc[3, j] = oc[3, j] * water[j]

    plan.planes(0, plan.width + 2, lambda j: mask(0, j))
    plan.planes(plan.width + 2, columns + 2, lambda j: mask(1, j))
    plan.planes(1, columns + 1, mask_x)
    plan.planes(2, columns, mask_yw)

    def bring_in(j):
        for f in range(3):
            vel[f, j] = vel_in[f, j]
        for f in range(6):
            stress[f, j] = stress_in[f, j]

    if not plan.unrolled:
        plan.planes(HALO, HALO + 2 * cells, bring_in)
    updates = Updates(plan, sh, vel, stress, mats, oc, water, bottom, loads)
    updates.run(lambda t, inset: (HALO + 2 * t + inset, HALO + 2 * cells - 2 * t - inset), True)


def outer_kernel(
    plan, table, border, water, bottom, vel_in, stress_in, mats_in, oc_in, loads_in,
    vel, stress, mats, oc, loads, message, gather,
):
    sub, chunks, n, strips, cells = plan.sub, plan.chunks, plan.n, plan.strips, plan.cells
    near = cells - 1
    sh = Shifts(plan)
    odd = odd_device()
    if not plan.unrolled:
        for here, there in (
            (vel, vel_in), (stress, stress_in), (mats, mats_in), (oc, oc_in), (loads, loads_in)
        ):
            here[...] = there[...]
    updates = Updates(plan, sh, vel, stress, mats, oc, water, bottom, loads)

    def side(core):
        low, far = ((1, 0), (HALO + 2 * cells, 2 * HALO + 2 * cells - 1))[core]
        state = (vel, stress, mats)
        plan.planes(
            0,
            near,
            lambda x: bring(plan, sh, table, state, border, near, x, low + x, 1 - core),
        )
        for i, f in enumerate((SXX, SXY, SXZ)):
            stress[f, far] = border[10 * near + i]

        def spans(t, inset):
            if core == 0:
                return 2 * t + inset, 2 * t + inset + HALO
            last = 2 * HALO + 2 * cells - 2 * t - inset
            return last - HALO, last

        updates.run(spans, False)
        for group in range(plan.own_groups):
            stacked = jnp.concatenate(
                [
                    oc[f, 1 + HALO + core * cells + group * chunks + i]
                    for i in range(chunks)
                    for f in range(4)
                ],
                axis=0,
            )
            gather[...] = stacked.T
            for kc in range(chunks):
                for yl in range(strips):
                    at = group * plan.lead + kc * strips + yl
                    message[pl.ds(at, n, stride=plan.back_rows), :] = gather[
                        pl.ds(kc * plan.ny + yl, n, stride=strips), :
                    ]

    for core in range(2):
        pl.when(odd == core)(functools.partial(side, core))


def end_kernel(plan, vel_all, stress_all, mats_all, loads_all, vel_out, stress_out, vel, stress):
    cells, sub, chunks, ny = plan.cells, plan.sub, plan.chunks, plan.ny
    sh = Shifts(plan)
    first, last = 2 * (STEPS - 1), plan.width - 2 * (STEPS - 1)
    window = pl.ds(cells * odd_device(), plan.width)
    vel_in, stress_in = vel_all.at[:, window], stress_all.at[:, window]
    mats, loads = mats_all.at[:, window], loads_all.at[window]

    def put(out, f, x, plane):
        for kc in range(chunks):
            out[f, x, kc * sub : (kc + 1) * sub, :] = plane[:, kc * ny : (kc + 1) * ny]

    def strain(j):
        for f, value in enumerate(strained(sh, vel_in, stress_in, mats, j)):
            stress[f, j] = value

    def move(j):
        ax, ay, az = acceleration(sh, stress, j)
        b = mats[BUOY, j]
        for f, a in enumerate((ax, ay, az + loads[j])):
            vel[f, j] = vel_in[f, j] + b * a

    def finish(x):
        for f in range(3):
            put(vel_out, f, x, vel[f, x + HALO])
        for f, value in enumerate(strained(sh, vel, stress, mats, x + HALO)):
            put(stress_out, f, x, value)

    plan.planes(first, last, strain)
    plan.planes(first + 1, last - 1, move)
    plan.planes(0, cells, finish)


def unpack_kernel(plan, arrived, ocean, turned):
    sub, chunks = plan.sub, plan.chunks
    block = 4 * sub
    for yl in range(plan.strips):
        by_chunk = [
            arrived[pl.ds(kc * plan.strips + yl, plan.nx // chunks, stride=plan.lead), :]
            for kc in range(chunks)
        ]
        for i in range(chunks):
            turned[pl.ds(i, plan.nx // chunks, stride=chunks), :] = place(
                by_chunk, [i] * chunks, block
            )
        whole = turned[...].T
        for kc in range(chunks):
            for f in range(4):
                at = (kc * 4 + f) * sub
                ocean[f, yl, kc * sub : (kc + 1) * sub, :] = whole[at : at + sub]


def on_device(plan, velocity, stress, ocean, zones, materials, slip, bathy):
    n, cells, sub, lanes, width = plan.n, plan.cells, plan.sub, plan.lanes, plan.width
    vmem = pl.BlockSpec(memory_space=pltpu.VMEM)
    smem = pl.BlockSpec(memory_space=pltpu.SMEM)
    hbm = pl.BlockSpec(memory_space=pltpu.HBM)

    def shape(*dims):
        return jax.ShapeDtypeStruct(dims, F32)

    def like(array):
        return jax.ShapeDtypeStruct(array.shape, array.dtype)

    def held(array):
        return pltpu.VMEM(array.shape, array.dtype)

    def call(kernel, name, out, ins, scratch, room=16, **rest):
        room = room if plan.unrolled else 56
        return pl.pallas_call(
            functools.partial(kernel, plan),
            out_shape=out,
            in_specs=ins,
            out_specs=jax.tree.map(lambda _: vmem, out),
            scratch_shapes=scratch,
            compiler_params=pltpu.CompilerParams(vmem_limit_bytes=room * 1024 * 1024),
            name=name,
            **rest,
        )

    def pinned(array):
        return pltpu.with_memory_space_constraint(array, pltpu.HBM)

    def near(array):
        return pltpu.with_memory_space_constraint(array, pltpu.VMEM) if plan.unrolled else array

    mates = [(i, i ^ 1) for i in range(n)]
    others = [(i, i + 1) for i in range(1, n - 1, 2)]
    others += [(target, source) for source, target in others]
    crust, border, message = call(
        pack_kernel,
        "pack",
        (
            shape(10 * cells + 1, sub, lanes),
            shape(10 * cells - 6, sub, lanes),
            shape(n * plan.rows, LANES),
        ),
        [hbm] * 6,
        [held(a) for a in (velocity, stress, zones, slip, ocean, bathy)]
        + [
            pltpu.VMEM((plan.strips, plan.nx, LANES), F32),
            pltpu.VMEM(
                (plan.lead, plan.nx // plan.chunks + 2 * plan.halo_groups, LANES), F32
            ),
            pltpu.VMEM((n * plan.strips, LANES), F32),
            pltpu.VMEM((n * plan.rows, LANES), F32),
            pltpu.SemaphoreType.DMA((6,)),
        ],
    )(*(pinned(a) for a in (velocity, stress, zones, slip, ocean, bathy)))
    arrived = lax.all_to_all(
        message.reshape(n // 2, 2 * plan.rows, LANES),
        "map",
        split_axis=0,
        concat_axis=0,
        axis_index_groups=[list(range(core, n, 2)) for core in range(2)],
        tiled=True,
    ).reshape(n * plan.rows, LANES)
    other = lax.ppermute(border, "map", others)
    mate = lax.ppermute(crust, "map", mates)
    columns = 2 * cells + 2 * HALO
    vel, strs, mats = call(
        begin_kernel,
        "first_velocity",
        (shape(3, columns, sub, lanes), shape(6, columns, sub, lanes), shape(5, columns, sub, lanes)),
        [smem] + [vmem] * 2,
        [],
    )(materials, crust, mate)
    arrived, vel = lax.optimization_barrier((arrived, vel))
    swapped = lax.ppermute(arrived, "map", mates)
    planes_of = {
        "vel": shape(3, columns, sub, lanes),
        "stress": shape(6, columns, sub, lanes),
        "mats": shape(5, columns, sub, lanes),
        "oc": shape(4, columns + 2, sub, lanes),
        "mask": shape(columns + 2, sub, lanes),
        "loads": shape(columns, sub, lanes),
    }
    vel, strs, oc, water, bottom, loads = call(
        inner_kernel,
        "inner_substeps",
        tuple(planes_of[k] for k in ("vel", "stress", "oc", "mask", "mask", "loads")),
        [vmem] * 5,
        [
            pltpu.VMEM((lanes, LANES), F32),
            pltpu.VMEM((2, plan.depth, lanes), F32),
        ],
        input_output_aliases={3: 0, 4: 1},
    )(*(near(a) for a in (arrived, swapped, mats, vel, strs)))
    vel, strs, mats, oc, loads, back = call(
        outer_kernel,
        "outer_substeps",
        tuple(planes_of[k] for k in ("vel", "stress", "mats", "oc", "loads"))
        + (shape(n * plan.back_rows, LANES),),
        [smem] + [vmem] * 8,
        [pltpu.VMEM((lanes, LANES), F32)],
        input_output_aliases={4: 0, 5: 1, 6: 2, 7: 3, 8: 4},
    )(materials, *(near(a) for a in (other, water, bottom, vel, strs, mats, oc, loads)))
    returned = lax.all_to_all(
        back.reshape(n, plan.back_rows, LANES), "map", split_axis=0, concat_axis=0, tiled=True
    ).reshape(n * plan.back_rows, LANES)
    new_velocity, new_stress = call(
        end_kernel,
        "last_updates",
        (shape(*velocity.shape), shape(*stress.shape)),
        [vmem] * 4,
        [
            pltpu.VMEM((3, width, sub, lanes), F32),
            pltpu.VMEM((6, width, sub, lanes), F32),
        ],
    )(vel, strs, mats, loads)
    new_ocean = call(
        unpack_kernel,
        "ocean_strips",
        shape(*ocean.shape),
        [vmem],
        [pltpu.VMEM((plan.nx, LANES), F32)],
    )(returned)
    return new_velocity, new_stress, new_ocean


def solution(mesh):
    n = mesh.shape["map"]

    def body(velocity, stress, ocean, zones, materials, slip, bathy):
        _, cells, depth, ny = velocity.shape
        plan = Plan(n, cells, depth, ny, ocean.shape[1])
        return on_device(plan, velocity, stress, ocean, zones, materials, slip, bathy)

    return jax.shard_map(
        body,
        mesh=mesh,
        in_specs=(
            P("parts", "map", None, None),
            P("parts", "map", None, None),
            P("parts", "map", None, None),
            P("map", "parts", None),
            P(),
            P("map", "parts"),
            P("map", "parts"),
        ),
        out_specs=(
            P("parts", "map", None, None),
            P("parts", "map", None, None),
            P("parts", "map", None, None),
        ),
        check_vma=False,
    )
```

```python
import functools

import jax
import jax.numpy as jnp
from jax import lax
from jax.experimental import pallas as pl
from jax.experimental.pallas import tpu as pltpu
from jax.sharding import PartitionSpec as P

STEPS = 4
ZONES = 8
DT = 0.25
HALF = 0.5 * DT
KBULK = 2.25
GRAV = 0.1
HALO = 2 * STEPS
LANES = 128
F32 = jnp.float32
VX, VY, VZ = range(3)
SXX, SYY, SZZ, SXY, SXZ, SYZ = range(6)
BUOY, LAMB, SHEAR, FAULT, FLOOR = range(5)


class Plan:
    def __init__(self, devices, cells, depth, ny, strips):
        self.n = devices
        self.cells = cells
        self.depth = depth
        self.ny = ny
        self.strips = strips
        self.chunks = max(1, LANES // ny)
        self.sub = depth // self.chunks
        self.lanes = self.chunks * ny
        self.width = cells + 2 * HALO
        self.own_groups = cells // self.chunks
        self.halo_groups = HALO // self.chunks
        self.sent_groups = self.own_groups + self.halo_groups
        self.lead = self.chunks * strips
        self.rows = self.lead * self.sent_groups
        self.back_rows = self.lead * self.own_groups
        self.nx = devices * cells
        self.block = 4 * self.sub
        self.unrolled = self.sub * self.lanes <= 1024
        assert devices % 2 == 0 and cells == HALO and self.block * self.chunks == LANES

    def planes(self, start, stop, body, batch=1):
        if self.unrolled:
            for j in range(start, stop, batch):
                body(j, min(batch, stop - j))
        else:
            def run(j, carry):
                body(j, 1)
                return carry

            lax.fori_loop(start, stop, run, 0)


BATCH = 8


def odd_device():
    return lax.rem(lax.axis_index("map"), 2)


def place(pieces, wanted, block):
    out = None
    for i, piece in enumerate(pieces):
        shift = (i - wanted[i]) * block % piece.shape[-1]
        moved = pltpu.roll(piece, shift, piece.ndim - 1) if shift else piece
        if out is None:
            out = moved
        else:
            lane = lax.broadcasted_iota(jnp.int32, moved.shape, moved.ndim - 1)
            out = jnp.where(lane >= i * block, moved, out)
    return out


def pack_kernel(
    plan, vel_ref, stress_ref, zones_ref, slip_ref, ocean_ref, bathy_ref, crust, border, message_out,
    vel, stress, zones, slip, ocean, bathy, turned, grouped, extra, message, sems,
):
    cells, sub, chunks, ny = plan.cells, plan.sub, plan.chunks, plan.ny
    n, strips, block, sent, rows = plan.n, plan.strips, plan.block, plan.sent_groups, plan.rows
    pairs = (
        (ocean_ref, ocean),
        (bathy_ref, bathy),
        (vel_ref, vel),
        (stress_ref, stress),
        (zones_ref, zones),
        (slip_ref, slip),
    )
    copies = [
        pltpu.make_async_copy(source, target, sems.at[i])
        for i, (source, target) in enumerate(pairs)
    ]
    for copy in copies:
        copy.start()
    copies[0].wait()
    copies[1].wait()
    outside = jnp.zeros((plan.lead, plan.halo_groups, LANES), F32)
    count = plan.nx // chunks
    grouped[:, : plan.halo_groups, :] = outside
    grouped[:, plan.halo_groups + count :, :] = outside
    for yl in range(strips):
        stacked = jnp.concatenate(
            [ocean[f, yl, kc * sub : (kc + 1) * sub, :] for kc in range(chunks) for f in range(4)],
            axis=0,
        )
        turned[yl] = stacked.T
        by_x = [turned[yl, pl.ds(i, count, stride=chunks), :] for i in range(chunks)]
        for kc in range(chunks):
            grouped[kc * strips + yl, pl.ds(plan.halo_groups, count), :] = place(
                by_x, [kc] * chunks, block
            )
    for d in range(n):
        start = d * plan.own_groups + (d % 2) * plan.halo_groups
        for q in range(plan.lead):
            message[d * rows + q * sent : d * rows + (q + 1) * sent, :] = grouped[
                q, start : start + sent, :
            ]
    depths = bathy[...].astype(F32)
    wide = lax.broadcasted_iota(jnp.int32, depths.shape, 1)
    for d in range(n):
        first = d * cells - HALO - 1
        moved = pltpu.roll(depths, -first % plan.nx, 1)
        moved = jnp.where((wide + first >= 0) & (wide + first < plan.nx), moved, 0.0)
        extra[d * strips : (d + 1) * strips, :] = moved[:, :LANES]
    pairs = n // 2
    lane = lax.broadcasted_iota(jnp.int32, (pairs, LANES), 1)
    blank = jnp.zeros((1, LANES), F32)
    for odd in range(2):
        slot = (odd * (chunks - 1) * 4 + 2) * sub
        group = odd * (sent - 1)
        for yl in range(strips):
            if odd:
                column = turned[yl, pl.ds(2 * cells + HALO, pairs - 1, stride=2 * cells), :]
                column = jnp.concatenate([column, blank], axis=0)
            else:
                column = turned[yl, pl.ds(2 * cells - HALO - 1, pairs - 1, stride=2 * cells), :]
                column = jnp.concatenate([blank, column], axis=0)
            deep = extra[pl.ds(odd * strips + yl, pairs, stride=2 * strips), :]
            for kc in range(chunks):
                at = odd * rows + (kc * strips + yl) * sent + group
                old = message[pl.ds(at, pairs, stride=2 * rows), :]
                edge = pltpu.roll(column, (slot - kc * block) % LANES, 1)
                floor = pltpu.roll(deep, (slot + sub - kc * sub) % LANES, 1)
                new = jnp.where((lane >= slot) & (lane < slot + sub), edge, old)
                new = jnp.where((lane >= slot + sub) & (lane < slot + 2 * sub), floor, new)
                message[pl.ds(at, pairs, stride=2 * rows), :] = new
    message_out[...] = message[...]

    def joined(ref, *at):
        parts = [ref[(*at, pl.ds(kc * sub, sub), slice(None))] for kc in range(chunks)]
        return jnp.concatenate(parts, axis=-1) if chunks > 1 else parts[0]

    copies[2].wait()
    for f in range(3):
        for x in range(cells):
            crust[f * cells + x] = joined(vel, f, x)
    copies[3].wait()
    for f in range(6):
        for x in range(cells):
            crust[(3 + f) * cells + x] = joined(stress, f, x)
    copies[4].wait()
    for x in range(cells):
        crust[9 * cells + x] = (joined(zones, x) + 1).astype(F32)
    copies[5].wait()
    fault_chunk = (plan.depth // 2) // sub
    pieces = [
        slip[...] if kc == fault_chunk else jnp.zeros((cells, ny), F32) for kc in range(chunks)
    ]
    fault = jnp.concatenate(pieces, axis=-1) if chunks > 1 else pieces[0]
    if sub > cells:
        fault = jnp.concatenate([fault, jnp.zeros((sub - cells, plan.lanes), F32)], axis=0)
    crust[10 * cells] = fault
    odd = odd_device()
    near = cells - 1
    for f in range(10):
        for i in range(near):
            border[f * near + i] = crust[f * cells + i + odd]
    for i, f in enumerate((SXX, SXY, SXZ)):
        border[10 * near + i] = crust[(3 + f) * cells + near * (1 - odd)]
    border[10 * near + 3] = fault


class Shifts:
    def __init__(self, plan):
        self.plan = plan
        shape = (plan.sub, plan.lanes)
        self.row = lax.broadcasted_iota(jnp.int32, shape, 0)
        self.lane = lax.broadcasted_iota(jnp.int32, shape, 1)
        self.y = lax.rem(self.lane, plan.ny)
        self.first_row = self.row == 0
        self.last_row = self.row == plan.sub - 1
        self.top = self.first_row & (self.lane < plan.ny)
        self.floor_cell = self.last_row & (self.lane >= plan.lanes - plan.ny)
        self.not_low_y = jnp.where(self.y == 0, 0.0, 1.0).astype(F32)
        self.not_high_y = jnp.where(self.y == plan.ny - 1, 0.0, 1.0).astype(F32)
        self.depth = (
            lax.div(self.lane, plan.ny) * plan.sub + self.row
        ).astype(F32)

    def by_lane(self, f, shift):
        return pltpu.roll(f, shift % self.plan.lanes, f.ndim - 1)

    def by_row(self, f, shift):
        return pltpu.roll(f, shift % self.plan.sub, f.ndim - 2)

    def dy(self, f):
        return self.by_lane(f, -1) * self.not_high_y - self.by_lane(f, 1) * self.not_low_y

    def below(self, f):
        plan = self.plan
        moved = self.by_row(f, -1)
        if plan.chunks > 1:
            moved = jnp.where(self.last_row, self.by_lane(moved, -plan.ny), moved)
        return jnp.where(self.floor_cell, 0.0, moved)

    def above(self, f, top):
        plan = self.plan
        moved = self.by_row(f, 1)
        if plan.chunks > 1:
            moved = jnp.where(self.first_row, self.by_lane(moved, plan.ny), moved)
        return jnp.where(self.top, top, moved)

    def seafloor(self, vz):
        row = self.over_chunks(jnp.where(self.top, vz, 0.0))
        return jnp.broadcast_to(row[..., 0:1, :], vz.shape)

    def on_top(self, f):
        shift = self.plan.sub // 2
        while shift:
            f = f + self.by_row(f, shift)
            shift //= 2
        return jnp.where(self.top, self.over_chunks(f), 0.0)

    def over_chunks(self, f):
        shift = self.plan.ny
        while shift < self.plan.lanes:
            f = f + self.by_lane(f, shift)
            shift *= 2
        return f


def acceleration(sh, stress, j, count):
    at, before, after = (pl.ds(j + k, count) for k in (0, -1, 1))
    sxy, sxz = stress[SXY, at], stress[SXZ, at]
    ax = stress[SXX, after] - stress[SXX, before] + sh.dy(sxy) + sh.below(sxz) - sh.above(sxz, 0.0)
    syz = stress[SYZ, at]
    ay = stress[SXY, after] - stress[SXY, before] + sh.dy(stress[SYY, at])
    ay = ay + sh.below(syz) - sh.above(syz, 0.0)
    szz = stress[SZZ, at]
    az = stress[SXZ, after] - stress[SXZ, before] + sh.dy(syz) + sh.below(szz) - sh.above(szz, 0.0)
    return ax, ay, az


def strained(sh, vel, stress, mats, j, count):
    at, before, after = (pl.ds(j + k, count) for k in (0, -1, 1))
    vx, vy, vz = vel[VX, at], vel[VY, at], vel[VZ, at]
    exx = vel[VX, after] - vel[VX, before]
    eyy = sh.dy(vy)
    ezz = sh.below(vz) - sh.above(vz, vz)
    mu = mats[SHEAR, at]
    mu2 = mu + mu
    common = mats[LAMB, at] * (exx + eyy + ezz)
    yield SXX, stress[SXX, at] + (common + mu2 * exx)
    yield SYY, stress[SYY, at] + (common + mu2 * eyy)
    yield SZZ, stress[SZZ, at] + (common + mu2 * ezz)
    exy = sh.dy(vx) + vel[VY, after] - vel[VY, before]
    yield SXY, stress[SXY, at] + mu * exy
    exz = sh.below(vx) - sh.above(vx, vx) + vel[VZ, after] - vel[VZ, before]
    yield SXZ, stress[SXZ, at] + (mu * exz + mats[FAULT, at])
    eyz = sh.below(vy) - sh.above(vy, vy) + sh.dy(vz)
    yield SYZ, stress[SYZ, at] + mu * eyz


def bring(plan, sh, table, state, ref, fields, x, count, column, first):
    vel, stress, mats = state
    to = pl.ds(column, count)

    def read(f):
        return ref[pl.ds(f * fields + x, count)]

    for f in range(3):
        vel[f, to] = read(f)
    for f in range(6):
        stress[f, to] = read(3 + f)
    zone = read(9)
    values = [jnp.zeros_like(zone) for _ in range(3)]
    for z in range(ZONES):
        here = zone == float(z + 1)
        values = [jnp.where(here, table[c, z], values[c]) for c in range(3)]
    for c in range(3):
        mats[c, to] = values[c] * HALF
    mats[FLOOR, to] = sh.seafloor(read(VZ))
    for i in range(count):
        slip = ref[ref.shape[0] - 1, pl.ds(first + x + i, 1), :]
        slip = jnp.broadcast_to(slip, (plan.sub, plan.lanes))
        mats[FAULT, column + i] = jnp.where(
            sh.row == (plan.depth // 2) % plan.sub, DT * slip, 0.0
        )


def begin_kernel(plan, table, own, mate, vel, stress, mats):
    cells = plan.cells
    sh = Shifts(plan)
    odd = odd_device()
    state = (vel, stress, mats)
    starts = (HALO + cells * odd, HALO + cells * (1 - odd))
    for start, ref in zip(starts, (own, mate)):
        plan.planes(
            0,
            cells,
            lambda x, count, start=start, ref=ref: bring(
                plan, sh, table, state, ref, cells, x, count, start + x, 0
            ),
            BATCH,
        )

    def move(j, count):
        at = pl.ds(j, count)
        b = mats[BUOY, at]
        for f, a in enumerate(acceleration(sh, stress, j, count)):
            vel[f, at] = vel[f, at] + b * a

    plan.planes(HALO + 1, HALO + 2 * cells - 1, move, BATCH)


class Updates:
    def __init__(self, plan, sh, vel, stress, mats, oc, water, bottom, loads):
        self.plan, self.sh = plan, sh
        self.vel, self.stress, self.mats = vel, stress, mats
        self.oc, self.water, self.bottom, self.loads = oc, water, bottom, loads

    def flow_x(self, j, count):
        oc = self.oc
        before, at, after = (pl.ds(j + k, count) for k in range(3))
        oc[1, at] = self.water[at] * (oc[1, at] - HALF * (oc[0, after] - oc[0, before]))

    def flow(self, j, count):
        oc, sh = self.oc, self.sh
        at = pl.ds(j + 1, count)
        p = oc[0, at]
        wet = self.water[at]
        rise = sh.below(p) + self.bottom[at] * p - sh.above(p, -p)
        oc[3, at] = wet * (oc[3, at] - (HALF * rise + (DT * GRAV) * p))
        oc[2, at] = wet * (oc[2, at] - HALF * sh.dy(p))

    def press(self, j, count, start):
        oc, sh = self.oc, self.sh
        before, at, after = (pl.ds(j + k, count) for k in range(3))
        crust = pl.ds(j, count)
        w = oc[3, at]
        floor = self.mats[FLOOR, crust] if start else sh.seafloor(self.vel[VZ, crust])
        rise = sh.below(w) + self.bottom[at] * floor - sh.above(w, w)
        total = oc[1, after] - oc[1, before] + sh.dy(oc[2, at]) + rise
        oc[0, at] = self.water[at] * (oc[0, at] - (HALF * KBULK) * total)

    def load(self, j, count):
        at = pl.ds(j + 1, count)
        return self.sh.on_top(self.bottom[at] * self.oc[0, at])

    def keep(self, j, count):
        self.loads[pl.ds(j, count)] = self.load(j, count)

    def add_load(self, j, count):
        at = pl.ds(j, count)
        self.vel[VZ, at] = self.vel[VZ, at] + self.mats[BUOY, at] * self.load(j, count)

    def move(self, j, count):
        vel = self.vel
        at = pl.ds(j, count)
        ax, ay, az = acceleration(self.sh, self.stress, j, count)
        b = self.mats[BUOY, at]
        vel[VX, at] = vel[VX, at] + b * ax
        vel[VY, at] = vel[VY, at] + b * ay
        vel[VZ, at] = vel[VZ, at] + b * (az + self.load(j, count))

    def strain(self, j, count):
        for f, value in strained(self.sh, self.vel, self.stress, self.mats, j, count):
            self.stress[f, pl.ds(j, count)] = value

    def run(self, spans, moved):
        for t in range(STEPS):
            def planes(inset, update, t=t):
                self.plan.planes(*spans(t, inset), update, BATCH)

            planes(0, self.flow_x)
            planes(1, self.flow)
            planes(1, functools.partial(self.press, start=t == 0))
            if t == STEPS - 1:
                planes(1, self.keep)
            elif t == 0 and moved:
                planes(1, self.add_load)
            else:
                planes(1, self.move)
            if t < STEPS - 2:
                planes(2, self.strain)


def inner_kernel(
    plan, arrived, swapped, mats, vel_in, stress_in, vel, stress, oc, water, bottom, loads,
    gather, depths,
):
    sub, chunks, n, strips = plan.sub, plan.chunks, plan.n, plan.strips
    cells, sent = plan.cells, plan.sent_groups
    sh = Shifts(plan)
    odd = odd_device()
    half = n // 2
    columns = 2 * cells + 2 * HALO

    def turn(owner, group):
        for core, ref in ((odd, arrived), (1 - odd, swapped)):
            for kc in range(chunks):
                for yl in range(strips):
                    at = owner * plan.rows + (kc * strips + yl) * sent + group
                    to = kc * plan.ny + core * strips + yl
                    gather[pl.ds(to, half, stride=2 * strips), :] = ref[
                        pl.ds(at, half, stride=2 * plan.rows), :
                    ]
        return gather[...].T

    deeps = []
    for owner in range(2):
        for group in range(sent):
            turned = turn(owner, group)
            for i in range(chunks):
                for f in range(4):
                    at = (i * 4 + f) * sub
                    column = 1 + owner * (cells + HALO) + group * chunks + i
                    oc[f, column] = turned[at : at + sub]
            if owner == 0 and group == 0:
                oc[0, 0] = turned[2 * sub : 3 * sub]
                deeps.append(turned[3 * sub : 4 * sub])
            if owner == 1 and group == sent - 1:
                oc[0, columns + 1] = turned[LANES - 2 * sub : LANES - sub]
                deeps.append(turned[LANES - sub :])
    for i, deep in enumerate(deeps):
        for kc in range(chunks):
            mine = (sh.lane >= kc * plan.ny) & (sh.lane < (kc + 1) * plan.ny)
            depths[i, kc * sub : (kc + 1) * sub, :] = sh.over_chunks(jnp.where(mine, deep, 0.0))

    def mask(owner, j, _):
        low = jnp.broadcast_to(depths[owner, pl.ds(j - owner * cells, 1), :], (sub, plan.lanes))
        wet = jnp.where(sh.depth < low, 1.0, 0.0).astype(F32)
        water[j] = wet
        bottom[j] = jnp.where(sh.depth == low - 1.0, 1.0, 0.0).astype(F32)
        oc[0, j] = oc[0, j] * wet

    def mask_x(j, _):
        oc[1, j] = oc[1, j] * water[j]

    def mask_yw(j, _):
        oc[2, j] = oc[2, j] * water[j]
        oc[3, j] = oc[3, j] * water[j]

    plan.planes(0, plan.width + 2, lambda j, _: mask(0, j, _))
    plan.planes(plan.width + 2, columns + 2, lambda j, _: mask(1, j, _))
    plan.planes(1, columns + 1, mask_x)
    plan.planes(2, columns, mask_yw)

    def bring_in(j, _):
        for f in range(3):
            vel[f, j] = vel_in[f, j]
        for f in range(6):
            stress[f, j] = stress_in[f, j]

    if not plan.unrolled:
        plan.planes(HALO, HALO + 2 * cells, bring_in)
    updates = Updates(plan, sh, vel, stress, mats, oc, water, bottom, loads)
    updates.run(lambda t, inset: (HALO + 2 * t + inset, HALO + 2 * cells - 2 * t - inset), True)


def outer_kernel(
    plan, table, border, water, bottom, vel_in, stress_in, mats_in, oc_in, loads_in,
    vel, stress, mats, oc, loads, message, gather,
):
    sub, chunks, n, strips, cells = plan.sub, plan.chunks, plan.n, plan.strips, plan.cells
    near = cells - 1
    sh = Shifts(plan)
    odd = odd_device()
    if not plan.unrolled:
        for here, there in (
            (vel, vel_in), (stress, stress_in), (mats, mats_in), (oc, oc_in), (loads, loads_in)
        ):
            here[...] = there[...]
    updates = Updates(plan, sh, vel, stress, mats, oc, water, bottom, loads)

    def side(core):
        low, far = ((1, 0), (HALO + 2 * cells, 2 * HALO + 2 * cells - 1))[core]
        state = (vel, stress, mats)
        plan.planes(
            0,
            near,
            lambda x, count: bring(
                plan, sh, table, state, border, near, x, count, low + x, 1 - core
            ),
            BATCH,
        )
        for i, f in enumerate((SXX, SXY, SXZ)):
            stress[f, far] = border[10 * near + i]

        def spans(t, inset):
            if core == 0:
                return 2 * t + inset, 2 * t + inset + HALO
            last = 2 * HALO + 2 * cells - 2 * t - inset
            return last - HALO, last

        updates.run(spans, False)
        for group in range(plan.own_groups):
            stacked = jnp.concatenate(
                [
                    oc[f, 1 + HALO + core * cells + group * chunks + i]
                    for i in range(chunks)
                    for f in range(4)
                ],
                axis=0,
            )
            gather[...] = stacked.T
            for kc in range(chunks):
                for yl in range(strips):
                    at = group * plan.lead + kc * strips + yl
                    message[pl.ds(at, n, stride=plan.back_rows), :] = gather[
                        pl.ds(kc * plan.ny + yl, n, stride=strips), :
                    ]

    for core in range(2):
        pl.when(odd == core)(functools.partial(side, core))


def end_kernel(plan, vel_all, stress_all, mats_all, loads_all, vel_out, stress_out, vel, stress):
    cells, sub, chunks, ny = plan.cells, plan.sub, plan.chunks, plan.ny
    sh = Shifts(plan)
    first, last = 2 * (STEPS - 1), plan.width - 2 * (STEPS - 1)
    window = pl.ds(cells * odd_device(), plan.width)
    vel_in, stress_in = vel_all.at[:, window], stress_all.at[:, window]
    mats, loads = mats_all.at[:, window], loads_all.at[window]

    def put(out, f, x, count, planes):
        for kc in range(chunks):
            out[f, pl.ds(x, count), kc * sub : (kc + 1) * sub, :] = planes[
                :, :, kc * ny : (kc + 1) * ny
            ]

    def strain(j, count):
        for f, value in strained(sh, vel_in, stress_in, mats, j, count):
            stress[f, pl.ds(j, count)] = value

    def move(j, count):
        at = pl.ds(j, count)
        ax, ay, az = acceleration(sh, stress, j, count)
        b = mats[BUOY, at]
        for f, a in enumerate((ax, ay, az + loads[at])):
            vel[f, at] = vel_in[f, at] + b * a

    def finish(x, count):
        for f in range(3):
            put(vel_out, f, x, count, vel[f, pl.ds(x + HALO, count)])
        for f, value in strained(sh, vel, stress, mats, x + HALO, count):
            put(stress_out, f, x, count, value)

    plan.planes(first, last, strain, BATCH)
    plan.planes(first + 1, last - 1, move, BATCH)
    plan.planes(0, cells, finish, BATCH)


def unpack_kernel(plan, arrived, ocean, turned):
    sub, chunks = plan.sub, plan.chunks
    block = 4 * sub
    for yl in range(plan.strips):
        by_chunk = [
            arrived[pl.ds(kc * plan.strips + yl, plan.nx // chunks, stride=plan.lead), :]
            for kc in range(chunks)
        ]
        for i in range(chunks):
            turned[pl.ds(i, plan.nx // chunks, stride=chunks), :] = place(
                by_chunk, [i] * chunks, block
            )
        whole = turned[...].T
        for kc in range(chunks):
            for f in range(4):
                at = (kc * 4 + f) * sub
                ocean[f, yl, kc * sub : (kc + 1) * sub, :] = whole[at : at + sub]


def on_device(plan, velocity, stress, ocean, zones, materials, slip, bathy):
    n, cells, sub, lanes, width = plan.n, plan.cells, plan.sub, plan.lanes, plan.width
    vmem = pl.BlockSpec(memory_space=pltpu.VMEM)
    smem = pl.BlockSpec(memory_space=pltpu.SMEM)
    hbm = pl.BlockSpec(memory_space=pltpu.HBM)

    def shape(*dims):
        return jax.ShapeDtypeStruct(dims, F32)

    def like(array):
        return jax.ShapeDtypeStruct(array.shape, array.dtype)

    def held(array):
        return pltpu.VMEM(array.shape, array.dtype)

    def call(kernel, name, out, ins, scratch, room=16, **rest):
        room = room if plan.unrolled else 56
        return pl.pallas_call(
            functools.partial(kernel, plan),
            out_shape=out,
            in_specs=ins,
            out_specs=jax.tree.map(lambda _: vmem, out),
            scratch_shapes=scratch,
            compiler_params=pltpu.CompilerParams(vmem_limit_bytes=room * 1024 * 1024),
            name=name,
            **rest,
        )

    def pinned(array):
        return pltpu.with_memory_space_constraint(array, pltpu.HBM)

    def near(array):
        return pltpu.with_memory_space_constraint(array, pltpu.VMEM) if plan.unrolled else array

    mates = [(i, i ^ 1) for i in range(n)]
    others = [(i, i + 1) for i in range(1, n - 1, 2)]
    others += [(target, source) for source, target in others]
    crust, border, message = call(
        pack_kernel,
        "pack",
        (
            shape(10 * cells + 1, sub, lanes),
            shape(10 * cells - 6, sub, lanes),
            shape(n * plan.rows, LANES),
        ),
        [hbm] * 6,
        [held(a) for a in (velocity, stress, zones, slip, ocean, bathy)]
        + [
            pltpu.VMEM((plan.strips, plan.nx, LANES), F32),
            pltpu.VMEM(
                (plan.lead, plan.nx // plan.chunks + 2 * plan.halo_groups, LANES), F32
            ),
            pltpu.VMEM((n * plan.strips, LANES), F32),
            pltpu.VMEM((n * plan.rows, LANES), F32),
            pltpu.SemaphoreType.DMA((6,)),
        ],
    )(*(pinned(a) for a in (velocity, stress, zones, slip, ocean, bathy)))
    arrived = lax.all_to_all(
        message.reshape(n // 2, 2 * plan.rows, LANES),
        "map",
        split_axis=0,
        concat_axis=0,
        axis_index_groups=[list(range(core, n, 2)) for core in range(2)],
        tiled=True,
    ).reshape(n * plan.rows, LANES)
    other = lax.ppermute(border, "map", others)
    mate = lax.ppermute(crust, "map", mates)
    columns = 2 * cells + 2 * HALO
    vel, strs, mats = call(
        begin_kernel,
        "first_velocity",
        (shape(3, columns, sub, lanes), shape(6, columns, sub, lanes), shape(5, columns, sub, lanes)),
        [smem] + [vmem] * 2,
        [],
    )(materials, crust, mate)
    arrived, vel = lax.optimization_barrier((arrived, vel))
    swapped = lax.ppermute(arrived, "map", mates)
    planes_of = {
        "vel": shape(3, columns, sub, lanes),
        "stress": shape(6, columns, sub, lanes),
        "mats": shape(5, columns, sub, lanes),
        "oc": shape(4, columns + 2, sub, lanes),
        "mask": shape(columns + 2, sub, lanes),
        "loads": shape(columns, sub, lanes),
    }
    vel, strs, oc, water, bottom, loads = call(
        inner_kernel,
        "inner_substeps",
        tuple(planes_of[k] for k in ("vel", "stress", "oc", "mask", "mask", "loads")),
        [vmem] * 5,
        [
            pltpu.VMEM((lanes, LANES), F32),
            pltpu.VMEM((2, plan.depth, lanes), F32),
        ],
        input_output_aliases={3: 0, 4: 1},
    )(*(near(a) for a in (arrived, swapped, mats, vel, strs)))
    vel, strs, mats, oc, loads, back = call(
        outer_kernel,
        "outer_substeps",
        tuple(planes_of[k] for k in ("vel", "stress", "mats", "oc", "loads"))
        + (shape(n * plan.back_rows, LANES),),
        [smem] + [vmem] * 8,
        [pltpu.VMEM((lanes, LANES), F32)],
        input_output_aliases={4: 0, 5: 1, 6: 2, 7: 3, 8: 4},
    )(materials, *(near(a) for a in (other, water, bottom, vel, strs, mats, oc, loads)))
    returned = lax.all_to_all(
        back.reshape(n, plan.back_rows, LANES), "map", split_axis=0, concat_axis=0, tiled=True
    ).reshape(n * plan.back_rows, LANES)
    new_velocity, new_stress = call(
        end_kernel,
        "last_updates",
        (shape(*velocity.shape), shape(*stress.shape)),
        [vmem] * 4,
        [
            pltpu.VMEM((3, width, sub, lanes), F32),
            pltpu.VMEM((6, width, sub, lanes), F32),
        ],
    )(vel, strs, mats, loads)
    new_ocean = call(
        unpack_kernel,
        "ocean_strips",
        shape(*ocean.shape),
        [vmem],
        [pltpu.VMEM((plan.nx, LANES), F32)],
    )(returned)
    return new_velocity, new_stress, new_ocean


def solution(mesh):
    n = mesh.shape["map"]

    def body(velocity, stress, ocean, zones, materials, slip, bathy):
        _, cells, depth, ny = velocity.shape
        plan = Plan(n, cells, depth, ny, ocean.shape[1])
        return on_device(plan, velocity, stress, ocean, zones, materials, slip, bathy)

    return jax.shard_map(
        body,
        mesh=mesh,
        in_specs=(
            P("parts", "map", None, None),
            P("parts", "map", None, None),
            P("parts", "map", None, None),
            P("map", "parts", None),
            P(),
            P("map", "parts"),
            P("map", "parts"),
        ),
        out_specs=(
            P("parts", "map", None, None),
            P("parts", "map", None, None),
            P("parts", "map", None, None),
        ),
        check_vma=False,
    )
```

```python
import functools

import jax
import jax.numpy as jnp
from jax import lax
from jax.experimental import pallas as pl
from jax.experimental.pallas import tpu as pltpu
from jax.sharding import PartitionSpec as P

STEPS = 4
ZONES = 8
DT = 0.25
HALF = 0.5 * DT
KBULK = 2.25
GRAV = 0.1
HALO = 2 * STEPS
LANES = 128
F32 = jnp.float32
VX, VY, VZ = range(3)
SXX, SYY, SZZ, SXY, SXZ, SYZ = range(6)
BUOY, LAMB, SHEAR, FAULT, FLOOR = range(5)


class Plan:
    def __init__(self, devices, cells, depth, ny, strips):
        self.n = devices
        self.cells = cells
        self.depth = depth
        self.ny = ny
        self.strips = strips
        self.chunks = max(1, LANES // ny)
        self.sub = depth // self.chunks
        self.lanes = self.chunks * ny
        self.width = cells + 2 * HALO
        self.own_groups = cells // self.chunks
        self.halo_groups = HALO // self.chunks
        self.sent_groups = self.own_groups + self.halo_groups
        self.lead = self.chunks * strips
        self.rows = self.lead * self.sent_groups
        self.back_rows = self.lead * self.own_groups
        self.nx = devices * cells
        self.block = 4 * self.sub
        self.unrolled = self.sub * self.lanes <= 1024
        assert devices % 2 == 0 and cells == HALO and self.block * self.chunks == LANES

    def planes(self, start, stop, body, batch=1):
        if self.unrolled:
            for j in range(start, stop, batch):
                body(j, min(batch, stop - j))
        else:
            def run(j, carry):
                body(j, 1)
                return carry

            lax.fori_loop(start, stop, run, 0)


BATCH = 8


def odd_device():
    return lax.rem(lax.axis_index("map"), 2)


def place(pieces, wanted, block):
    out = None
    for i, piece in enumerate(pieces):
        shift = (i - wanted[i]) * block % piece.shape[-1]
        moved = pltpu.roll(piece, shift, piece.ndim - 1) if shift else piece
        if out is None:
            out = moved
        else:
            lane = lax.broadcasted_iota(jnp.int32, moved.shape, moved.ndim - 1)
            out = jnp.where(lane >= i * block, moved, out)
    return out


def ocean_kernel(
    plan, vel_ref, stress_ref, zones_ref, slip_ref, ocean_ref, bathy_ref,
    message_out, vel, stress, zones, slip, ocean, bathy, turned, grouped, extra, message, sems,
):
    cells, sub, chunks = plan.cells, plan.sub, plan.chunks
    n, strips, block, sent, rows = plan.n, plan.strips, plan.block, plan.sent_groups, plan.rows
    pairs = (
        (ocean_ref, ocean),
        (bathy_ref, bathy),
        (vel_ref, vel),
        (stress_ref, stress),
        (zones_ref, zones),
        (slip_ref, slip),
    )
    copies = [
        pltpu.make_async_copy(source, target, sems.at[i])
        for i, (source, target) in enumerate(pairs)
    ]
    for copy in copies:
        copy.start()
    copies[0].wait()
    copies[1].wait()
    outside = jnp.zeros((plan.lead, plan.halo_groups, LANES), F32)
    count = plan.nx // chunks
    grouped[:, : plan.halo_groups, :] = outside
    grouped[:, plan.halo_groups + count :, :] = outside
    for yl in range(strips):
        stacked = jnp.concatenate(
            [ocean[f, yl, kc * sub : (kc + 1) * sub, :] for kc in range(chunks) for f in range(4)],
            axis=0,
        )
        turned[yl] = stacked.T
        by_x = [turned[yl, pl.ds(i, count, stride=chunks), :] for i in range(chunks)]
        for kc in range(chunks):
            grouped[kc * strips + yl, pl.ds(plan.halo_groups, count), :] = place(
                by_x, [kc] * chunks, block
            )
    for d in range(n):
        start = d * plan.own_groups + (d % 2) * plan.halo_groups
        for q in range(plan.lead):
            message[d * rows + q * sent : d * rows + (q + 1) * sent, :] = grouped[
                q, start : start + sent, :
            ]
    depths = bathy[...].astype(F32)
    wide = lax.broadcasted_iota(jnp.int32, depths.shape, 1)
    for d in range(n):
        first = d * cells - HALO - 1
        moved = pltpu.roll(depths, -first % plan.nx, 1)
        moved = jnp.where((wide + first >= 0) & (wide + first < plan.nx), moved, 0.0)
        extra[d * strips : (d + 1) * strips, :] = moved[:, :LANES]
    pairs = n // 2
    lane = lax.broadcasted_iota(jnp.int32, (pairs, LANES), 1)
    blank = jnp.zeros((1, LANES), F32)
    for odd in range(2):
        slot = (odd * (chunks - 1) * 4 + 2) * sub
        group = odd * (sent - 1)
        for yl in range(strips):
            if odd:
                column = turned[yl, pl.ds(2 * cells + HALO, pairs - 1, stride=2 * cells), :]
                column = jnp.concatenate([column, blank], axis=0)
            else:
                column = turned[yl, pl.ds(2 * cells - HALO - 1, pairs - 1, stride=2 * cells), :]
                column = jnp.concatenate([blank, column], axis=0)
            deep = extra[pl.ds(odd * strips + yl, pairs, stride=2 * strips), :]
            for kc in range(chunks):
                at = odd * rows + (kc * strips + yl) * sent + group
                old = message[pl.ds(at, pairs, stride=2 * rows), :]
                edge = pltpu.roll(column, (slot - kc * block) % LANES, 1)
                floor = pltpu.roll(deep, (slot + sub - kc * sub) % LANES, 1)
                new = jnp.where((lane >= slot) & (lane < slot + sub), edge, old)
                new = jnp.where((lane >= slot + sub) & (lane < slot + 2 * sub), floor, new)
                message[pl.ds(at, pairs, stride=2 * rows), :] = new
    message_out[...] = message[...]
    for copy in copies[2:]:
        copy.wait()


def crust_kernel(plan, vel, stress, zones, slip, crust, border):
    cells, sub, chunks, ny = plan.cells, plan.sub, plan.chunks, plan.ny

    def joined(ref, *at):
        parts = [ref[(*at, pl.ds(kc * sub, sub), slice(None))] for kc in range(chunks)]
        return jnp.concatenate(parts, axis=-1) if chunks > 1 else parts[0]

    for f in range(3):
        for x in range(cells):
            crust[f * cells + x] = joined(vel, f, x)
    for f in range(6):
        for x in range(cells):
            crust[(3 + f) * cells + x] = joined(stress, f, x)
    for x in range(cells):
        crust[9 * cells + x] = (joined(zones, x) + 1).astype(F32)
    fault_chunk = (plan.depth // 2) // sub
    pieces = [
        slip[...] if kc == fault_chunk else jnp.zeros((cells, ny), F32) for kc in range(chunks)
    ]
    fault = jnp.concatenate(pieces, axis=-1) if chunks > 1 else pieces[0]
    if sub > cells:
        fault = jnp.concatenate([fault, jnp.zeros((sub - cells, plan.lanes), F32)], axis=0)
    crust[10 * cells] = fault
    odd = odd_device()
    near = cells - 1
    for f in range(10):
        for i in range(near):
            border[f * near + i] = crust[f * cells + i + odd]
    for i, f in enumerate((SXX, SXY, SXZ)):
        border[10 * near + i] = crust[(3 + f) * cells + near * (1 - odd)]
    border[10 * near + 3] = fault


class Shifts:
    def __init__(self, plan):
        self.plan = plan
        shape = (plan.sub, plan.lanes)
        self.row = lax.broadcasted_iota(jnp.int32, shape, 0)
        self.lane = lax.broadcasted_iota(jnp.int32, shape, 1)
        self.y = lax.rem(self.lane, plan.ny)
        self.first_row = self.row == 0
        self.last_row = self.row == plan.sub - 1
        self.top = self.first_row & (self.lane < plan.ny)
        self.floor_cell = self.last_row & (self.lane >= plan.lanes - plan.ny)
        self.not_low_y = jnp.where(self.y == 0, 0.0, 1.0).astype(F32)
        self.not_high_y = jnp.where(self.y == plan.ny - 1, 0.0, 1.0).astype(F32)
        self.depth = (
            lax.div(self.lane, plan.ny) * plan.sub + self.row
        ).astype(F32)

    def by_lane(self, f, shift):
        return pltpu.roll(f, shift % self.plan.lanes, f.ndim - 1)

    def by_row(self, f, shift):
        return pltpu.roll(f, shift % self.plan.sub, f.ndim - 2)

    def dy(self, f):
        return self.by_lane(f, -1) * self.not_high_y - self.by_lane(f, 1) * self.not_low_y

    def below(self, f):
        plan = self.plan
        moved = self.by_row(f, -1)
        if plan.chunks > 1:
            moved = jnp.where(self.last_row, self.by_lane(moved, -plan.ny), moved)
        return jnp.where(self.floor_cell, 0.0, moved)

    def above(self, f, top):
        plan = self.plan
        moved = self.by_row(f, 1)
        if plan.chunks > 1:
            moved = jnp.where(self.first_row, self.by_lane(moved, plan.ny), moved)
        return jnp.where(self.top, top, moved)

    def seafloor(self, vz):
        row = self.over_chunks(jnp.where(self.top, vz, 0.0))
        return jnp.broadcast_to(row[..., 0:1, :], vz.shape)

    def on_top(self, f):
        shift = self.plan.sub // 2
        while shift:
            f = f + self.by_row(f, shift)
            shift //= 2
        return jnp.where(self.top, self.over_chunks(f), 0.0)

    def over_chunks(self, f):
        shift = self.plan.ny
        while shift < self.plan.lanes:
            f = f + self.by_lane(f, shift)
            shift *= 2
        return f


def acceleration(sh, stress, j, count):
    at, before, after = (pl.ds(j + k, count) for k in (0, -1, 1))
    sxy, sxz = stress[SXY, at], stress[SXZ, at]
    ax = stress[SXX, after] - stress[SXX, before] + sh.dy(sxy) + sh.below(sxz) - sh.above(sxz, 0.0)
    syz = stress[SYZ, at]
    ay = stress[SXY, after] - stress[SXY, before] + sh.dy(stress[SYY, at])
    ay = ay + sh.below(syz) - sh.above(syz, 0.0)
    szz = stress[SZZ, at]
    az = stress[SXZ, after] - stress[SXZ, before] + sh.dy(syz) + sh.below(szz) - sh.above(szz, 0.0)
    return ax, ay, az


def strained(sh, vel, stress, mats, j, count):
    at, before, after = (pl.ds(j + k, count) for k in (0, -1, 1))
    vx, vy, vz = vel[VX, at], vel[VY, at], vel[VZ, at]
    exx = vel[VX, after] - vel[VX, before]
    eyy = sh.dy(vy)
    ezz = sh.below(vz) - sh.above(vz, vz)
    mu = mats[SHEAR, at]
    mu2 = mu + mu
    common = mats[LAMB, at] * (exx + eyy + ezz)
    yield SXX, stress[SXX, at] + (common + mu2 * exx)
    yield SYY, stress[SYY, at] + (common + mu2 * eyy)
    yield SZZ, stress[SZZ, at] + (common + mu2 * ezz)
    exy = sh.dy(vx) + vel[VY, after] - vel[VY, before]
    yield SXY, stress[SXY, at] + mu * exy
    exz = sh.below(vx) - sh.above(vx, vx) + vel[VZ, after] - vel[VZ, before]
    yield SXZ, stress[SXZ, at] + (mu * exz + mats[FAULT, at])
    eyz = sh.below(vy) - sh.above(vy, vy) + sh.dy(vz)
    yield SYZ, stress[SYZ, at] + mu * eyz


def bring(plan, sh, material, state, ref, fields, x, count, column, first):
    vel, stress, mats = state
    to = pl.ds(column, count)

    def read(f):
        return ref[pl.ds(f * fields + x, count)]

    for f in range(3):
        vel[f, to] = read(f)
    for f in range(6):
        stress[f, to] = read(3 + f)
    zone = read(9)
    values = [jnp.zeros_like(zone) for _ in range(3)]
    for z in range(ZONES):
        here = zone == float(z + 1)
        values = [jnp.where(here, material(c, z), values[c]) for c in range(3)]
    for c in range(3):
        mats[c, to] = values[c] * HALF
    mats[FLOOR, to] = sh.seafloor(read(VZ))
    for i in range(count):
        slip = ref[ref.shape[0] - 1, pl.ds(first + x + i, 1), :]
        slip = jnp.broadcast_to(slip, (plan.sub, plan.lanes))
        mats[FAULT, column + i] = jnp.where(
            sh.row == (plan.depth // 2) % plan.sub, DT * slip, 0.0
        )


def begin_kernel(plan, table, own, mate, vel, stress, mats, rows):
    cells = plan.cells
    sh = Shifts(plan)
    odd = odd_device()
    state = (vel, stress, mats)
    starts = (HALO + cells * odd, HALO + cells * (1 - odd))
    for start, ref in zip(starts, (own, mate)):
        plan.planes(
            0,
            cells,
            lambda x, count, start=start, ref=ref: bring(
                plan, sh, lambda c, z: table[c, z], state, ref, cells, x, count, start + x, 0
            ),
            BATCH,
        )

    def move(j, count):
        at = pl.ds(j, count)
        b = mats[BUOY, at]
        for f, a in enumerate(acceleration(sh, stress, j, count)):
            vel[f, at] = vel[f, at] + b * a

    plan.planes(HALO + 1, HALO + 2 * cells - 1, move, BATCH)
    for c in range(3):
        for z in range(ZONES):
            at = c * ZONES + z
            rows[at : at + 1, :] = jnp.full((1, plan.lanes), table[c, z], F32)


class Updates:
    def __init__(self, plan, sh, vel, stress, mats, oc, water, bottom, loads):
        self.plan, self.sh = plan, sh
        self.vel, self.stress, self.mats = vel, stress, mats
        self.oc, self.water, self.bottom, self.loads = oc, water, bottom, loads

    def flow_x(self, j, count):
        oc = self.oc
        before, at, after = (pl.ds(j + k, count) for k in range(3))
        oc[1, at] = self.water[at] * (oc[1, at] - HALF * (oc[0, after] - oc[0, before]))

    def flow(self, j, count):
        oc, sh = self.oc, self.sh
        at = pl.ds(j + 1, count)
        p = oc[0, at]
        wet = self.water[at]
        rise = sh.below(p) + self.bottom[at] * p - sh.above(p, -p)
        oc[3, at] = wet * (oc[3, at] - (HALF * rise + (DT * GRAV) * p))
        oc[2, at] = wet * (oc[2, at] - HALF * sh.dy(p))

    def press(self, j, count, start):
        oc, sh = self.oc, self.sh
        before, at, after = (pl.ds(j + k, count) for k in range(3))
        crust = pl.ds(j, count)
        w = oc[3, at]
        floor = self.mats[FLOOR, crust] if start else sh.seafloor(self.vel[VZ, crust])
        rise = sh.below(w) + self.bottom[at] * floor - sh.above(w, w)
        total = oc[1, after] - oc[1, before] + sh.dy(oc[2, at]) + rise
        oc[0, at] = self.water[at] * (oc[0, at] - (HALF * KBULK) * total)

    def load(self, j, count):
        at = pl.ds(j + 1, count)
        return self.sh.on_top(self.bottom[at] * self.oc[0, at])

    def keep(self, j, count):
        self.loads[pl.ds(j, count)] = self.load(j, count)

    def add_load(self, j, count):
        at = pl.ds(j, count)
        self.vel[VZ, at] = self.vel[VZ, at] + self.mats[BUOY, at] * self.load(j, count)

    def move(self, j, count):
        vel = self.vel
        at = pl.ds(j, count)
        ax, ay, az = acceleration(self.sh, self.stress, j, count)
        b = self.mats[BUOY, at]
        vel[VX, at] = vel[VX, at] + b * ax
        vel[VY, at] = vel[VY, at] + b * ay
        vel[VZ, at] = vel[VZ, at] + b * (az + self.load(j, count))

    def strain(self, j, count):
        for f, value in strained(self.sh, self.vel, self.stress, self.mats, j, count):
            self.stress[f, pl.ds(j, count)] = value

    def run(self, spans, moved, send=None):
        for t in range(STEPS):
            def planes(inset, update, t=t):
                self.plan.planes(*spans(t, inset), update, BATCH)

            planes(0, self.flow_x)
            planes(1, self.flow)
            planes(1, functools.partial(self.press, start=t == 0))
            if t == STEPS - 1:
                if send is not None:
                    send()
                planes(1, self.keep)
            elif t == 0 and moved:
                planes(1, self.add_load)
            else:
                planes(1, self.move)
            if t < STEPS - 2:
                planes(2, self.strain)


def inner_kernel(
    plan, arrived, swapped, mats, vel_in, stress_in, vel, stress, oc, water, bottom, loads,
    gather, depths,
):
    sub, chunks, n, strips = plan.sub, plan.chunks, plan.n, plan.strips
    cells, sent = plan.cells, plan.sent_groups
    sh = Shifts(plan)
    odd = odd_device()
    half = n // 2
    columns = 2 * cells + 2 * HALO

    def turn(owner, group):
        for core, ref in ((odd, arrived), (1 - odd, swapped)):
            for kc in range(chunks):
                for yl in range(strips):
                    at = owner * plan.rows + (kc * strips + yl) * sent + group
                    to = kc * plan.ny + core * strips + yl
                    gather[pl.ds(to, half, stride=2 * strips), :] = ref[
                        pl.ds(at, half, stride=2 * plan.rows), :
                    ]
        return gather[...].T

    deeps = []
    for owner in range(2):
        for group in range(sent):
            turned = turn(owner, group)
            for i in range(chunks):
                for f in range(4):
                    at = (i * 4 + f) * sub
                    column = 1 + owner * (cells + HALO) + group * chunks + i
                    oc[f, column] = turned[at : at + sub]
            if owner == 0 and group == 0:
                oc[0, 0] = turned[2 * sub : 3 * sub]
                deeps.append(turned[3 * sub : 4 * sub])
            if owner == 1 and group == sent - 1:
                oc[0, columns + 1] = turned[LANES - 2 * sub : LANES - sub]
                deeps.append(turned[LANES - sub :])
    for i, deep in enumerate(deeps):
        for kc in range(chunks):
            mine = (sh.lane >= kc * plan.ny) & (sh.lane < (kc + 1) * plan.ny)
            depths[i, kc * sub : (kc + 1) * sub, :] = sh.over_chunks(jnp.where(mine, deep, 0.0))

    def mask(owner, j, _):
        low = jnp.broadcast_to(depths[owner, pl.ds(j - owner * cells, 1), :], (sub, plan.lanes))
        wet = jnp.where(sh.depth < low, 1.0, 0.0).astype(F32)
        water[j] = wet
        bottom[j] = jnp.where(sh.depth == low - 1.0, 1.0, 0.0).astype(F32)
        oc[0, j] = oc[0, j] * wet

    def mask_x(j, _):
        oc[1, j] = oc[1, j] * water[j]

    def mask_yw(j, _):
        oc[2, j] = oc[2, j] * water[j]
        oc[3, j] = oc[3, j] * water[j]

    plan.planes(0, plan.width + 2, lambda j, _: mask(0, j, _))
    plan.planes(plan.width + 2, columns + 2, lambda j, _: mask(1, j, _))
    plan.planes(1, columns + 1, mask_x)
    plan.planes(2, columns, mask_yw)

    def bring_in(j, _):
        for f in range(3):
            vel[f, j] = vel_in[f, j]
        for f in range(6):
            stress[f, j] = stress_in[f, j]

    if not plan.unrolled:
        plan.planes(HALO, HALO + 2 * cells, bring_in)
    updates = Updates(plan, sh, vel, stress, mats, oc, water, bottom, loads)
    updates.run(lambda t, inset: (HALO + 2 * t + inset, HALO + 2 * cells - 2 * t - inset), True)


def outer_kernel(
    plan, materials, border, water, bottom, vel_in, stress_in, mats_in, oc_in, loads_in,
    vel, stress, mats, oc, loads, message, gather, rows, sem,
):
    sub, chunks, n, strips, cells = plan.sub, plan.chunks, plan.n, plan.strips, plan.cells
    near = cells - 1
    sh = Shifts(plan)
    odd = odd_device()
    if not plan.unrolled:
        for here, there in (
            (vel, vel_in), (stress, stress_in), (mats, mats_in), (oc, oc_in), (loads, loads_in)
        ):
            here[...] = there[...]
    updates = Updates(plan, sh, vel, stress, mats, oc, water, bottom, loads)

    def material(c, z):
        row = materials[pl.ds(c * ZONES + z, 1), :]
        return jnp.broadcast_to(row, (sub, plan.lanes))

    def side(core):
        low, far = ((1, 0), (HALO + 2 * cells, 2 * HALO + 2 * cells - 1))[core]
        state = (vel, stress, mats)
        plan.planes(
            0,
            near,
            lambda x, count: bring(
                plan, sh, material, state, border, near, x, count, low + x, 1 - core
            ),
            BATCH,
        )
        for i, f in enumerate((SXX, SXY, SXZ)):
            stress[f, far] = border[10 * near + i]

        def spans(t, inset):
            if core == 0:
                return 2 * t + inset, 2 * t + inset + HALO
            last = 2 * HALO + 2 * cells - 2 * t - inset
            return last - HALO, last

        copy = pltpu.make_async_copy(rows, message, sem)

        def send():
            for group in range(plan.own_groups):
                stacked = jnp.concatenate(
                    [
                        oc[f, 1 + HALO + core * cells + group * chunks + i]
                        for i in range(chunks)
                        for f in range(4)
                    ],
                    axis=0,
                )
                gather[group] = stacked.T
                for kc in range(chunks):
                    for yl in range(strips):
                        at = group * plan.lead + kc * strips + yl
                        rows[pl.ds(at, n, stride=plan.back_rows), :] = gather[
                            group, pl.ds(kc * plan.ny + yl, n, stride=strips), :
                        ]
            copy.start()

        updates.run(spans, False, send)
        copy.wait()

    for core in range(2):
        pl.when(odd == core)(functools.partial(side, core))


def end_kernel(plan, vel_all, stress_all, mats_all, loads_all, vel_out, stress_out, vel, stress):
    cells, sub, chunks, ny = plan.cells, plan.sub, plan.chunks, plan.ny
    sh = Shifts(plan)
    first, last = 2 * (STEPS - 1), plan.width - 2 * (STEPS - 1)
    window = pl.ds(cells * odd_device(), plan.width)
    vel_in, stress_in = vel_all.at[:, window], stress_all.at[:, window]
    mats, loads = mats_all.at[:, window], loads_all.at[window]

    def put(out, f, x, count, planes):
        for kc in range(chunks):
            out[f, pl.ds(x, count), kc * sub : (kc + 1) * sub, :] = planes[
                :, :, kc * ny : (kc + 1) * ny
            ]

    def strain(j, count):
        for f, value in strained(sh, vel_in, stress_in, mats, j, count):
            stress[f, pl.ds(j, count)] = value

    def move(j, count):
        at = pl.ds(j, count)
        ax, ay, az = acceleration(sh, stress, j, count)
        b = mats[BUOY, at]
        for f, a in enumerate((ax, ay, az + loads[at])):
            vel[f, at] = vel_in[f, at] + b * a

    def finish(x, count):
        for f in range(3):
            put(vel_out, f, x, count, vel[f, pl.ds(x + HALO, count)])
        for f, value in strained(sh, vel, stress, mats, x + HALO, count):
            put(stress_out, f, x, count, value)

    plan.planes(first, last, strain, BATCH)
    plan.planes(first + 1, last - 1, move, BATCH)
    plan.planes(0, cells, finish, BATCH)


def unpack_kernel(plan, arrived, ocean, turned, strips, sems):
    sub, chunks = plan.sub, plan.chunks
    block = 4 * sub
    copies = [
        pltpu.make_async_copy(strips.at[yl], ocean.at[:, yl], sems.at[yl])
        for yl in range(plan.strips)
    ]
    for yl in range(plan.strips):
        by_chunk = [
            arrived[pl.ds(kc * plan.strips + yl, plan.nx // chunks, stride=plan.lead), :]
            for kc in range(chunks)
        ]
        for i in range(chunks):
            turned[yl, pl.ds(i, plan.nx // chunks, stride=chunks), :] = place(
                by_chunk, [i] * chunks, block
            )
        whole = turned[yl].T
        for kc in range(chunks):
            for f in range(4):
                at = (kc * 4 + f) * sub
                strips[yl, f, kc * sub : (kc + 1) * sub, :] = whole[at : at + sub]
        copies[yl].start()
    for copy in copies:
        copy.wait()


def on_device(plan, velocity, stress, ocean, zones, materials, slip, bathy):
    n, cells, sub, lanes, width = plan.n, plan.cells, plan.sub, plan.lanes, plan.width
    vmem = pl.BlockSpec(memory_space=pltpu.VMEM)
    smem = pl.BlockSpec(memory_space=pltpu.SMEM)
    hbm = pl.BlockSpec(memory_space=pltpu.HBM)

    def shape(*dims):
        return jax.ShapeDtypeStruct(dims, F32)

    def like(array):
        return jax.ShapeDtypeStruct(array.shape, array.dtype)

    def held(array):
        return pltpu.VMEM(array.shape, array.dtype)

    def call(kernel, name, out, ins, scratch, room=16, outs=None, **rest):
        room = room if plan.unrolled else 56
        return pl.pallas_call(
            functools.partial(kernel, plan),
            out_shape=out,
            in_specs=ins,
            out_specs=jax.tree.map(lambda _: vmem, out) if outs is None else outs,
            scratch_shapes=scratch,
            compiler_params=pltpu.CompilerParams(vmem_limit_bytes=room * 1024 * 1024),
            name=name,
            **rest,
        )

    def pinned(array):
        return pltpu.with_memory_space_constraint(array, pltpu.HBM)

    def near(array):
        return pltpu.with_memory_space_constraint(array, pltpu.VMEM) if plan.unrolled else array

    mates = [(i, i ^ 1) for i in range(n)]
    others = [(i, i + 1) for i in range(1, n - 1, 2)]
    others += [(target, source) for source, target in others]
    crust_args = (velocity, stress, zones, slip)
    message, *near_args = call(
        ocean_kernel,
        "ocean_rows",
        (shape(n * plan.rows, LANES), *(like(a) for a in crust_args)),
        [hbm] * 6,
        [
            held(ocean),
            held(bathy),
            pltpu.VMEM((plan.strips, plan.nx, LANES), F32),
            pltpu.VMEM(
                (plan.lead, plan.nx // plan.chunks + 2 * plan.halo_groups, LANES), F32
            ),
            pltpu.VMEM((n * plan.strips, LANES), F32),
            pltpu.VMEM((n * plan.rows, LANES), F32),
            pltpu.SemaphoreType.DMA((6,)),
        ],
    )(*(pinned(a) for a in (*crust_args, ocean, bathy)))
    arrived = lax.all_to_all(
        message.reshape(n // 2, 2 * plan.rows, LANES),
        "map",
        split_axis=0,
        concat_axis=0,
        axis_index_groups=[list(range(core, n, 2)) for core in range(2)],
        tiled=True,
    ).reshape(n * plan.rows, LANES)
    crust, border = call(
        crust_kernel,
        "crust_planes",
        (shape(10 * cells + 1, sub, lanes), shape(10 * cells - 6, sub, lanes)),
        [vmem] * 4,
        [],
    )(*near_args)
    other = lax.ppermute(border, "map", others)
    mate = lax.ppermute(crust, "map", mates)
    columns = 2 * cells + 2 * HALO
    vel, strs, mats, material_rows = call(
        begin_kernel,
        "first_velocity",
        (
            shape(3, columns, sub, lanes),
            shape(6, columns, sub, lanes),
            shape(5, columns, sub, lanes),
            shape(3 * ZONES, lanes),
        ),
        [smem] + [vmem] * 2,
        [],
    )(materials, crust, mate)
    arrived, vel = lax.optimization_barrier((arrived, vel))
    swapped = lax.ppermute(arrived, "map", mates)
    planes_of = {
        "vel": shape(3, columns, sub, lanes),
        "stress": shape(6, columns, sub, lanes),
        "mats": shape(5, columns, sub, lanes),
        "oc": shape(4, columns + 2, sub, lanes),
        "mask": shape(columns + 2, sub, lanes),
        "loads": shape(columns, sub, lanes),
    }
    vel, strs, oc, water, bottom, loads = call(
        inner_kernel,
        "inner_substeps",
        tuple(planes_of[k] for k in ("vel", "stress", "oc", "mask", "mask", "loads")),
        [vmem] * 5,
        [
            pltpu.VMEM((lanes, LANES), F32),
            pltpu.VMEM((2, plan.depth, lanes), F32),
        ],
        input_output_aliases={3: 0, 4: 1},
    )(*(near(a) for a in (arrived, swapped, mats, vel, strs)))
    vel, strs, mats, oc, loads, back = call(
        outer_kernel,
        "outer_substeps",
        tuple(planes_of[k] for k in ("vel", "stress", "mats", "oc", "loads"))
        + (shape(n * plan.back_rows, LANES),),
        [vmem] * 9,
        [
            pltpu.VMEM((plan.own_groups, lanes, LANES), F32),
            pltpu.VMEM((n * plan.back_rows, LANES), F32),
            pltpu.SemaphoreType.DMA,
        ],
        outs=(vmem,) * 5 + (hbm,),
        input_output_aliases={4: 0, 5: 1, 6: 2, 7: 3, 8: 4},
    )(*(near(a) for a in (material_rows, other, water, bottom, vel, strs, mats, oc, loads)))
    returned = lax.all_to_all(
        back.reshape(n, plan.back_rows, LANES), "map", split_axis=0, concat_axis=0, tiled=True
    ).reshape(n * plan.back_rows, LANES)
    new_velocity, new_stress = call(
        end_kernel,
        "last_updates",
        (shape(*velocity.shape), shape(*stress.shape)),
        [vmem] * 4,
        [
            pltpu.VMEM((3, width, sub, lanes), F32),
            pltpu.VMEM((6, width, sub, lanes), F32),
        ],
    )(vel, strs, mats, loads)
    new_ocean = call(
        unpack_kernel,
        "ocean_strips",
        shape(*ocean.shape),
        [vmem],
        [
            pltpu.VMEM((plan.strips, plan.nx, LANES), F32),
            pltpu.VMEM((plan.strips, 4, plan.depth, plan.nx), F32),
            pltpu.SemaphoreType.DMA((plan.strips,)),
        ],
        outs=hbm,
    )(returned)
    return new_velocity, new_stress, new_ocean


def solution(mesh):
    n = mesh.shape["map"]

    def body(velocity, stress, ocean, zones, materials, slip, bathy):
        _, cells, depth, ny = velocity.shape
        plan = Plan(n, cells, depth, ny, ocean.shape[1])
        return on_device(plan, velocity, stress, ocean, zones, materials, slip, bathy)

    return jax.shard_map(
        body,
        mesh=mesh,
        in_specs=(
            P("parts", "map", None, None),
            P("parts", "map", None, None),
            P("parts", "map", None, None),
            P("map", "parts", None),
            P(),
            P("map", "parts"),
            P("map", "parts"),
        ),
        out_specs=(
            P("parts", "map", None, None),
            P("parts", "map", None, None),
            P("parts", "map", None, None),
        ),
        check_vma=False,
    )
```

```python
import functools

import jax
import jax.numpy as jnp
from jax import lax
from jax.experimental import pallas as pl
from jax.experimental.pallas import tpu as pltpu
from jax.sharding import PartitionSpec as P

STEPS = 4
ZONES = 8
DT = 0.25
HALF = 0.5 * DT
KBULK = 2.25
GRAV = 0.1
HALO = 2 * STEPS
LANES = 128
F32 = jnp.float32
VX, VY, VZ = range(3)
SXX, SYY, SZZ, SXY, SXZ, SYZ = range(6)
BUOY, LAMB, SHEAR, FAULT, FLOOR = range(5)


class Plan:
    def __init__(self, devices, cells, depth, ny, strips):
        self.n = devices
        self.cells = cells
        self.depth = depth
        self.ny = ny
        self.strips = strips
        self.chunks = max(1, LANES // ny)
        self.sub = depth // self.chunks
        self.lanes = self.chunks * ny
        self.width = cells + 2 * HALO
        self.own_groups = cells // self.chunks
        self.halo_groups = HALO // self.chunks
        self.sent_groups = self.own_groups + self.halo_groups
        self.lead = self.chunks * strips
        self.rows = self.lead * self.sent_groups
        self.back_rows = self.lead * self.own_groups
        self.nx = devices * cells
        self.block = 4 * self.sub
        self.unrolled = self.sub * self.lanes <= 1024
        assert devices % 2 == 0 and cells == HALO and self.block * self.chunks == LANES

    def planes(self, start, stop, body, batch=1):
        if self.unrolled:
            for j in range(start, stop, batch):
                body(j, min(batch, stop - j))
        else:
            def run(j, carry):
                body(j, 1)
                return carry

            lax.fori_loop(start, stop, run, 0)


BATCH = 8


def odd_device():
    return lax.rem(lax.axis_index("map"), 2)


def place(pieces, wanted, block):
    out = None
    for i, piece in enumerate(pieces):
        shift = (i - wanted[i]) * block % piece.shape[-1]
        moved = pltpu.roll(piece, shift, piece.ndim - 1) if shift else piece
        if out is None:
            out = moved
        else:
            lane = lax.broadcasted_iota(jnp.int32, moved.shape, moved.ndim - 1)
            out = jnp.where(lane >= i * block, moved, out)
    return out


def ocean_kernel(
    plan, vel_ref, stress_ref, zones_ref, slip_ref, ocean_ref, bathy_ref,
    message_out, vel, stress, zones, slip, ocean, bathy, turned, grouped, extra, message, sems,
):
    cells, sub, chunks = plan.cells, plan.sub, plan.chunks
    n, strips, block, sent, rows = plan.n, plan.strips, plan.block, plan.sent_groups, plan.rows
    pairs = (
        (ocean_ref, ocean),
        (bathy_ref, bathy),
        (vel_ref, vel),
        (stress_ref, stress),
        (zones_ref, zones),
        (slip_ref, slip),
    )
    copies = [
        pltpu.make_async_copy(source, target, sems.at[i])
        for i, (source, target) in enumerate(pairs)
    ]
    for copy in copies:
        copy.start()
    copies[0].wait()
    copies[1].wait()
    count = plan.nx // chunks
    lead = plan.lead
    pad = plan.halo_groups * lead
    grouped[:pad, :] = jnp.zeros((pad, LANES), F32)
    grouped[pad + count * lead :, :] = jnp.zeros((pad, LANES), F32)
    for yl in range(strips):
        stacked = jnp.concatenate(
            [ocean[f, yl, kc * sub : (kc + 1) * sub, :] for kc in range(chunks) for f in range(4)],
            axis=0,
        )
        turned[yl] = stacked.T
        by_x = [turned[yl, pl.ds(i, count, stride=chunks), :] for i in range(chunks)]
        for kc in range(chunks):
            grouped[pl.ds(pad + kc * strips + yl, count, stride=lead), :] = place(
                by_x, [kc] * chunks, block
            )
    for d in range(n):
        start = (d * plan.own_groups + (d % 2) * plan.halo_groups) * lead
        message[d * rows : (d + 1) * rows, :] = grouped[start : start + rows, :]
    depths = bathy[...].astype(F32)
    wide = lax.broadcasted_iota(jnp.int32, depths.shape, 1)
    for d in range(n):
        first = d * cells - HALO - 1
        moved = pltpu.roll(depths, -first % plan.nx, 1)
        moved = jnp.where((wide + first >= 0) & (wide + first < plan.nx), moved, 0.0)
        extra[d * strips : (d + 1) * strips, :] = moved[:, :LANES]
    pairs = n // 2
    lane = lax.broadcasted_iota(jnp.int32, (pairs, LANES), 1)
    blank = jnp.zeros((1, LANES), F32)
    for odd in range(2):
        slot = (odd * (chunks - 1) * 4 + 2) * sub
        group = odd * (sent - 1)
        for yl in range(strips):
            if odd:
                column = turned[yl, pl.ds(2 * cells + HALO, pairs - 1, stride=2 * cells), :]
                column = jnp.concatenate([column, blank], axis=0)
            else:
                column = turned[yl, pl.ds(2 * cells - HALO - 1, pairs - 1, stride=2 * cells), :]
                column = jnp.concatenate([blank, column], axis=0)
            deep = extra[pl.ds(odd * strips + yl, pairs, stride=2 * strips), :]
            for kc in range(chunks):
                at = odd * rows + group * lead + kc * strips + yl
                old = message[pl.ds(at, pairs, stride=2 * rows), :]
                edge = pltpu.roll(column, (slot - kc * block) % LANES, 1)
                floor = pltpu.roll(deep, (slot + sub - kc * sub) % LANES, 1)
                new = jnp.where((lane >= slot) & (lane < slot + sub), edge, old)
                new = jnp.where((lane >= slot + sub) & (lane < slot + 2 * sub), floor, new)
                message[pl.ds(at, pairs, stride=2 * rows), :] = new
    message_out[...] = message[...]
    for copy in copies[2:]:
        copy.wait()


def crust_kernel(plan, vel, stress, zones, slip, crust, border):
    cells, sub, chunks, ny = plan.cells, plan.sub, plan.chunks, plan.ny

    def joined(ref, *at):
        parts = [ref[(*at, pl.ds(kc * sub, sub), slice(None))] for kc in range(chunks)]
        return jnp.concatenate(parts, axis=-1) if chunks > 1 else parts[0]

    for f in range(3):
        for x in range(cells):
            crust[f * cells + x] = joined(vel, f, x)
    for f in range(6):
        for x in range(cells):
            crust[(3 + f) * cells + x] = joined(stress, f, x)
    for x in range(cells):
        crust[9 * cells + x] = (joined(zones, x) + 1).astype(F32)
    fault_chunk = (plan.depth // 2) // sub
    pieces = [
        slip[...] if kc == fault_chunk else jnp.zeros((cells, ny), F32) for kc in range(chunks)
    ]
    fault = jnp.concatenate(pieces, axis=-1) if chunks > 1 else pieces[0]
    if sub > cells:
        fault = jnp.concatenate([fault, jnp.zeros((sub - cells, plan.lanes), F32)], axis=0)
    crust[10 * cells] = fault
    odd = odd_device()
    near = cells - 1
    for f in range(10):
        for i in range(near):
            border[f * near + i] = crust[f * cells + i + odd]
    for i, f in enumerate((SXX, SXY, SXZ)):
        border[10 * near + i] = crust[(3 + f) * cells + near * (1 - odd)]
    border[10 * near + 3] = fault


class Shifts:
    def __init__(self, plan):
        self.plan = plan
        shape = (plan.sub, plan.lanes)
        self.row = lax.broadcasted_iota(jnp.int32, shape, 0)
        self.lane = lax.broadcasted_iota(jnp.int32, shape, 1)
        self.y = lax.rem(self.lane, plan.ny)
        self.first_row = self.row == 0
        self.last_row = self.row == plan.sub - 1
        self.top = self.first_row & (self.lane < plan.ny)
        self.floor_cell = self.last_row & (self.lane >= plan.lanes - plan.ny)
        self.not_low_y = jnp.where(self.y == 0, 0.0, 1.0).astype(F32)
        self.not_high_y = jnp.where(self.y == plan.ny - 1, 0.0, 1.0).astype(F32)
        self.depth = (
            lax.div(self.lane, plan.ny) * plan.sub + self.row
        ).astype(F32)

    def by_lane(self, f, shift):
        return pltpu.roll(f, shift % self.plan.lanes, f.ndim - 1)

    def by_row(self, f, shift):
        return pltpu.roll(f, shift % self.plan.sub, f.ndim - 2)

    def dy(self, f):
        return self.by_lane(f, -1) * self.not_high_y - self.by_lane(f, 1) * self.not_low_y

    def below(self, f):
        plan = self.plan
        moved = self.by_row(f, -1)
        if plan.chunks > 1:
            moved = jnp.where(self.last_row, self.by_lane(moved, -plan.ny), moved)
        return jnp.where(self.floor_cell, 0.0, moved)

    def above(self, f, top):
        plan = self.plan
        moved = self.by_row(f, 1)
        if plan.chunks > 1:
            moved = jnp.where(self.first_row, self.by_lane(moved, plan.ny), moved)
        return jnp.where(self.top, top, moved)

    def seafloor(self, vz):
        row = self.over_chunks(jnp.where(self.top, vz, 0.0))
        return jnp.broadcast_to(row[..., 0:1, :], vz.shape)

    def on_top(self, f):
        shift = self.plan.sub // 2
        while shift:
            f = f + self.by_row(f, shift)
            shift //= 2
        return jnp.where(self.top, self.over_chunks(f), 0.0)

    def over_chunks(self, f):
        shift = self.plan.ny
        while shift < self.plan.lanes:
            f = f + self.by_lane(f, shift)
            shift *= 2
        return f


def acceleration(sh, stress, j, count):
    at, before, after = (pl.ds(j + k, count) for k in (0, -1, 1))
    sxy, sxz = stress[SXY, at], stress[SXZ, at]
    ax = stress[SXX, after] - stress[SXX, before] + sh.dy(sxy) + sh.below(sxz) - sh.above(sxz, 0.0)
    syz = stress[SYZ, at]
    ay = stress[SXY, after] - stress[SXY, before] + sh.dy(stress[SYY, at])
    ay = ay + sh.below(syz) - sh.above(syz, 0.0)
    szz = stress[SZZ, at]
    az = stress[SXZ, after] - stress[SXZ, before] + sh.dy(syz) + sh.below(szz) - sh.above(szz, 0.0)
    return ax, ay, az


def strained(sh, vel, stress, mats, j, count):
    at, before, after = (pl.ds(j + k, count) for k in (0, -1, 1))
    vx, vy, vz = vel[VX, at], vel[VY, at], vel[VZ, at]
    exx = vel[VX, after] - vel[VX, before]
    eyy = sh.dy(vy)
    ezz = sh.below(vz) - sh.above(vz, vz)
    mu = mats[SHEAR, at]
    mu2 = mu + mu
    common = mats[LAMB, at] * (exx + eyy + ezz)
    yield SXX, stress[SXX, at] + (common + mu2 * exx)
    yield SYY, stress[SYY, at] + (common + mu2 * eyy)
    yield SZZ, stress[SZZ, at] + (common + mu2 * ezz)
    exy = sh.dy(vx) + vel[VY, after] - vel[VY, before]
    yield SXY, stress[SXY, at] + mu * exy
    exz = sh.below(vx) - sh.above(vx, vx) + vel[VZ, after] - vel[VZ, before]
    yield SXZ, stress[SXZ, at] + (mu * exz + mats[FAULT, at])
    eyz = sh.below(vy) - sh.above(vy, vy) + sh.dy(vz)
    yield SYZ, stress[SYZ, at] + mu * eyz


def bring(plan, sh, material, state, ref, fields, x, count, column, first):
    vel, stress, mats = state
    to = pl.ds(column, count)

    def read(f):
        return ref[pl.ds(f * fields + x, count)]

    for f in range(3):
        vel[f, to] = read(f)
    for f in range(6):
        stress[f, to] = read(3 + f)
    zone = read(9)
    values = [jnp.zeros_like(zone) for _ in range(3)]
    for z in range(ZONES):
        here = zone == float(z + 1)
        values = [jnp.where(here, material(c, z), values[c]) for c in range(3)]
    for c in range(3):
        mats[c, to] = values[c] * HALF
    mats[FLOOR, to] = sh.seafloor(read(VZ))
    for i in range(count):
        slip = ref[ref.shape[0] - 1, pl.ds(first + x + i, 1), :]
        slip = jnp.broadcast_to(slip, (plan.sub, plan.lanes))
        mats[FAULT, column + i] = jnp.where(
            sh.row == (plan.depth // 2) % plan.sub, DT * slip, 0.0
        )


def begin_kernel(plan, table, own, mate, vel, stress, mats, rows):
    cells = plan.cells
    sh = Shifts(plan)
    odd = odd_device()
    state = (vel, stress, mats)
    starts = (HALO + cells * odd, HALO + cells * (1 - odd))
    for start, ref in zip(starts, (own, mate)):
        plan.planes(
            0,
            cells,
            lambda x, count, start=start, ref=ref: bring(
                plan, sh, lambda c, z: table[c, z], state, ref, cells, x, count, start + x, 0
            ),
            BATCH,
        )

    def move(j, count):
        at = pl.ds(j, count)
        b = mats[BUOY, at]
        for f, a in enumerate(acceleration(sh, stress, j, count)):
            vel[f, at] = vel[f, at] + b * a

    plan.planes(HALO + 1, HALO + 2 * cells - 1, move, BATCH)
    for c in range(3):
        for z in range(ZONES):
            at = c * ZONES + z
            rows[at : at + 1, :] = jnp.full((1, plan.lanes), table[c, z], F32)


class Updates:
    def __init__(self, plan, sh, vel, stress, mats, oc, water, bottom, loads):
        self.plan, self.sh = plan, sh
        self.vel, self.stress, self.mats = vel, stress, mats
        self.oc, self.water, self.bottom, self.loads = oc, water, bottom, loads

    def flow_x(self, j, count):
        oc = self.oc
        before, at, after = (pl.ds(j + k, count) for k in range(3))
        oc[1, at] = self.water[at] * (oc[1, at] - HALF * (oc[0, after] - oc[0, before]))

    def flow(self, j, count):
        oc, sh = self.oc, self.sh
        at = pl.ds(j + 1, count)
        p = oc[0, at]
        wet = self.water[at]
        rise = sh.below(p) + self.bottom[at] * p - sh.above(p, -p)
        oc[3, at] = wet * (oc[3, at] - (HALF * rise + (DT * GRAV) * p))
        oc[2, at] = wet * (oc[2, at] - HALF * sh.dy(p))

    def press(self, j, count, start):
        oc, sh = self.oc, self.sh
        before, at, after = (pl.ds(j + k, count) for k in range(3))
        crust = pl.ds(j, count)
        w = oc[3, at]
        floor = self.mats[FLOOR, crust] if start else sh.seafloor(self.vel[VZ, crust])
        rise = sh.below(w) + self.bottom[at] * floor - sh.above(w, w)
        total = oc[1, after] - oc[1, before] + sh.dy(oc[2, at]) + rise
        oc[0, at] = self.water[at] * (oc[0, at] - (HALF * KBULK) * total)

    def load(self, j, count):
        at = pl.ds(j + 1, count)
        return self.sh.on_top(self.bottom[at] * self.oc[0, at])

    def keep(self, j, count):
        self.loads[pl.ds(j, count)] = self.load(j, count)

    def add_load(self, j, count):
        at = pl.ds(j, count)
        self.vel[VZ, at] = self.vel[VZ, at] + self.mats[BUOY, at] * self.load(j, count)

    def move(self, j, count):
        vel = self.vel
        at = pl.ds(j, count)
        ax, ay, az = acceleration(self.sh, self.stress, j, count)
        b = self.mats[BUOY, at]
        vel[VX, at] = vel[VX, at] + b * ax
        vel[VY, at] = vel[VY, at] + b * ay
        vel[VZ, at] = vel[VZ, at] + b * (az + self.load(j, count))

    def strain(self, j, count):
        for f, value in strained(self.sh, self.vel, self.stress, self.mats, j, count):
            self.stress[f, pl.ds(j, count)] = value

    def run(self, spans, moved, send=None):
        for t in range(STEPS):
            def planes(inset, update, t=t):
                self.plan.planes(*spans(t, inset), update, BATCH)

            planes(0, self.flow_x)
            planes(1, self.flow)
            planes(1, functools.partial(self.press, start=t == 0))
            if t == STEPS - 1:
                if send is not None:
                    send()
                planes(1, self.keep)
            elif t == 0 and moved:
                planes(1, self.add_load)
            else:
                planes(1, self.move)
            if t < STEPS - 2:
                planes(2, self.strain)


def inner_kernel(
    plan, arrived, swapped, mats, vel_in, stress_in, vel, stress, oc, water, bottom, loads,
    gather, depths,
):
    sub, chunks, n, strips = plan.sub, plan.chunks, plan.n, plan.strips
    cells, sent = plan.cells, plan.sent_groups
    sh = Shifts(plan)
    odd = odd_device()
    half = n // 2
    columns = 2 * cells + 2 * HALO

    def turn(owner, group):
        for core, ref in ((odd, arrived), (1 - odd, swapped)):
            for kc in range(chunks):
                for yl in range(strips):
                    at = owner * plan.rows + group * plan.lead + kc * strips + yl
                    to = kc * plan.ny + core * strips + yl
                    gather[pl.ds(to, half, stride=2 * strips), :] = ref[
                        pl.ds(at, half, stride=2 * plan.rows), :
                    ]
        return gather[...].T

    deeps = []
    for owner in range(2):
        for group in range(sent):
            turned = turn(owner, group)
            for i in range(chunks):
                for f in range(4):
                    at = (i * 4 + f) * sub
                    column = 1 + owner * (cells + HALO) + group * chunks + i
                    oc[f, column] = turned[at : at + sub]
            if owner == 0 and group == 0:
                oc[0, 0] = turned[2 * sub : 3 * sub]
                deeps.append(turned[3 * sub : 4 * sub])
            if owner == 1 and group == sent - 1:
                oc[0, columns + 1] = turned[LANES - 2 * sub : LANES - sub]
                deeps.append(turned[LANES - sub :])
    for i, deep in enumerate(deeps):
        for kc in range(chunks):
            mine = (sh.lane >= kc * plan.ny) & (sh.lane < (kc + 1) * plan.ny)
            depths[i, kc * sub : (kc + 1) * sub, :] = sh.over_chunks(jnp.where(mine, deep, 0.0))

    def mask(owner, j, _):
        low = jnp.broadcast_to(depths[owner, pl.ds(j - owner * cells, 1), :], (sub, plan.lanes))
        wet = jnp.where(sh.depth < low, 1.0, 0.0).astype(F32)
        water[j] = wet
        bottom[j] = jnp.where(sh.depth == low - 1.0, 1.0, 0.0).astype(F32)
        oc[0, j] = oc[0, j] * wet

    def mask_x(j, _):
        oc[1, j] = oc[1, j] * water[j]

    def mask_yw(j, _):
        oc[2, j] = oc[2, j] * water[j]
        oc[3, j] = oc[3, j] * water[j]

    plan.planes(0, plan.width + 2, lambda j, _: mask(0, j, _))
    plan.planes(plan.width + 2, columns + 2, lambda j, _: mask(1, j, _))
    plan.planes(1, columns + 1, mask_x)
    plan.planes(2, columns, mask_yw)

    def bring_in(j, _):
        for f in range(3):
            vel[f, j] = vel_in[f, j]
        for f in range(6):
            stress[f, j] = stress_in[f, j]

    if not plan.unrolled:
        plan.planes(HALO, HALO + 2 * cells, bring_in)
    updates = Updates(plan, sh, vel, stress, mats, oc, water, bottom, loads)
    updates.run(lambda t, inset: (HALO + 2 * t + inset, HALO + 2 * cells - 2 * t - inset), True)


def outer_kernel(
    plan, materials, border, water, bottom, vel_in, stress_in, mats_in, oc_in, loads_in,
    vel, stress, mats, oc, loads, message, gather, rows, sem,
):
    sub, chunks, n, strips, cells = plan.sub, plan.chunks, plan.n, plan.strips, plan.cells
    near = cells - 1
    sh = Shifts(plan)
    odd = odd_device()
    if not plan.unrolled:
        for here, there in (
            (vel, vel_in), (stress, stress_in), (mats, mats_in), (oc, oc_in), (loads, loads_in)
        ):
            here[...] = there[...]
    updates = Updates(plan, sh, vel, stress, mats, oc, water, bottom, loads)

    def material(c, z):
        row = materials[pl.ds(c * ZONES + z, 1), :]
        return jnp.broadcast_to(row, (sub, plan.lanes))

    def side(core):
        low, far = ((1, 0), (HALO + 2 * cells, 2 * HALO + 2 * cells - 1))[core]
        state = (vel, stress, mats)
        plan.planes(
            0,
            near,
            lambda x, count: bring(
                plan, sh, material, state, border, near, x, count, low + x, 1 - core
            ),
            BATCH,
        )
        for i, f in enumerate((SXX, SXY, SXZ)):
            stress[f, far] = border[10 * near + i]

        def spans(t, inset):
            if core == 0:
                return 2 * t + inset, 2 * t + inset + HALO
            last = 2 * HALO + 2 * cells - 2 * t - inset
            return last - HALO, last

        copy = pltpu.make_async_copy(rows, message, sem)

        def send():
            for group in range(plan.own_groups):
                stacked = jnp.concatenate(
                    [
                        oc[f, 1 + HALO + core * cells + group * chunks + i]
                        for i in range(chunks)
                        for f in range(4)
                    ],
                    axis=0,
                )
                gather[group] = stacked.T
                for kc in range(chunks):
                    for yl in range(strips):
                        at = group * plan.lead + kc * strips + yl
                        rows[pl.ds(at, n, stride=plan.back_rows), :] = gather[
                            group, pl.ds(kc * plan.ny + yl, n, stride=strips), :
                        ]
            copy.start()

        updates.run(spans, False, send)
        copy.wait()

    for core in range(2):
        pl.when(odd == core)(functools.partial(side, core))


def end_kernel(plan, vel_all, stress_all, mats_all, loads_all, vel_out, stress_out, vel, stress):
    cells, sub, chunks, ny = plan.cells, plan.sub, plan.chunks, plan.ny
    sh = Shifts(plan)
    first, last = 2 * (STEPS - 1), plan.width - 2 * (STEPS - 1)
    window = pl.ds(cells * odd_device(), plan.width)
    vel_in, stress_in = vel_all.at[:, window], stress_all.at[:, window]
    mats, loads = mats_all.at[:, window], loads_all.at[window]

    def put(out, f, x, count, planes):
        for kc in range(chunks):
            out[f, pl.ds(x, count), kc * sub : (kc + 1) * sub, :] = planes[
                :, :, kc * ny : (kc + 1) * ny
            ]

    def strain(j, count):
        for f, value in strained(sh, vel_in, stress_in, mats, j, count):
            stress[f, pl.ds(j, count)] = value

    def move(j, count):
        at = pl.ds(j, count)
        ax, ay, az = acceleration(sh, stress, j, count)
        b = mats[BUOY, at]
        for f, a in enumerate((ax, ay, az + loads[at])):
            vel[f, at] = vel_in[f, at] + b * a

    def finish(x, count):
        for f in range(3):
            put(vel_out, f, x, count, vel[f, pl.ds(x + HALO, count)])
        for f, value in strained(sh, vel, stress, mats, x + HALO, count):
            put(stress_out, f, x, count, value)

    plan.planes(first, last, strain, BATCH)
    plan.planes(first + 1, last - 1, move, BATCH)
    plan.planes(0, cells, finish, BATCH)


def unpack_kernel(plan, arrived, ocean, turned, strips, sems):
    sub, chunks = plan.sub, plan.chunks
    block = 4 * sub
    copies = [
        pltpu.make_async_copy(strips.at[yl], ocean.at[:, yl], sems.at[yl])
        for yl in range(plan.strips)
    ]
    for yl in range(plan.strips):
        by_chunk = [
            arrived[pl.ds(kc * plan.strips + yl, plan.nx // chunks, stride=plan.lead), :]
            for kc in range(chunks)
        ]
        for i in range(chunks):
            turned[yl, pl.ds(i, plan.nx // chunks, stride=chunks), :] = place(
                by_chunk, [i] * chunks, block
            )
        whole = turned[yl].T
        for kc in range(chunks):
            for f in range(4):
                at = (kc * 4 + f) * sub
                strips[yl, f, kc * sub : (kc + 1) * sub, :] = whole[at : at + sub]
        copies[yl].start()
    for copy in copies:
        copy.wait()


def on_device(plan, velocity, stress, ocean, zones, materials, slip, bathy):
    n, cells, sub, lanes, width = plan.n, plan.cells, plan.sub, plan.lanes, plan.width
    vmem = pl.BlockSpec(memory_space=pltpu.VMEM)
    smem = pl.BlockSpec(memory_space=pltpu.SMEM)
    hbm = pl.BlockSpec(memory_space=pltpu.HBM)

    def shape(*dims):
        return jax.ShapeDtypeStruct(dims, F32)

    def like(array):
        return jax.ShapeDtypeStruct(array.shape, array.dtype)

    def held(array):
        return pltpu.VMEM(array.shape, array.dtype)

    def call(kernel, name, out, ins, scratch, room=16, outs=None, **rest):
        room = room if plan.unrolled else 56
        return pl.pallas_call(
            functools.partial(kernel, plan),
            out_shape=out,
            in_specs=ins,
            out_specs=jax.tree.map(lambda _: vmem, out) if outs is None else outs,
            scratch_shapes=scratch,
            compiler_params=pltpu.CompilerParams(vmem_limit_bytes=room * 1024 * 1024),
            name=name,
            **rest,
        )

    def pinned(array):
        return pltpu.with_memory_space_constraint(array, pltpu.HBM)

    def near(array):
        return pltpu.with_memory_space_constraint(array, pltpu.VMEM) if plan.unrolled else array

    mates = [(i, i ^ 1) for i in range(n)]
    others = [(i, i + 1) for i in range(1, n - 1, 2)]
    others += [(target, source) for source, target in others]
    crust_args = (velocity, stress, zones, slip)
    message, *near_args = call(
        ocean_kernel,
        "ocean_rows",
        (shape(n * plan.rows, LANES), *(like(a) for a in crust_args)),
        [hbm] * 6,
        [
            held(ocean),
            held(bathy),
            pltpu.VMEM((plan.strips, plan.nx, LANES), F32),
            pltpu.VMEM(
                ((plan.nx // plan.chunks + 2 * plan.halo_groups) * plan.lead, LANES), F32
            ),
            pltpu.VMEM((n * plan.strips, LANES), F32),
            pltpu.VMEM((n * plan.rows, LANES), F32),
            pltpu.SemaphoreType.DMA((6,)),
        ],
    )(*(pinned(a) for a in (*crust_args, ocean, bathy)))
    arrived = lax.all_to_all(
        message.reshape(n // 2, 2 * plan.rows, LANES),
        "map",
        split_axis=0,
        concat_axis=0,
        axis_index_groups=[list(range(core, n, 2)) for core in range(2)],
        tiled=True,
    ).reshape(n * plan.rows, LANES)
    crust, border = call(
        crust_kernel,
        "crust_planes",
        (shape(10 * cells + 1, sub, lanes), shape(10 * cells - 6, sub, lanes)),
        [vmem] * 4,
        [],
    )(*near_args)
    other = lax.ppermute(border, "map", others)
    arrived, crust = lax.optimization_barrier((arrived, crust))
    swapped = lax.ppermute(arrived, "map", mates)
    mate = lax.ppermute(crust, "map", mates)
    columns = 2 * cells + 2 * HALO
    vel, strs, mats, material_rows = call(
        begin_kernel,
        "first_velocity",
        (
            shape(3, columns, sub, lanes),
            shape(6, columns, sub, lanes),
            shape(5, columns, sub, lanes),
            shape(3 * ZONES, lanes),
        ),
        [smem] + [vmem] * 2,
        [],
    )(materials, crust, mate)
    planes_of = {
        "vel": shape(3, columns, sub, lanes),
        "stress": shape(6, columns, sub, lanes),
        "mats": shape(5, columns, sub, lanes),
        "oc": shape(4, columns + 2, sub, lanes),
        "mask": shape(columns + 2, sub, lanes),
        "loads": shape(columns, sub, lanes),
    }
    vel, strs, oc, water, bottom, loads = call(
        inner_kernel,
        "inner_substeps",
        tuple(planes_of[k] for k in ("vel", "stress", "oc", "mask", "mask", "loads")),
        [vmem] * 5,
        [
            pltpu.VMEM((lanes, LANES), F32),
            pltpu.VMEM((2, plan.depth, lanes), F32),
        ],
        input_output_aliases={3: 0, 4: 1},
    )(*(near(a) for a in (arrived, swapped, mats, vel, strs)))
    vel, strs, mats, oc, loads, back = call(
        outer_kernel,
        "outer_substeps",
        tuple(planes_of[k] for k in ("vel", "stress", "mats", "oc", "loads"))
        + (shape(n * plan.back_rows, LANES),),
        [vmem] * 9,
        [
            pltpu.VMEM((plan.own_groups, lanes, LANES), F32),
            pltpu.VMEM((n * plan.back_rows, LANES), F32),
            pltpu.SemaphoreType.DMA,
        ],
        outs=(vmem,) * 5 + (hbm,),
        input_output_aliases={4: 0, 5: 1, 6: 2, 7: 3, 8: 4},
    )(*(near(a) for a in (material_rows, other, water, bottom, vel, strs, mats, oc, loads)))
    returned = lax.all_to_all(
        back.reshape(n, plan.back_rows, LANES), "map", split_axis=0, concat_axis=0, tiled=True
    ).reshape(n * plan.back_rows, LANES)
    new_velocity, new_stress = call(
        end_kernel,
        "last_updates",
        (shape(*velocity.shape), shape(*stress.shape)),
        [vmem] * 4,
        [
            pltpu.VMEM((3, width, sub, lanes), F32),
            pltpu.VMEM((6, width, sub, lanes), F32),
        ],
    )(vel, strs, mats, loads)
    new_ocean = call(
        unpack_kernel,
        "ocean_strips",
        shape(*ocean.shape),
        [vmem],
        [
            pltpu.VMEM((plan.strips, plan.nx, LANES), F32),
            pltpu.VMEM((plan.strips, 4, plan.depth, plan.nx), F32),
            pltpu.SemaphoreType.DMA((plan.strips,)),
        ],
        outs=hbm,
    )(returned)
    return new_velocity, new_stress, new_ocean


def solution(mesh):
    n = mesh.shape["map"]

    def body(velocity, stress, ocean, zones, materials, slip, bathy):
        _, cells, depth, ny = velocity.shape
        plan = Plan(n, cells, depth, ny, ocean.shape[1])
        return on_device(plan, velocity, stress, ocean, zones, materials, slip, bathy)

    return jax.shard_map(
        body,
        mesh=mesh,
        in_specs=(
            P("parts", "map", None, None),
            P("parts", "map", None, None),
            P("parts", "map", None, None),
            P("map", "parts", None),
            P(),
            P("map", "parts"),
            P("map", "parts"),
        ),
        out_specs=(
            P("parts", "map", None, None),
            P("parts", "map", None, None),
            P("parts", "map", None, None),
        ),
        check_vma=False,
    )
```

```python
import functools

import jax
import jax.numpy as jnp
from jax import lax
from jax.experimental import pallas as pl
from jax.experimental.pallas import tpu as pltpu
from jax.sharding import PartitionSpec as P

STEPS = 4
ZONES = 8
DT = 0.25
HALF = 0.5 * DT
KBULK = 2.25
GRAV = 0.1
HALO = 2 * STEPS
LANES = 128
F32 = jnp.float32
VX, VY, VZ = range(3)
SXX, SYY, SZZ, SXY, SXZ, SYZ = range(6)
BUOY, LAMB, SHEAR, FAULT, FLOOR = range(5)


class Plan:
    def __init__(self, devices, cells, depth, ny, strips):
        self.n = devices
        self.cells = cells
        self.depth = depth
        self.ny = ny
        self.strips = strips
        self.chunks = max(1, LANES // ny)
        self.sub = depth // self.chunks
        self.lanes = self.chunks * ny
        self.width = cells + 2 * HALO
        self.own_groups = cells // self.chunks
        self.halo_groups = HALO // self.chunks
        self.sent_groups = self.own_groups + self.halo_groups
        self.lead = self.chunks * strips
        self.rows = self.lead * self.sent_groups
        self.back_rows = self.lead * self.own_groups
        self.nx = devices * cells
        self.block = 4 * self.sub
        self.unrolled = self.sub * self.lanes <= 1024
        assert devices % 2 == 0 and cells == HALO and self.block * self.chunks == LANES

    def planes(self, start, stop, body, batch=1):
        if self.unrolled:
            for j in range(start, stop, batch):
                body(j, min(batch, stop - j))
        else:
            def run(j, carry):
                body(j, 1)
                return carry

            lax.fori_loop(start, stop, run, 0)


BATCH = 8


def odd_device():
    return lax.rem(lax.axis_index("map"), 2)


def place(pieces, wanted, block):
    out = None
    for i, piece in enumerate(pieces):
        shift = (i - wanted[i]) * block % piece.shape[-1]
        moved = pltpu.roll(piece, shift, piece.ndim - 1) if shift else piece
        if out is None:
            out = moved
        else:
            lane = lax.broadcasted_iota(jnp.int32, moved.shape, moved.ndim - 1)
            out = jnp.where(lane >= i * block, moved, out)
    return out


def ocean_kernel(
    plan, vel_ref, stress_ref, zones_ref, slip_ref, ocean_ref, bathy_ref,
    message_out, vel, stress, zones, slip, ocean, bathy, turned, grouped, extra, message, sems,
):
    cells, sub, chunks = plan.cells, plan.sub, plan.chunks
    n, strips, block, sent, rows = plan.n, plan.strips, plan.block, plan.sent_groups, plan.rows
    pairs = (
        (ocean_ref, ocean),
        (bathy_ref, bathy),
        (vel_ref, vel),
        (stress_ref, stress),
        (zones_ref, zones),
        (slip_ref, slip),
    )
    copies = [
        pltpu.make_async_copy(source, target, sems.at[i])
        for i, (source, target) in enumerate(pairs)
    ]
    for copy in copies:
        copy.start()
    copies[0].wait()
    copies[1].wait()
    count = plan.nx // chunks
    lead = plan.lead
    pad = plan.halo_groups * lead
    grouped[:pad, :] = jnp.zeros((pad, LANES), F32)
    grouped[pad + count * lead :, :] = jnp.zeros((pad, LANES), F32)
    for yl in range(strips):
        stacked = jnp.concatenate(
            [ocean[f, yl, kc * sub : (kc + 1) * sub, :] for kc in range(chunks) for f in range(4)],
            axis=0,
        )
        turned[yl] = stacked.T
        by_x = [turned[yl, pl.ds(i, count, stride=chunks), :] for i in range(chunks)]
        for kc in range(chunks):
            grouped[pl.ds(pad + kc * strips + yl, count, stride=lead), :] = place(
                by_x, [kc] * chunks, block
            )
    for d in range(n):
        start = (d * plan.own_groups + (d % 2) * plan.halo_groups) * lead
        message[d * rows : (d + 1) * rows, :] = grouped[start : start + rows, :]
    depths = bathy[...].astype(F32)
    wide = lax.broadcasted_iota(jnp.int32, depths.shape, 1)
    for d in range(n):
        first = d * cells - HALO - 1
        moved = pltpu.roll(depths, -first % plan.nx, 1)
        moved = jnp.where((wide + first >= 0) & (wide + first < plan.nx), moved, 0.0)
        extra[d * strips : (d + 1) * strips, :] = moved[:, :LANES]
    pairs = n // 2
    lane = lax.broadcasted_iota(jnp.int32, (pairs, LANES), 1)
    blank = jnp.zeros((1, LANES), F32)
    for odd in range(2):
        slot = (odd * (chunks - 1) * 4 + 2) * sub
        group = odd * (sent - 1)
        for yl in range(strips):
            if odd:
                column = turned[yl, pl.ds(2 * cells + HALO, pairs - 1, stride=2 * cells), :]
                column = jnp.concatenate([column, blank], axis=0)
            else:
                column = turned[yl, pl.ds(2 * cells - HALO - 1, pairs - 1, stride=2 * cells), :]
                column = jnp.concatenate([blank, column], axis=0)
            deep = extra[pl.ds(odd * strips + yl, pairs, stride=2 * strips), :]
            for kc in range(chunks):
                at = odd * rows + group * lead + kc * strips + yl
                old = message[pl.ds(at, pairs, stride=2 * rows), :]
                edge = pltpu.roll(column, (slot - kc * block) % LANES, 1)
                floor = pltpu.roll(deep, (slot + sub - kc * sub) % LANES, 1)
                new = jnp.where((lane >= slot) & (lane < slot + sub), edge, old)
                new = jnp.where((lane >= slot + sub) & (lane < slot + 2 * sub), floor, new)
                message[pl.ds(at, pairs, stride=2 * rows), :] = new
    message_out[...] = message[...]
    for copy in copies[2:]:
        copy.wait()


def crust_kernel(plan, vel, stress, zones, slip, crust, border):
    cells, sub, chunks, ny = plan.cells, plan.sub, plan.chunks, plan.ny

    def joined(ref, *at):
        parts = [ref[(*at, pl.ds(kc * sub, sub), slice(None))] for kc in range(chunks)]
        return jnp.concatenate(parts, axis=-1) if chunks > 1 else parts[0]

    for f in range(3):
        for x in range(cells):
            crust[f * cells + x] = joined(vel, f, x)
    for f in range(6):
        for x in range(cells):
            crust[(3 + f) * cells + x] = joined(stress, f, x)
    for x in range(cells):
        crust[9 * cells + x] = (joined(zones, x) + 1).astype(F32)
    fault_chunk = (plan.depth // 2) // sub
    pieces = [
        slip[...] if kc == fault_chunk else jnp.zeros((cells, ny), F32) for kc in range(chunks)
    ]
    fault = jnp.concatenate(pieces, axis=-1) if chunks > 1 else pieces[0]
    if sub > cells:
        fault = jnp.concatenate([fault, jnp.zeros((sub - cells, plan.lanes), F32)], axis=0)
    crust[10 * cells] = fault
    odd = odd_device()
    near = cells - 1
    for f in range(10):
        for i in range(near):
            border[f * near + i] = crust[f * cells + i + odd]
    for i, f in enumerate((SXX, SXY, SXZ)):
        border[10 * near + i] = crust[(3 + f) * cells + near * (1 - odd)]
    border[10 * near + 3] = fault


class Shifts:
    def __init__(self, plan):
        self.plan = plan
        shape = (plan.sub, plan.lanes)
        self.row = lax.broadcasted_iota(jnp.int32, shape, 0)
        self.lane = lax.broadcasted_iota(jnp.int32, shape, 1)
        self.y = lax.rem(self.lane, plan.ny)
        self.first_row = self.row == 0
        self.last_row = self.row == plan.sub - 1
        self.top = self.first_row & (self.lane < plan.ny)
        self.floor_cell = self.last_row & (self.lane >= plan.lanes - plan.ny)
        self.not_low_y = jnp.where(self.y == 0, 0.0, 1.0).astype(F32)
        self.not_high_y = jnp.where(self.y == plan.ny - 1, 0.0, 1.0).astype(F32)
        self.depth = (
            lax.div(self.lane, plan.ny) * plan.sub + self.row
        ).astype(F32)

    def by_lane(self, f, shift):
        return pltpu.roll(f, shift % self.plan.lanes, f.ndim - 1)

    def by_row(self, f, shift):
        return pltpu.roll(f, shift % self.plan.sub, f.ndim - 2)

    def dy(self, f):
        return self.by_lane(f, -1) * self.not_high_y - self.by_lane(f, 1) * self.not_low_y

    def below(self, f):
        plan = self.plan
        moved = self.by_row(f, -1)
        if plan.chunks > 1:
            moved = jnp.where(self.last_row, self.by_lane(moved, -plan.ny), moved)
        return jnp.where(self.floor_cell, 0.0, moved)

    def above(self, f, top):
        plan = self.plan
        moved = self.by_row(f, 1)
        if plan.chunks > 1:
            moved = jnp.where(self.first_row, self.by_lane(moved, plan.ny), moved)
        return jnp.where(self.top, top, moved)

    def seafloor(self, vz):
        row = self.over_chunks(jnp.where(self.top, vz, 0.0))
        return jnp.broadcast_to(row[..., 0:1, :], vz.shape)

    def on_top(self, f):
        shift = self.plan.sub // 2
        while shift:
            f = f + self.by_row(f, shift)
            shift //= 2
        return jnp.where(self.top, self.over_chunks(f), 0.0)

    def over_chunks(self, f):
        shift = self.plan.ny
        while shift < self.plan.lanes:
            f = f + self.by_lane(f, shift)
            shift *= 2
        return f


def acceleration(sh, stress, j, count):
    at, before, after = (pl.ds(j + k, count) for k in (0, -1, 1))
    sxy, sxz = stress[SXY, at], stress[SXZ, at]
    ax = stress[SXX, after] - stress[SXX, before] + sh.dy(sxy) + sh.below(sxz) - sh.above(sxz, 0.0)
    syz = stress[SYZ, at]
    ay = stress[SXY, after] - stress[SXY, before] + sh.dy(stress[SYY, at])
    ay = ay + sh.below(syz) - sh.above(syz, 0.0)
    szz = stress[SZZ, at]
    az = stress[SXZ, after] - stress[SXZ, before] + sh.dy(syz) + sh.below(szz) - sh.above(szz, 0.0)
    return ax, ay, az


def strained(sh, vel, stress, mats, j, count):
    at, before, after = (pl.ds(j + k, count) for k in (0, -1, 1))
    vx, vy, vz = vel[VX, at], vel[VY, at], vel[VZ, at]
    exx = vel[VX, after] - vel[VX, before]
    eyy = sh.dy(vy)
    ezz = sh.below(vz) - sh.above(vz, vz)
    mu = mats[SHEAR, at]
    mu2 = mu + mu
    common = mats[LAMB, at] * (exx + eyy + ezz)
    yield SXX, stress[SXX, at] + (common + mu2 * exx)
    yield SYY, stress[SYY, at] + (common + mu2 * eyy)
    yield SZZ, stress[SZZ, at] + (common + mu2 * ezz)
    exy = sh.dy(vx) + vel[VY, after] - vel[VY, before]
    yield SXY, stress[SXY, at] + mu * exy
    exz = sh.below(vx) - sh.above(vx, vx) + vel[VZ, after] - vel[VZ, before]
    yield SXZ, stress[SXZ, at] + (mu * exz + mats[FAULT, at])
    eyz = sh.below(vy) - sh.above(vy, vy) + sh.dy(vz)
    yield SYZ, stress[SYZ, at] + mu * eyz


def bring(plan, sh, material, state, ref, fields, x, count, column, first):
    vel, stress, mats = state
    to = pl.ds(column, count)

    def read(f):
        return ref[pl.ds(f * fields + x, count)]

    for f in range(3):
        vel[f, to] = read(f)
    for f in range(6):
        stress[f, to] = read(3 + f)
    zone = read(9)
    values = [jnp.zeros_like(zone) for _ in range(3)]
    for z in range(ZONES):
        here = zone == float(z + 1)
        values = [jnp.where(here, material(c, z), values[c]) for c in range(3)]
    for c in range(3):
        mats[c, to] = values[c] * HALF
    mats[FLOOR, to] = sh.seafloor(read(VZ))
    for i in range(count):
        slip = ref[ref.shape[0] - 1, pl.ds(first + x + i, 1), :]
        slip = jnp.broadcast_to(slip, (plan.sub, plan.lanes))
        mats[FAULT, column + i] = jnp.where(
            sh.row == (plan.depth // 2) % plan.sub, DT * slip, 0.0
        )


def begin_kernel(plan, table, own, mate, vel, stress, mats, rows):
    cells = plan.cells
    sh = Shifts(plan)
    odd = odd_device()
    state = (vel, stress, mats)
    starts = (HALO + cells * odd, HALO + cells * (1 - odd))
    for start, ref in zip(starts, (own, mate)):
        plan.planes(
            0,
            cells,
            lambda x, count, start=start, ref=ref: bring(
                plan, sh, lambda c, z: table[c, z], state, ref, cells, x, count, start + x, 0
            ),
            BATCH,
        )

    def move(j, count):
        at = pl.ds(j, count)
        b = mats[BUOY, at]
        for f, a in enumerate(acceleration(sh, stress, j, count)):
            vel[f, at] = vel[f, at] + b * a

    plan.planes(HALO + 1, HALO + 2 * cells - 1, move, BATCH)
    for c in range(3):
        for z in range(ZONES):
            at = c * ZONES + z
            rows[at : at + 1, :] = jnp.full((1, plan.lanes), table[c, z], F32)


class Updates:
    def __init__(self, plan, sh, vel, stress, mats, oc, water, bottom, loads):
        self.plan, self.sh = plan, sh
        self.vel, self.stress, self.mats = vel, stress, mats
        self.oc, self.water, self.bottom, self.loads = oc, water, bottom, loads

    def flow_x(self, j, count):
        oc = self.oc
        before, at, after = (pl.ds(j + k, count) for k in range(3))
        oc[1, at] = self.water[at] * (oc[1, at] - HALF * (oc[0, after] - oc[0, before]))

    def flow(self, j, count):
        oc, sh = self.oc, self.sh
        at = pl.ds(j + 1, count)
        p = oc[0, at]
        wet = self.water[at]
        rise = sh.below(p) + self.bottom[at] * p - sh.above(p, -p)
        oc[3, at] = wet * (oc[3, at] - (HALF * rise + (DT * GRAV) * p))
        oc[2, at] = wet * (oc[2, at] - HALF * sh.dy(p))

    def press(self, j, count, floor):
        oc, sh = self.oc, self.sh
        before, at, after = (pl.ds(j + k, count) for k in range(3))
        w = oc[3, at]
        rise = sh.below(w) - sh.above(w, w)
        if floor is not None:
            rise = rise + self.bottom[at] * floor(pl.ds(j, count))
        total = oc[1, after] - oc[1, before] + sh.dy(oc[2, at]) + rise
        oc[0, at] = self.water[at] * (oc[0, at] - (HALF * KBULK) * total)

    def add_floor(self, j, count):
        at = pl.ds(j + 1, count)
        floor = self.first_floor(pl.ds(j, count))
        self.oc[0, at] = self.oc[0, at] - (HALF * KBULK) * (self.bottom[at] * floor)

    def first_floor(self, at):
        return self.mats[FLOOR, at]

    def floor(self, at):
        return self.sh.seafloor(self.vel[VZ, at])

    def load(self, j, count):
        at = pl.ds(j + 1, count)
        return self.sh.on_top(self.bottom[at] * self.oc[0, at])

    def keep(self, j, count):
        self.loads[pl.ds(j, count)] = self.load(j, count)

    def add_load(self, j, count):
        at = pl.ds(j, count)
        self.vel[VZ, at] = self.vel[VZ, at] + self.mats[BUOY, at] * self.load(j, count)

    def move(self, j, count):
        vel = self.vel
        at = pl.ds(j, count)
        ax, ay, az = acceleration(self.sh, self.stress, j, count)
        b = self.mats[BUOY, at]
        vel[VX, at] = vel[VX, at] + b * ax
        vel[VY, at] = vel[VY, at] + b * ay
        vel[VZ, at] = vel[VZ, at] + b * (az + self.load(j, count))

    def strain(self, j, count):
        for f, value in strained(self.sh, self.vel, self.stress, self.mats, j, count):
            self.stress[f, pl.ds(j, count)] = value

    def run(self, spans, inner, send=None):
        for t in range(STEPS):
            def planes(inset, update, t=t):
                self.plan.planes(*spans(t, inset), update, BATCH)

            if t:
                planes(0, self.flow_x)
                planes(1, self.flow)
                planes(1, functools.partial(self.press, floor=self.floor))
            elif inner:
                columns = self.vel.shape[1]
                first, last = spans(0, 1)
                self.plan.planes(0, columns, self.flow_x, BATCH)
                self.plan.planes(1, columns - 1, self.flow, BATCH)
                planes(1, functools.partial(self.press, floor=self.first_floor))
                self.plan.planes(1, first, functools.partial(self.press, floor=None), BATCH)
                self.plan.planes(
                    last, columns - 1, functools.partial(self.press, floor=None), BATCH
                )
            else:
                planes(1, self.add_floor)
            if t == STEPS - 1:
                if send is not None:
                    send()
                planes(1, self.keep)
            elif t == 0 and inner:
                planes(1, self.add_load)
            else:
                planes(1, self.move)
            if t < STEPS - 2:
                planes(2, self.strain)


def inner_kernel(
    plan, arrived, swapped, mats, vel_in, stress_in, vel, stress, oc, water, bottom, loads,
    gather, depths,
):
    sub, chunks, n, strips = plan.sub, plan.chunks, plan.n, plan.strips
    cells, sent = plan.cells, plan.sent_groups
    sh = Shifts(plan)
    odd = odd_device()
    half = n // 2
    columns = 2 * cells + 2 * HALO

    def turn(owner, group):
        for core, ref in ((odd, arrived), (1 - odd, swapped)):
            for kc in range(chunks):
                for yl in range(strips):
                    at = owner * plan.rows + group * plan.lead + kc * strips + yl
                    to = kc * plan.ny + core * strips + yl
                    gather[pl.ds(to, half, stride=2 * strips), :] = ref[
                        pl.ds(at, half, stride=2 * plan.rows), :
                    ]
        return gather[...].T

    deeps = []
    for owner in range(2):
        for group in range(sent):
            turned = turn(owner, group)
            for i in range(chunks):
                for f in range(4):
                    at = (i * 4 + f) * sub
                    column = 1 + owner * (cells + HALO) + group * chunks + i
                    oc[f, column] = turned[at : at + sub]
            if owner == 0 and group == 0:
                oc[0, 0] = turned[2 * sub : 3 * sub]
                deeps.append(turned[3 * sub : 4 * sub])
            if owner == 1 and group == sent - 1:
                oc[0, columns + 1] = turned[LANES - 2 * sub : LANES - sub]
                deeps.append(turned[LANES - sub :])
    for i, deep in enumerate(deeps):
        for kc in range(chunks):
            mine = (sh.lane >= kc * plan.ny) & (sh.lane < (kc + 1) * plan.ny)
            depths[i, kc * sub : (kc + 1) * sub, :] = sh.over_chunks(jnp.where(mine, deep, 0.0))

    def mask(owner, j, _):
        low = jnp.broadcast_to(depths[owner, pl.ds(j - owner * cells, 1), :], (sub, plan.lanes))
        wet = jnp.where(sh.depth < low, 1.0, 0.0).astype(F32)
        water[j] = wet
        bottom[j] = jnp.where(sh.depth == low - 1.0, 1.0, 0.0).astype(F32)
        oc[0, j] = oc[0, j] * wet

    def mask_x(j, _):
        oc[1, j] = oc[1, j] * water[j]

    def mask_yw(j, _):
        oc[2, j] = oc[2, j] * water[j]
        oc[3, j] = oc[3, j] * water[j]

    plan.planes(0, plan.width + 2, lambda j, _: mask(0, j, _))
    plan.planes(plan.width + 2, columns + 2, lambda j, _: mask(1, j, _))
    plan.planes(1, columns + 1, mask_x)
    plan.planes(2, columns, mask_yw)

    def bring_in(j, _):
        for f in range(3):
            vel[f, j] = vel_in[f, j]
        for f in range(6):
            stress[f, j] = stress_in[f, j]

    if not plan.unrolled:
        plan.planes(HALO, HALO + 2 * cells, bring_in)
    updates = Updates(plan, sh, vel, stress, mats, oc, water, bottom, loads)
    updates.run(lambda t, inset: (HALO + 2 * t + inset, HALO + 2 * cells - 2 * t - inset), True)


def outer_kernel(
    plan, materials, border, water, bottom, vel_in, stress_in, mats_in, oc_in, loads_in,
    vel, stress, mats, oc, loads, message, gather, rows, sem,
):
    sub, chunks, n, strips, cells = plan.sub, plan.chunks, plan.n, plan.strips, plan.cells
    near = cells - 1
    sh = Shifts(plan)
    odd = odd_device()
    if not plan.unrolled:
        for here, there in (
            (vel, vel_in), (stress, stress_in), (mats, mats_in), (oc, oc_in), (loads, loads_in)
        ):
            here[...] = there[...]
    updates = Updates(plan, sh, vel, stress, mats, oc, water, bottom, loads)

    def material(c, z):
        row = materials[pl.ds(c * ZONES + z, 1), :]
        return jnp.broadcast_to(row, (sub, plan.lanes))

    def side(core):
        low, far = ((1, 0), (HALO + 2 * cells, 2 * HALO + 2 * cells - 1))[core]
        state = (vel, stress, mats)
        plan.planes(
            0,
            near,
            lambda x, count: bring(
                plan, sh, material, state, border, near, x, count, low + x, 1 - core
            ),
            BATCH,
        )
        for i, f in enumerate((SXX, SXY, SXZ)):
            stress[f, far] = border[10 * near + i]

        def spans(t, inset):
            if core == 0:
                return 2 * t + inset, 2 * t + inset + HALO
            last = 2 * HALO + 2 * cells - 2 * t - inset
            return last - HALO, last

        copy = pltpu.make_async_copy(rows, message, sem)

        def send():
            for group in range(plan.own_groups):
                stacked = jnp.concatenate(
                    [
                        oc[f, 1 + HALO + core * cells + group * chunks + i]
                        for i in range(chunks)
                        for f in range(4)
                    ],
                    axis=0,
                )
                gather[group] = stacked.T
                for kc in range(chunks):
                    for yl in range(strips):
                        at = group * plan.lead + kc * strips + yl
                        rows[pl.ds(at, n, stride=plan.back_rows), :] = gather[
                            group, pl.ds(kc * plan.ny + yl, n, stride=strips), :
                        ]
            copy.start()

        updates.run(spans, False, send)
        copy.wait()

    for core in range(2):
        pl.when(odd == core)(functools.partial(side, core))


def end_kernel(plan, vel_all, stress_all, mats_all, loads_all, vel_out, stress_out, vel, stress):
    cells, sub, chunks, ny = plan.cells, plan.sub, plan.chunks, plan.ny
    sh = Shifts(plan)
    first, last = 2 * (STEPS - 1), plan.width - 2 * (STEPS - 1)
    window = pl.ds(cells * odd_device(), plan.width)
    vel_in, stress_in = vel_all.at[:, window], stress_all.at[:, window]
    mats, loads = mats_all.at[:, window], loads_all.at[window]

    def put(out, f, x, count, planes):
        for kc in range(chunks):
            out[f, pl.ds(x, count), kc * sub : (kc + 1) * sub, :] = planes[
                :, :, kc * ny : (kc + 1) * ny
            ]

    def strain(j, count):
        for f, value in strained(sh, vel_in, stress_in, mats, j, count):
            stress[f, pl.ds(j, count)] = value

    def move(j, count):
        at = pl.ds(j, count)
        ax, ay, az = acceleration(sh, stress, j, count)
        b = mats[BUOY, at]
        for f, a in enumerate((ax, ay, az + loads[at])):
            vel[f, at] = vel_in[f, at] + b * a

    def finish(x, count):
        for f in range(3):
            put(vel_out, f, x, count, vel[f, pl.ds(x + HALO, count)])
        for f, value in strained(sh, vel, stress, mats, x + HALO, count):
            put(stress_out, f, x, count, value)

    plan.planes(first, last, strain, BATCH)
    plan.planes(first + 1, last - 1, move, BATCH)
    plan.planes(0, cells, finish, BATCH)


def unpack_kernel(plan, arrived, ocean, turned, strips, sems):
    sub, chunks = plan.sub, plan.chunks
    block = 4 * sub
    copies = [
        pltpu.make_async_copy(strips.at[yl], ocean.at[:, yl], sems.at[yl])
        for yl in range(plan.strips)
    ]
    for yl in range(plan.strips):
        by_chunk = [
            arrived[pl.ds(kc * plan.strips + yl, plan.nx // chunks, stride=plan.lead), :]
            for kc in range(chunks)
        ]
        for i in range(chunks):
            turned[yl, pl.ds(i, plan.nx // chunks, stride=chunks), :] = place(
                by_chunk, [i] * chunks, block
            )
        whole = turned[yl].T
        for kc in range(chunks):
            for f in range(4):
                at = (kc * 4 + f) * sub
                strips[yl, f, kc * sub : (kc + 1) * sub, :] = whole[at : at + sub]
        copies[yl].start()
    for copy in copies:
        copy.wait()


def on_device(plan, velocity, stress, ocean, zones, materials, slip, bathy):
    n, cells, sub, lanes, width = plan.n, plan.cells, plan.sub, plan.lanes, plan.width
    vmem = pl.BlockSpec(memory_space=pltpu.VMEM)
    smem = pl.BlockSpec(memory_space=pltpu.SMEM)
    hbm = pl.BlockSpec(memory_space=pltpu.HBM)

    def shape(*dims):
        return jax.ShapeDtypeStruct(dims, F32)

    def like(array):
        return jax.ShapeDtypeStruct(array.shape, array.dtype)

    def held(array):
        return pltpu.VMEM(array.shape, array.dtype)

    def call(kernel, name, out, ins, scratch, room=16, outs=None, **rest):
        room = room if plan.unrolled else 56
        return pl.pallas_call(
            functools.partial(kernel, plan),
            out_shape=out,
            in_specs=ins,
            out_specs=jax.tree.map(lambda _: vmem, out) if outs is None else outs,
            scratch_shapes=scratch,
            compiler_params=pltpu.CompilerParams(vmem_limit_bytes=room * 1024 * 1024),
            name=name,
            **rest,
        )

    def pinned(array):
        return pltpu.with_memory_space_constraint(array, pltpu.HBM)

    def near(array):
        return pltpu.with_memory_space_constraint(array, pltpu.VMEM) if plan.unrolled else array

    mates = [(i, i ^ 1) for i in range(n)]
    others = [(i, i + 1) for i in range(1, n - 1, 2)]
    others += [(target, source) for source, target in others]
    crust_args = (velocity, stress, zones, slip)
    message, *near_args = call(
        ocean_kernel,
        "ocean_rows",
        (shape(n * plan.rows, LANES), *(like(a) for a in crust_args)),
        [hbm] * 6,
        [
            held(ocean),
            held(bathy),
            pltpu.VMEM((plan.strips, plan.nx, LANES), F32),
            pltpu.VMEM(
                ((plan.nx // plan.chunks + 2 * plan.halo_groups) * plan.lead, LANES), F32
            ),
            pltpu.VMEM((n * plan.strips, LANES), F32),
            pltpu.VMEM((n * plan.rows, LANES), F32),
            pltpu.SemaphoreType.DMA((6,)),
        ],
    )(*(pinned(a) for a in (*crust_args, ocean, bathy)))
    arrived = lax.all_to_all(
        message.reshape(n // 2, 2 * plan.rows, LANES),
        "map",
        split_axis=0,
        concat_axis=0,
        axis_index_groups=[list(range(core, n, 2)) for core in range(2)],
        tiled=True,
    ).reshape(n * plan.rows, LANES)
    crust, border = call(
        crust_kernel,
        "crust_planes",
        (shape(10 * cells + 1, sub, lanes), shape(10 * cells - 6, sub, lanes)),
        [vmem] * 4,
        [],
    )(*near_args)
    other = lax.ppermute(border, "map", others)
    mate = lax.ppermute(crust, "map", mates)
    columns = 2 * cells + 2 * HALO
    vel, strs, mats, material_rows = call(
        begin_kernel,
        "first_velocity",
        (
            shape(3, columns, sub, lanes),
            shape(6, columns, sub, lanes),
            shape(5, columns, sub, lanes),
            shape(3 * ZONES, lanes),
        ),
        [smem] + [vmem] * 2,
        [],
    )(materials, crust, mate)
    arrived, vel = lax.optimization_barrier((arrived, vel))
    swapped = lax.ppermute(arrived, "map", mates)
    planes_of = {
        "vel": shape(3, columns, sub, lanes),
        "stress": shape(6, columns, sub, lanes),
        "mats": shape(5, columns, sub, lanes),
        "oc": shape(4, columns + 2, sub, lanes),
        "mask": shape(columns + 2, sub, lanes),
        "loads": shape(columns, sub, lanes),
    }
    vel, strs, oc, water, bottom, loads = call(
        inner_kernel,
        "inner_substeps",
        tuple(planes_of[k] for k in ("vel", "stress", "oc", "mask", "mask", "loads")),
        [vmem] * 5,
        [
            pltpu.VMEM((lanes, LANES), F32),
            pltpu.VMEM((2, plan.depth, lanes), F32),
        ],
        input_output_aliases={3: 0, 4: 1},
    )(*(near(a) for a in (arrived, swapped, mats, vel, strs)))
    vel, strs, mats, oc, loads, back = call(
        outer_kernel,
        "outer_substeps",
        tuple(planes_of[k] for k in ("vel", "stress", "mats", "oc", "loads"))
        + (shape(n * plan.back_rows, LANES),),
        [vmem] * 9,
        [
            pltpu.VMEM((plan.own_groups, lanes, LANES), F32),
            pltpu.VMEM((n * plan.back_rows, LANES), F32),
            pltpu.SemaphoreType.DMA,
        ],
        outs=(vmem,) * 5 + (hbm,),
        input_output_aliases={4: 0, 5: 1, 6: 2, 7: 3, 8: 4},
    )(*(near(a) for a in (material_rows, other, water, bottom, vel, strs, mats, oc, loads)))
    returned = lax.all_to_all(
        back.reshape(n, plan.back_rows, LANES), "map", split_axis=0, concat_axis=0, tiled=True
    ).reshape(n * plan.back_rows, LANES)
    new_velocity, new_stress = call(
        end_kernel,
        "last_updates",
        (shape(*velocity.shape), shape(*stress.shape)),
        [vmem] * 4,
        [
            pltpu.VMEM((3, width, sub, lanes), F32),
            pltpu.VMEM((6, width, sub, lanes), F32),
        ],
    )(vel, strs, mats, loads)
    new_ocean = call(
        unpack_kernel,
        "ocean_strips",
        shape(*ocean.shape),
        [vmem],
        [
            pltpu.VMEM((plan.strips, plan.nx, LANES), F32),
            pltpu.VMEM((plan.strips, 4, plan.depth, plan.nx), F32),
            pltpu.SemaphoreType.DMA((plan.strips,)),
        ],
        outs=hbm,
    )(returned)
    return new_velocity, new_stress, new_ocean


def solution(mesh):
    n = mesh.shape["map"]

    def body(velocity, stress, ocean, zones, materials, slip, bathy):
        _, cells, depth, ny = velocity.shape
        plan = Plan(n, cells, depth, ny, ocean.shape[1])
        return on_device(plan, velocity, stress, ocean, zones, materials, slip, bathy)

    return jax.shard_map(
        body,
        mesh=mesh,
        in_specs=(
            P("parts", "map", None, None),
            P("parts", "map", None, None),
            P("parts", "map", None, None),
            P("map", "parts", None),
            P(),
            P("map", "parts"),
            P("map", "parts"),
        ),
        out_specs=(
            P("parts", "map", None, None),
            P("parts", "map", None, None),
            P("parts", "map", None, None),
        ),
        check_vma=False,
    )
```

```python
import functools

import jax
import jax.numpy as jnp
from jax import lax
from jax.experimental import pallas as pl
from jax.experimental.pallas import tpu as pltpu
from jax.sharding import PartitionSpec as P

STEPS = 4
ZONES = 8
DT = 0.25
HALF = 0.5 * DT
KBULK = 2.25
GRAV = 0.1
HALO = 2 * STEPS
LANES = 128
F32 = jnp.float32
VX, VY, VZ = range(3)
SXX, SYY, SZZ, SXY, SXZ, SYZ = range(6)
BUOY, LAMB, SHEAR, FAULT, FLOOR = range(5)


class Plan:
    def __init__(self, devices, cells, depth, ny, strips):
        self.n = devices
        self.cells = cells
        self.depth = depth
        self.ny = ny
        self.strips = strips
        self.chunks = max(1, LANES // ny)
        self.sub = depth // self.chunks
        self.lanes = self.chunks * ny
        self.width = cells + 2 * HALO
        self.own_groups = cells // self.chunks
        self.halo_groups = HALO // self.chunks
        self.sent_groups = self.own_groups + self.halo_groups
        self.lead = self.chunks * strips
        self.rows = self.lead * self.sent_groups
        self.back_rows = self.lead * self.own_groups
        self.nx = devices * cells
        self.block = 4 * self.sub
        self.unrolled = self.sub * self.lanes <= 1024
        assert devices % 2 == 0 and cells == HALO and self.block * self.chunks == LANES

    def planes(self, start, stop, body, batch=1):
        if self.unrolled:
            for j in range(start, stop, batch):
                body(j, min(batch, stop - j))
        else:
            def run(j, carry):
                body(j, 1)
                return carry

            lax.fori_loop(start, stop, run, 0)


BATCH = 8
SLOTS = 16


def slot_rows(plan):
    return BATCH * 2 * (plan.sub + 2)


def odd_device():
    return lax.rem(lax.axis_index("map"), 2)


def place(pieces, wanted, block):
    out = None
    for i, piece in enumerate(pieces):
        shift = (i - wanted[i]) * block % piece.shape[-1]
        moved = pltpu.roll(piece, shift, piece.ndim - 1) if shift else piece
        if out is None:
            out = moved
        else:
            lane = lax.broadcasted_iota(jnp.int32, moved.shape, moved.ndim - 1)
            out = jnp.where(lane >= i * block, moved, out)
    return out


def ocean_kernel(
    plan, vel_ref, stress_ref, zones_ref, slip_ref, ocean_ref, bathy_ref,
    message_out, vel, stress, zones, slip, ocean, bathy, turned, grouped, extra, message, sems,
):
    cells, sub, chunks = plan.cells, plan.sub, plan.chunks
    n, strips, block, sent, rows = plan.n, plan.strips, plan.block, plan.sent_groups, plan.rows
    pairs = (
        (ocean_ref, ocean),
        (bathy_ref, bathy),
        (vel_ref, vel),
        (stress_ref, stress),
        (zones_ref, zones),
        (slip_ref, slip),
    )
    copies = [
        pltpu.make_async_copy(source, target, sems.at[i])
        for i, (source, target) in enumerate(pairs)
    ]
    for copy in copies:
        copy.start()
    copies[0].wait()
    copies[1].wait()
    count = plan.nx // chunks
    lead = plan.lead
    pad = plan.halo_groups * lead
    grouped[:pad, :] = jnp.zeros((pad, LANES), F32)
    grouped[pad + count * lead :, :] = jnp.zeros((pad, LANES), F32)
    for yl in range(strips):
        stacked = jnp.concatenate(
            [ocean[f, yl, kc * sub : (kc + 1) * sub, :] for kc in range(chunks) for f in range(4)],
            axis=0,
        )
        turned[yl] = stacked.T
        by_x = [turned[yl, pl.ds(i, count, stride=chunks), :] for i in range(chunks)]
        for kc in range(chunks):
            grouped[pl.ds(pad + kc * strips + yl, count, stride=lead), :] = place(
                by_x, [kc] * chunks, block
            )
    for d in range(n):
        start = (d * plan.own_groups + (d % 2) * plan.halo_groups) * lead
        message[d * rows : (d + 1) * rows, :] = grouped[start : start + rows, :]
    depths = bathy[...].astype(F32)
    wide = lax.broadcasted_iota(jnp.int32, depths.shape, 1)
    for d in range(n):
        first = d * cells - HALO - 1
        moved = pltpu.roll(depths, -first % plan.nx, 1)
        moved = jnp.where((wide + first >= 0) & (wide + first < plan.nx), moved, 0.0)
        extra[d * strips : (d + 1) * strips, :] = moved[:, :LANES]
    pairs = n // 2
    lane = lax.broadcasted_iota(jnp.int32, (pairs, LANES), 1)
    blank = jnp.zeros((1, LANES), F32)
    for odd in range(2):
        slot = (odd * (chunks - 1) * 4 + 2) * sub
        group = odd * (sent - 1)
        for yl in range(strips):
            if odd:
                column = turned[yl, pl.ds(2 * cells + HALO, pairs - 1, stride=2 * cells), :]
                column = jnp.concatenate([column, blank], axis=0)
            else:
                column = turned[yl, pl.ds(2 * cells - HALO - 1, pairs - 1, stride=2 * cells), :]
                column = jnp.concatenate([blank, column], axis=0)
            deep = extra[pl.ds(odd * strips + yl, pairs, stride=2 * strips), :]
            for kc in range(chunks):
                at = odd * rows + group * lead + kc * strips + yl
                old = message[pl.ds(at, pairs, stride=2 * rows), :]
                edge = pltpu.roll(column, (slot - kc * block) % LANES, 1)
                floor = pltpu.roll(deep, (slot + sub - kc * sub) % LANES, 1)
                new = jnp.where((lane >= slot) & (lane < slot + sub), edge, old)
                new = jnp.where((lane >= slot + sub) & (lane < slot + 2 * sub), floor, new)
                message[pl.ds(at, pairs, stride=2 * rows), :] = new
    message_out[...] = message[...]
    for copy in copies[2:]:
        copy.wait()


def crust_kernel(plan, vel, stress, zones, slip, crust, border):
    cells, sub, chunks, ny = plan.cells, plan.sub, plan.chunks, plan.ny

    def joined(ref, *at):
        parts = [ref[(*at, pl.ds(kc * sub, sub), slice(None))] for kc in range(chunks)]
        return jnp.concatenate(parts, axis=-1) if chunks > 1 else parts[0]

    for f in range(3):
        for x in range(cells):
            crust[f * cells + x] = joined(vel, f, x)
    for f in range(6):
        for x in range(cells):
            crust[(3 + f) * cells + x] = joined(stress, f, x)
    for x in range(cells):
        crust[9 * cells + x] = (joined(zones, x) + 1).astype(F32)
    fault_chunk = (plan.depth // 2) // sub
    pieces = [
        slip[...] if kc == fault_chunk else jnp.zeros((cells, ny), F32) for kc in range(chunks)
    ]
    fault = jnp.concatenate(pieces, axis=-1) if chunks > 1 else pieces[0]
    if sub > cells:
        fault = jnp.concatenate([fault, jnp.zeros((sub - cells, plan.lanes), F32)], axis=0)
    crust[10 * cells] = fault
    odd = odd_device()
    near = cells - 1
    for f in range(10):
        for i in range(near):
            border[f * near + i] = crust[f * cells + i + odd]
    for i, f in enumerate((SXX, SXY, SXZ)):
        border[10 * near + i] = crust[(3 + f) * cells + near * (1 - odd)]
    border[10 * near + 3] = fault


class Shifts:
    def __init__(self, plan, memory=None):
        self.plan = plan
        self.memory = memory if plan.unrolled else None
        self.slot = 0
        shape = (plan.sub, plan.lanes)
        self.row = lax.broadcasted_iota(jnp.int32, shape, 0)
        self.lane = lax.broadcasted_iota(jnp.int32, shape, 1)
        self.y = lax.rem(self.lane, plan.ny)
        self.first_row = self.row == 0
        self.last_row = self.row == plan.sub - 1
        self.top = self.first_row & (self.lane < plan.ny)
        self.floor_cell = self.last_row & (self.lane >= plan.lanes - plan.ny)
        self.not_low_y = jnp.where(self.y == 0, 0.0, 1.0).astype(F32)
        self.not_high_y = jnp.where(self.y == plan.ny - 1, 0.0, 1.0).astype(F32)
        self.depth = (
            lax.div(self.lane, plan.ny) * plan.sub + self.row
        ).astype(F32)

    def by_lane(self, f, shift):
        return pltpu.roll(f, shift % self.plan.lanes, f.ndim - 1)

    def by_row(self, f, shift):
        return pltpu.roll(f, shift % self.plan.sub, f.ndim - 2)

    def dy(self, f):
        return self.by_lane(f, -1) * self.not_high_y - self.by_lane(f, 1) * self.not_low_y

    def below(self, f):
        plan = self.plan
        moved = self.by_row(f, -1)
        if plan.chunks > 1:
            moved = jnp.where(self.last_row, self.by_lane(moved, -plan.ny), moved)
        return jnp.where(self.floor_cell, 0.0, moved)

    def above(self, f, top):
        plan = self.plan
        moved = self.by_row(f, 1)
        if plan.chunks > 1:
            moved = jnp.where(self.first_row, self.by_lane(moved, plan.ny), moved)
        return jnp.where(self.top, top, moved)

    def block(self):
        start = self.slot * slot_rows(self.plan)
        self.slot = (self.slot + 1) % SLOTS
        return start

    def dz(self, f, top):
        if self.memory is None or f.ndim == 2:
            return self.below(f) - self.above(f, top * f if top else 0.0)
        plan, memory = self.plan, self.memory
        count, sub = f.shape[:2]
        start, size = self.block(), 2 * (sub + 2)
        for i in range(count):
            memory[pl.ds(start + i * size + 2, sub, stride=2), :] = f[i]
        lane = lax.broadcasted_iota(jnp.int32, (count, plan.lanes), 1)
        first = memory[pl.ds(start + 2, count, stride=size), :]
        last = memory[pl.ds(start + 2 * sub, count, stride=size), :]
        after = jnp.where(lane < plan.lanes - plan.ny, self.by_lane(first, -plan.ny), 0.0)
        before = jnp.where(lane >= plan.ny, self.by_lane(last, plan.ny), top * first)
        memory[pl.ds(start, count, stride=size), :] = before
        memory[pl.ds(start + 2 * (sub + 1), count, stride=size), :] = after
        return jnp.stack(
            [
                memory[pl.ds(start + i * size + 4, sub, stride=2), :]
                - memory[pl.ds(start + i * size, sub, stride=2), :]
                for i in range(count)
            ]
        )

    def spread_rows(self, start, rows):
        plan, memory = self.plan, self.memory
        count = rows.shape[0]
        memory[pl.ds(start, count), :] = rows
        return jnp.stack(
            [
                jnp.broadcast_to(memory[pl.ds(start + i, 1), :], (plan.sub, plan.lanes))
                for i in range(count)
            ]
        )

    def seafloor(self, vz):
        if self.memory is None or vz.ndim == 2:
            row = self.over_chunks(jnp.where(self.top, vz, 0.0))
            return jnp.broadcast_to(row[..., 0:1, :], vz.shape)
        memory, start = self.memory, self.block()
        count, sub, lanes = vz.shape
        for i in range(count):
            memory[pl.ds(start + i * sub, sub), :] = vz[i]
        rows = memory[pl.ds(start, count, stride=sub), :]
        lane = lax.broadcasted_iota(jnp.int32, rows.shape, 1)
        rows = self.over_chunks(jnp.where(lane < self.plan.ny, rows, 0.0))
        return self.spread_rows(start + BATCH * sub, rows)

    def on_top(self, f):
        if self.memory is None or f.ndim == 2:
            shift = self.plan.sub // 2
            while shift:
                f = f + self.by_row(f, shift)
                shift //= 2
            return jnp.where(self.top, self.over_chunks(f), 0.0)
        memory, start = self.memory, self.block()
        count, sub, lanes = f.shape
        for i in range(count):
            memory[pl.ds(start + i * sub, sub), :] = f[i]
        rows = memory[pl.ds(start, count, stride=sub), :]
        for k in range(1, sub):
            rows = rows + memory[pl.ds(start + k, count, stride=sub), :]
        rows = self.spread_rows(start + BATCH * sub, self.over_chunks(rows))
        return jnp.where(self.top, rows, 0.0)

    def over_chunks(self, f):
        shift = self.plan.ny
        while shift < self.plan.lanes:
            f = f + self.by_lane(f, shift)
            shift *= 2
        return f


def acceleration(sh, stress, j, count):
    at, before, after = (pl.ds(j + k, count) for k in (0, -1, 1))
    sxy, sxz = stress[SXY, at], stress[SXZ, at]
    ax = stress[SXX, after] - stress[SXX, before] + sh.dy(sxy) + sh.dz(sxz, 0.0)
    syz = stress[SYZ, at]
    ay = stress[SXY, after] - stress[SXY, before] + sh.dy(stress[SYY, at])
    ay = ay + sh.dz(syz, 0.0)
    szz = stress[SZZ, at]
    az = stress[SXZ, after] - stress[SXZ, before] + sh.dy(syz) + sh.dz(szz, 0.0)
    return ax, ay, az


def strained(sh, vel, stress, mats, j, count):
    at, before, after = (pl.ds(j + k, count) for k in (0, -1, 1))
    vx, vy, vz = vel[VX, at], vel[VY, at], vel[VZ, at]
    exx = vel[VX, after] - vel[VX, before]
    eyy = sh.dy(vy)
    ezz = sh.dz(vz, 1.0)
    mu = mats[SHEAR, at]
    mu2 = mu + mu
    common = mats[LAMB, at] * (exx + eyy + ezz)
    yield SXX, stress[SXX, at] + (common + mu2 * exx)
    yield SYY, stress[SYY, at] + (common + mu2 * eyy)
    yield SZZ, stress[SZZ, at] + (common + mu2 * ezz)
    exy = sh.dy(vx) + vel[VY, after] - vel[VY, before]
    yield SXY, stress[SXY, at] + mu * exy
    exz = sh.dz(vx, 1.0) + vel[VZ, after] - vel[VZ, before]
    yield SXZ, stress[SXZ, at] + (mu * exz + mats[FAULT, at])
    eyz = sh.dz(vy, 1.0) + sh.dy(vz)
    yield SYZ, stress[SYZ, at] + mu * eyz


def bring(plan, sh, material, state, ref, fields, x, count, column, first):
    vel, stress, mats = state
    to = pl.ds(column, count)

    def read(f):
        return ref[pl.ds(f * fields + x, count)]

    for f in range(3):
        vel[f, to] = read(f)
    for f in range(6):
        stress[f, to] = read(3 + f)
    zone = read(9)
    values = [jnp.zeros_like(zone) for _ in range(3)]
    for z in range(ZONES):
        here = zone == float(z + 1)
        values = [jnp.where(here, material(c, z), values[c]) for c in range(3)]
    for c in range(3):
        mats[c, to] = values[c] * HALF
    mats[FLOOR, to] = sh.seafloor(read(VZ))
    for i in range(count):
        slip = ref[ref.shape[0] - 1, pl.ds(first + x + i, 1), :]
        slip = jnp.broadcast_to(slip, (plan.sub, plan.lanes))
        mats[FAULT, column + i] = jnp.where(
            sh.row == (plan.depth // 2) % plan.sub, DT * slip, 0.0
        )


def begin_kernel(plan, table, own, mate, vel, stress, mats, rows):
    cells = plan.cells
    sh = Shifts(plan)
    odd = odd_device()
    state = (vel, stress, mats)
    starts = (HALO + cells * odd, HALO + cells * (1 - odd))
    for start, ref in zip(starts, (own, mate)):
        plan.planes(
            0,
            cells,
            lambda x, count, start=start, ref=ref: bring(
                plan, sh, lambda c, z: table[c, z], state, ref, cells, x, count, start + x, 0
            ),
            BATCH,
        )

    def move(j, count):
        at = pl.ds(j, count)
        b = mats[BUOY, at]
        for f, a in enumerate(acceleration(sh, stress, j, count)):
            vel[f, at] = vel[f, at] + b * a

    plan.planes(HALO + 1, HALO + 2 * cells - 1, move, BATCH)
    for c in range(3):
        for z in range(ZONES):
            at = c * ZONES + z
            rows[at : at + 1, :] = jnp.full((1, plan.lanes), table[c, z], F32)


class Updates:
    def __init__(self, plan, sh, vel, stress, mats, oc, water, bottom, loads):
        self.plan, self.sh = plan, sh
        self.vel, self.stress, self.mats = vel, stress, mats
        self.oc, self.water, self.bottom, self.loads = oc, water, bottom, loads

    def flow_x(self, j, count):
        oc = self.oc
        before, at, after = (pl.ds(j + k, count) for k in range(3))
        oc[1, at] = self.water[at] * (oc[1, at] - HALF * (oc[0, after] - oc[0, before]))

    def flow(self, j, count):
        oc, sh = self.oc, self.sh
        at = pl.ds(j + 1, count)
        p = oc[0, at]
        wet = self.water[at]
        rise = sh.dz(p, -1.0) + self.bottom[at] * p
        oc[3, at] = wet * (oc[3, at] - (HALF * rise + (DT * GRAV) * p))
        oc[2, at] = wet * (oc[2, at] - HALF * sh.dy(p))

    def press(self, j, count, floor):
        oc, sh = self.oc, self.sh
        before, at, after = (pl.ds(j + k, count) for k in range(3))
        w = oc[3, at]
        rise = sh.dz(w, 1.0)
        if floor is not None:
            rise = rise + self.bottom[at] * floor(pl.ds(j, count))
        total = oc[1, after] - oc[1, before] + sh.dy(oc[2, at]) + rise
        oc[0, at] = self.water[at] * (oc[0, at] - (HALF * KBULK) * total)

    def add_floor(self, j, count):
        at = pl.ds(j + 1, count)
        floor = self.first_floor(pl.ds(j, count))
        self.oc[0, at] = self.oc[0, at] - (HALF * KBULK) * (self.bottom[at] * floor)

    def first_floor(self, at):
        return self.mats[FLOOR, at]

    def floor(self, at):
        return self.sh.seafloor(self.vel[VZ, at])

    def load(self, j, count):
        at = pl.ds(j + 1, count)
        return self.sh.on_top(self.bottom[at] * self.oc[0, at])

    def keep(self, j, count):
        self.loads[pl.ds(j, count)] = self.load(j, count)

    def add_load(self, j, count):
        at = pl.ds(j, count)
        self.vel[VZ, at] = self.vel[VZ, at] + self.mats[BUOY, at] * self.load(j, count)

    def move(self, j, count):
        vel = self.vel
        at = pl.ds(j, count)
        ax, ay, az = acceleration(self.sh, self.stress, j, count)
        b = self.mats[BUOY, at]
        vel[VX, at] = vel[VX, at] + b * ax
        vel[VY, at] = vel[VY, at] + b * ay
        vel[VZ, at] = vel[VZ, at] + b * (az + self.load(j, count))

    def strain(self, j, count):
        for f, value in strained(self.sh, self.vel, self.stress, self.mats, j, count):
            self.stress[f, pl.ds(j, count)] = value

    def run(self, spans, inner, send=None):
        for t in range(STEPS):
            def planes(inset, update, t=t):
                self.plan.planes(*spans(t, inset), update, BATCH)

            if t:
                planes(0, self.flow_x)
                planes(1, self.flow)
                planes(1, functools.partial(self.press, floor=self.floor))
            elif inner:
                columns = self.vel.shape[1]
                first, last = spans(0, 1)
                self.plan.planes(0, columns, self.flow_x, BATCH)
                self.plan.planes(1, columns - 1, self.flow, BATCH)
                planes(1, functools.partial(self.press, floor=self.first_floor))
                self.plan.planes(1, first, functools.partial(self.press, floor=None), BATCH)
                self.plan.planes(
                    last, columns - 1, functools.partial(self.press, floor=None), BATCH
                )
            else:
                planes(1, self.add_floor)
            if t == STEPS - 1:
                if send is not None:
                    send()
                planes(1, self.keep)
            elif t == 0 and inner:
                planes(1, self.add_load)
            else:
                planes(1, self.move)
            if t < STEPS - 2:
                planes(2, self.strain)


def inner_kernel(
    plan, arrived, swapped, mats, vel_in, stress_in, vel, stress, oc, water, bottom, loads,
    gather, depths, memory,
):
    sub, chunks, n, strips = plan.sub, plan.chunks, plan.n, plan.strips
    cells, sent = plan.cells, plan.sent_groups
    sh = Shifts(plan, memory)
    odd = odd_device()
    half = n // 2
    columns = 2 * cells + 2 * HALO

    def turn(owner, group):
        for core, ref in ((odd, arrived), (1 - odd, swapped)):
            for kc in range(chunks):
                for yl in range(strips):
                    at = owner * plan.rows + group * plan.lead + kc * strips + yl
                    to = kc * plan.ny + core * strips + yl
                    gather[pl.ds(to, half, stride=2 * strips), :] = ref[
                        pl.ds(at, half, stride=2 * plan.rows), :
                    ]
        return gather[...].T

    deeps = []
    for owner in range(2):
        for group in range(sent):
            turned = turn(owner, group)
            for i in range(chunks):
                for f in range(4):
                    at = (i * 4 + f) * sub
                    column = 1 + owner * (cells + HALO) + group * chunks + i
                    oc[f, column] = turned[at : at + sub]
            if owner == 0 and group == 0:
                oc[0, 0] = turned[2 * sub : 3 * sub]
                deeps.append(turned[3 * sub : 4 * sub])
            if owner == 1 and group == sent - 1:
                oc[0, columns + 1] = turned[LANES - 2 * sub : LANES - sub]
                deeps.append(turned[LANES - sub :])
    for i, deep in enumerate(deeps):
        for kc in range(chunks):
            mine = (sh.lane >= kc * plan.ny) & (sh.lane < (kc + 1) * plan.ny)
            depths[i, kc * sub : (kc + 1) * sub, :] = sh.over_chunks(jnp.where(mine, deep, 0.0))

    def mask(owner, j, _):
        low = jnp.broadcast_to(depths[owner, pl.ds(j - owner * cells, 1), :], (sub, plan.lanes))
        wet = jnp.where(sh.depth < low, 1.0, 0.0).astype(F32)
        water[j] = wet
        bottom[j] = jnp.where(sh.depth == low - 1.0, 1.0, 0.0).astype(F32)
        oc[0, j] = oc[0, j] * wet

    def mask_x(j, _):
        oc[1, j] = oc[1, j] * water[j]

    def mask_yw(j, _):
        oc[2, j] = oc[2, j] * water[j]
        oc[3, j] = oc[3, j] * water[j]

    plan.planes(0, plan.width + 2, lambda j, _: mask(0, j, _))
    plan.planes(plan.width + 2, columns + 2, lambda j, _: mask(1, j, _))
    plan.planes(1, columns + 1, mask_x)
    plan.planes(2, columns, mask_yw)

    def bring_in(j, _):
        for f in range(3):
            vel[f, j] = vel_in[f, j]
        for f in range(6):
            stress[f, j] = stress_in[f, j]

    if not plan.unrolled:
        plan.planes(HALO, HALO + 2 * cells, bring_in)
    updates = Updates(plan, sh, vel, stress, mats, oc, water, bottom, loads)
    updates.run(lambda t, inset: (HALO + 2 * t + inset, HALO + 2 * cells - 2 * t - inset), True)


def outer_kernel(
    plan, materials, border, water, bottom, vel_in, stress_in, mats_in, oc_in, loads_in,
    vel, stress, mats, oc, loads, message, gather, rows, memory, sem,
):
    sub, chunks, n, strips, cells = plan.sub, plan.chunks, plan.n, plan.strips, plan.cells
    near = cells - 1
    sh = Shifts(plan, memory)
    odd = odd_device()
    if not plan.unrolled:
        for here, there in (
            (vel, vel_in), (stress, stress_in), (mats, mats_in), (oc, oc_in), (loads, loads_in)
        ):
            here[...] = there[...]
    updates = Updates(plan, sh, vel, stress, mats, oc, water, bottom, loads)

    def material(c, z):
        row = materials[pl.ds(c * ZONES + z, 1), :]
        return jnp.broadcast_to(row, (sub, plan.lanes))

    def side(core):
        low, far = ((1, 0), (HALO + 2 * cells, 2 * HALO + 2 * cells - 1))[core]
        state = (vel, stress, mats)
        plan.planes(
            0,
            near,
            lambda x, count: bring(
                plan, sh, material, state, border, near, x, count, low + x, 1 - core
            ),
            BATCH,
        )
        for i, f in enumerate((SXX, SXY, SXZ)):
            stress[f, far] = border[10 * near + i]

        def spans(t, inset):
            if core == 0:
                return 2 * t + inset, 2 * t + inset + HALO
            last = 2 * HALO + 2 * cells - 2 * t - inset
            return last - HALO, last

        copy = pltpu.make_async_copy(rows, message, sem)

        def send():
            for group in range(plan.own_groups):
                stacked = jnp.concatenate(
                    [
                        oc[f, 1 + HALO + core * cells + group * chunks + i]
                        for i in range(chunks)
                        for f in range(4)
                    ],
                    axis=0,
                )
                gather[group] = stacked.T
                for kc in range(chunks):
                    for yl in range(strips):
                        at = group * plan.lead + kc * strips + yl
                        rows[pl.ds(at, n, stride=plan.back_rows), :] = gather[
                            group, pl.ds(kc * plan.ny + yl, n, stride=strips), :
                        ]
            copy.start()

        updates.run(spans, False, send)
        copy.wait()

    for core in range(2):
        pl.when(odd == core)(functools.partial(side, core))


def end_kernel(plan, vel_all, stress_all, mats_all, loads_all, vel_out, stress_out, vel, stress):
    cells, sub, chunks, ny = plan.cells, plan.sub, plan.chunks, plan.ny
    sh = Shifts(plan)
    first, last = 2 * (STEPS - 1), plan.width - 2 * (STEPS - 1)
    window = pl.ds(cells * odd_device(), plan.width)
    vel_in, stress_in = vel_all.at[:, window], stress_all.at[:, window]
    mats, loads = mats_all.at[:, window], loads_all.at[window]

    def put(out, f, x, count, planes):
        for kc in range(chunks):
            out[f, pl.ds(x, count), kc * sub : (kc + 1) * sub, :] = planes[
                :, :, kc * ny : (kc + 1) * ny
            ]

    def strain(j, count):
        for f, value in strained(sh, vel_in, stress_in, mats, j, count):
            stress[f, pl.ds(j, count)] = value

    def move(j, count):
        at = pl.ds(j, count)
        ax, ay, az = acceleration(sh, stress, j, count)
        b = mats[BUOY, at]
        for f, a in enumerate((ax, ay, az + loads[at])):
            vel[f, at] = vel_in[f, at] + b * a

    def finish(x, count):
        for f in range(3):
            put(vel_out, f, x, count, vel[f, pl.ds(x + HALO, count)])
        for f, value in strained(sh, vel, stress, mats, x + HALO, count):
            put(stress_out, f, x, count, value)

    plan.planes(first, last, strain, BATCH)
    plan.planes(first + 1, last - 1, move, BATCH)
    plan.planes(0, cells, finish, BATCH)


def unpack_kernel(plan, arrived, ocean, turned, strips, sems):
    sub, chunks = plan.sub, plan.chunks
    block = 4 * sub
    copies = [
        pltpu.make_async_copy(strips.at[yl], ocean.at[:, yl], sems.at[yl])
        for yl in range(plan.strips)
    ]
    for yl in range(plan.strips):
        by_chunk = [
            arrived[pl.ds(kc * plan.strips + yl, plan.nx // chunks, stride=plan.lead), :]
            for kc in range(chunks)
        ]
        for i in range(chunks):
            turned[yl, pl.ds(i, plan.nx // chunks, stride=chunks), :] = place(
                by_chunk, [i] * chunks, block
            )
        whole = turned[yl].T
        for kc in range(chunks):
            for f in range(4):
                at = (kc * 4 + f) * sub
                strips[yl, f, kc * sub : (kc + 1) * sub, :] = whole[at : at + sub]
        copies[yl].start()
    for copy in copies:
        copy.wait()


def on_device(plan, velocity, stress, ocean, zones, materials, slip, bathy):
    n, cells, sub, lanes, width = plan.n, plan.cells, plan.sub, plan.lanes, plan.width
    vmem = pl.BlockSpec(memory_space=pltpu.VMEM)
    smem = pl.BlockSpec(memory_space=pltpu.SMEM)
    hbm = pl.BlockSpec(memory_space=pltpu.HBM)

    def shape(*dims):
        return jax.ShapeDtypeStruct(dims, F32)

    def like(array):
        return jax.ShapeDtypeStruct(array.shape, array.dtype)

    def held(array):
        return pltpu.VMEM(array.shape, array.dtype)

    def call(kernel, name, out, ins, scratch, room=16, outs=None, **rest):
        room = room if plan.unrolled else 56
        return pl.pallas_call(
            functools.partial(kernel, plan),
            out_shape=out,
            in_specs=ins,
            out_specs=jax.tree.map(lambda _: vmem, out) if outs is None else outs,
            scratch_shapes=scratch,
            compiler_params=pltpu.CompilerParams(vmem_limit_bytes=room * 1024 * 1024),
            name=name,
            **rest,
        )

    def pinned(array):
        return pltpu.with_memory_space_constraint(array, pltpu.HBM)

    def near(array):
        return pltpu.with_memory_space_constraint(array, pltpu.VMEM) if plan.unrolled else array

    mates = [(i, i ^ 1) for i in range(n)]
    others = [(i, i + 1) for i in range(1, n - 1, 2)]
    others += [(target, source) for source, target in others]
    crust_args = (velocity, stress, zones, slip)
    message, *near_args = call(
        ocean_kernel,
        "ocean_rows",
        (shape(n * plan.rows, LANES), *(like(a) for a in crust_args)),
        [hbm] * 6,
        [
            held(ocean),
            held(bathy),
            pltpu.VMEM((plan.strips, plan.nx, LANES), F32),
            pltpu.VMEM(
                ((plan.nx // plan.chunks + 2 * plan.halo_groups) * plan.lead, LANES), F32
            ),
            pltpu.VMEM((n * plan.strips, LANES), F32),
            pltpu.VMEM((n * plan.rows, LANES), F32),
            pltpu.SemaphoreType.DMA((6,)),
        ],
    )(*(pinned(a) for a in (*crust_args, ocean, bathy)))
    arrived = lax.all_to_all(
        message.reshape(n // 2, 2 * plan.rows, LANES),
        "map",
        split_axis=0,
        concat_axis=0,
        axis_index_groups=[list(range(core, n, 2)) for core in range(2)],
        tiled=True,
    ).reshape(n * plan.rows, LANES)
    crust, border = call(
        crust_kernel,
        "crust_planes",
        (shape(10 * cells + 1, sub, lanes), shape(10 * cells - 6, sub, lanes)),
        [vmem] * 4,
        [],
    )(*near_args)
    other = lax.ppermute(border, "map", others)
    mate = lax.ppermute(crust, "map", mates)
    columns = 2 * cells + 2 * HALO
    vel, strs, mats, material_rows = call(
        begin_kernel,
        "first_velocity",
        (
            shape(3, columns, sub, lanes),
            shape(6, columns, sub, lanes),
            shape(5, columns, sub, lanes),
            shape(3 * ZONES, lanes),
        ),
        [smem] + [vmem] * 2,
        [],
    )(materials, crust, mate)
    arrived, vel = lax.optimization_barrier((arrived, vel))
    swapped = lax.ppermute(arrived, "map", mates)
    planes_of = {
        "vel": shape(3, columns, sub, lanes),
        "stress": shape(6, columns, sub, lanes),
        "mats": shape(5, columns, sub, lanes),
        "oc": shape(4, columns + 2, sub, lanes),
        "mask": shape(columns + 2, sub, lanes),
        "loads": shape(columns, sub, lanes),
    }
    vel, strs, oc, water, bottom, loads = call(
        inner_kernel,
        "inner_substeps",
        tuple(planes_of[k] for k in ("vel", "stress", "oc", "mask", "mask", "loads")),
        [vmem] * 5,
        [
            pltpu.VMEM((lanes, LANES), F32),
            pltpu.VMEM((2, plan.depth, lanes), F32),
            pltpu.VMEM((SLOTS * slot_rows(plan), lanes), F32),
        ],
        input_output_aliases={3: 0, 4: 1},
    )(*(near(a) for a in (arrived, swapped, mats, vel, strs)))
    vel, strs, mats, oc, loads, back = call(
        outer_kernel,
        "outer_substeps",
        tuple(planes_of[k] for k in ("vel", "stress", "mats", "oc", "loads"))
        + (shape(n * plan.back_rows, LANES),),
        [vmem] * 9,
        [
            pltpu.VMEM((plan.own_groups, lanes, LANES), F32),
            pltpu.VMEM((n * plan.back_rows, LANES), F32),
            pltpu.VMEM((SLOTS * slot_rows(plan), lanes), F32),
            pltpu.SemaphoreType.DMA,
        ],
        outs=(vmem,) * 5 + (hbm,),
        input_output_aliases={4: 0, 5: 1, 6: 2, 7: 3, 8: 4},
    )(*(near(a) for a in (material_rows, other, water, bottom, vel, strs, mats, oc, loads)))
    returned = lax.all_to_all(
        back.reshape(n, plan.back_rows, LANES), "map", split_axis=0, concat_axis=0, tiled=True
    ).reshape(n * plan.back_rows, LANES)
    new_velocity, new_stress = call(
        end_kernel,
        "last_updates",
        (shape(*velocity.shape), shape(*stress.shape)),
        [vmem] * 4,
        [
            pltpu.VMEM((3, width, sub, lanes), F32),
            pltpu.VMEM((6, width, sub, lanes), F32),
        ],
    )(vel, strs, mats, loads)
    new_ocean = call(
        unpack_kernel,
        "ocean_strips",
        shape(*ocean.shape),
        [vmem],
        [
            pltpu.VMEM((plan.strips, plan.nx, LANES), F32),
            pltpu.VMEM((plan.strips, 4, plan.depth, plan.nx), F32),
            pltpu.SemaphoreType.DMA((plan.strips,)),
        ],
        outs=hbm,
    )(returned)
    return new_velocity, new_stress, new_ocean


def solution(mesh):
    n = mesh.shape["map"]

    def body(velocity, stress, ocean, zones, materials, slip, bathy):
        _, cells, depth, ny = velocity.shape
        plan = Plan(n, cells, depth, ny, ocean.shape[1])
        return on_device(plan, velocity, stress, ocean, zones, materials, slip, bathy)

    return jax.shard_map(
        body,
        mesh=mesh,
        in_specs=(
            P("parts", "map", None, None),
            P("parts", "map", None, None),
            P("parts", "map", None, None),
            P("map", "parts", None),
            P(),
            P("map", "parts"),
            P("map", "parts"),
        ),
        out_specs=(
            P("parts", "map", None, None),
            P("parts", "map", None, None),
            P("parts", "map", None, None),
        ),
        check_vma=False,
    )
```

```python
import functools

import jax
import jax.numpy as jnp
from jax import lax
from jax.experimental import pallas as pl
from jax.experimental.pallas import tpu as pltpu
from jax.sharding import PartitionSpec as P

STEPS = 4
ZONES = 8
DT = 0.25
HALF = 0.5 * DT
KBULK = 2.25
GRAV = 0.1
HALO = 2 * STEPS
LANES = 128
F32 = jnp.float32
VX, VY, VZ = range(3)
SXX, SYY, SZZ, SXY, SXZ, SYZ = range(6)
BUOY, LAMB, SHEAR, FAULT, FLOOR = range(5)


class Plan:
    def __init__(self, devices, cells, depth, ny, strips):
        self.n = devices
        self.cells = cells
        self.depth = depth
        self.ny = ny
        self.strips = strips
        self.chunks = max(1, LANES // ny)
        self.sub = depth // self.chunks
        self.lanes = self.chunks * ny
        self.width = cells + 2 * HALO
        self.own_groups = cells // self.chunks
        self.halo_groups = HALO // self.chunks
        self.sent_groups = self.own_groups + self.halo_groups
        self.lead = self.chunks * strips
        self.rows = self.lead * self.sent_groups
        self.back_rows = self.lead * self.own_groups
        self.nx = devices * cells
        self.block = 4 * self.sub
        self.unrolled = self.sub * self.lanes <= 1024
        assert devices % 2 == 0 and cells == HALO and self.block * self.chunks == LANES

    def planes(self, start, stop, body, batch=1):
        if self.unrolled:
            for j in range(start, stop, batch):
                body(j, min(batch, stop - j))
        else:
            def run(j, carry):
                body(j, 1)
                return carry

            lax.fori_loop(start, stop, run, 0)


BATCH = 8
SLOTS = 16


def slot_rows(plan):
    return BATCH * 2 * (plan.sub + 2)


def odd_device():
    return lax.rem(lax.axis_index("map"), 2)


def place(pieces, wanted, block):
    out = None
    for i, piece in enumerate(pieces):
        shift = (i - wanted[i]) * block % piece.shape[-1]
        moved = pltpu.roll(piece, shift, piece.ndim - 1) if shift else piece
        if out is None:
            out = moved
        else:
            lane = lax.broadcasted_iota(jnp.int32, moved.shape, moved.ndim - 1)
            out = jnp.where(lane >= i * block, moved, out)
    return out


def ocean_kernel(
    plan, vel_ref, stress_ref, zones_ref, slip_ref, ocean_ref, bathy_ref,
    message_out, vel, stress, zones, slip, ocean, bathy, turned, grouped, extra, message, sems,
):
    cells, sub, chunks = plan.cells, plan.sub, plan.chunks
    n, strips, block, sent, rows = plan.n, plan.strips, plan.block, plan.sent_groups, plan.rows
    pairs = (
        (ocean_ref, ocean),
        (bathy_ref, bathy),
        (vel_ref, vel),
        (stress_ref, stress),
        (zones_ref, zones),
        (slip_ref, slip),
    )
    copies = [
        pltpu.make_async_copy(source, target, sems.at[i])
        for i, (source, target) in enumerate(pairs)
    ]
    for copy in copies:
        copy.start()
    copies[0].wait()
    copies[1].wait()
    count = plan.nx // chunks
    lead = plan.lead
    pad = plan.halo_groups * lead
    grouped[:pad, :] = jnp.zeros((pad, LANES), F32)
    grouped[pad + count * lead :, :] = jnp.zeros((pad, LANES), F32)
    for yl in range(strips):
        stacked = jnp.concatenate(
            [ocean[f, yl, kc * sub : (kc + 1) * sub, :] for kc in range(chunks) for f in range(4)],
            axis=0,
        )
        turned[yl] = stacked.T
        by_x = [turned[yl, pl.ds(i, count, stride=chunks), :] for i in range(chunks)]
        for kc in range(chunks):
            grouped[pl.ds(pad + kc * strips + yl, count, stride=lead), :] = place(
                by_x, [kc] * chunks, block
            )
    for d in range(n):
        start = (d * plan.own_groups + (d % 2) * plan.halo_groups) * lead
        message[d * rows : (d + 1) * rows, :] = grouped[start : start + rows, :]
    depths = bathy[...].astype(F32)
    wide = lax.broadcasted_iota(jnp.int32, depths.shape, 1)
    for d in range(n):
        first = d * cells - HALO - 1
        moved = pltpu.roll(depths, -first % plan.nx, 1)
        moved = jnp.where((wide + first >= 0) & (wide + first < plan.nx), moved, 0.0)
        extra[d * strips : (d + 1) * strips, :] = moved[:, :LANES]
    pairs = n // 2
    lane = lax.broadcasted_iota(jnp.int32, (pairs, LANES), 1)
    blank = jnp.zeros((1, LANES), F32)
    for odd in range(2):
        slot = (odd * (chunks - 1) * 4 + 2) * sub
        group = odd * (sent - 1)
        for yl in range(strips):
            if odd:
                column = turned[yl, pl.ds(2 * cells + HALO, pairs - 1, stride=2 * cells), :]
                column = jnp.concatenate([column, blank], axis=0)
            else:
                column = turned[yl, pl.ds(2 * cells - HALO - 1, pairs - 1, stride=2 * cells), :]
                column = jnp.concatenate([blank, column], axis=0)
            deep = extra[pl.ds(odd * strips + yl, pairs, stride=2 * strips), :]
            for kc in range(chunks):
                at = odd * rows + group * lead + kc * strips + yl
                old = message[pl.ds(at, pairs, stride=2 * rows), :]
                edge = pltpu.roll(column, (slot - kc * block) % LANES, 1)
                floor = pltpu.roll(deep, (slot + sub - kc * sub) % LANES, 1)
                new = jnp.where((lane >= slot) & (lane < slot + sub), edge, old)
                new = jnp.where((lane >= slot + sub) & (lane < slot + 2 * sub), floor, new)
                message[pl.ds(at, pairs, stride=2 * rows), :] = new
    out = pltpu.make_async_copy(message, message_out, sems.at[6])
    out.start()
    for copy in copies[2:]:
        copy.wait()
    out.wait()


def crust_kernel(plan, vel, stress, zones, slip, crust, border):
    cells, sub, chunks, ny = plan.cells, plan.sub, plan.chunks, plan.ny

    def joined(ref, *at):
        parts = [ref[(*at, pl.ds(kc * sub, sub), slice(None))] for kc in range(chunks)]
        return jnp.concatenate(parts, axis=-1) if chunks > 1 else parts[0]

    for f in range(3):
        for x in range(cells):
            crust[f * cells + x] = joined(vel, f, x)
    for f in range(6):
        for x in range(cells):
            crust[(3 + f) * cells + x] = joined(stress, f, x)
    for x in range(cells):
        crust[9 * cells + x] = (joined(zones, x) + 1).astype(F32)
    fault_chunk = (plan.depth // 2) // sub
    pieces = [
        slip[...] if kc == fault_chunk else jnp.zeros((cells, ny), F32) for kc in range(chunks)
    ]
    fault = jnp.concatenate(pieces, axis=-1) if chunks > 1 else pieces[0]
    if sub > cells:
        fault = jnp.concatenate([fault, jnp.zeros((sub - cells, plan.lanes), F32)], axis=0)
    crust[10 * cells] = fault
    odd = odd_device()
    near = cells - 1
    for f in range(10):
        for i in range(near):
            border[f * near + i] = crust[f * cells + i + odd]
    for i, f in enumerate((SXX, SXY, SXZ)):
        border[10 * near + i] = crust[(3 + f) * cells + near * (1 - odd)]
    border[10 * near + 3] = fault


class Shifts:
    def __init__(self, plan, memory=None):
        self.plan = plan
        self.memory = memory if plan.unrolled else None
        self.slot = 0
        shape = (plan.sub, plan.lanes)
        self.row = lax.broadcasted_iota(jnp.int32, shape, 0)
        self.lane = lax.broadcasted_iota(jnp.int32, shape, 1)
        self.y = lax.rem(self.lane, plan.ny)
        self.first_row = self.row == 0
        self.last_row = self.row == plan.sub - 1
        self.top = self.first_row & (self.lane < plan.ny)
        self.floor_cell = self.last_row & (self.lane >= plan.lanes - plan.ny)
        self.not_low_y = jnp.where(self.y == 0, 0.0, 1.0).astype(F32)
        self.not_high_y = jnp.where(self.y == plan.ny - 1, 0.0, 1.0).astype(F32)
        self.depth = (
            lax.div(self.lane, plan.ny) * plan.sub + self.row
        ).astype(F32)

    def by_lane(self, f, shift):
        return pltpu.roll(f, shift % self.plan.lanes, f.ndim - 1)

    def by_row(self, f, shift):
        return pltpu.roll(f, shift % self.plan.sub, f.ndim - 2)

    def dy(self, f):
        return self.by_lane(f, -1) * self.not_high_y - self.by_lane(f, 1) * self.not_low_y

    def below(self, f):
        plan = self.plan
        moved = self.by_row(f, -1)
        if plan.chunks > 1:
            moved = jnp.where(self.last_row, self.by_lane(moved, -plan.ny), moved)
        return jnp.where(self.floor_cell, 0.0, moved)

    def above(self, f, top):
        plan = self.plan
        moved = self.by_row(f, 1)
        if plan.chunks > 1:
            moved = jnp.where(self.first_row, self.by_lane(moved, plan.ny), moved)
        return jnp.where(self.top, top, moved)

    def block(self):
        start = self.slot * slot_rows(self.plan)
        self.slot = (self.slot + 1) % SLOTS
        return start

    def dz(self, f, top):
        if self.memory is None or f.ndim == 2:
            return self.below(f) - self.above(f, top * f if top else 0.0)
        plan, memory = self.plan, self.memory
        count, sub = f.shape[:2]
        start, size = self.block(), 2 * (sub + 2)
        for i in range(count):
            memory[pl.ds(start + i * size + 2, sub, stride=2), :] = f[i]
        lane = lax.broadcasted_iota(jnp.int32, (count, plan.lanes), 1)
        first = memory[pl.ds(start + 2, count, stride=size), :]
        last = memory[pl.ds(start + 2 * sub, count, stride=size), :]
        after = jnp.where(lane < plan.lanes - plan.ny, self.by_lane(first, -plan.ny), 0.0)
        before = jnp.where(lane >= plan.ny, self.by_lane(last, plan.ny), top * first)
        memory[pl.ds(start, count, stride=size), :] = before
        memory[pl.ds(start + 2 * (sub + 1), count, stride=size), :] = after
        return jnp.stack(
            [
                memory[pl.ds(start + i * size + 4, sub, stride=2), :]
                - memory[pl.ds(start + i * size, sub, stride=2), :]
                for i in range(count)
            ]
        )

    def spread_rows(self, start, rows):
        plan, memory = self.plan, self.memory
        count = rows.shape[0]
        memory[pl.ds(start, count), :] = rows
        return jnp.stack(
            [
                jnp.broadcast_to(memory[pl.ds(start + i, 1), :], (plan.sub, plan.lanes))
                for i in range(count)
            ]
        )

    def seafloor(self, vz):
        if self.memory is None or vz.ndim == 2:
            row = self.over_chunks(jnp.where(self.top, vz, 0.0))
            return jnp.broadcast_to(row[..., 0:1, :], vz.shape)
        memory, start = self.memory, self.block()
        count, sub, lanes = vz.shape
        for i in range(count):
            memory[pl.ds(start + i * sub, sub), :] = vz[i]
        rows = memory[pl.ds(start, count, stride=sub), :]
        lane = lax.broadcasted_iota(jnp.int32, rows.shape, 1)
        rows = self.over_chunks(jnp.where(lane < self.plan.ny, rows, 0.0))
        return self.spread_rows(start + BATCH * sub, rows)

    def on_top(self, f):
        if self.memory is None or f.ndim == 2:
            shift = self.plan.sub // 2
            while shift:
                f = f + self.by_row(f, shift)
                shift //= 2
            return jnp.where(self.top, self.over_chunks(f), 0.0)
        memory, start = self.memory, self.block()
        count, sub, lanes = f.shape
        for i in range(count):
            memory[pl.ds(start + i * sub, sub), :] = f[i]
        rows = memory[pl.ds(start, count, stride=sub), :]
        for k in range(1, sub):
            rows = rows + memory[pl.ds(start + k, count, stride=sub), :]
        rows = self.spread_rows(start + BATCH * sub, self.over_chunks(rows))
        return jnp.where(self.top, rows, 0.0)

    def over_chunks(self, f):
        shift = self.plan.ny
        while shift < self.plan.lanes:
            f = f + self.by_lane(f, shift)
            shift *= 2
        return f


def acceleration(sh, stress, j, count):
    at, before, after = (pl.ds(j + k, count) for k in (0, -1, 1))
    sxy, sxz = stress[SXY, at], stress[SXZ, at]
    ax = stress[SXX, after] - stress[SXX, before] + sh.dy(sxy) + sh.dz(sxz, 0.0)
    syz = stress[SYZ, at]
    ay = stress[SXY, after] - stress[SXY, before] + sh.dy(stress[SYY, at])
    ay = ay + sh.dz(syz, 0.0)
    szz = stress[SZZ, at]
    az = stress[SXZ, after] - stress[SXZ, before] + sh.dy(syz) + sh.dz(szz, 0.0)
    return ax, ay, az


def strained(sh, vel, stress, mats, j, count):
    at, before, after = (pl.ds(j + k, count) for k in (0, -1, 1))
    vx, vy, vz = vel[VX, at], vel[VY, at], vel[VZ, at]
    exx = vel[VX, after] - vel[VX, before]
    eyy = sh.dy(vy)
    ezz = sh.dz(vz, 1.0)
    mu = mats[SHEAR, at]
    mu2 = mu + mu
    common = mats[LAMB, at] * (exx + eyy + ezz)
    yield SXX, stress[SXX, at] + (common + mu2 * exx)
    yield SYY, stress[SYY, at] + (common + mu2 * eyy)
    yield SZZ, stress[SZZ, at] + (common + mu2 * ezz)
    exy = sh.dy(vx) + vel[VY, after] - vel[VY, before]
    yield SXY, stress[SXY, at] + mu * exy
    exz = sh.dz(vx, 1.0) + vel[VZ, after] - vel[VZ, before]
    yield SXZ, stress[SXZ, at] + (mu * exz + mats[FAULT, at])
    eyz = sh.dz(vy, 1.0) + sh.dy(vz)
    yield SYZ, stress[SYZ, at] + mu * eyz


def bring(plan, sh, material, state, ref, fields, x, count, column, first):
    vel, stress, mats = state
    to = pl.ds(column, count)

    def read(f):
        return ref[pl.ds(f * fields + x, count)]

    for f in range(3):
        vel[f, to] = read(f)
    for f in range(6):
        stress[f, to] = read(3 + f)
    zone = read(9)
    values = [jnp.zeros_like(zone) for _ in range(3)]
    for z in range(ZONES):
        here = zone == float(z + 1)
        values = [jnp.where(here, material(c, z), values[c]) for c in range(3)]
    for c in range(3):
        mats[c, to] = values[c] * HALF
    mats[FLOOR, to] = sh.seafloor(read(VZ))
    for i in range(count):
        slip = ref[ref.shape[0] - 1, pl.ds(first + x + i, 1), :]
        slip = jnp.broadcast_to(slip, (plan.sub, plan.lanes))
        mats[FAULT, column + i] = jnp.where(
            sh.row == (plan.depth // 2) % plan.sub, DT * slip, 0.0
        )


def begin_kernel(plan, table, own, mate, vel, stress, mats, rows):
    cells = plan.cells
    sh = Shifts(plan)
    odd = odd_device()
    state = (vel, stress, mats)
    starts = (HALO + cells * odd, HALO + cells * (1 - odd))
    for start, ref in zip(starts, (own, mate)):
        plan.planes(
            0,
            cells,
            lambda x, count, start=start, ref=ref: bring(
                plan, sh, lambda c, z: table[c, z], state, ref, cells, x, count, start + x, 0
            ),
            BATCH,
        )

    def move(j, count):
        at = pl.ds(j, count)
        b = mats[BUOY, at]
        for f, a in enumerate(acceleration(sh, stress, j, count)):
            vel[f, at] = vel[f, at] + b * a

    plan.planes(HALO + 1, HALO + 2 * cells - 1, move, BATCH)
    for c in range(3):
        for z in range(ZONES):
            at = c * ZONES + z
            rows[at : at + 1, :] = jnp.full((1, plan.lanes), table[c, z], F32)


class Updates:
    def __init__(self, plan, sh, vel, stress, mats, oc, water, bottom, loads):
        self.plan, self.sh = plan, sh
        self.vel, self.stress, self.mats = vel, stress, mats
        self.oc, self.water, self.bottom, self.loads = oc, water, bottom, loads

    def flow_x(self, j, count):
        oc = self.oc
        before, at, after = (pl.ds(j + k, count) for k in range(3))
        oc[1, at] = self.water[at] * (oc[1, at] - HALF * (oc[0, after] - oc[0, before]))

    def flow(self, j, count):
        oc, sh = self.oc, self.sh
        at = pl.ds(j + 1, count)
        p = oc[0, at]
        wet = self.water[at]
        rise = sh.dz(p, -1.0) + self.bottom[at] * p
        oc[3, at] = wet * (oc[3, at] - (HALF * rise + (DT * GRAV) * p))
        oc[2, at] = wet * (oc[2, at] - HALF * sh.dy(p))

    def press(self, j, count, floor):
        oc, sh = self.oc, self.sh
        before, at, after = (pl.ds(j + k, count) for k in range(3))
        w = oc[3, at]
        rise = sh.dz(w, 1.0)
        if floor is not None:
            rise = rise + self.bottom[at] * floor(pl.ds(j, count))
        total = oc[1, after] - oc[1, before] + sh.dy(oc[2, at]) + rise
        oc[0, at] = self.water[at] * (oc[0, at] - (HALF * KBULK) * total)

    def add_floor(self, j, count):
        at = pl.ds(j + 1, count)
        floor = self.first_floor(pl.ds(j, count))
        self.oc[0, at] = self.oc[0, at] - (HALF * KBULK) * (self.bottom[at] * floor)

    def first_floor(self, at):
        return self.mats[FLOOR, at]

    def floor(self, at):
        return self.sh.seafloor(self.vel[VZ, at])

    def load(self, j, count):
        at = pl.ds(j + 1, count)
        return self.sh.on_top(self.bottom[at] * self.oc[0, at])

    def keep(self, j, count):
        self.loads[pl.ds(j, count)] = self.load(j, count)

    def add_load(self, j, count):
        at = pl.ds(j, count)
        self.vel[VZ, at] = self.vel[VZ, at] + self.mats[BUOY, at] * self.load(j, count)

    def move(self, j, count):
        vel = self.vel
        at = pl.ds(j, count)
        ax, ay, az = acceleration(self.sh, self.stress, j, count)
        b = self.mats[BUOY, at]
        vel[VX, at] = vel[VX, at] + b * ax
        vel[VY, at] = vel[VY, at] + b * ay
        vel[VZ, at] = vel[VZ, at] + b * (az + self.load(j, count))

    def strain(self, j, count):
        for f, value in strained(self.sh, self.vel, self.stress, self.mats, j, count):
            self.stress[f, pl.ds(j, count)] = value

    def run(self, spans, inner, send=None):
        def planes(t, inset, update):
            self.plan.planes(*spans(t, inset), update, BATCH)

        def flows(t):
            planes(t, 0, self.flow_x)
            planes(t, 1, self.flow)

        if inner:
            columns = self.vel.shape[1]
            first, last = spans(0, 1)
            self.plan.planes(0, columns, self.flow_x, BATCH)
            self.plan.planes(1, columns - 1, self.flow, BATCH)
            planes(0, 1, functools.partial(self.press, floor=self.first_floor))
            later = functools.partial(self.press, floor=None)
            self.plan.planes(1, first, later, BATCH)
            self.plan.planes(last, columns - 1, later, BATCH)
        else:
            planes(0, 1, self.add_floor)
        for t in range(STEPS - 1):
            flows(t + 1)
            planes(t, 1, self.add_load if inner and t == 0 else self.move)
            if t < STEPS - 2:
                planes(t, 2, self.strain)
            planes(t + 1, 1, functools.partial(self.press, floor=self.floor))
        if send is not None:
            send()
        planes(STEPS - 1, 1, self.keep)


def inner_kernel(
    plan, arrived, swapped, mats, vel_in, stress_in, vel, stress, oc, water, bottom, loads,
    gather, depths, memory,
):
    sub, chunks, n, strips = plan.sub, plan.chunks, plan.n, plan.strips
    cells, sent = plan.cells, plan.sent_groups
    sh = Shifts(plan, memory)
    odd = odd_device()
    half = n // 2
    columns = 2 * cells + 2 * HALO

    def turn(owner, group):
        for core, ref in ((odd, arrived), (1 - odd, swapped)):
            for kc in range(chunks):
                for yl in range(strips):
                    at = owner * plan.rows + group * plan.lead + kc * strips + yl
                    to = kc * plan.ny + core * strips + yl
                    gather[pl.ds(to, half, stride=2 * strips), :] = ref[
                        pl.ds(at, half, stride=2 * plan.rows), :
                    ]
        return gather[...].T

    deeps = []
    for owner in range(2):
        for group in range(sent):
            turned = turn(owner, group)
            for i in range(chunks):
                for f in range(4):
                    at = (i * 4 + f) * sub
                    column = 1 + owner * (cells + HALO) + group * chunks + i
                    oc[f, column] = turned[at : at + sub]
            if owner == 0 and group == 0:
                oc[0, 0] = turned[2 * sub : 3 * sub]
                deeps.append(turned[3 * sub : 4 * sub])
            if owner == 1 and group == sent - 1:
                oc[0, columns + 1] = turned[LANES - 2 * sub : LANES - sub]
                deeps.append(turned[LANES - sub :])
    for i, deep in enumerate(deeps):
        for kc in range(chunks):
            mine = (sh.lane >= kc * plan.ny) & (sh.lane < (kc + 1) * plan.ny)
            depths[i, kc * sub : (kc + 1) * sub, :] = sh.over_chunks(jnp.where(mine, deep, 0.0))

    def mask(owner, j, _):
        low = jnp.broadcast_to(depths[owner, pl.ds(j - owner * cells, 1), :], (sub, plan.lanes))
        wet = jnp.where(sh.depth < low, 1.0, 0.0).astype(F32)
        water[j] = wet
        bottom[j] = jnp.where(sh.depth == low - 1.0, 1.0, 0.0).astype(F32)
        oc[0, j] = oc[0, j] * wet

    def mask_x(j, _):
        oc[1, j] = oc[1, j] * water[j]

    def mask_yw(j, _):
        oc[2, j] = oc[2, j] * water[j]
        oc[3, j] = oc[3, j] * water[j]

    plan.planes(0, plan.width + 2, lambda j, _: mask(0, j, _))
    plan.planes(plan.width + 2, columns + 2, lambda j, _: mask(1, j, _))
    plan.planes(1, columns + 1, mask_x)
    plan.planes(2, columns, mask_yw)

    def bring_in(j, _):
        for f in range(3):
            vel[f, j] = vel_in[f, j]
        for f in range(6):
            stress[f, j] = stress_in[f, j]

    if not plan.unrolled:
        plan.planes(HALO, HALO + 2 * cells, bring_in)
    updates = Updates(plan, sh, vel, stress, mats, oc, water, bottom, loads)
    updates.run(lambda t, inset: (HALO + 2 * t + inset, HALO + 2 * cells - 2 * t - inset), True)


def outer_kernel(
    plan, materials, border, water, bottom, vel_in, stress_in, mats_in, oc_in, loads_in,
    vel, stress, mats, oc, loads, message, gather, rows, memory, sem,
):
    sub, chunks, n, strips, cells = plan.sub, plan.chunks, plan.n, plan.strips, plan.cells
    near = cells - 1
    sh = Shifts(plan, memory)
    odd = odd_device()
    if not plan.unrolled:
        for here, there in (
            (vel, vel_in), (stress, stress_in), (mats, mats_in), (oc, oc_in), (loads, loads_in)
        ):
            here[...] = there[...]
    updates = Updates(plan, sh, vel, stress, mats, oc, water, bottom, loads)

    def material(c, z):
        row = materials[pl.ds(c * ZONES + z, 1), :]
        return jnp.broadcast_to(row, (sub, plan.lanes))

    def side(core):
        low, far = ((1, 0), (HALO + 2 * cells, 2 * HALO + 2 * cells - 1))[core]
        state = (vel, stress, mats)
        plan.planes(
            0,
            near,
            lambda x, count: bring(
                plan, sh, material, state, border, near, x, count, low + x, 1 - core
            ),
            BATCH,
        )
        for i, f in enumerate((SXX, SXY, SXZ)):
            stress[f, far] = border[10 * near + i]

        def spans(t, inset):
            if core == 0:
                return 2 * t + inset, 2 * t + inset + HALO
            last = 2 * HALO + 2 * cells - 2 * t - inset
            return last - HALO, last

        copy = pltpu.make_async_copy(rows, message, sem)

        def send():
            for group in range(plan.own_groups):
                stacked = jnp.concatenate(
                    [
                        oc[f, 1 + HALO + core * cells + group * chunks + i]
                        for i in range(chunks)
                        for f in range(4)
                    ],
                    axis=0,
                )
                gather[group] = stacked.T
                for kc in range(chunks):
                    for yl in range(strips):
                        at = group * plan.lead + kc * strips + yl
                        rows[pl.ds(at, n, stride=plan.back_rows), :] = gather[
                            group, pl.ds(kc * plan.ny + yl, n, stride=strips), :
                        ]
            copy.start()

        updates.run(spans, False, send)
        copy.wait()

    for core in range(2):
        pl.when(odd == core)(functools.partial(side, core))


def end_kernel(plan, vel_all, stress_all, mats_all, loads_all, vel_out, stress_out, vel, stress):
    cells, sub, chunks, ny = plan.cells, plan.sub, plan.chunks, plan.ny
    sh = Shifts(plan)
    first, last = 2 * (STEPS - 1), plan.width - 2 * (STEPS - 1)
    window = pl.ds(cells * odd_device(), plan.width)
    vel_in, stress_in = vel_all.at[:, window], stress_all.at[:, window]
    mats, loads = mats_all.at[:, window], loads_all.at[window]

    def put(out, f, x, count, planes):
        for kc in range(chunks):
            out[f, pl.ds(x, count), kc * sub : (kc + 1) * sub, :] = planes[
                :, :, kc * ny : (kc + 1) * ny
            ]

    def strain(j, count):
        for f, value in strained(sh, vel_in, stress_in, mats, j, count):
            stress[f, pl.ds(j, count)] = value

    def move(j, count):
        at = pl.ds(j, count)
        ax, ay, az = acceleration(sh, stress, j, count)
        b = mats[BUOY, at]
        for f, a in enumerate((ax, ay, az + loads[at])):
            vel[f, at] = vel_in[f, at] + b * a

    def finish(x, count):
        for f in range(3):
            put(vel_out, f, x, count, vel[f, pl.ds(x + HALO, count)])
        for f, value in strained(sh, vel, stress, mats, x + HALO, count):
            put(stress_out, f, x, count, value)

    plan.planes(first, last, strain, BATCH)
    plan.planes(first + 1, last - 1, move, BATCH)
    plan.planes(0, cells, finish, BATCH)


def unpack_kernel(plan, arrived, ocean, turned, strips, sems):
    sub, chunks = plan.sub, plan.chunks
    block = 4 * sub
    copies = [
        pltpu.make_async_copy(strips.at[yl], ocean.at[:, yl], sems.at[yl])
        for yl in range(plan.strips)
    ]
    for yl in range(plan.strips):
        by_chunk = [
            arrived[pl.ds(kc * plan.strips + yl, plan.nx // chunks, stride=plan.lead), :]
            for kc in range(chunks)
        ]
        for i in range(chunks):
            turned[yl, pl.ds(i, plan.nx // chunks, stride=chunks), :] = place(
                by_chunk, [i] * chunks, block
            )
        whole = turned[yl].T
        for kc in range(chunks):
            for f in range(4):
                at = (kc * 4 + f) * sub
                strips[yl, f, kc * sub : (kc + 1) * sub, :] = whole[at : at + sub]
        copies[yl].start()
    for copy in copies:
        copy.wait()


def on_device(plan, velocity, stress, ocean, zones, materials, slip, bathy):
    n, cells, sub, lanes, width = plan.n, plan.cells, plan.sub, plan.lanes, plan.width
    vmem = pl.BlockSpec(memory_space=pltpu.VMEM)
    smem = pl.BlockSpec(memory_space=pltpu.SMEM)
    hbm = pl.BlockSpec(memory_space=pltpu.HBM)

    def shape(*dims):
        return jax.ShapeDtypeStruct(dims, F32)

    def like(array):
        return jax.ShapeDtypeStruct(array.shape, array.dtype)

    def held(array):
        return pltpu.VMEM(array.shape, array.dtype)

    def call(kernel, name, out, ins, scratch, room=16, outs=None, **rest):
        room = room if plan.unrolled else 56
        return pl.pallas_call(
            functools.partial(kernel, plan),
            out_shape=out,
            in_specs=ins,
            out_specs=jax.tree.map(lambda _: vmem, out) if outs is None else outs,
            scratch_shapes=scratch,
            compiler_params=pltpu.CompilerParams(vmem_limit_bytes=room * 1024 * 1024),
            name=name,
            **rest,
        )

    def pinned(array):
        return pltpu.with_memory_space_constraint(array, pltpu.HBM)

    def near(array):
        return pltpu.with_memory_space_constraint(array, pltpu.VMEM) if plan.unrolled else array

    mates = [(i, i ^ 1) for i in range(n)]
    others = [(i, i + 1) for i in range(1, n - 1, 2)]
    others += [(target, source) for source, target in others]
    crust_args = (velocity, stress, zones, slip)
    message, *near_args = call(
        ocean_kernel,
        "ocean_rows",
        (shape(n * plan.rows, LANES), *(like(a) for a in crust_args)),
        [hbm] * 6,
        [
            held(ocean),
            held(bathy),
            pltpu.VMEM((plan.strips, plan.nx, LANES), F32),
            pltpu.VMEM(
                ((plan.nx // plan.chunks + 2 * plan.halo_groups) * plan.lead, LANES), F32
            ),
            pltpu.VMEM((n * plan.strips, LANES), F32),
            pltpu.VMEM((n * plan.rows, LANES), F32),
            pltpu.SemaphoreType.DMA((7,)),
        ],
        outs=(hbm,) + (vmem,) * 4,
    )(*(pinned(a) for a in (*crust_args, ocean, bathy)))
    arrived = lax.all_to_all(
        message.reshape(n // 2, 2 * plan.rows, LANES),
        "map",
        split_axis=0,
        concat_axis=0,
        axis_index_groups=[list(range(core, n, 2)) for core in range(2)],
        tiled=True,
    ).reshape(n * plan.rows, LANES)
    crust, border = call(
        crust_kernel,
        "crust_planes",
        (shape(10 * cells + 1, sub, lanes), shape(10 * cells - 6, sub, lanes)),
        [vmem] * 4,
        [],
    )(*near_args)
    other = lax.ppermute(border, "map", others)
    mate = lax.ppermute(crust, "map", mates)
    columns = 2 * cells + 2 * HALO
    vel, strs, mats, material_rows = call(
        begin_kernel,
        "first_velocity",
        (
            shape(3, columns, sub, lanes),
            shape(6, columns, sub, lanes),
            shape(5, columns, sub, lanes),
            shape(3 * ZONES, lanes),
        ),
        [smem] + [vmem] * 2,
        [],
    )(materials, crust, mate)
    arrived, vel = lax.optimization_barrier((arrived, vel))
    swapped = lax.ppermute(arrived, "map", mates)
    planes_of = {
        "vel": shape(3, columns, sub, lanes),
        "stress": shape(6, columns, sub, lanes),
        "mats": shape(5, columns, sub, lanes),
        "oc": shape(4, columns + 2, sub, lanes),
        "mask": shape(columns + 2, sub, lanes),
        "loads": shape(columns, sub, lanes),
    }
    vel, strs, oc, water, bottom, loads = call(
        inner_kernel,
        "inner_substeps",
        tuple(planes_of[k] for k in ("vel", "stress", "oc", "mask", "mask", "loads")),
        [vmem] * 5,
        [
            pltpu.VMEM((lanes, LANES), F32),
            pltpu.VMEM((2, plan.depth, lanes), F32),
            pltpu.VMEM((SLOTS * slot_rows(plan), lanes), F32),
        ],
        input_output_aliases={3: 0, 4: 1},
    )(*(near(a) for a in (arrived, swapped, mats, vel, strs)))
    vel, strs, mats, oc, loads, back = call(
        outer_kernel,
        "outer_substeps",
        tuple(planes_of[k] for k in ("vel", "stress", "mats", "oc", "loads"))
        + (shape(n * plan.back_rows, LANES),),
        [vmem] * 9,
        [
            pltpu.VMEM((plan.own_groups, lanes, LANES), F32),
            pltpu.VMEM((n * plan.back_rows, LANES), F32),
            pltpu.VMEM((SLOTS * slot_rows(plan), lanes), F32),
            pltpu.SemaphoreType.DMA,
        ],
        outs=(vmem,) * 5 + (hbm,),
        input_output_aliases={4: 0, 5: 1, 6: 2, 7: 3, 8: 4},
    )(*(near(a) for a in (material_rows, other, water, bottom, vel, strs, mats, oc, loads)))
    returned = lax.all_to_all(
        back.reshape(n, plan.back_rows, LANES), "map", split_axis=0, concat_axis=0, tiled=True
    ).reshape(n * plan.back_rows, LANES)
    new_velocity, new_stress = call(
        end_kernel,
        "last_updates",
        (shape(*velocity.shape), shape(*stress.shape)),
        [vmem] * 4,
        [
            pltpu.VMEM((3, width, sub, lanes), F32),
            pltpu.VMEM((6, width, sub, lanes), F32),
        ],
    )(vel, strs, mats, loads)
    new_ocean = call(
        unpack_kernel,
        "ocean_strips",
        shape(*ocean.shape),
        [vmem],
        [
            pltpu.VMEM((plan.strips, plan.nx, LANES), F32),
            pltpu.VMEM((plan.strips, 4, plan.depth, plan.nx), F32),
            pltpu.SemaphoreType.DMA((plan.strips,)),
        ],
        outs=hbm,
    )(returned)
    return new_velocity, new_stress, new_ocean


def solution(mesh):
    n = mesh.shape["map"]

    def body(velocity, stress, ocean, zones, materials, slip, bathy):
        _, cells, depth, ny = velocity.shape
        plan = Plan(n, cells, depth, ny, ocean.shape[1])
        return on_device(plan, velocity, stress, ocean, zones, materials, slip, bathy)

    return jax.shard_map(
        body,
        mesh=mesh,
        in_specs=(
            P("parts", "map", None, None),
            P("parts", "map", None, None),
            P("parts", "map", None, None),
            P("map", "parts", None),
            P(),
            P("map", "parts"),
            P("map", "parts"),
        ),
        out_specs=(
            P("parts", "map", None, None),
            P("parts", "map", None, None),
            P("parts", "map", None, None),
        ),
        check_vma=False,
    )
```

```python
import functools

import jax
import jax.numpy as jnp
from jax import lax
from jax.experimental import pallas as pl
from jax.experimental.pallas import tpu as pltpu
from jax.sharding import PartitionSpec as P

STEPS = 4
ZONES = 8
DT = 0.25
HALF = 0.5 * DT
KBULK = 2.25
GRAV = 0.1
HALO = 2 * STEPS
LANES = 128
F32 = jnp.float32
VX, VY, VZ = range(3)
SXX, SYY, SZZ, SXY, SXZ, SYZ = range(6)
BUOY, LAMB, SHEAR, FAULT, FLOOR = range(5)


class Plan:
    def __init__(self, devices, cells, depth, ny, strips):
        self.n = devices
        self.cells = cells
        self.depth = depth
        self.ny = ny
        self.strips = strips
        self.chunks = max(1, LANES // ny)
        self.sub = depth // self.chunks
        self.lanes = self.chunks * ny
        self.width = cells + 2 * HALO
        self.own_groups = cells // self.chunks
        self.halo_groups = HALO // self.chunks
        self.sent_groups = self.own_groups + self.halo_groups
        self.lead = self.chunks * strips
        self.rows = self.lead * self.sent_groups
        self.back_rows = self.lead * self.own_groups
        self.nx = devices * cells
        self.block = 4 * self.sub
        self.unrolled = self.sub * self.lanes <= 1024
        assert devices % 2 == 0 and cells == HALO and self.block * self.chunks == LANES

    def planes(self, start, stop, body, batch=1):
        if self.unrolled:
            for j in range(start, stop, batch):
                body(j, min(batch, stop - j))
        else:
            def run(j, carry):
                body(j, 1)
                return carry

            lax.fori_loop(start, stop, run, 0)


BATCH = 8
SLOTS = 16


def slot_rows(plan):
    return BATCH * 2 * (plan.sub + 2)


def odd_device():
    return lax.rem(lax.axis_index("map"), 2)


def place(pieces, wanted, block):
    out = None
    for i, piece in enumerate(pieces):
        shift = (i - wanted[i]) * block % piece.shape[-1]
        moved = pltpu.roll(piece, shift, piece.ndim - 1) if shift else piece
        if out is None:
            out = moved
        else:
            lane = lax.broadcasted_iota(jnp.int32, moved.shape, moved.ndim - 1)
            out = jnp.where(lane >= i * block, moved, out)
    return out


def ocean_kernel(
    plan, vel_ref, stress_ref, zones_ref, slip_ref, ocean_ref, bathy_ref,
    message_out, vel, stress, zones, slip, ocean, bathy, turned, grouped, extra, message, sems,
):
    cells, sub, chunks = plan.cells, plan.sub, plan.chunks
    n, strips, block, sent, rows = plan.n, plan.strips, plan.block, plan.sent_groups, plan.rows
    pairs = (
        (ocean_ref, ocean),
        (bathy_ref, bathy),
        (vel_ref, vel),
        (stress_ref, stress),
        (zones_ref, zones),
        (slip_ref, slip),
    )
    copies = [
        pltpu.make_async_copy(source, target, sems.at[i])
        for i, (source, target) in enumerate(pairs)
    ]
    for copy in copies:
        copy.start()
    copies[0].wait()
    copies[1].wait()
    count = plan.nx // chunks
    lead = plan.lead
    pad = plan.halo_groups * lead
    grouped[:pad, :] = jnp.zeros((pad, LANES), F32)
    grouped[pad + count * lead :, :] = jnp.zeros((pad, LANES), F32)
    for yl in range(strips):
        stacked = jnp.concatenate(
            [ocean[f, yl, kc * sub : (kc + 1) * sub, :] for kc in range(chunks) for f in range(4)],
            axis=0,
        )
        turned[yl] = stacked.T
        by_x = [turned[yl, pl.ds(i, count, stride=chunks), :] for i in range(chunks)]
        for kc in range(chunks):
            grouped[pl.ds(pad + kc * strips + yl, count, stride=lead), :] = place(
                by_x, [kc] * chunks, block
            )
    for d in range(n):
        start = (d * plan.own_groups + (d % 2) * plan.halo_groups) * lead
        message[d * rows : (d + 1) * rows, :] = grouped[start : start + rows, :]
    depths = bathy[...].astype(F32)
    wide = lax.broadcasted_iota(jnp.int32, depths.shape, 1)
    for d in range(n):
        first = d * cells - HALO - 1
        moved = pltpu.roll(depths, -first % plan.nx, 1)
        moved = jnp.where((wide + first >= 0) & (wide + first < plan.nx), moved, 0.0)
        extra[d * strips : (d + 1) * strips, :] = moved[:, :LANES]
    pairs = n // 2
    lane = lax.broadcasted_iota(jnp.int32, (pairs, LANES), 1)
    blank = jnp.zeros((1, LANES), F32)
    for odd in range(2):
        slot = (odd * (chunks - 1) * 4 + 2) * sub
        group = odd * (sent - 1)
        for yl in range(strips):
            if odd:
                column = turned[yl, pl.ds(2 * cells + HALO, pairs - 1, stride=2 * cells), :]
                column = jnp.concatenate([column, blank], axis=0)
            else:
                column = turned[yl, pl.ds(2 * cells - HALO - 1, pairs - 1, stride=2 * cells), :]
                column = jnp.concatenate([blank, column], axis=0)
            deep = extra[pl.ds(odd * strips + yl, pairs, stride=2 * strips), :]
            for kc in range(chunks):
                at = odd * rows + group * lead + kc * strips + yl
                old = message[pl.ds(at, pairs, stride=2 * rows), :]
                edge = pltpu.roll(column, (slot - kc * block) % LANES, 1)
                floor = pltpu.roll(deep, (slot + sub - kc * sub) % LANES, 1)
                new = jnp.where((lane >= slot) & (lane < slot + sub), edge, old)
                new = jnp.where((lane >= slot + sub) & (lane < slot + 2 * sub), floor, new)
                message[pl.ds(at, pairs, stride=2 * rows), :] = new
    out = pltpu.make_async_copy(message, message_out, sems.at[6])
    out.start()
    for copy in copies[2:]:
        copy.wait()
    out.wait()


def crust_kernel(plan, vel, stress, zones, slip, crust, border):
    cells, sub, chunks, ny = plan.cells, plan.sub, plan.chunks, plan.ny

    def joined(ref, *at):
        parts = [ref[(*at, pl.ds(kc * sub, sub), slice(None))] for kc in range(chunks)]
        return jnp.concatenate(parts, axis=-1) if chunks > 1 else parts[0]

    for f in range(3):
        for x in range(cells):
            crust[f * cells + x] = joined(vel, f, x)
    for f in range(6):
        for x in range(cells):
            crust[(3 + f) * cells + x] = joined(stress, f, x)
    for x in range(cells):
        crust[9 * cells + x] = (joined(zones, x) + 1).astype(F32)
    fault_chunk = (plan.depth // 2) // sub
    pieces = [
        slip[...] if kc == fault_chunk else jnp.zeros((cells, ny), F32) for kc in range(chunks)
    ]
    fault = jnp.concatenate(pieces, axis=-1) if chunks > 1 else pieces[0]
    if sub > cells:
        fault = jnp.concatenate([fault, jnp.zeros((sub - cells, plan.lanes), F32)], axis=0)
    crust[10 * cells] = fault
    odd = odd_device()
    near = cells - 1
    for f in range(10):
        for i in range(near):
            border[f * near + i] = crust[f * cells + i + odd]
    for i, f in enumerate((SXX, SXY, SXZ)):
        border[10 * near + i] = crust[(3 + f) * cells + near * (1 - odd)]
    border[10 * near + 3] = fault


class Shifts:
    def __init__(self, plan, memory=None):
        self.plan = plan
        self.memory = memory if plan.unrolled else None
        self.slot = 0
        shape = (plan.sub, plan.lanes)
        self.row = lax.broadcasted_iota(jnp.int32, shape, 0)
        self.lane = lax.broadcasted_iota(jnp.int32, shape, 1)
        self.y = lax.rem(self.lane, plan.ny)
        self.first_row = self.row == 0
        self.last_row = self.row == plan.sub - 1
        self.top = self.first_row & (self.lane < plan.ny)
        self.floor_cell = self.last_row & (self.lane >= plan.lanes - plan.ny)
        self.not_low_y = jnp.where(self.y == 0, 0.0, 1.0).astype(F32)
        self.not_high_y = jnp.where(self.y == plan.ny - 1, 0.0, 1.0).astype(F32)
        self.depth = (
            lax.div(self.lane, plan.ny) * plan.sub + self.row
        ).astype(F32)

    def by_lane(self, f, shift):
        return pltpu.roll(f, shift % self.plan.lanes, f.ndim - 1)

    def by_row(self, f, shift):
        return pltpu.roll(f, shift % self.plan.sub, f.ndim - 2)

    def dy(self, f):
        return self.by_lane(f, -1) * self.not_high_y - self.by_lane(f, 1) * self.not_low_y

    def below(self, f):
        plan = self.plan
        moved = self.by_row(f, -1)
        if plan.chunks > 1:
            moved = jnp.where(self.last_row, self.by_lane(moved, -plan.ny), moved)
        return jnp.where(self.floor_cell, 0.0, moved)

    def above(self, f, top):
        plan = self.plan
        moved = self.by_row(f, 1)
        if plan.chunks > 1:
            moved = jnp.where(self.first_row, self.by_lane(moved, plan.ny), moved)
        return jnp.where(self.top, top, moved)

    def block(self):
        start = self.slot * slot_rows(self.plan)
        self.slot = (self.slot + 1) % SLOTS
        return start

    def dz(self, f, top):
        if self.memory is None or f.ndim == 2:
            return self.below(f) - self.above(f, top * f if top else 0.0)
        plan, memory = self.plan, self.memory
        count, sub = f.shape[:2]
        start, size = self.block(), 2 * (sub + 2)
        for i in range(count):
            memory[pl.ds(start + i * size + 2, sub, stride=2), :] = f[i]
        lane = lax.broadcasted_iota(jnp.int32, (count, plan.lanes), 1)
        first = memory[pl.ds(start + 2, count, stride=size), :]
        last = memory[pl.ds(start + 2 * sub, count, stride=size), :]
        after = jnp.where(lane < plan.lanes - plan.ny, self.by_lane(first, -plan.ny), 0.0)
        before = jnp.where(lane >= plan.ny, self.by_lane(last, plan.ny), top * first)
        memory[pl.ds(start, count, stride=size), :] = before
        memory[pl.ds(start + 2 * (sub + 1), count, stride=size), :] = after
        return jnp.stack(
            [
                memory[pl.ds(start + i * size + 4, sub, stride=2), :]
                - memory[pl.ds(start + i * size, sub, stride=2), :]
                for i in range(count)
            ]
        )

    def spread_rows(self, start, rows):
        plan, memory = self.plan, self.memory
        count = rows.shape[0]
        memory[pl.ds(start, count), :] = rows
        return jnp.stack(
            [
                jnp.broadcast_to(memory[pl.ds(start + i, 1), :], (plan.sub, plan.lanes))
                for i in range(count)
            ]
        )

    def seafloor(self, vz):
        if self.memory is None or vz.ndim == 2:
            row = self.over_chunks(jnp.where(self.top, vz, 0.0))
            return jnp.broadcast_to(row[..., 0:1, :], vz.shape)
        memory, start = self.memory, self.block()
        count, sub, lanes = vz.shape
        for i in range(count):
            memory[pl.ds(start + i * sub, sub), :] = vz[i]
        rows = memory[pl.ds(start, count, stride=sub), :]
        lane = lax.broadcasted_iota(jnp.int32, rows.shape, 1)
        rows = self.over_chunks(jnp.where(lane < self.plan.ny, rows, 0.0))
        return self.spread_rows(start + BATCH * sub, rows)

    def on_top(self, f):
        if self.memory is None or f.ndim == 2:
            shift = self.plan.sub // 2
            while shift:
                f = f + self.by_row(f, shift)
                shift //= 2
            return jnp.where(self.top, self.over_chunks(f), 0.0)
        memory, start = self.memory, self.block()
        count, sub, lanes = f.shape
        for i in range(count):
            memory[pl.ds(start + i * sub, sub), :] = f[i]
        rows = memory[pl.ds(start, count, stride=sub), :]
        for k in range(1, sub):
            rows = rows + memory[pl.ds(start + k, count, stride=sub), :]
        rows = self.spread_rows(start + BATCH * sub, self.over_chunks(rows))
        return jnp.where(self.top, rows, 0.0)

    def over_chunks(self, f):
        shift = self.plan.ny
        while shift < self.plan.lanes:
            f = f + self.by_lane(f, shift)
            shift *= 2
        return f


def acceleration(sh, stress, j, count):
    at, before, after = (pl.ds(j + k, count) for k in (0, -1, 1))
    sxy, sxz = stress[SXY, at], stress[SXZ, at]
    ax = stress[SXX, after] - stress[SXX, before] + sh.dy(sxy) + sh.dz(sxz, 0.0)
    syz = stress[SYZ, at]
    ay = stress[SXY, after] - stress[SXY, before] + sh.dy(stress[SYY, at])
    ay = ay + sh.dz(syz, 0.0)
    szz = stress[SZZ, at]
    az = stress[SXZ, after] - stress[SXZ, before] + sh.dy(syz) + sh.dz(szz, 0.0)
    return ax, ay, az


def strained(sh, vel, stress, mats, j, count):
    at, before, after = (pl.ds(j + k, count) for k in (0, -1, 1))
    vx, vy, vz = vel[VX, at], vel[VY, at], vel[VZ, at]
    exx = vel[VX, after] - vel[VX, before]
    eyy = sh.dy(vy)
    ezz = sh.dz(vz, 1.0)
    mu = mats[SHEAR, at]
    mu2 = mu + mu
    common = mats[LAMB, at] * (exx + eyy + ezz)
    yield SXX, stress[SXX, at] + (common + mu2 * exx)
    yield SYY, stress[SYY, at] + (common + mu2 * eyy)
    yield SZZ, stress[SZZ, at] + (common + mu2 * ezz)
    exy = sh.dy(vx) + vel[VY, after] - vel[VY, before]
    yield SXY, stress[SXY, at] + mu * exy
    exz = sh.dz(vx, 1.0) + vel[VZ, after] - vel[VZ, before]
    yield SXZ, stress[SXZ, at] + (mu * exz + mats[FAULT, at])
    eyz = sh.dz(vy, 1.0) + sh.dy(vz)
    yield SYZ, stress[SYZ, at] + mu * eyz


def bring(plan, sh, material, state, ref, fields, x, count, column, first):
    vel, stress, mats = state
    to = pl.ds(column, count)

    def read(f):
        return ref[pl.ds(f * fields + x, count)]

    for f in range(3):
        vel[f, to] = read(f)
    for f in range(6):
        stress[f, to] = read(3 + f)
    zone = read(9)
    values = [jnp.zeros_like(zone) for _ in range(3)]
    for z in range(ZONES):
        here = zone == float(z + 1)
        values = [jnp.where(here, material(c, z), values[c]) for c in range(3)]
    for c in range(3):
        mats[c, to] = values[c] * HALF
    mats[FLOOR, to] = sh.seafloor(read(VZ))
    for i in range(count):
        slip = ref[ref.shape[0] - 1, pl.ds(first + x + i, 1), :]
        slip = jnp.broadcast_to(slip, (plan.sub, plan.lanes))
        mats[FAULT, column + i] = jnp.where(
            sh.row == (plan.depth // 2) % plan.sub, DT * slip, 0.0
        )


def begin_kernel(plan, table, own, mate, vel, stress, mats, rows):
    cells = plan.cells
    sh = Shifts(plan)
    odd = odd_device()
    state = (vel, stress, mats)
    starts = (HALO + cells * odd, HALO + cells * (1 - odd))
    for start, ref in zip(starts, (own, mate)):
        plan.planes(
            0,
            cells,
            lambda x, count, start=start, ref=ref: bring(
                plan, sh, lambda c, z: table[c, z], state, ref, cells, x, count, start + x, 0
            ),
            BATCH,
        )

    def move(j, count):
        at = pl.ds(j, count)
        b = mats[BUOY, at]
        for f, a in enumerate(acceleration(sh, stress, j, count)):
            vel[f, at] = vel[f, at] + b * a

    plan.planes(HALO + 1, HALO + 2 * cells - 1, move, BATCH)
    for c in range(3):
        for z in range(ZONES):
            at = c * ZONES + z
            rows[at : at + 1, :] = jnp.full((1, plan.lanes), table[c, z], F32)


class Updates:
    def __init__(self, plan, sh, vel, stress, mats, oc, water, bottom, loads):
        self.plan, self.sh = plan, sh
        self.vel, self.stress, self.mats = vel, stress, mats
        self.oc, self.water, self.bottom, self.loads = oc, water, bottom, loads

    def flow_x(self, j, count):
        oc = self.oc
        before, at, after = (pl.ds(j + k, count) for k in range(3))
        oc[1, at] = self.water[at] * (oc[1, at] - HALF * (oc[0, after] - oc[0, before]))

    def flow(self, j, count):
        oc, sh = self.oc, self.sh
        at = pl.ds(j + 1, count)
        p = oc[0, at]
        wet = self.water[at]
        rise = sh.dz(p, -1.0) + self.bottom[at] * p
        oc[3, at] = wet * (oc[3, at] - (HALF * rise + (DT * GRAV) * p))
        oc[2, at] = wet * (oc[2, at] - HALF * sh.dy(p))

    def press(self, j, count, floor):
        oc, sh = self.oc, self.sh
        before, at, after = (pl.ds(j + k, count) for k in range(3))
        w = oc[3, at]
        rise = sh.dz(w, 1.0)
        if floor is not None:
            rise = rise + self.bottom[at] * floor(pl.ds(j, count))
        total = oc[1, after] - oc[1, before] + sh.dy(oc[2, at]) + rise
        oc[0, at] = self.water[at] * (oc[0, at] - (HALF * KBULK) * total)

    def add_floor(self, j, count):
        at = pl.ds(j + 1, count)
        floor = self.first_floor(pl.ds(j, count))
        self.oc[0, at] = self.oc[0, at] - (HALF * KBULK) * (self.bottom[at] * floor)

    def first_floor(self, at):
        return self.mats[FLOOR, at]

    def floor(self, at):
        return self.sh.seafloor(self.vel[VZ, at])

    def load(self, j, count):
        at = pl.ds(j + 1, count)
        return self.sh.on_top(self.bottom[at] * self.oc[0, at])

    def keep(self, j, count):
        self.loads[pl.ds(j, count)] = self.load(j, count)

    def add_load(self, j, count):
        at = pl.ds(j, count)
        self.vel[VZ, at] = self.vel[VZ, at] + self.mats[BUOY, at] * self.load(j, count)

    def move(self, j, count):
        vel = self.vel
        at = pl.ds(j, count)
        ax, ay, az = acceleration(self.sh, self.stress, j, count)
        b = self.mats[BUOY, at]
        vel[VX, at] = vel[VX, at] + b * ax
        vel[VY, at] = vel[VY, at] + b * ay
        vel[VZ, at] = vel[VZ, at] + b * (az + self.load(j, count))

    def strain(self, j, count):
        for f, value in strained(self.sh, self.vel, self.stress, self.mats, j, count):
            self.stress[f, pl.ds(j, count)] = value

    def run(self, spans):
        def planes(t, inset, update):
            self.plan.planes(*spans(t, inset), update, BATCH)

        columns = self.vel.shape[1]
        first, last = spans(0, 1)
        self.plan.planes(0, columns, self.flow_x, BATCH)
        self.plan.planes(1, columns - 1, self.flow, BATCH)
        planes(0, 1, functools.partial(self.press, floor=self.first_floor))
        later = functools.partial(self.press, floor=None)
        self.plan.planes(1, first, later, BATCH)
        self.plan.planes(last, columns - 1, later, BATCH)
        for t in range(STEPS - 1):
            planes(t + 1, 0, self.flow_x)
            planes(t + 1, 1, self.flow)
            planes(t, 1, self.add_load if t == 0 else self.move)
            if t < STEPS - 2:
                planes(t, 2, self.strain)
            planes(t + 1, 1, functools.partial(self.press, floor=self.floor))
        planes(STEPS - 1, 1, self.keep)


def inner_kernel(
    plan, arrived, swapped, mats, vel_in, stress_in, vel, stress, oc, water, bottom, loads,
    gather, depths, memory,
):
    sub, chunks, n, strips = plan.sub, plan.chunks, plan.n, plan.strips
    cells, sent = plan.cells, plan.sent_groups
    sh = Shifts(plan, memory)
    odd = odd_device()
    half = n // 2
    columns = 2 * cells + 2 * HALO

    def turn(owner, group):
        for core, ref in ((odd, arrived), (1 - odd, swapped)):
            for kc in range(chunks):
                for yl in range(strips):
                    at = owner * plan.rows + group * plan.lead + kc * strips + yl
                    to = kc * plan.ny + core * strips + yl
                    gather[pl.ds(to, half, stride=2 * strips), :] = ref[
                        pl.ds(at, half, stride=2 * plan.rows), :
                    ]
        return gather[...].T

    deeps = []
    for owner in range(2):
        for group in range(sent):
            turned = turn(owner, group)
            for i in range(chunks):
                for f in range(4):
                    at = (i * 4 + f) * sub
                    column = 1 + owner * (cells + HALO) + group * chunks + i
                    oc[f, column] = turned[at : at + sub]
            if owner == 0 and group == 0:
                oc[0, 0] = turned[2 * sub : 3 * sub]
                deeps.append(turned[3 * sub : 4 * sub])
            if owner == 1 and group == sent - 1:
                oc[0, columns + 1] = turned[LANES - 2 * sub : LANES - sub]
                deeps.append(turned[LANES - sub :])
    for i, deep in enumerate(deeps):
        for kc in range(chunks):
            mine = (sh.lane >= kc * plan.ny) & (sh.lane < (kc + 1) * plan.ny)
            depths[i, kc * sub : (kc + 1) * sub, :] = sh.over_chunks(jnp.where(mine, deep, 0.0))

    def mask(owner, j, _):
        low = jnp.broadcast_to(depths[owner, pl.ds(j - owner * cells, 1), :], (sub, plan.lanes))
        wet = jnp.where(sh.depth < low, 1.0, 0.0).astype(F32)
        water[j] = wet
        bottom[j] = jnp.where(sh.depth == low - 1.0, 1.0, 0.0).astype(F32)
        oc[0, j] = oc[0, j] * wet

    def mask_x(j, _):
        oc[1, j] = oc[1, j] * water[j]

    def mask_yw(j, _):
        oc[2, j] = oc[2, j] * water[j]
        oc[3, j] = oc[3, j] * water[j]

    plan.planes(0, plan.width + 2, lambda j, _: mask(0, j, _))
    plan.planes(plan.width + 2, columns + 2, lambda j, _: mask(1, j, _))
    plan.planes(1, columns + 1, mask_x)
    plan.planes(2, columns, mask_yw)

    def bring_in(j, _):
        for f in range(3):
            vel[f, j] = vel_in[f, j]
        for f in range(6):
            stress[f, j] = stress_in[f, j]

    if not plan.unrolled:
        plan.planes(HALO, HALO + 2 * cells, bring_in)
    updates = Updates(plan, sh, vel, stress, mats, oc, water, bottom, loads)
    updates.run(lambda t, inset: (HALO + 2 * t + inset, HALO + 2 * cells - 2 * t - inset))


def outer_kernel(
    plan, materials, border, water, bottom, vel_in, stress_in, mats_in, oc_in, loads_in,
    vel, stress, mats, oc, loads, message, gather, rows, memory, sem,
):
    sub, chunks, n, strips, cells = plan.sub, plan.chunks, plan.n, plan.strips, plan.cells
    near = cells - 1
    sh = Shifts(plan, memory)
    odd = odd_device()
    if not plan.unrolled:
        for here, there in (
            (vel, vel_in), (stress, stress_in), (mats, mats_in), (oc, oc_in), (loads, loads_in)
        ):
            here[...] = there[...]
    updates = Updates(plan, sh, vel, stress, mats, oc, water, bottom, loads)

    def material(c, z):
        row = materials[pl.ds(c * ZONES + z, 1), :]
        return jnp.broadcast_to(row, (sub, plan.lanes))

    low = 1 + (HALO + 2 * cells - 1) * odd
    far = (2 * HALO + 2 * cells - 1) * odd

    def planes(t, inset, update):
        start = odd * (HALO + 2 * cells) + (1 - 2 * odd) * (2 * t + inset)
        if plan.unrolled:
            update(start, HALO)
        else:
            lax.fori_loop(0, HALO, lambda j, _: [update(start + j, 1), 0][1], 0)

    plan.planes(
        0,
        near,
        lambda x, count: bring(
            plan, sh, material, (vel, stress, mats), border, near, x, count, low + x, 1 - odd
        ),
        BATCH,
    )
    for i, f in enumerate((SXX, SXY, SXZ)):
        stress[f, far] = border[10 * near + i]
    planes(0, 1, updates.add_floor)

    def substep(t, carry):
        planes(t, 1, updates.move)

        @pl.when(t < STEPS - 2)
        def _():
            planes(t, 2, updates.strain)

        planes(t + 1, 0, updates.flow_x)
        planes(t + 1, 1, updates.flow)
        planes(t + 1, 1, functools.partial(updates.press, floor=updates.floor))
        return carry

    lax.fori_loop(0, STEPS - 1, substep, 0)
    for group in range(plan.own_groups):
        stacked = jnp.concatenate(
            [
                oc[f, 1 + HALO + odd * cells + group * chunks + i]
                for i in range(chunks)
                for f in range(4)
            ],
            axis=0,
        )
        gather[group] = stacked.T
        for kc in range(chunks):
            for yl in range(strips):
                at = group * plan.lead + kc * strips + yl
                rows[pl.ds(at, n, stride=plan.back_rows), :] = gather[
                    group, pl.ds(kc * plan.ny + yl, n, stride=strips), :
                ]
    copy = pltpu.make_async_copy(rows, message, sem)
    copy.start()
    planes(STEPS - 1, 1, updates.keep)
    copy.wait()


def end_kernel(plan, vel_all, stress_all, mats_all, loads_all, vel_out, stress_out, vel, stress):
    cells, sub, chunks, ny = plan.cells, plan.sub, plan.chunks, plan.ny
    sh = Shifts(plan)
    first, last = 2 * (STEPS - 1), plan.width - 2 * (STEPS - 1)
    window = pl.ds(cells * odd_device(), plan.width)
    vel_in, stress_in = vel_all.at[:, window], stress_all.at[:, window]
    mats, loads = mats_all.at[:, window], loads_all.at[window]

    def put(out, f, x, count, planes):
        for kc in range(chunks):
            out[f, pl.ds(x, count), kc * sub : (kc + 1) * sub, :] = planes[
                :, :, kc * ny : (kc + 1) * ny
            ]

    def strain(j, count):
        for f, value in strained(sh, vel_in, stress_in, mats, j, count):
            stress[f, pl.ds(j, count)] = value

    def move(j, count):
        at = pl.ds(j, count)
        ax, ay, az = acceleration(sh, stress, j, count)
        b = mats[BUOY, at]
        for f, a in enumerate((ax, ay, az + loads[at])):
            vel[f, at] = vel_in[f, at] + b * a

    def finish(x, count):
        for f in range(3):
            put(vel_out, f, x, count, vel[f, pl.ds(x + HALO, count)])
        for f, value in strained(sh, vel, stress, mats, x + HALO, count):
            put(stress_out, f, x, count, value)

    plan.planes(first, last, strain, BATCH)
    plan.planes(first + 1, last - 1, move, BATCH)
    plan.planes(0, cells, finish, BATCH)


def unpack_kernel(plan, arrived, ocean, turned, strips, sems):
    sub, chunks = plan.sub, plan.chunks
    block = 4 * sub
    copies = [
        pltpu.make_async_copy(strips.at[yl], ocean.at[:, yl], sems.at[yl])
        for yl in range(plan.strips)
    ]
    for yl in range(plan.strips):
        by_chunk = [
            arrived[pl.ds(kc * plan.strips + yl, plan.nx // chunks, stride=plan.lead), :]
            for kc in range(chunks)
        ]
        for i in range(chunks):
            turned[yl, pl.ds(i, plan.nx // chunks, stride=chunks), :] = place(
                by_chunk, [i] * chunks, block
            )
        whole = turned[yl].T
        for kc in range(chunks):
            for f in range(4):
                at = (kc * 4 + f) * sub
                strips[yl, f, kc * sub : (kc + 1) * sub, :] = whole[at : at + sub]
        copies[yl].start()
    for copy in copies:
        copy.wait()


def on_device(plan, velocity, stress, ocean, zones, materials, slip, bathy):
    n, cells, sub, lanes, width = plan.n, plan.cells, plan.sub, plan.lanes, plan.width
    vmem = pl.BlockSpec(memory_space=pltpu.VMEM)
    smem = pl.BlockSpec(memory_space=pltpu.SMEM)
    hbm = pl.BlockSpec(memory_space=pltpu.HBM)

    def shape(*dims):
        return jax.ShapeDtypeStruct(dims, F32)

    def like(array):
        return jax.ShapeDtypeStruct(array.shape, array.dtype)

    def held(array):
        return pltpu.VMEM(array.shape, array.dtype)

    def call(kernel, name, out, ins, scratch, room=16, outs=None, **rest):
        room = room if plan.unrolled else 56
        return pl.pallas_call(
            functools.partial(kernel, plan),
            out_shape=out,
            in_specs=ins,
            out_specs=jax.tree.map(lambda _: vmem, out) if outs is None else outs,
            scratch_shapes=scratch,
            compiler_params=pltpu.CompilerParams(vmem_limit_bytes=room * 1024 * 1024),
            name=name,
            **rest,
        )

    def pinned(array):
        return pltpu.with_memory_space_constraint(array, pltpu.HBM)

    def near(array):
        return pltpu.with_memory_space_constraint(array, pltpu.VMEM) if plan.unrolled else array

    mates = [(i, i ^ 1) for i in range(n)]
    others = [(i, i + 1) for i in range(1, n - 1, 2)]
    others += [(target, source) for source, target in others]
    crust_args = (velocity, stress, zones, slip)
    message, *near_args = call(
        ocean_kernel,
        "ocean_rows",
        (shape(n * plan.rows, LANES), *(like(a) for a in crust_args)),
        [hbm] * 6,
        [
            held(ocean),
            held(bathy),
            pltpu.VMEM((plan.strips, plan.nx, LANES), F32),
            pltpu.VMEM(
                ((plan.nx // plan.chunks + 2 * plan.halo_groups) * plan.lead, LANES), F32
            ),
            pltpu.VMEM((n * plan.strips, LANES), F32),
            pltpu.VMEM((n * plan.rows, LANES), F32),
            pltpu.SemaphoreType.DMA((7,)),
        ],
        outs=(hbm,) + (vmem,) * 4,
    )(*(pinned(a) for a in (*crust_args, ocean, bathy)))
    arrived = lax.all_to_all(
        message.reshape(n // 2, 2 * plan.rows, LANES),
        "map",
        split_axis=0,
        concat_axis=0,
        axis_index_groups=[list(range(core, n, 2)) for core in range(2)],
        tiled=True,
    ).reshape(n * plan.rows, LANES)
    crust, border = call(
        crust_kernel,
        "crust_planes",
        (shape(10 * cells + 1, sub, lanes), shape(10 * cells - 6, sub, lanes)),
        [vmem] * 4,
        [],
    )(*near_args)
    other = lax.ppermute(border, "map", others)
    mate = lax.ppermute(crust, "map", mates)
    columns = 2 * cells + 2 * HALO
    vel, strs, mats, material_rows = call(
        begin_kernel,
        "first_velocity",
        (
            shape(3, columns, sub, lanes),
            shape(6, columns, sub, lanes),
            shape(5, columns, sub, lanes),
            shape(3 * ZONES, lanes),
        ),
        [smem] + [vmem] * 2,
        [],
    )(materials, crust, mate)
    arrived, vel = lax.optimization_barrier((arrived, vel))
    swapped = lax.ppermute(arrived, "map", mates)
    planes_of = {
        "vel": shape(3, columns, sub, lanes),
        "stress": shape(6, columns, sub, lanes),
        "mats": shape(5, columns, sub, lanes),
        "oc": shape(4, columns + 2, sub, lanes),
        "mask": shape(columns + 2, sub, lanes),
        "loads": shape(columns, sub, lanes),
    }
    vel, strs, oc, water, bottom, loads = call(
        inner_kernel,
        "inner_substeps",
        tuple(planes_of[k] for k in ("vel", "stress", "oc", "mask", "mask", "loads")),
        [vmem] * 5,
        [
            pltpu.VMEM((lanes, LANES), F32),
            pltpu.VMEM((2, plan.depth, lanes), F32),
            pltpu.VMEM((SLOTS * slot_rows(plan), lanes), F32),
        ],
        input_output_aliases={3: 0, 4: 1},
    )(*(near(a) for a in (arrived, swapped, mats, vel, strs)))
    vel, strs, mats, oc, loads, back = call(
        outer_kernel,
        "outer_substeps",
        tuple(planes_of[k] for k in ("vel", "stress", "mats", "oc", "loads"))
        + (shape(n * plan.back_rows, LANES),),
        [vmem] * 9,
        [
            pltpu.VMEM((plan.own_groups, lanes, LANES), F32),
            pltpu.VMEM((n * plan.back_rows, LANES), F32),
            pltpu.VMEM((SLOTS * slot_rows(plan), lanes), F32),
            pltpu.SemaphoreType.DMA,
        ],
        outs=(vmem,) * 5 + (hbm,),
        input_output_aliases={4: 0, 5: 1, 6: 2, 7: 3, 8: 4},
    )(*(near(a) for a in (material_rows, other, water, bottom, vel, strs, mats, oc, loads)))
    returned = lax.all_to_all(
        back.reshape(n, plan.back_rows, LANES), "map", split_axis=0, concat_axis=0, tiled=True
    ).reshape(n * plan.back_rows, LANES)
    new_velocity, new_stress = call(
        end_kernel,
        "last_updates",
        (shape(*velocity.shape), shape(*stress.shape)),
        [vmem] * 4,
        [
            pltpu.VMEM((3, width, sub, lanes), F32),
            pltpu.VMEM((6, width, sub, lanes), F32),
        ],
    )(vel, strs, mats, loads)
    new_ocean = call(
        unpack_kernel,
        "ocean_strips",
        shape(*ocean.shape),
        [vmem],
        [
            pltpu.VMEM((plan.strips, plan.nx, LANES), F32),
            pltpu.VMEM((plan.strips, 4, plan.depth, plan.nx), F32),
            pltpu.SemaphoreType.DMA((plan.strips,)),
        ],
        outs=hbm,
    )(returned)
    return new_velocity, new_stress, new_ocean


def solution(mesh):
    n = mesh.shape["map"]

    def body(velocity, stress, ocean, zones, materials, slip, bathy):
        _, cells, depth, ny = velocity.shape
        plan = Plan(n, cells, depth, ny, ocean.shape[1])
        return on_device(plan, velocity, stress, ocean, zones, materials, slip, bathy)

    return jax.shard_map(
        body,
        mesh=mesh,
        in_specs=(
            P("parts", "map", None, None),
            P("parts", "map", None, None),
            P("parts", "map", None, None),
            P("map", "parts", None),
            P(),
            P("map", "parts"),
            P("map", "parts"),
        ),
        out_specs=(
            P("parts", "map", None, None),
            P("parts", "map", None, None),
            P("parts", "map", None, None),
        ),
        check_vma=False,
    )
```

```python
import functools

import jax
import jax.numpy as jnp
from jax import lax
from jax.experimental import pallas as pl
from jax.experimental.pallas import tpu as pltpu
from jax.sharding import PartitionSpec as P

STEPS = 4
ZONES = 8
DT = 0.25
HALF = 0.5 * DT
KBULK = 2.25
GRAV = 0.1
HALO = 2 * STEPS
LANES = 128
F32 = jnp.float32
VX, VY, VZ = range(3)
SXX, SYY, SZZ, SXY, SXZ, SYZ = range(6)
BUOY, LAMB, SHEAR, FAULT, FLOOR = range(5)


class Plan:
    def __init__(self, devices, cells, depth, ny, strips):
        self.n = devices
        self.cells = cells
        self.depth = depth
        self.ny = ny
        self.strips = strips
        self.chunks = max(1, LANES // ny)
        self.sub = depth // self.chunks
        self.lanes = self.chunks * ny
        self.width = cells + 2 * HALO
        self.own_groups = cells // self.chunks
        self.halo_groups = HALO // self.chunks
        self.sent_groups = self.own_groups + self.halo_groups
        self.lead = self.chunks * strips
        self.rows = self.lead * self.sent_groups
        self.back_rows = self.lead * self.own_groups
        self.nx = devices * cells
        self.block = 4 * self.sub
        self.unrolled = self.sub * self.lanes <= 1024
        assert devices % 2 == 0 and cells == HALO and self.block * self.chunks == LANES

    def planes(self, start, stop, body, batch=1):
        if self.unrolled:
            for j in range(start, stop, batch):
                body(j, min(batch, stop - j))
        else:
            def run(j, carry):
                body(j, 1)
                return carry

            lax.fori_loop(start, stop, run, 0)


BATCH = 8
SLOTS = 16


def slot_rows(plan):
    return BATCH * 2 * (plan.sub + 2)


def odd_device():
    return lax.rem(lax.axis_index("map"), 2)


def place(pieces, wanted, block):
    out = None
    for i, piece in enumerate(pieces):
        shift = (i - wanted[i]) * block % piece.shape[-1]
        moved = pltpu.roll(piece, shift, piece.ndim - 1) if shift else piece
        if out is None:
            out = moved
        else:
            lane = lax.broadcasted_iota(jnp.int32, moved.shape, moved.ndim - 1)
            out = jnp.where(lane >= i * block, moved, out)
    return out


def pack_kernel(
    plan, vel_ref, stress_ref, zones_ref, slip_ref, ocean_ref, bathy_ref,
    message_out, crust, border,
    vel, stress, zones, slip, ocean, bathy, turned, grouped, extra, message, sems,
):
    cells, sub, chunks, ny = plan.cells, plan.sub, plan.chunks, plan.ny
    n, strips, block, sent, rows = plan.n, plan.strips, plan.block, plan.sent_groups, plan.rows
    pairs = (
        (ocean_ref, ocean),
        (bathy_ref, bathy),
        (vel_ref, vel),
        (stress_ref, stress),
        (zones_ref, zones),
        (slip_ref, slip),
    )
    copies = [
        pltpu.make_async_copy(source, target, sems.at[i])
        for i, (source, target) in enumerate(pairs)
    ]
    for copy in copies:
        copy.start()
    copies[1].wait()
    depths = bathy[...].astype(F32)
    wide = lax.broadcasted_iota(jnp.int32, depths.shape, 1)
    for d in range(n):
        first = d * cells - HALO - 1
        moved = pltpu.roll(depths, -first % plan.nx, 1)
        moved = jnp.where((wide + first >= 0) & (wide + first < plan.nx), moved, 0.0)
        extra[d * strips : (d + 1) * strips, :] = moved[:, :LANES]
    copies[0].wait()
    count = plan.nx // chunks
    lead = plan.lead
    pad = plan.halo_groups * lead
    grouped[:pad, :] = jnp.zeros((pad, LANES), F32)
    grouped[pad + count * lead :, :] = jnp.zeros((pad, LANES), F32)
    for yl in range(strips):
        stacked = jnp.concatenate(
            [ocean[f, yl, kc * sub : (kc + 1) * sub, :] for kc in range(chunks) for f in range(4)],
            axis=0,
        )
        turned[yl] = stacked.T
        by_x = [turned[yl, pl.ds(i, count, stride=chunks), :] for i in range(chunks)]
        for kc in range(chunks):
            grouped[pl.ds(pad + kc * strips + yl, count, stride=lead), :] = place(
                by_x, [kc] * chunks, block
            )
    for d in range(n):
        start = (d * plan.own_groups + (d % 2) * plan.halo_groups) * lead
        message[d * rows : (d + 1) * rows, :] = grouped[start : start + rows, :]
    pairs = n // 2
    lane = lax.broadcasted_iota(jnp.int32, (pairs, LANES), 1)
    blank = jnp.zeros((1, LANES), F32)
    for odd in range(2):
        slot = (odd * (chunks - 1) * 4 + 2) * sub
        group = odd * (sent - 1)
        for yl in range(strips):
            if odd:
                column = turned[yl, pl.ds(2 * cells + HALO, pairs - 1, stride=2 * cells), :]
                column = jnp.concatenate([column, blank], axis=0)
            else:
                column = turned[yl, pl.ds(2 * cells - HALO - 1, pairs - 1, stride=2 * cells), :]
                column = jnp.concatenate([blank, column], axis=0)
            deep = extra[pl.ds(odd * strips + yl, pairs, stride=2 * strips), :]
            for kc in range(chunks):
                at = odd * rows + group * lead + kc * strips + yl
                old = message[pl.ds(at, pairs, stride=2 * rows), :]
                edge = pltpu.roll(column, (slot - kc * block) % LANES, 1)
                floor = pltpu.roll(deep, (slot + sub - kc * sub) % LANES, 1)
                new = jnp.where((lane >= slot) & (lane < slot + sub), edge, old)
                new = jnp.where((lane >= slot + sub) & (lane < slot + 2 * sub), floor, new)
                message[pl.ds(at, pairs, stride=2 * rows), :] = new
    out = pltpu.make_async_copy(message, message_out, sems.at[6])
    out.start()

    for copy in copies[2:]:
        copy.wait()

    def joined(ref, *at):
        parts = [ref[(*at, pl.ds(kc * sub, sub), slice(None))] for kc in range(chunks)]
        return jnp.concatenate(parts, axis=-1) if chunks > 1 else parts[0]

    for f in range(3):
        for x in range(cells):
            crust[f * cells + x] = joined(vel, f, x)
    for f in range(6):
        for x in range(cells):
            crust[(3 + f) * cells + x] = joined(stress, f, x)
    for x in range(cells):
        crust[9 * cells + x] = (joined(zones, x) + 1).astype(F32)
    fault_chunk = (plan.depth // 2) // sub
    pieces = [
        slip[...] if kc == fault_chunk else jnp.zeros((cells, ny), F32) for kc in range(chunks)
    ]
    fault = jnp.concatenate(pieces, axis=-1) if chunks > 1 else pieces[0]
    if sub > cells:
        fault = jnp.concatenate([fault, jnp.zeros((sub - cells, plan.lanes), F32)], axis=0)
    crust[10 * cells] = fault
    odd = odd_device()
    near = cells - 1
    for f in range(10):
        for i in range(near):
            border[f * near + i] = crust[f * cells + i + odd]
    for i, f in enumerate((SXX, SXY, SXZ)):
        border[10 * near + i] = crust[(3 + f) * cells + near * (1 - odd)]
    border[10 * near + 3] = fault
    out.wait()


class Shifts:
    def __init__(self, plan, memory=None):
        self.plan = plan
        self.memory = memory if plan.unrolled else None
        self.slot = 0
        shape = (plan.sub, plan.lanes)
        self.row = lax.broadcasted_iota(jnp.int32, shape, 0)
        self.lane = lax.broadcasted_iota(jnp.int32, shape, 1)
        self.y = lax.rem(self.lane, plan.ny)
        self.first_row = self.row == 0
        self.last_row = self.row == plan.sub - 1
        self.top = self.first_row & (self.lane < plan.ny)
        self.floor_cell = self.last_row & (self.lane >= plan.lanes - plan.ny)
        self.not_low_y = jnp.where(self.y == 0, 0.0, 1.0).astype(F32)
        self.not_high_y = jnp.where(self.y == plan.ny - 1, 0.0, 1.0).astype(F32)
        self.depth = (
            lax.div(self.lane, plan.ny) * plan.sub + self.row
        ).astype(F32)

    def by_lane(self, f, shift):
        return pltpu.roll(f, shift % self.plan.lanes, f.ndim - 1)

    def by_row(self, f, shift):
        return pltpu.roll(f, shift % self.plan.sub, f.ndim - 2)

    def dy(self, f):
        return self.by_lane(f, -1) * self.not_high_y - self.by_lane(f, 1) * self.not_low_y

    def below(self, f):
        plan = self.plan
        moved = self.by_row(f, -1)
        if plan.chunks > 1:
            moved = jnp.where(self.last_row, self.by_lane(moved, -plan.ny), moved)
        return jnp.where(self.floor_cell, 0.0, moved)

    def above(self, f, top):
        plan = self.plan
        moved = self.by_row(f, 1)
        if plan.chunks > 1:
            moved = jnp.where(self.first_row, self.by_lane(moved, plan.ny), moved)
        return jnp.where(self.top, top, moved)

    def block(self):
        start = self.slot * slot_rows(self.plan)
        self.slot = (self.slot + 1) % SLOTS
        return start

    def dz(self, f, top):
        if self.memory is None or f.ndim == 2:
            return self.below(f) - self.above(f, top * f if top else 0.0)
        plan, memory = self.plan, self.memory
        count, sub = f.shape[:2]
        start, size = self.block(), 2 * (sub + 2)
        for i in range(count):
            memory[pl.ds(start + i * size + 2, sub, stride=2), :] = f[i]
        lane = lax.broadcasted_iota(jnp.int32, (count, plan.lanes), 1)
        first = memory[pl.ds(start + 2, count, stride=size), :]
        last = memory[pl.ds(start + 2 * sub, count, stride=size), :]
        after = jnp.where(lane < plan.lanes - plan.ny, self.by_lane(first, -plan.ny), 0.0)
        before = jnp.where(lane >= plan.ny, self.by_lane(last, plan.ny), top * first)
        memory[pl.ds(start, count, stride=size), :] = before
        memory[pl.ds(start + 2 * (sub + 1), count, stride=size), :] = after
        return jnp.stack(
            [
                memory[pl.ds(start + i * size + 4, sub, stride=2), :]
                - memory[pl.ds(start + i * size, sub, stride=2), :]
                for i in range(count)
            ]
        )

    def spread_rows(self, start, rows):
        plan, memory = self.plan, self.memory
        count = rows.shape[0]
        memory[pl.ds(start, count), :] = rows
        return jnp.stack(
            [
                jnp.broadcast_to(memory[pl.ds(start + i, 1), :], (plan.sub, plan.lanes))
                for i in range(count)
            ]
        )

    def seafloor(self, vz):
        if self.memory is None or vz.ndim == 2:
            row = self.over_chunks(jnp.where(self.top, vz, 0.0))
            return jnp.broadcast_to(row[..., 0:1, :], vz.shape)
        memory, start = self.memory, self.block()
        count, sub, lanes = vz.shape
        for i in range(count):
            memory[pl.ds(start + i * sub, sub), :] = vz[i]
        rows = memory[pl.ds(start, count, stride=sub), :]
        lane = lax.broadcasted_iota(jnp.int32, rows.shape, 1)
        rows = self.over_chunks(jnp.where(lane < self.plan.ny, rows, 0.0))
        return self.spread_rows(start + BATCH * sub, rows)

    def on_top(self, f):
        if self.memory is None or f.ndim == 2:
            shift = self.plan.sub // 2
            while shift:
                f = f + self.by_row(f, shift)
                shift //= 2
            return jnp.where(self.top, self.over_chunks(f), 0.0)
        memory, start = self.memory, self.block()
        count, sub, lanes = f.shape
        for i in range(count):
            memory[pl.ds(start + i * sub, sub), :] = f[i]
        rows = memory[pl.ds(start, count, stride=sub), :]
        for k in range(1, sub):
            rows = rows + memory[pl.ds(start + k, count, stride=sub), :]
        rows = self.spread_rows(start + BATCH * sub, self.over_chunks(rows))
        return jnp.where(self.top, rows, 0.0)

    def over_chunks(self, f):
        shift = self.plan.ny
        while shift < self.plan.lanes:
            f = f + self.by_lane(f, shift)
            shift *= 2
        return f


def acceleration(sh, stress, j, count):
    at, before, after = (pl.ds(j + k, count) for k in (0, -1, 1))
    sxy, sxz = stress[SXY, at], stress[SXZ, at]
    ax = stress[SXX, after] - stress[SXX, before] + sh.dy(sxy) + sh.dz(sxz, 0.0)
    syz = stress[SYZ, at]
    ay = stress[SXY, after] - stress[SXY, before] + sh.dy(stress[SYY, at])
    ay = ay + sh.dz(syz, 0.0)
    szz = stress[SZZ, at]
    az = stress[SXZ, after] - stress[SXZ, before] + sh.dy(syz) + sh.dz(szz, 0.0)
    return ax, ay, az


def strained(sh, vel, stress, mats, j, count):
    at, before, after = (pl.ds(j + k, count) for k in (0, -1, 1))
    vx, vy, vz = vel[VX, at], vel[VY, at], vel[VZ, at]
    exx = vel[VX, after] - vel[VX, before]
    eyy = sh.dy(vy)
    ezz = sh.dz(vz, 1.0)
    mu = mats[SHEAR, at]
    mu2 = mu + mu
    common = mats[LAMB, at] * (exx + eyy + ezz)
    yield SXX, stress[SXX, at] + (common + mu2 * exx)
    yield SYY, stress[SYY, at] + (common + mu2 * eyy)
    yield SZZ, stress[SZZ, at] + (common + mu2 * ezz)
    exy = sh.dy(vx) + vel[VY, after] - vel[VY, before]
    yield SXY, stress[SXY, at] + mu * exy
    exz = sh.dz(vx, 1.0) + vel[VZ, after] - vel[VZ, before]
    yield SXZ, stress[SXZ, at] + (mu * exz + mats[FAULT, at])
    eyz = sh.dz(vy, 1.0) + sh.dy(vz)
    yield SYZ, stress[SYZ, at] + mu * eyz


def bring(plan, sh, material, state, ref, fields, x, count, column, first):
    vel, stress, mats = state
    to = pl.ds(column, count)

    def read(f):
        return ref[pl.ds(f * fields + x, count)]

    for f in range(3):
        vel[f, to] = read(f)
    for f in range(6):
        stress[f, to] = read(3 + f)
    zone = read(9)
    values = [jnp.zeros_like(zone) for _ in range(3)]
    for z in range(ZONES):
        here = zone == float(z + 1)
        values = [jnp.where(here, material(c, z), values[c]) for c in range(3)]
    for c in range(3):
        mats[c, to] = values[c] * HALF
    mats[FLOOR, to] = sh.seafloor(read(VZ))
    for i in range(count):
        slip = ref[ref.shape[0] - 1, pl.ds(first + x + i, 1), :]
        slip = jnp.broadcast_to(slip, (plan.sub, plan.lanes))
        mats[FAULT, column + i] = jnp.where(
            sh.row == (plan.depth // 2) % plan.sub, DT * slip, 0.0
        )


def begin_kernel(plan, table, own, mate, vel, stress, mats, rows):
    cells = plan.cells
    sh = Shifts(plan)
    odd = odd_device()
    state = (vel, stress, mats)
    starts = (HALO + cells * odd, HALO + cells * (1 - odd))
    for start, ref in zip(starts, (own, mate)):
        plan.planes(
            0,
            cells,
            lambda x, count, start=start, ref=ref: bring(
                plan, sh, lambda c, z: table[c, z], state, ref, cells, x, count, start + x, 0
            ),
            BATCH,
        )

    def move(j, count):
        at = pl.ds(j, count)
        b = mats[BUOY, at]
        for f, a in enumerate(acceleration(sh, stress, j, count)):
            vel[f, at] = vel[f, at] + b * a

    plan.planes(HALO + 1, HALO + 2 * cells - 1, move, BATCH)
    for c in range(3):
        for z in range(ZONES):
            at = c * ZONES + z
            rows[at : at + 1, :] = jnp.full((1, plan.lanes), table[c, z], F32)


class Updates:
    def __init__(self, plan, sh, vel, stress, mats, oc, water, bottom, loads):
        self.plan, self.sh = plan, sh
        self.vel, self.stress, self.mats = vel, stress, mats
        self.oc, self.water, self.bottom, self.loads = oc, water, bottom, loads

    def flow_x(self, j, count):
        oc = self.oc
        before, at, after = (pl.ds(j + k, count) for k in range(3))
        oc[1, at] = self.water[at] * (oc[1, at] - HALF * (oc[0, after] - oc[0, before]))

    def flow(self, j, count):
        oc, sh = self.oc, self.sh
        at = pl.ds(j + 1, count)
        p = oc[0, at]
        wet = self.water[at]
        rise = sh.dz(p, -1.0) + self.bottom[at] * p
        oc[3, at] = wet * (oc[3, at] - (HALF * rise + (DT * GRAV) * p))
        oc[2, at] = wet * (oc[2, at] - HALF * sh.dy(p))

    def press(self, j, count, floor):
        oc, sh = self.oc, self.sh
        before, at, after = (pl.ds(j + k, count) for k in range(3))
        w = oc[3, at]
        rise = sh.dz(w, 1.0)
        if floor is not None:
            rise = rise + self.bottom[at] * floor(pl.ds(j, count))
        total = oc[1, after] - oc[1, before] + sh.dy(oc[2, at]) + rise
        oc[0, at] = self.water[at] * (oc[0, at] - (HALF * KBULK) * total)

    def add_floor(self, j, count):
        at = pl.ds(j + 1, count)
        floor = self.first_floor(pl.ds(j, count))
        self.oc[0, at] = self.oc[0, at] - (HALF * KBULK) * (self.bottom[at] * floor)

    def first_floor(self, at):
        return self.mats[FLOOR, at]

    def floor(self, at):
        return self.sh.seafloor(self.vel[VZ, at])

    def load(self, j, count):
        at = pl.ds(j + 1, count)
        return self.sh.on_top(self.bottom[at] * self.oc[0, at])

    def keep(self, j, count):
        self.loads[pl.ds(j, count)] = self.load(j, count)

    def add_load(self, j, count):
        at = pl.ds(j, count)
        self.vel[VZ, at] = self.vel[VZ, at] + self.mats[BUOY, at] * self.load(j, count)

    def move(self, j, count):
        vel = self.vel
        at = pl.ds(j, count)
        ax, ay, az = acceleration(self.sh, self.stress, j, count)
        b = self.mats[BUOY, at]
        vel[VX, at] = vel[VX, at] + b * ax
        vel[VY, at] = vel[VY, at] + b * ay
        vel[VZ, at] = vel[VZ, at] + b * (az + self.load(j, count))

    def strain(self, j, count):
        for f, value in strained(self.sh, self.vel, self.stress, self.mats, j, count):
            self.stress[f, pl.ds(j, count)] = value

    def run(self, spans, inner, send=None):
        def planes(t, inset, update):
            self.plan.planes(*spans(t, inset), update, BATCH)

        def flows(t):
            planes(t, 0, self.flow_x)
            planes(t, 1, self.flow)

        if inner:
            columns = self.vel.shape[1]
            first, last = spans(0, 1)
            self.plan.planes(0, columns, self.flow_x, BATCH)
            self.plan.planes(1, columns - 1, self.flow, BATCH)
            planes(0, 1, functools.partial(self.press, floor=self.first_floor))
            later = functools.partial(self.press, floor=None)
            self.plan.planes(1, first, later, BATCH)
            self.plan.planes(last, columns - 1, later, BATCH)
        else:
            planes(0, 1, self.add_floor)
        for t in range(STEPS - 1):
            flows(t + 1)
            planes(t, 1, self.add_load if inner and t == 0 else self.move)
            if t < STEPS - 2:
                planes(t, 2, self.strain)
            planes(t + 1, 1, functools.partial(self.press, floor=self.floor))
        if send is not None:
            send()
        planes(STEPS - 1, 1, self.keep)


def inner_kernel(
    plan, arrived, swapped, mats, vel_in, stress_in, vel, stress, oc, water, bottom, loads,
    gather, depths, memory,
):
    sub, chunks, n, strips = plan.sub, plan.chunks, plan.n, plan.strips
    cells, sent = plan.cells, plan.sent_groups
    sh = Shifts(plan, memory)
    odd = odd_device()
    half = n // 2
    columns = 2 * cells + 2 * HALO

    def turn(owner, group):
        for core, ref in ((odd, arrived), (1 - odd, swapped)):
            for kc in range(chunks):
                for yl in range(strips):
                    at = owner * plan.rows + group * plan.lead + kc * strips + yl
                    to = kc * plan.ny + core * strips + yl
                    gather[pl.ds(to, half, stride=2 * strips), :] = ref[
                        pl.ds(at, half, stride=2 * plan.rows), :
                    ]
        return gather[...].T

    deeps = []
    for owner in range(2):
        for group in range(sent):
            turned = turn(owner, group)
            for i in range(chunks):
                for f in range(4):
                    at = (i * 4 + f) * sub
                    column = 1 + owner * (cells + HALO) + group * chunks + i
                    oc[f, column] = turned[at : at + sub]
            if owner == 0 and group == 0:
                oc[0, 0] = turned[2 * sub : 3 * sub]
                deeps.append(turned[3 * sub : 4 * sub])
            if owner == 1 and group == sent - 1:
                oc[0, columns + 1] = turned[LANES - 2 * sub : LANES - sub]
                deeps.append(turned[LANES - sub :])
    for i, deep in enumerate(deeps):
        for kc in range(chunks):
            mine = (sh.lane >= kc * plan.ny) & (sh.lane < (kc + 1) * plan.ny)
            depths[i, kc * sub : (kc + 1) * sub, :] = sh.over_chunks(jnp.where(mine, deep, 0.0))

    def mask(owner, j, _):
        low = jnp.broadcast_to(depths[owner, pl.ds(j - owner * cells, 1), :], (sub, plan.lanes))
        wet = jnp.where(sh.depth < low, 1.0, 0.0).astype(F32)
        water[j] = wet
        bottom[j] = jnp.where(sh.depth == low - 1.0, 1.0, 0.0).astype(F32)
        oc[0, j] = oc[0, j] * wet

    def mask_x(j, _):
        oc[1, j] = oc[1, j] * water[j]

    def mask_yw(j, _):
        oc[2, j] = oc[2, j] * water[j]
        oc[3, j] = oc[3, j] * water[j]

    plan.planes(0, plan.width + 2, lambda j, _: mask(0, j, _))
    plan.planes(plan.width + 2, columns + 2, lambda j, _: mask(1, j, _))
    plan.planes(1, columns + 1, mask_x)
    plan.planes(2, columns, mask_yw)

    def bring_in(j, _):
        for f in range(3):
            vel[f, j] = vel_in[f, j]
        for f in range(6):
            stress[f, j] = stress_in[f, j]

    if not plan.unrolled:
        plan.planes(HALO, HALO + 2 * cells, bring_in)
    updates = Updates(plan, sh, vel, stress, mats, oc, water, bottom, loads)
    updates.run(lambda t, inset: (HALO + 2 * t + inset, HALO + 2 * cells - 2 * t - inset), True)


def outer_kernel(
    plan, materials, border, water, bottom, vel_in, stress_in, mats_in, oc_in, loads_in,
    vel, stress, mats, oc, loads, message, gather, rows, memory, sem,
):
    sub, chunks, n, strips, cells = plan.sub, plan.chunks, plan.n, plan.strips, plan.cells
    near = cells - 1
    sh = Shifts(plan, memory)
    odd = odd_device()
    if not plan.unrolled:
        for here, there in (
            (vel, vel_in), (stress, stress_in), (mats, mats_in), (oc, oc_in), (loads, loads_in)
        ):
            here[...] = there[...]
    updates = Updates(plan, sh, vel, stress, mats, oc, water, bottom, loads)

    def material(c, z):
        row = materials[pl.ds(c * ZONES + z, 1), :]
        return jnp.broadcast_to(row, (sub, plan.lanes))

    def side(core):
        low, far = ((1, 0), (HALO + 2 * cells, 2 * HALO + 2 * cells - 1))[core]
        state = (vel, stress, mats)
        plan.planes(
            0,
            near,
            lambda x, count: bring(
                plan, sh, material, state, border, near, x, count, low + x, 1 - core
            ),
            BATCH,
        )
        for i, f in enumerate((SXX, SXY, SXZ)):
            stress[f, far] = border[10 * near + i]

        def spans(t, inset):
            if core == 0:
                return 2 * t + inset, 2 * t + inset + HALO
            last = 2 * HALO + 2 * cells - 2 * t - inset
            return last - HALO, last

        copy = pltpu.make_async_copy(rows, message, sem)

        def send():
            for group in range(plan.own_groups):
                stacked = jnp.concatenate(
                    [
                        oc[f, 1 + HALO + core * cells + group * chunks + i]
                        for i in range(chunks)
                        for f in range(4)
                    ],
                    axis=0,
                )
                gather[group] = stacked.T
                for kc in range(chunks):
                    for yl in range(strips):
                        at = group * plan.lead + kc * strips + yl
                        rows[pl.ds(at, n, stride=plan.back_rows), :] = gather[
                            group, pl.ds(kc * plan.ny + yl, n, stride=strips), :
                        ]
            copy.start()

        updates.run(spans, False, send)
        copy.wait()

    for core in range(2):
        pl.when(odd == core)(functools.partial(side, core))


def end_kernel(plan, vel_all, stress_all, mats_all, loads_all, vel_out, stress_out, vel, stress):
    cells, sub, chunks, ny = plan.cells, plan.sub, plan.chunks, plan.ny
    sh = Shifts(plan)
    first, last = 2 * (STEPS - 1), plan.width - 2 * (STEPS - 1)
    window = pl.ds(cells * odd_device(), plan.width)
    vel_in, stress_in = vel_all.at[:, window], stress_all.at[:, window]
    mats, loads = mats_all.at[:, window], loads_all.at[window]

    def put(out, f, x, count, planes):
        for kc in range(chunks):
            out[f, pl.ds(x, count), kc * sub : (kc + 1) * sub, :] = planes[
                :, :, kc * ny : (kc + 1) * ny
            ]

    def strain(j, count):
        for f, value in strained(sh, vel_in, stress_in, mats, j, count):
            stress[f, pl.ds(j, count)] = value

    def move(j, count):
        at = pl.ds(j, count)
        ax, ay, az = acceleration(sh, stress, j, count)
        b = mats[BUOY, at]
        for f, a in enumerate((ax, ay, az + loads[at])):
            vel[f, at] = vel_in[f, at] + b * a

    def finish(x, count):
        for f in range(3):
            put(vel_out, f, x, count, vel[f, pl.ds(x + HALO, count)])
        for f, value in strained(sh, vel, stress, mats, x + HALO, count):
            put(stress_out, f, x, count, value)

    plan.planes(first, last, strain, BATCH)
    plan.planes(first + 1, last - 1, move, BATCH)
    plan.planes(0, cells, finish, BATCH)


def unpack_kernel(plan, arrived, ocean, turned, strips, sems):
    sub, chunks = plan.sub, plan.chunks
    block = 4 * sub
    copies = [
        pltpu.make_async_copy(strips.at[yl], ocean.at[:, yl], sems.at[yl])
        for yl in range(plan.strips)
    ]
    for yl in range(plan.strips):
        by_chunk = [
            arrived[pl.ds(kc * plan.strips + yl, plan.nx // chunks, stride=plan.lead), :]
            for kc in range(chunks)
        ]
        for i in range(chunks):
            turned[yl, pl.ds(i, plan.nx // chunks, stride=chunks), :] = place(
                by_chunk, [i] * chunks, block
            )
        whole = turned[yl].T
        for kc in range(chunks):
            for f in range(4):
                at = (kc * 4 + f) * sub
                strips[yl, f, kc * sub : (kc + 1) * sub, :] = whole[at : at + sub]
        copies[yl].start()
    for copy in copies:
        copy.wait()


def on_device(plan, velocity, stress, ocean, zones, materials, slip, bathy):
    n, cells, sub, lanes, width = plan.n, plan.cells, plan.sub, plan.lanes, plan.width
    vmem = pl.BlockSpec(memory_space=pltpu.VMEM)
    smem = pl.BlockSpec(memory_space=pltpu.SMEM)
    hbm = pl.BlockSpec(memory_space=pltpu.HBM)

    def shape(*dims):
        return jax.ShapeDtypeStruct(dims, F32)

    def like(array):
        return jax.ShapeDtypeStruct(array.shape, array.dtype)

    def held(array):
        return pltpu.VMEM(array.shape, array.dtype)

    def call(kernel, name, out, ins, scratch, room=16, outs=None, **rest):
        room = room if plan.unrolled else 56
        return pl.pallas_call(
            functools.partial(kernel, plan),
            out_shape=out,
            in_specs=ins,
            out_specs=jax.tree.map(lambda _: vmem, out) if outs is None else outs,
            scratch_shapes=scratch,
            compiler_params=pltpu.CompilerParams(vmem_limit_bytes=room * 1024 * 1024),
            name=name,
            **rest,
        )

    def pinned(array):
        return pltpu.with_memory_space_constraint(array, pltpu.HBM)

    def near(array):
        return pltpu.with_memory_space_constraint(array, pltpu.VMEM) if plan.unrolled else array

    mates = [(i, i ^ 1) for i in range(n)]
    others = [(i, i + 1) for i in range(1, n - 1, 2)]
    others += [(target, source) for source, target in others]
    message, crust, border = call(
        pack_kernel,
        "pack",
        (
            shape(n * plan.rows, LANES),
            shape(10 * cells + 1, sub, lanes),
            shape(10 * cells - 6, sub, lanes),
        ),
        [hbm] * 6,
        [held(a) for a in (velocity, stress, zones, slip, ocean, bathy)]
        + [
            pltpu.VMEM((plan.strips, plan.nx, LANES), F32),
            pltpu.VMEM(
                ((plan.nx // plan.chunks + 2 * plan.halo_groups) * plan.lead, LANES), F32
            ),
            pltpu.VMEM((n * plan.strips, LANES), F32),
            pltpu.VMEM((n * plan.rows, LANES), F32),
            pltpu.SemaphoreType.DMA((7,)),
        ],
        outs=(hbm, vmem, vmem),
    )(*(pinned(a) for a in (velocity, stress, zones, slip, ocean, bathy)))
    arrived = lax.all_to_all(
        message.reshape(n // 2, 2 * plan.rows, LANES),
        "map",
        split_axis=0,
        concat_axis=0,
        axis_index_groups=[list(range(core, n, 2)) for core in range(2)],
        tiled=True,
    ).reshape(n * plan.rows, LANES)
    other = lax.ppermute(border, "map", others)
    mate = lax.ppermute(crust, "map", mates)
    columns = 2 * cells + 2 * HALO
    vel, strs, mats, material_rows = call(
        begin_kernel,
        "first_velocity",
        (
            shape(3, columns, sub, lanes),
            shape(6, columns, sub, lanes),
            shape(5, columns, sub, lanes),
            shape(3 * ZONES, lanes),
        ),
        [smem] + [vmem] * 2,
        [],
    )(materials, crust, mate)
    arrived, vel = lax.optimization_barrier((arrived, vel))
    swapped = lax.ppermute(arrived, "map", mates)
    planes_of = {
        "vel": shape(3, columns, sub, lanes),
        "stress": shape(6, columns, sub, lanes),
        "mats": shape(5, columns, sub, lanes),
        "oc": shape(4, columns + 2, sub, lanes),
        "mask": shape(columns + 2, sub, lanes),
        "loads": shape(columns, sub, lanes),
    }
    vel, strs, oc, water, bottom, loads = call(
        inner_kernel,
        "inner_substeps",
        tuple(planes_of[k] for k in ("vel", "stress", "oc", "mask", "mask", "loads")),
        [vmem] * 5,
        [
            pltpu.VMEM((lanes, LANES), F32),
            pltpu.VMEM((2, plan.depth, lanes), F32),
            pltpu.VMEM((SLOTS * slot_rows(plan), lanes), F32),
        ],
        input_output_aliases={3: 0, 4: 1},
    )(*(near(a) for a in (arrived, swapped, mats, vel, strs)))
    vel, strs, mats, oc, loads, back = call(
        outer_kernel,
        "outer_substeps",
        tuple(planes_of[k] for k in ("vel", "stress", "mats", "oc", "loads"))
        + (shape(n * plan.back_rows, LANES),),
        [vmem] * 9,
        [
            pltpu.VMEM((plan.own_groups, lanes, LANES), F32),
            pltpu.VMEM((n * plan.back_rows, LANES), F32),
            pltpu.VMEM((SLOTS * slot_rows(plan), lanes), F32),
            pltpu.SemaphoreType.DMA,
        ],
        outs=(vmem,) * 5 + (hbm,),
        input_output_aliases={4: 0, 5: 1, 6: 2, 7: 3, 8: 4},
    )(*(near(a) for a in (material_rows, other, water, bottom, vel, strs, mats, oc, loads)))
    returned = lax.all_to_all(
        back.reshape(n, plan.back_rows, LANES), "map", split_axis=0, concat_axis=0, tiled=True
    ).reshape(n * plan.back_rows, LANES)
    new_velocity, new_stress = call(
        end_kernel,
        "last_updates",
        (shape(*velocity.shape), shape(*stress.shape)),
        [vmem] * 4,
        [
            pltpu.VMEM((3, width, sub, lanes), F32),
            pltpu.VMEM((6, width, sub, lanes), F32),
        ],
    )(vel, strs, mats, loads)
    new_ocean = call(
        unpack_kernel,
        "ocean_strips",
        shape(*ocean.shape),
        [vmem],
        [
            pltpu.VMEM((plan.strips, plan.nx, LANES), F32),
            pltpu.VMEM((plan.strips, 4, plan.depth, plan.nx), F32),
            pltpu.SemaphoreType.DMA((plan.strips,)),
        ],
        outs=hbm,
    )(returned)
    return new_velocity, new_stress, new_ocean


def solution(mesh):
    n = mesh.shape["map"]

    def body(velocity, stress, ocean, zones, materials, slip, bathy):
        _, cells, depth, ny = velocity.shape
        plan = Plan(n, cells, depth, ny, ocean.shape[1])
        return on_device(plan, velocity, stress, ocean, zones, materials, slip, bathy)

    return jax.shard_map(
        body,
        mesh=mesh,
        in_specs=(
            P("parts", "map", None, None),
            P("parts", "map", None, None),
            P("parts", "map", None, None),
            P("map", "parts", None),
            P(),
            P("map", "parts"),
            P("map", "parts"),
        ),
        out_specs=(
            P("parts", "map", None, None),
            P("parts", "map", None, None),
            P("parts", "map", None, None),
        ),
        check_vma=False,
    )
```

```python
import functools

import jax
import jax.numpy as jnp
from jax import lax
from jax.experimental import pallas as pl
from jax.experimental.pallas import tpu as pltpu
from jax.sharding import PartitionSpec as P

STEPS = 4
ZONES = 8
DT = 0.25
HALF = 0.5 * DT
KBULK = 2.25
GRAV = 0.1
HALO = 2 * STEPS
LANES = 128
F32 = jnp.float32
VX, VY, VZ = range(3)
SXX, SYY, SZZ, SXY, SXZ, SYZ = range(6)
BUOY, LAMB, SHEAR, FAULT, FLOOR = range(5)


class Plan:
    def __init__(self, devices, cells, depth, ny, strips):
        self.n = devices
        self.cells = cells
        self.depth = depth
        self.ny = ny
        self.strips = strips
        self.chunks = max(1, LANES // ny)
        self.sub = depth // self.chunks
        self.lanes = self.chunks * ny
        self.width = cells + 2 * HALO
        self.own_groups = cells // self.chunks
        self.halo_groups = HALO // self.chunks
        self.sent_groups = self.own_groups + self.halo_groups
        self.lead = self.chunks * strips
        self.rows = self.lead * self.sent_groups
        self.back_rows = self.lead * self.own_groups
        self.nx = devices * cells
        self.block = 4 * self.sub
        self.unrolled = self.sub * self.lanes <= 1024
        assert devices % 2 == 0 and cells == HALO and self.block * self.chunks == LANES

    def planes(self, start, stop, body, batch=1):
        if self.unrolled:
            for j in range(start, stop, batch):
                body(j, min(batch, stop - j))
        else:
            def run(j, carry):
                body(j, 1)
                return carry

            lax.fori_loop(start, stop, run, 0)


BATCH = 4
SLOTS = 16


def slot_rows(plan):
    return BATCH * 2 * (plan.sub + 2)


def odd_device():
    return lax.rem(lax.axis_index("map"), 2)


def place(pieces, wanted, block):
    out = None
    for i, piece in enumerate(pieces):
        shift = (i - wanted[i]) * block % piece.shape[-1]
        moved = pltpu.roll(piece, shift, piece.ndim - 1) if shift else piece
        if out is None:
            out = moved
        else:
            lane = lax.broadcasted_iota(jnp.int32, moved.shape, moved.ndim - 1)
            out = jnp.where(lane >= i * block, moved, out)
    return out


def pack_kernel(
    plan, vel_ref, stress_ref, zones_ref, slip_ref, ocean_ref, bathy_ref,
    message_out, crust, border,
    vel, stress, zones, slip, ocean, bathy, turned, grouped, extra, message, sems,
):
    cells, sub, chunks, ny = plan.cells, plan.sub, plan.chunks, plan.ny
    n, strips, block, sent, rows = plan.n, plan.strips, plan.block, plan.sent_groups, plan.rows
    pairs = (
        (ocean_ref, ocean),
        (bathy_ref, bathy),
        (vel_ref, vel),
        (stress_ref, stress),
        (zones_ref, zones),
        (slip_ref, slip),
    )
    copies = [
        pltpu.make_async_copy(source, target, sems.at[i])
        for i, (source, target) in enumerate(pairs)
    ]
    for copy in copies:
        copy.start()
    copies[1].wait()
    depths = bathy[...].astype(F32)
    wide = lax.broadcasted_iota(jnp.int32, depths.shape, 1)
    for d in range(n):
        first = d * cells - HALO - 1
        moved = pltpu.roll(depths, -first % plan.nx, 1)
        moved = jnp.where((wide + first >= 0) & (wide + first < plan.nx), moved, 0.0)
        extra[d * strips : (d + 1) * strips, :] = moved[:, :LANES]
    copies[0].wait()
    count = plan.nx // chunks
    lead = plan.lead
    pad = plan.halo_groups * lead
    grouped[:pad, :] = jnp.zeros((pad, LANES), F32)
    grouped[pad + count * lead :, :] = jnp.zeros((pad, LANES), F32)
    for yl in range(strips):
        stacked = jnp.concatenate(
            [ocean[f, yl, kc * sub : (kc + 1) * sub, :] for kc in range(chunks) for f in range(4)],
            axis=0,
        )
        turned[yl] = stacked.T
        by_x = [turned[yl, pl.ds(i, count, stride=chunks), :] for i in range(chunks)]
        for kc in range(chunks):
            grouped[pl.ds(pad + kc * strips + yl, count, stride=lead), :] = place(
                by_x, [kc] * chunks, block
            )
    for d in range(n):
        start = (d * plan.own_groups + (d % 2) * plan.halo_groups) * lead
        message[d * rows : (d + 1) * rows, :] = grouped[start : start + rows, :]
    pairs = n // 2
    lane = lax.broadcasted_iota(jnp.int32, (pairs, LANES), 1)
    blank = jnp.zeros((1, LANES), F32)
    for odd in range(2):
        slot = (odd * (chunks - 1) * 4 + 2) * sub
        group = odd * (sent - 1)
        for yl in range(strips):
            if odd:
                column = turned[yl, pl.ds(2 * cells + HALO, pairs - 1, stride=2 * cells), :]
                column = jnp.concatenate([column, blank], axis=0)
            else:
                column = turned[yl, pl.ds(2 * cells - HALO - 1, pairs - 1, stride=2 * cells), :]
                column = jnp.concatenate([blank, column], axis=0)
            deep = extra[pl.ds(odd * strips + yl, pairs, stride=2 * strips), :]
            for kc in range(chunks):
                at = odd * rows + group * lead + kc * strips + yl
                old = message[pl.ds(at, pairs, stride=2 * rows), :]
                edge = pltpu.roll(column, (slot - kc * block) % LANES, 1)
                floor = pltpu.roll(deep, (slot + sub - kc * sub) % LANES, 1)
                new = jnp.where((lane >= slot) & (lane < slot + sub), edge, old)
                new = jnp.where((lane >= slot + sub) & (lane < slot + 2 * sub), floor, new)
                message[pl.ds(at, pairs, stride=2 * rows), :] = new
    out = pltpu.make_async_copy(message, message_out, sems.at[6])
    out.start()

    for copy in copies[2:]:
        copy.wait()

    def joined(ref, *at):
        parts = [ref[(*at, pl.ds(kc * sub, sub), slice(None))] for kc in range(chunks)]
        return jnp.concatenate(parts, axis=-1) if chunks > 1 else parts[0]

    for f in range(3):
        for x in range(cells):
            crust[f * cells + x] = joined(vel, f, x)
    for f in range(6):
        for x in range(cells):
            crust[(3 + f) * cells + x] = joined(stress, f, x)
    for x in range(cells):
        crust[9 * cells + x] = (joined(zones, x) + 1).astype(F32)
    fault_chunk = (plan.depth // 2) // sub
    pieces = [
        slip[...] if kc == fault_chunk else jnp.zeros((cells, ny), F32) for kc in range(chunks)
    ]
    fault = jnp.concatenate(pieces, axis=-1) if chunks > 1 else pieces[0]
    if sub > cells:
        fault = jnp.concatenate([fault, jnp.zeros((sub - cells, plan.lanes), F32)], axis=0)
    crust[10 * cells] = fault
    odd = odd_device()
    near = cells - 1
    for f in range(10):
        for i in range(near):
            border[f * near + i] = crust[f * cells + i + odd]
    for i, f in enumerate((SXX, SXY, SXZ)):
        border[10 * near + i] = crust[(3 + f) * cells + near * (1 - odd)]
    border[10 * near + 3] = fault
    out.wait()


class Shifts:
    def __init__(self, plan, memory=None):
        self.plan = plan
        self.memory = memory if plan.unrolled else None
        self.slot = 0
        shape = (plan.sub, plan.lanes)
        self.row = lax.broadcasted_iota(jnp.int32, shape, 0)
        self.lane = lax.broadcasted_iota(jnp.int32, shape, 1)
        self.y = lax.rem(self.lane, plan.ny)
        self.first_row = self.row == 0
        self.last_row = self.row == plan.sub - 1
        self.top = self.first_row & (self.lane < plan.ny)
        self.floor_cell = self.last_row & (self.lane >= plan.lanes - plan.ny)
        self.not_low_y = jnp.where(self.y == 0, 0.0, 1.0).astype(F32)
        self.not_high_y = jnp.where(self.y == plan.ny - 1, 0.0, 1.0).astype(F32)
        self.depth = (
            lax.div(self.lane, plan.ny) * plan.sub + self.row
        ).astype(F32)

    def by_lane(self, f, shift):
        return pltpu.roll(f, shift % self.plan.lanes, f.ndim - 1)

    def by_row(self, f, shift):
        return pltpu.roll(f, shift % self.plan.sub, f.ndim - 2)

    def dy(self, f):
        return self.by_lane(f, -1) * self.not_high_y - self.by_lane(f, 1) * self.not_low_y

    def below(self, f):
        plan = self.plan
        moved = self.by_row(f, -1)
        if plan.chunks > 1:
            moved = jnp.where(self.last_row, self.by_lane(moved, -plan.ny), moved)
        return jnp.where(self.floor_cell, 0.0, moved)

    def above(self, f, top):
        plan = self.plan
        moved = self.by_row(f, 1)
        if plan.chunks > 1:
            moved = jnp.where(self.first_row, self.by_lane(moved, plan.ny), moved)
        return jnp.where(self.top, top, moved)

    def block(self):
        start = self.slot * slot_rows(self.plan)
        self.slot = (self.slot + 1) % SLOTS
        return start

    def dz(self, f, top):
        if self.memory is None or f.ndim == 2:
            return self.below(f) - self.above(f, top * f if top else 0.0)
        plan, memory = self.plan, self.memory
        count, sub = f.shape[:2]
        start, size = self.block(), 2 * (sub + 2)
        for i in range(count):
            memory[pl.ds(start + i * size + 2, sub, stride=2), :] = f[i]
        lane = lax.broadcasted_iota(jnp.int32, (count, plan.lanes), 1)
        first = memory[pl.ds(start + 2, count, stride=size), :]
        last = memory[pl.ds(start + 2 * sub, count, stride=size), :]
        after = jnp.where(lane < plan.lanes - plan.ny, self.by_lane(first, -plan.ny), 0.0)
        before = jnp.where(lane >= plan.ny, self.by_lane(last, plan.ny), top * first)
        memory[pl.ds(start, count, stride=size), :] = before
        memory[pl.ds(start + 2 * (sub + 1), count, stride=size), :] = after
        return jnp.stack(
            [
                memory[pl.ds(start + i * size + 4, sub, stride=2), :]
                - memory[pl.ds(start + i * size, sub, stride=2), :]
                for i in range(count)
            ]
        )

    def spread_rows(self, start, rows):
        plan, memory = self.plan, self.memory
        count = rows.shape[0]
        memory[pl.ds(start, count), :] = rows
        return jnp.stack(
            [
                jnp.broadcast_to(memory[pl.ds(start + i, 1), :], (plan.sub, plan.lanes))
                for i in range(count)
            ]
        )

    def seafloor(self, vz):
        if self.memory is None or vz.ndim == 2:
            row = self.over_chunks(jnp.where(self.top, vz, 0.0))
            return jnp.broadcast_to(row[..., 0:1, :], vz.shape)
        memory, start = self.memory, self.block()
        count, sub, lanes = vz.shape
        for i in range(count):
            memory[pl.ds(start + i * sub, sub), :] = vz[i]
        rows = memory[pl.ds(start, count, stride=sub), :]
        lane = lax.broadcasted_iota(jnp.int32, rows.shape, 1)
        rows = self.over_chunks(jnp.where(lane < self.plan.ny, rows, 0.0))
        return self.spread_rows(start + BATCH * sub, rows)

    def on_top(self, f):
        if self.memory is None or f.ndim == 2:
            shift = self.plan.sub // 2
            while shift:
                f = f + self.by_row(f, shift)
                shift //= 2
            return jnp.where(self.top, self.over_chunks(f), 0.0)
        memory, start = self.memory, self.block()
        count, sub, lanes = f.shape
        for i in range(count):
            memory[pl.ds(start + i * sub, sub), :] = f[i]
        rows = memory[pl.ds(start, count, stride=sub), :]
        for k in range(1, sub):
            rows = rows + memory[pl.ds(start + k, count, stride=sub), :]
        rows = self.spread_rows(start + BATCH * sub, self.over_chunks(rows))
        return jnp.where(self.top, rows, 0.0)

    def over_chunks(self, f):
        shift = self.plan.ny
        while shift < self.plan.lanes:
            f = f + self.by_lane(f, shift)
            shift *= 2
        return f


def acceleration(sh, stress, j, count):
    at, before, after = (pl.ds(j + k, count) for k in (0, -1, 1))
    sxy, sxz = stress[SXY, at], stress[SXZ, at]
    ax = stress[SXX, after] - stress[SXX, before] + sh.dy(sxy) + sh.dz(sxz, 0.0)
    syz = stress[SYZ, at]
    ay = stress[SXY, after] - stress[SXY, before] + sh.dy(stress[SYY, at])
    ay = ay + sh.dz(syz, 0.0)
    szz = stress[SZZ, at]
    az = stress[SXZ, after] - stress[SXZ, before] + sh.dy(syz) + sh.dz(szz, 0.0)
    return ax, ay, az


def strained(sh, vel, stress, mats, j, count):
    at, before, after = (pl.ds(j + k, count) for k in (0, -1, 1))
    vx, vy, vz = vel[VX, at], vel[VY, at], vel[VZ, at]
    exx = vel[VX, after] - vel[VX, before]
    eyy = sh.dy(vy)
    ezz = sh.dz(vz, 1.0)
    mu = mats[SHEAR, at]
    mu2 = mu + mu
    common = mats[LAMB, at] * (exx + eyy + ezz)
    yield SXX, stress[SXX, at] + (common + mu2 * exx)
    yield SYY, stress[SYY, at] + (common + mu2 * eyy)
    yield SZZ, stress[SZZ, at] + (common + mu2 * ezz)
    exy = sh.dy(vx) + vel[VY, after] - vel[VY, before]
    yield SXY, stress[SXY, at] + mu * exy
    exz = sh.dz(vx, 1.0) + vel[VZ, after] - vel[VZ, before]
    yield SXZ, stress[SXZ, at] + (mu * exz + mats[FAULT, at])
    eyz = sh.dz(vy, 1.0) + sh.dy(vz)
    yield SYZ, stress[SYZ, at] + mu * eyz


def bring(plan, sh, material, state, ref, fields, x, count, column, first):
    vel, stress, mats = state
    to = pl.ds(column, count)

    def read(f):
        return ref[pl.ds(f * fields + x, count)]

    for f in range(3):
        vel[f, to] = read(f)
    for f in range(6):
        stress[f, to] = read(3 + f)
    zone = read(9)
    values = [jnp.zeros_like(zone) for _ in range(3)]
    for z in range(ZONES):
        here = zone == float(z + 1)
        values = [jnp.where(here, material(c, z), values[c]) for c in range(3)]
    for c in range(3):
        mats[c, to] = values[c] * HALF
    mats[FLOOR, to] = sh.seafloor(read(VZ))
    for i in range(count):
        slip = ref[ref.shape[0] - 1, pl.ds(first + x + i, 1), :]
        slip = jnp.broadcast_to(slip, (plan.sub, plan.lanes))
        mats[FAULT, column + i] = jnp.where(
            sh.row == (plan.depth // 2) % plan.sub, DT * slip, 0.0
        )


def begin_kernel(plan, table, own, mate, vel, stress, mats, rows):
    cells = plan.cells
    sh = Shifts(plan)
    odd = odd_device()
    state = (vel, stress, mats)
    starts = (HALO + cells * odd, HALO + cells * (1 - odd))
    for start, ref in zip(starts, (own, mate)):
        plan.planes(
            0,
            cells,
            lambda x, count, start=start, ref=ref: bring(
                plan, sh, lambda c, z: table[c, z], state, ref, cells, x, count, start + x, 0
            ),
            BATCH,
        )

    def move(j, count):
        at = pl.ds(j, count)
        b = mats[BUOY, at]
        for f, a in enumerate(acceleration(sh, stress, j, count)):
            vel[f, at] = vel[f, at] + b * a

    plan.planes(HALO + 1, HALO + 2 * cells - 1, move, BATCH)
    for c in range(3):
        for z in range(ZONES):
            at = c * ZONES + z
            rows[at : at + 1, :] = jnp.full((1, plan.lanes), table[c, z], F32)


class Updates:
    def __init__(self, plan, sh, vel, stress, mats, oc, water, bottom, loads):
        self.plan, self.sh = plan, sh
        self.vel, self.stress, self.mats = vel, stress, mats
        self.oc, self.water, self.bottom, self.loads = oc, water, bottom, loads

    def flow_x(self, j, count):
        oc = self.oc
        before, at, after = (pl.ds(j + k, count) for k in range(3))
        oc[1, at] = self.water[at] * (oc[1, at] - HALF * (oc[0, after] - oc[0, before]))

    def flow(self, j, count):
        oc, sh = self.oc, self.sh
        at = pl.ds(j + 1, count)
        p = oc[0, at]
        wet = self.water[at]
        rise = sh.dz(p, -1.0) + self.bottom[at] * p
        oc[3, at] = wet * (oc[3, at] - (HALF * rise + (DT * GRAV) * p))
        oc[2, at] = wet * (oc[2, at] - HALF * sh.dy(p))

    def press(self, j, count, floor):
        oc, sh = self.oc, self.sh
        before, at, after = (pl.ds(j + k, count) for k in range(3))
        w = oc[3, at]
        rise = sh.dz(w, 1.0)
        if floor is not None:
            rise = rise + self.bottom[at] * floor(pl.ds(j, count))
        total = oc[1, after] - oc[1, before] + sh.dy(oc[2, at]) + rise
        oc[0, at] = self.water[at] * (oc[0, at] - (HALF * KBULK) * total)

    def add_floor(self, j, count):
        at = pl.ds(j + 1, count)
        floor = self.first_floor(pl.ds(j, count))
        self.oc[0, at] = self.oc[0, at] - (HALF * KBULK) * (self.bottom[at] * floor)

    def first_floor(self, at):
        return self.mats[FLOOR, at]

    def floor(self, at):
        return self.sh.seafloor(self.vel[VZ, at])

    def load(self, j, count):
        at = pl.ds(j + 1, count)
        return self.sh.on_top(self.bottom[at] * self.oc[0, at])

    def keep(self, j, count):
        self.loads[pl.ds(j, count)] = self.load(j, count)

    def add_load(self, j, count):
        at = pl.ds(j, count)
        self.vel[VZ, at] = self.vel[VZ, at] + self.mats[BUOY, at] * self.load(j, count)

    def move(self, j, count):
        vel = self.vel
        at = pl.ds(j, count)
        ax, ay, az = acceleration(self.sh, self.stress, j, count)
        b = self.mats[BUOY, at]
        vel[VX, at] = vel[VX, at] + b * ax
        vel[VY, at] = vel[VY, at] + b * ay
        vel[VZ, at] = vel[VZ, at] + b * (az + self.load(j, count))

    def strain(self, j, count):
        for f, value in strained(self.sh, self.vel, self.stress, self.mats, j, count):
            self.stress[f, pl.ds(j, count)] = value

    def run(self, spans, inner, send=None):
        def planes(t, inset, update):
            self.plan.planes(*spans(t, inset), update, BATCH)

        def flows(t):
            planes(t, 0, self.flow_x)
            planes(t, 1, self.flow)

        if inner:
            columns = self.vel.shape[1]
            first, last = spans(0, 1)
            self.plan.planes(0, columns, self.flow_x, BATCH)
            self.plan.planes(1, columns - 1, self.flow, BATCH)
            planes(0, 1, functools.partial(self.press, floor=self.first_floor))
            later = functools.partial(self.press, floor=None)
            self.plan.planes(1, first, later, BATCH)
            self.plan.planes(last, columns - 1, later, BATCH)
        else:
            planes(0, 1, self.add_floor)
        for t in range(STEPS - 1):
            flows(t + 1)
            planes(t, 1, self.add_load if inner and t == 0 else self.move)
            if t < STEPS - 2:
                planes(t, 2, self.strain)
            planes(t + 1, 1, functools.partial(self.press, floor=self.floor))
        if send is not None:
            send()
        planes(STEPS - 1, 1, self.keep)


def inner_kernel(
    plan, arrived, swapped, mats, vel_in, stress_in, vel, stress, oc, water, bottom, loads,
    gather, depths, memory,
):
    sub, chunks, n, strips = plan.sub, plan.chunks, plan.n, plan.strips
    cells, sent = plan.cells, plan.sent_groups
    sh = Shifts(plan, memory)
    odd = odd_device()
    half = n // 2
    columns = 2 * cells + 2 * HALO

    def turn(owner, group):
        for core, ref in ((odd, arrived), (1 - odd, swapped)):
            for kc in range(chunks):
                for yl in range(strips):
                    at = owner * plan.rows + group * plan.lead + kc * strips + yl
                    to = kc * plan.ny + core * strips + yl
                    gather[pl.ds(to, half, stride=2 * strips), :] = ref[
                        pl.ds(at, half, stride=2 * plan.rows), :
                    ]
        return gather[...].T

    deeps = []
    for owner in range(2):
        for group in range(sent):
            turned = turn(owner, group)
            for i in range(chunks):
                for f in range(4):
                    at = (i * 4 + f) * sub
                    column = 1 + owner * (cells + HALO) + group * chunks + i
                    oc[f, column] = turned[at : at + sub]
            if owner == 0 and group == 0:
                oc[0, 0] = turned[2 * sub : 3 * sub]
                deeps.append(turned[3 * sub : 4 * sub])
            if owner == 1 and group == sent - 1:
                oc[0, columns + 1] = turned[LANES - 2 * sub : LANES - sub]
                deeps.append(turned[LANES - sub :])
    for i, deep in enumerate(deeps):
        for kc in range(chunks):
            mine = (sh.lane >= kc * plan.ny) & (sh.lane < (kc + 1) * plan.ny)
            depths[i, kc * sub : (kc + 1) * sub, :] = sh.over_chunks(jnp.where(mine, deep, 0.0))

    def mask(owner, j, _):
        low = jnp.broadcast_to(depths[owner, pl.ds(j - owner * cells, 1), :], (sub, plan.lanes))
        wet = jnp.where(sh.depth < low, 1.0, 0.0).astype(F32)
        water[j] = wet
        bottom[j] = jnp.where(sh.depth == low - 1.0, 1.0, 0.0).astype(F32)
        oc[0, j] = oc[0, j] * wet

    def mask_x(j, _):
        oc[1, j] = oc[1, j] * water[j]

    def mask_yw(j, _):
        oc[2, j] = oc[2, j] * water[j]
        oc[3, j] = oc[3, j] * water[j]

    plan.planes(0, plan.width + 2, lambda j, _: mask(0, j, _))
    plan.planes(plan.width + 2, columns + 2, lambda j, _: mask(1, j, _))
    plan.planes(1, columns + 1, mask_x)
    plan.planes(2, columns, mask_yw)

    def bring_in(j, _):
        for f in range(3):
            vel[f, j] = vel_in[f, j]
        for f in range(6):
            stress[f, j] = stress_in[f, j]

    if not plan.unrolled:
        plan.planes(HALO, HALO + 2 * cells, bring_in)
    updates = Updates(plan, sh, vel, stress, mats, oc, water, bottom, loads)
    updates.run(lambda t, inset: (HALO + 2 * t + inset, HALO + 2 * cells - 2 * t - inset), True)


def outer_kernel(
    plan, materials, border, water, bottom, vel_in, stress_in, mats_in, oc_in, loads_in,
    vel, stress, mats, oc, loads, message, gather, rows, memory, sem,
):
    sub, chunks, n, strips, cells = plan.sub, plan.chunks, plan.n, plan.strips, plan.cells
    near = cells - 1
    sh = Shifts(plan, memory)
    odd = odd_device()
    if not plan.unrolled:
        for here, there in (
            (vel, vel_in), (stress, stress_in), (mats, mats_in), (oc, oc_in), (loads, loads_in)
        ):
            here[...] = there[...]
    updates = Updates(plan, sh, vel, stress, mats, oc, water, bottom, loads)

    def material(c, z):
        row = materials[pl.ds(c * ZONES + z, 1), :]
        return jnp.broadcast_to(row, (sub, plan.lanes))

    def side(core):
        low, far = ((1, 0), (HALO + 2 * cells, 2 * HALO + 2 * cells - 1))[core]
        state = (vel, stress, mats)
        plan.planes(
            0,
            near,
            lambda x, count: bring(
                plan, sh, material, state, border, near, x, count, low + x, 1 - core
            ),
            BATCH,
        )
        for i, f in enumerate((SXX, SXY, SXZ)):
            stress[f, far] = border[10 * near + i]

        def spans(t, inset):
            if core == 0:
                return 2 * t + inset, 2 * t + inset + HALO
            last = 2 * HALO + 2 * cells - 2 * t - inset
            return last - HALO, last

        copy = pltpu.make_async_copy(rows, message, sem)

        def send():
            for group in range(plan.own_groups):
                stacked = jnp.concatenate(
                    [
                        oc[f, 1 + HALO + core * cells + group * chunks + i]
                        for i in range(chunks)
                        for f in range(4)
                    ],
                    axis=0,
                )
                gather[group] = stacked.T
                for kc in range(chunks):
                    for yl in range(strips):
                        at = group * plan.lead + kc * strips + yl
                        rows[pl.ds(at, n, stride=plan.back_rows), :] = gather[
                            group, pl.ds(kc * plan.ny + yl, n, stride=strips), :
                        ]
            copy.start()

        updates.run(spans, False, send)
        copy.wait()

    for core in range(2):
        pl.when(odd == core)(functools.partial(side, core))


def end_kernel(plan, vel_all, stress_all, mats_all, loads_all, vel_out, stress_out, vel, stress):
    cells, sub, chunks, ny = plan.cells, plan.sub, plan.chunks, plan.ny
    sh = Shifts(plan)
    first, last = 2 * (STEPS - 1), plan.width - 2 * (STEPS - 1)
    window = pl.ds(cells * odd_device(), plan.width)
    vel_in, stress_in = vel_all.at[:, window], stress_all.at[:, window]
    mats, loads = mats_all.at[:, window], loads_all.at[window]

    def put(out, f, x, count, planes):
        for kc in range(chunks):
            out[f, pl.ds(x, count), kc * sub : (kc + 1) * sub, :] = planes[
                :, :, kc * ny : (kc + 1) * ny
            ]

    def strain(j, count):
        for f, value in strained(sh, vel_in, stress_in, mats, j, count):
            stress[f, pl.ds(j, count)] = value

    def move(j, count):
        at = pl.ds(j, count)
        ax, ay, az = acceleration(sh, stress, j, count)
        b = mats[BUOY, at]
        for f, a in enumerate((ax, ay, az + loads[at])):
            vel[f, at] = vel_in[f, at] + b * a

    def finish(x, count):
        for f in range(3):
            put(vel_out, f, x, count, vel[f, pl.ds(x + HALO, count)])
        for f, value in strained(sh, vel, stress, mats, x + HALO, count):
            put(stress_out, f, x, count, value)

    plan.planes(first, last, strain, BATCH)
    plan.planes(first + 1, last - 1, move, BATCH)
    plan.planes(0, cells, finish, BATCH)


def unpack_kernel(plan, arrived, ocean, turned, strips, sems):
    sub, chunks = plan.sub, plan.chunks
    block = 4 * sub
    copies = [
        pltpu.make_async_copy(strips.at[yl], ocean.at[:, yl], sems.at[yl])
        for yl in range(plan.strips)
    ]
    for yl in range(plan.strips):
        by_chunk = [
            arrived[pl.ds(kc * plan.strips + yl, plan.nx // chunks, stride=plan.lead), :]
            for kc in range(chunks)
        ]
        for i in range(chunks):
            turned[yl, pl.ds(i, plan.nx // chunks, stride=chunks), :] = place(
                by_chunk, [i] * chunks, block
            )
        whole = turned[yl].T
        for kc in range(chunks):
            for f in range(4):
                at = (kc * 4 + f) * sub
                strips[yl, f, kc * sub : (kc + 1) * sub, :] = whole[at : at + sub]
        copies[yl].start()
    for copy in copies:
        copy.wait()


def on_device(plan, velocity, stress, ocean, zones, materials, slip, bathy):
    n, cells, sub, lanes, width = plan.n, plan.cells, plan.sub, plan.lanes, plan.width
    vmem = pl.BlockSpec(memory_space=pltpu.VMEM)
    smem = pl.BlockSpec(memory_space=pltpu.SMEM)
    hbm = pl.BlockSpec(memory_space=pltpu.HBM)

    def shape(*dims):
        return jax.ShapeDtypeStruct(dims, F32)

    def like(array):
        return jax.ShapeDtypeStruct(array.shape, array.dtype)

    def held(array):
        return pltpu.VMEM(array.shape, array.dtype)

    def call(kernel, name, out, ins, scratch, room=16, outs=None, **rest):
        room = room if plan.unrolled else 56
        return pl.pallas_call(
            functools.partial(kernel, plan),
            out_shape=out,
            in_specs=ins,
            out_specs=jax.tree.map(lambda _: vmem, out) if outs is None else outs,
            scratch_shapes=scratch,
            compiler_params=pltpu.CompilerParams(vmem_limit_bytes=room * 1024 * 1024),
            name=name,
            **rest,
        )

    def pinned(array):
        return pltpu.with_memory_space_constraint(array, pltpu.HBM)

    def near(array):
        return pltpu.with_memory_space_constraint(array, pltpu.VMEM) if plan.unrolled else array

    mates = [(i, i ^ 1) for i in range(n)]
    others = [(i, i + 1) for i in range(1, n - 1, 2)]
    others += [(target, source) for source, target in others]
    message, crust, border = call(
        pack_kernel,
        "pack",
        (
            shape(n * plan.rows, LANES),
            shape(10 * cells + 1, sub, lanes),
            shape(10 * cells - 6, sub, lanes),
        ),
        [hbm] * 6,
        [held(a) for a in (velocity, stress, zones, slip, ocean, bathy)]
        + [
            pltpu.VMEM((plan.strips, plan.nx, LANES), F32),
            pltpu.VMEM(
                ((plan.nx // plan.chunks + 2 * plan.halo_groups) * plan.lead, LANES), F32
            ),
            pltpu.VMEM((n * plan.strips, LANES), F32),
            pltpu.VMEM((n * plan.rows, LANES), F32),
            pltpu.SemaphoreType.DMA((7,)),
        ],
        outs=(hbm, vmem, vmem),
    )(*(pinned(a) for a in (velocity, stress, zones, slip, ocean, bathy)))
    arrived = lax.all_to_all(
        message.reshape(n // 2, 2 * plan.rows, LANES),
        "map",
        split_axis=0,
        concat_axis=0,
        axis_index_groups=[list(range(core, n, 2)) for core in range(2)],
        tiled=True,
    ).reshape(n * plan.rows, LANES)
    other = lax.ppermute(border, "map", others)
    mate = lax.ppermute(crust, "map", mates)
    columns = 2 * cells + 2 * HALO
    vel, strs, mats, material_rows = call(
        begin_kernel,
        "first_velocity",
        (
            shape(3, columns, sub, lanes),
            shape(6, columns, sub, lanes),
            shape(5, columns, sub, lanes),
            shape(3 * ZONES, lanes),
        ),
        [smem] + [vmem] * 2,
        [],
    )(materials, crust, mate)
    arrived, vel = lax.optimization_barrier((arrived, vel))
    swapped = lax.ppermute(arrived, "map", mates)
    planes_of = {
        "vel": shape(3, columns, sub, lanes),
        "stress": shape(6, columns, sub, lanes),
        "mats": shape(5, columns, sub, lanes),
        "oc": shape(4, columns + 2, sub, lanes),
        "mask": shape(columns + 2, sub, lanes),
        "loads": shape(columns, sub, lanes),
    }
    vel, strs, oc, water, bottom, loads = call(
        inner_kernel,
        "inner_substeps",
        tuple(planes_of[k] for k in ("vel", "stress", "oc", "mask", "mask", "loads")),
        [vmem] * 5,
        [
            pltpu.VMEM((lanes, LANES), F32),
            pltpu.VMEM((2, plan.depth, lanes), F32),
            pltpu.VMEM((SLOTS * slot_rows(plan), lanes), F32),
        ],
        input_output_aliases={3: 0, 4: 1},
    )(*(near(a) for a in (arrived, swapped, mats, vel, strs)))
    vel, strs, mats, oc, loads, back = call(
        outer_kernel,
        "outer_substeps",
        tuple(planes_of[k] for k in ("vel", "stress", "mats", "oc", "loads"))
        + (shape(n * plan.back_rows, LANES),),
        [vmem] * 9,
        [
            pltpu.VMEM((plan.own_groups, lanes, LANES), F32),
            pltpu.VMEM((n * plan.back_rows, LANES), F32),
            pltpu.VMEM((SLOTS * slot_rows(plan), lanes), F32),
            pltpu.SemaphoreType.DMA,
        ],
        outs=(vmem,) * 5 + (hbm,),
        input_output_aliases={4: 0, 5: 1, 6: 2, 7: 3, 8: 4},
    )(*(near(a) for a in (material_rows, other, water, bottom, vel, strs, mats, oc, loads)))
    returned = lax.all_to_all(
        back.reshape(n, plan.back_rows, LANES), "map", split_axis=0, concat_axis=0, tiled=True
    ).reshape(n * plan.back_rows, LANES)
    new_velocity, new_stress = call(
        end_kernel,
        "last_updates",
        (shape(*velocity.shape), shape(*stress.shape)),
        [vmem] * 4,
        [
            pltpu.VMEM((3, width, sub, lanes), F32),
            pltpu.VMEM((6, width, sub, lanes), F32),
        ],
    )(vel, strs, mats, loads)
    new_ocean = call(
        unpack_kernel,
        "ocean_strips",
        shape(*ocean.shape),
        [vmem],
        [
            pltpu.VMEM((plan.strips, plan.nx, LANES), F32),
            pltpu.VMEM((plan.strips, 4, plan.depth, plan.nx), F32),
            pltpu.SemaphoreType.DMA((plan.strips,)),
        ],
        outs=hbm,
    )(returned)
    return new_velocity, new_stress, new_ocean


def solution(mesh):
    n = mesh.shape["map"]

    def body(velocity, stress, ocean, zones, materials, slip, bathy):
        _, cells, depth, ny = velocity.shape
        plan = Plan(n, cells, depth, ny, ocean.shape[1])
        return on_device(plan, velocity, stress, ocean, zones, materials, slip, bathy)

    return jax.shard_map(
        body,
        mesh=mesh,
        in_specs=(
            P("parts", "map", None, None),
            P("parts", "map", None, None),
            P("parts", "map", None, None),
            P("map", "parts", None),
            P(),
            P("map", "parts"),
            P("map", "parts"),
        ),
        out_specs=(
            P("parts", "map", None, None),
            P("parts", "map", None, None),
            P("parts", "map", None, None),
        ),
        check_vma=False,
    )
```

```python
import functools

import jax
import jax.numpy as jnp
from jax import lax
from jax.experimental import pallas as pl
from jax.experimental.pallas import tpu as pltpu
from jax.sharding import PartitionSpec as P

STEPS = 4
ZONES = 8
DT = 0.25
HALF = 0.5 * DT
KBULK = 2.25
GRAV = 0.1
HALO = 2 * STEPS
LANES = 128
F32 = jnp.float32
VX, VY, VZ = range(3)
SXX, SYY, SZZ, SXY, SXZ, SYZ = range(6)
BUOY, LAMB, SHEAR, FAULT, FLOOR = range(5)


class Plan:
    def __init__(self, devices, cells, depth, ny, strips):
        self.n = devices
        self.cells = cells
        self.depth = depth
        self.ny = ny
        self.strips = strips
        self.chunks = max(1, LANES // ny)
        self.sub = depth // self.chunks
        self.lanes = self.chunks * ny
        self.width = cells + 2 * HALO
        self.own_groups = cells // self.chunks
        self.halo_groups = HALO // self.chunks
        self.sent_groups = self.own_groups + self.halo_groups
        self.lead = self.chunks * strips
        self.rows = self.lead * self.sent_groups
        self.back_rows = self.lead * self.own_groups
        self.nx = devices * cells
        self.block = 4 * self.sub
        self.unrolled = self.sub * self.lanes <= 1024
        assert devices % 2 == 0 and cells == HALO and self.block * self.chunks == LANES

    def planes(self, start, stop, body, batch=1):
        if self.unrolled:
            for j in range(start, stop, batch):
                body(j, min(batch, stop - j))
        else:
            def run(j, carry):
                body(j, 1)
                return carry

            lax.fori_loop(start, stop, run, 0)


BATCH = 8
SLOTS = 16


def slot_rows(plan):
    return BATCH * 2 * (plan.sub + 2)


def odd_device():
    return lax.rem(lax.axis_index("map"), 2)


def place(pieces, wanted, block):
    out = None
    for i, piece in enumerate(pieces):
        shift = (i - wanted[i]) * block % piece.shape[-1]
        moved = pltpu.roll(piece, shift, piece.ndim - 1) if shift else piece
        if out is None:
            out = moved
        else:
            lane = lax.broadcasted_iota(jnp.int32, moved.shape, moved.ndim - 1)
            out = jnp.where(lane >= i * block, moved, out)
    return out


def pack_kernel(
    plan, vel_ref, stress_ref, zones_ref, slip_ref, ocean_ref, bathy_ref,
    message_out, crust, border,
    vel, stress, zones, slip, ocean, bathy, turned, grouped, extra, message, sems,
):
    cells, sub, chunks, ny = plan.cells, plan.sub, plan.chunks, plan.ny
    n, strips, block, sent, rows = plan.n, plan.strips, plan.block, plan.sent_groups, plan.rows
    pairs = (
        (ocean_ref, ocean),
        (bathy_ref, bathy),
        (vel_ref, vel),
        (stress_ref, stress),
        (zones_ref, zones),
        (slip_ref, slip),
    )
    copies = [
        pltpu.make_async_copy(source, target, sems.at[i])
        for i, (source, target) in enumerate(pairs)
    ]
    for copy in copies:
        copy.start()
    copies[1].wait()
    depths = bathy[...].astype(F32)
    wide = lax.broadcasted_iota(jnp.int32, depths.shape, 1)
    for d in range(n):
        first = d * cells - HALO - 1
        moved = pltpu.roll(depths, -first % plan.nx, 1)
        moved = jnp.where((wide + first >= 0) & (wide + first < plan.nx), moved, 0.0)
        extra[d * strips : (d + 1) * strips, :] = moved[:, :LANES]
    copies[0].wait()
    count = plan.nx // chunks
    lead = plan.lead
    pad = plan.halo_groups * lead
    grouped[:pad, :] = jnp.zeros((pad, LANES), F32)
    grouped[pad + count * lead :, :] = jnp.zeros((pad, LANES), F32)
    for yl in range(strips):
        stacked = jnp.concatenate(
            [ocean[f, yl, kc * sub : (kc + 1) * sub, :] for kc in range(chunks) for f in range(4)],
            axis=0,
        )
        turned[yl] = stacked.T
        by_x = [turned[yl, pl.ds(i, count, stride=chunks), :] for i in range(chunks)]
        for kc in range(chunks):
            grouped[pl.ds(pad + kc * strips + yl, count, stride=lead), :] = place(
                by_x, [kc] * chunks, block
            )
    for d in range(n):
        start = (d * plan.own_groups + (d % 2) * plan.halo_groups) * lead
        message[d * rows : (d + 1) * rows, :] = grouped[start : start + rows, :]
    pairs = n // 2
    lane = lax.broadcasted_iota(jnp.int32, (pairs, LANES), 1)
    blank = jnp.zeros((1, LANES), F32)
    for odd in range(2):
        slot = (odd * (chunks - 1) * 4 + 2) * sub
        group = odd * (sent - 1)
        for yl in range(strips):
            if odd:
                column = turned[yl, pl.ds(2 * cells + HALO, pairs - 1, stride=2 * cells), :]
                column = jnp.concatenate([column, blank], axis=0)
            else:
                column = turned[yl, pl.ds(2 * cells - HALO - 1, pairs - 1, stride=2 * cells), :]
                column = jnp.concatenate([blank, column], axis=0)
            deep = extra[pl.ds(odd * strips + yl, pairs, stride=2 * strips), :]
            for kc in range(chunks):
                at = odd * rows + group * lead + kc * strips + yl
                old = message[pl.ds(at, pairs, stride=2 * rows), :]
                edge = pltpu.roll(column, (slot - kc * block) % LANES, 1)
                floor = pltpu.roll(deep, (slot + sub - kc * sub) % LANES, 1)
                new = jnp.where((lane >= slot) & (lane < slot + sub), edge, old)
                new = jnp.where((lane >= slot + sub) & (lane < slot + 2 * sub), floor, new)
                message[pl.ds(at, pairs, stride=2 * rows), :] = new
    out = pltpu.make_async_copy(message, message_out, sems.at[6])
    out.start()

    for copy in copies[2:]:
        copy.wait()

    def joined(ref, *at):
        parts = [ref[(*at, pl.ds(kc * sub, sub), slice(None))] for kc in range(chunks)]
        return jnp.concatenate(parts, axis=-1) if chunks > 1 else parts[0]

    for f in range(3):
        for x in range(cells):
            crust[f * cells + x] = joined(vel, f, x)
    for f in range(6):
        for x in range(cells):
            crust[(3 + f) * cells + x] = joined(stress, f, x)
    for x in range(cells):
        crust[9 * cells + x] = (joined(zones, x) + 1).astype(F32)
    fault_chunk = (plan.depth // 2) // sub
    pieces = [
        slip[...] if kc == fault_chunk else jnp.zeros((cells, ny), F32) for kc in range(chunks)
    ]
    fault = jnp.concatenate(pieces, axis=-1) if chunks > 1 else pieces[0]
    if sub > cells:
        fault = jnp.concatenate([fault, jnp.zeros((sub - cells, plan.lanes), F32)], axis=0)
    crust[10 * cells] = fault
    odd = odd_device()
    near = cells - 1
    for f in range(10):
        for i in range(near):
            border[f * near + i] = crust[f * cells + i + odd]
    for i, f in enumerate((SXX, SXY, SXZ)):
        border[10 * near + i] = crust[(3 + f) * cells + near * (1 - odd)]
    border[10 * near + 3] = fault
    out.wait()


class Shifts:
    def __init__(self, plan, memory=None):
        self.plan = plan
        self.memory = memory if plan.unrolled else None
        self.slot = 0
        shape = (plan.sub, plan.lanes)
        self.row = lax.broadcasted_iota(jnp.int32, shape, 0)
        self.lane = lax.broadcasted_iota(jnp.int32, shape, 1)
        self.y = lax.rem(self.lane, plan.ny)
        self.first_row = self.row == 0
        self.last_row = self.row == plan.sub - 1
        self.top = self.first_row & (self.lane < plan.ny)
        self.floor_cell = self.last_row & (self.lane >= plan.lanes - plan.ny)
        self.not_low_y = jnp.where(self.y == 0, 0.0, 1.0).astype(F32)
        self.not_high_y = jnp.where(self.y == plan.ny - 1, 0.0, 1.0).astype(F32)
        self.depth = (
            lax.div(self.lane, plan.ny) * plan.sub + self.row
        ).astype(F32)

    def by_lane(self, f, shift):
        return pltpu.roll(f, shift % self.plan.lanes, f.ndim - 1)

    def by_row(self, f, shift):
        return pltpu.roll(f, shift % self.plan.sub, f.ndim - 2)

    def dy(self, f):
        return self.by_lane(f, -1) * self.not_high_y - self.by_lane(f, 1) * self.not_low_y

    def below(self, f):
        plan = self.plan
        moved = self.by_row(f, -1)
        if plan.chunks > 1:
            moved = jnp.where(self.last_row, self.by_lane(moved, -plan.ny), moved)
        return jnp.where(self.floor_cell, 0.0, moved)

    def above(self, f, top):
        plan = self.plan
        moved = self.by_row(f, 1)
        if plan.chunks > 1:
            moved = jnp.where(self.first_row, self.by_lane(moved, plan.ny), moved)
        return jnp.where(self.top, top, moved)

    def block(self):
        start = self.slot * slot_rows(self.plan)
        self.slot = (self.slot + 1) % SLOTS
        return start

    def dz(self, f, top):
        if self.memory is None or f.ndim == 2:
            return self.below(f) - self.above(f, top * f if top else 0.0)
        plan, memory = self.plan, self.memory
        count, sub = f.shape[:2]
        start, size = self.block(), 2 * (sub + 2)
        for i in range(count):
            memory[pl.ds(start + i * size + 2, sub, stride=2), :] = f[i]
        lane = lax.broadcasted_iota(jnp.int32, (count, plan.lanes), 1)
        first = memory[pl.ds(start + 2, count, stride=size), :]
        last = memory[pl.ds(start + 2 * sub, count, stride=size), :]
        after = jnp.where(lane < plan.lanes - plan.ny, self.by_lane(first, -plan.ny), 0.0)
        before = jnp.where(lane >= plan.ny, self.by_lane(last, plan.ny), top * first)
        memory[pl.ds(start, count, stride=size), :] = before
        memory[pl.ds(start + 2 * (sub + 1), count, stride=size), :] = after
        return jnp.stack(
            [
                memory[pl.ds(start + i * size + 4, sub, stride=2), :]
                - memory[pl.ds(start + i * size, sub, stride=2), :]
                for i in range(count)
            ]
        )

    def spread_rows(self, start, rows):
        plan, memory = self.plan, self.memory
        count = rows.shape[0]
        memory[pl.ds(start, count), :] = rows
        return jnp.stack(
            [
                jnp.broadcast_to(memory[pl.ds(start + i, 1), :], (plan.sub, plan.lanes))
                for i in range(count)
            ]
        )

    def seafloor(self, vz):
        if self.memory is None or vz.ndim == 2:
            row = self.over_chunks(jnp.where(self.top, vz, 0.0))
            return jnp.broadcast_to(row[..., 0:1, :], vz.shape)
        memory, start = self.memory, self.block()
        count, sub, lanes = vz.shape
        for i in range(count):
            memory[pl.ds(start + i * sub, sub), :] = vz[i]
        rows = memory[pl.ds(start, count, stride=sub), :]
        lane = lax.broadcasted_iota(jnp.int32, rows.shape, 1)
        rows = self.over_chunks(jnp.where(lane < self.plan.ny, rows, 0.0))
        return self.spread_rows(start + BATCH * sub, rows)

    def on_top(self, f):
        if self.memory is None or f.ndim == 2:
            shift = self.plan.sub // 2
            while shift:
                f = f + self.by_row(f, shift)
                shift //= 2
            return jnp.where(self.top, self.over_chunks(f), 0.0)
        memory, start = self.memory, self.block()
        count, sub, lanes = f.shape
        for i in range(count):
            memory[pl.ds(start + i * sub, sub), :] = f[i]
        rows = memory[pl.ds(start, count, stride=sub), :]
        for k in range(1, sub):
            rows = rows + memory[pl.ds(start + k, count, stride=sub), :]
        rows = self.spread_rows(start + BATCH * sub, self.over_chunks(rows))
        return jnp.where(self.top, rows, 0.0)

    def over_chunks(self, f):
        shift = self.plan.ny
        while shift < self.plan.lanes:
            f = f + self.by_lane(f, shift)
            shift *= 2
        return f


def acceleration(sh, stress, j, count):
    at, before, after = (pl.ds(j + k, count) for k in (0, -1, 1))
    sxy, sxz = stress[SXY, at], stress[SXZ, at]
    ax = stress[SXX, after] - stress[SXX, before] + sh.dy(sxy) + sh.dz(sxz, 0.0)
    syz = stress[SYZ, at]
    ay = stress[SXY, after] - stress[SXY, before] + sh.dy(stress[SYY, at])
    ay = ay + sh.dz(syz, 0.0)
    szz = stress[SZZ, at]
    az = stress[SXZ, after] - stress[SXZ, before] + sh.dy(syz) + sh.dz(szz, 0.0)
    return ax, ay, az


def strained(sh, vel, stress, mats, j, count):
    at, before, after = (pl.ds(j + k, count) for k in (0, -1, 1))
    vx, vy, vz = vel[VX, at], vel[VY, at], vel[VZ, at]
    exx = vel[VX, after] - vel[VX, before]
    eyy = sh.dy(vy)
    ezz = sh.dz(vz, 1.0)
    mu = mats[SHEAR, at]
    mu2 = mu + mu
    common = mats[LAMB, at] * (exx + eyy + ezz)
    yield SXX, stress[SXX, at] + (common + mu2 * exx)
    yield SYY, stress[SYY, at] + (common + mu2 * eyy)
    yield SZZ, stress[SZZ, at] + (common + mu2 * ezz)
    exy = sh.dy(vx) + vel[VY, after] - vel[VY, before]
    yield SXY, stress[SXY, at] + mu * exy
    exz = sh.dz(vx, 1.0) + vel[VZ, after] - vel[VZ, before]
    yield SXZ, stress[SXZ, at] + (mu * exz + mats[FAULT, at])
    eyz = sh.dz(vy, 1.0) + sh.dy(vz)
    yield SYZ, stress[SYZ, at] + mu * eyz


def bring(plan, sh, material, state, ref, fields, x, count, column, first):
    vel, stress, mats = state
    to = pl.ds(column, count)

    def read(f):
        return ref[pl.ds(f * fields + x, count)]

    for f in range(3):
        vel[f, to] = read(f)
    for f in range(6):
        stress[f, to] = read(3 + f)
    zone = read(9)
    values = [jnp.zeros_like(zone) for _ in range(3)]
    for z in range(ZONES):
        here = zone == float(z + 1)
        values = [jnp.where(here, material(c, z), values[c]) for c in range(3)]
    for c in range(3):
        mats[c, to] = values[c] * HALF
    mats[FLOOR, to] = sh.seafloor(read(VZ))
    for i in range(count):
        slip = ref[ref.shape[0] - 1, pl.ds(first + x + i, 1), :]
        slip = jnp.broadcast_to(slip, (plan.sub, plan.lanes))
        mats[FAULT, column + i] = jnp.where(
            sh.row == (plan.depth // 2) % plan.sub, DT * slip, 0.0
        )


def begin_kernel(plan, table, own, mate, vel, stress, mats, rows):
    cells = plan.cells
    sh = Shifts(plan)
    odd = odd_device()
    state = (vel, stress, mats)
    starts = (HALO + cells * odd, HALO + cells * (1 - odd))
    for start, ref in zip(starts, (own, mate)):
        plan.planes(
            0,
            cells,
            lambda x, count, start=start, ref=ref: bring(
                plan, sh, lambda c, z: table[c, z], state, ref, cells, x, count, start + x, 0
            ),
            BATCH,
        )

    def move(j, count):
        at = pl.ds(j, count)
        b = mats[BUOY, at]
        for f, a in enumerate(acceleration(sh, stress, j, count)):
            vel[f, at] = vel[f, at] + b * a

    plan.planes(HALO + 1, HALO + 2 * cells - 1, move, BATCH)
    for c in range(3):
        for z in range(ZONES):
            at = c * ZONES + z
            rows[at : at + 1, :] = jnp.full((1, plan.lanes), table[c, z], F32)


class Updates:
    def __init__(self, plan, sh, vel, stress, mats, oc, water, bottom, loads):
        self.plan, self.sh = plan, sh
        self.vel, self.stress, self.mats = vel, stress, mats
        self.oc, self.water, self.bottom, self.loads = oc, water, bottom, loads

    def flow_x(self, j, count):
        oc = self.oc
        before, at, after = (pl.ds(j + k, count) for k in range(3))
        oc[1, at] = self.water[at] * (oc[1, at] - HALF * (oc[0, after] - oc[0, before]))

    def flow(self, j, count):
        oc, sh = self.oc, self.sh
        at = pl.ds(j + 1, count)
        p = oc[0, at]
        wet = self.water[at]
        rise = sh.dz(p, -1.0) + self.bottom[at] * p
        oc[3, at] = wet * (oc[3, at] - (HALF * rise + (DT * GRAV) * p))
        oc[2, at] = wet * (oc[2, at] - HALF * sh.dy(p))

    def press(self, j, count, floor):
        oc, sh = self.oc, self.sh
        before, at, after = (pl.ds(j + k, count) for k in range(3))
        w = oc[3, at]
        rise = sh.dz(w, 1.0)
        if floor is not None:
            rise = rise + self.bottom[at] * floor(pl.ds(j, count))
        total = oc[1, after] - oc[1, before] + sh.dy(oc[2, at]) + rise
        oc[0, at] = self.water[at] * (oc[0, at] - (HALF * KBULK) * total)

    def add_floor(self, j, count):
        at = pl.ds(j + 1, count)
        floor = self.first_floor(pl.ds(j, count))
        self.oc[0, at] = self.oc[0, at] - (HALF * KBULK) * (self.bottom[at] * floor)

    def first_floor(self, at):
        return self.mats[FLOOR, at]

    def floor(self, at):
        return self.sh.seafloor(self.vel[VZ, at])

    def load(self, j, count):
        at = pl.ds(j + 1, count)
        return self.sh.on_top(self.bottom[at] * self.oc[0, at])

    def keep(self, j, count):
        self.loads[pl.ds(j, count)] = self.load(j, count)

    def add_load(self, j, count):
        at = pl.ds(j, count)
        self.vel[VZ, at] = self.vel[VZ, at] + self.mats[BUOY, at] * self.load(j, count)

    def move(self, j, count):
        vel = self.vel
        at = pl.ds(j, count)
        ax, ay, az = acceleration(self.sh, self.stress, j, count)
        b = self.mats[BUOY, at]
        vel[VX, at] = vel[VX, at] + b * ax
        vel[VY, at] = vel[VY, at] + b * ay
        vel[VZ, at] = vel[VZ, at] + b * (az + self.load(j, count))

    def strain(self, j, count):
        for f, value in strained(self.sh, self.vel, self.stress, self.mats, j, count):
            self.stress[f, pl.ds(j, count)] = value

    def run(self, spans, inner, send=None):
        def planes(t, inset, update):
            self.plan.planes(*spans(t, inset), update, BATCH)

        def flows(t):
            planes(t, 0, self.flow_x)
            planes(t, 1, self.flow)

        if inner:
            columns = self.vel.shape[1]
            first, last = spans(0, 1)
            self.plan.planes(0, columns, self.flow_x, BATCH)
            self.plan.planes(1, columns - 1, self.flow, BATCH)
            planes(0, 1, functools.partial(self.press, floor=self.first_floor))
            later = functools.partial(self.press, floor=None)
            self.plan.planes(1, first, later, BATCH)
            self.plan.planes(last, columns - 1, later, BATCH)
        else:
            planes(0, 1, self.add_floor)
        for t in range(STEPS - 1):
            flows(t + 1)
            planes(t, 1, self.add_load if inner and t == 0 else self.move)
            if t < STEPS - 2:
                planes(t, 2, self.strain)
            planes(t + 1, 1, functools.partial(self.press, floor=self.floor))
        if send is not None:
            send()
        planes(STEPS - 1, 1, self.keep)


def inner_kernel(
    plan, arrived, swapped, mats, vel_in, stress_in, vel, stress, oc, water, bottom, loads,
    gather, depths, memory,
):
    sub, chunks, n, strips = plan.sub, plan.chunks, plan.n, plan.strips
    cells, sent = plan.cells, plan.sent_groups
    sh = Shifts(plan, memory)
    odd = odd_device()
    half = n // 2
    columns = 2 * cells + 2 * HALO

    def turn(owner, group):
        for core, ref in ((odd, arrived), (1 - odd, swapped)):
            for kc in range(chunks):
                for yl in range(strips):
                    at = owner * plan.rows + group * plan.lead + kc * strips + yl
                    to = kc * plan.ny + core * strips + yl
                    gather[pl.ds(to, half, stride=2 * strips), :] = ref[
                        pl.ds(at, half, stride=2 * plan.rows), :
                    ]
        return gather[...].T

    deeps = []
    for owner in range(2):
        for group in range(sent):
            turned = turn(owner, group)
            for i in range(chunks):
                for f in range(4):
                    at = (i * 4 + f) * sub
                    column = 1 + owner * (cells + HALO) + group * chunks + i
                    oc[f, column] = turned[at : at + sub]
            if owner == 0 and group == 0:
                oc[0, 0] = turned[2 * sub : 3 * sub]
                deeps.append(turned[3 * sub : 4 * sub])
            if owner == 1 and group == sent - 1:
                oc[0, columns + 1] = turned[LANES - 2 * sub : LANES - sub]
                deeps.append(turned[LANES - sub :])
    for i, deep in enumerate(deeps):
        for kc in range(chunks):
            mine = (sh.lane >= kc * plan.ny) & (sh.lane < (kc + 1) * plan.ny)
            depths[i, kc * sub : (kc + 1) * sub, :] = sh.over_chunks(jnp.where(mine, deep, 0.0))

    def mask(owner, j, _):
        low = jnp.broadcast_to(depths[owner, pl.ds(j - owner * cells, 1), :], (sub, plan.lanes))
        wet = jnp.where(sh.depth < low, 1.0, 0.0).astype(F32)
        water[j] = wet
        bottom[j] = jnp.where(sh.depth == low - 1.0, 1.0, 0.0).astype(F32)
        oc[0, j] = oc[0, j] * wet

    def mask_x(j, _):
        oc[1, j] = oc[1, j] * water[j]

    def mask_yw(j, _):
        oc[2, j] = oc[2, j] * water[j]
        oc[3, j] = oc[3, j] * water[j]

    plan.planes(0, plan.width + 2, lambda j, _: mask(0, j, _))
    plan.planes(plan.width + 2, columns + 2, lambda j, _: mask(1, j, _))
    plan.planes(1, columns + 1, mask_x)
    plan.planes(2, columns, mask_yw)

    def bring_in(j, _):
        for f in range(3):
            vel[f, j] = vel_in[f, j]
        for f in range(6):
            stress[f, j] = stress_in[f, j]

    if not plan.unrolled:
        plan.planes(HALO, HALO + 2 * cells, bring_in)
    updates = Updates(plan, sh, vel, stress, mats, oc, water, bottom, loads)
    updates.run(lambda t, inset: (HALO + 2 * t + inset, HALO + 2 * cells - 2 * t - inset), True)


def outer_kernel(
    plan, materials, border, water, bottom, vel_in, stress_in, mats_in, oc_in, loads_in,
    vel, stress, mats, oc, loads, rows, gather, memory,
):
    sub, chunks, n, strips, cells = plan.sub, plan.chunks, plan.n, plan.strips, plan.cells
    near = cells - 1
    sh = Shifts(plan, memory)
    odd = odd_device()
    if not plan.unrolled:
        for here, there in (
            (vel, vel_in), (stress, stress_in), (mats, mats_in), (oc, oc_in), (loads, loads_in)
        ):
            here[...] = there[...]
    updates = Updates(plan, sh, vel, stress, mats, oc, water, bottom, loads)

    def material(c, z):
        row = materials[pl.ds(c * ZONES + z, 1), :]
        return jnp.broadcast_to(row, (sub, plan.lanes))

    def side(core):
        low, far = ((1, 0), (HALO + 2 * cells, 2 * HALO + 2 * cells - 1))[core]
        state = (vel, stress, mats)
        plan.planes(
            0,
            near,
            lambda x, count: bring(
                plan, sh, material, state, border, near, x, count, low + x, 1 - core
            ),
            BATCH,
        )
        for i, f in enumerate((SXX, SXY, SXZ)):
            stress[f, far] = border[10 * near + i]

        def spans(t, inset):
            if core == 0:
                return 2 * t + inset, 2 * t + inset + HALO
            last = 2 * HALO + 2 * cells - 2 * t - inset
            return last - HALO, last

        def send():
            for group in range(plan.own_groups):
                stacked = jnp.concatenate(
                    [
                        oc[f, 1 + HALO + core * cells + group * chunks + i]
                        for i in range(chunks)
                        for f in range(4)
                    ],
                    axis=0,
                )
                gather[group] = stacked.T
                for kc in range(chunks):
                    for yl in range(strips):
                        at = group * plan.lead + kc * strips + yl
                        rows[pl.ds(at, n, stride=plan.back_rows), :] = gather[
                            group, pl.ds(kc * plan.ny + yl, n, stride=strips), :
                        ]

        updates.run(spans, False, send)

    for core in range(2):
        pl.when(odd == core)(functools.partial(side, core))


def end_kernel(plan, vel_all, stress_all, mats_all, loads_all, vel_out, stress_out, vel, stress):
    cells, sub, chunks, ny = plan.cells, plan.sub, plan.chunks, plan.ny
    sh = Shifts(plan)
    first, last = 2 * (STEPS - 1), plan.width - 2 * (STEPS - 1)
    window = pl.ds(cells * odd_device(), plan.width)
    vel_in, stress_in = vel_all.at[:, window], stress_all.at[:, window]
    mats, loads = mats_all.at[:, window], loads_all.at[window]

    def put(out, f, x, count, planes):
        for kc in range(chunks):
            out[f, pl.ds(x, count), kc * sub : (kc + 1) * sub, :] = planes[
                :, :, kc * ny : (kc + 1) * ny
            ]

    def strain(j, count):
        for f, value in strained(sh, vel_in, stress_in, mats, j, count):
            stress[f, pl.ds(j, count)] = value

    def move(j, count):
        at = pl.ds(j, count)
        ax, ay, az = acceleration(sh, stress, j, count)
        b = mats[BUOY, at]
        for f, a in enumerate((ax, ay, az + loads[at])):
            vel[f, at] = vel_in[f, at] + b * a

    def finish(x, count):
        for f in range(3):
            put(vel_out, f, x, count, vel[f, pl.ds(x + HALO, count)])
        for f, value in strained(sh, vel, stress, mats, x + HALO, count):
            put(stress_out, f, x, count, value)

    plan.planes(first, last, strain, BATCH)
    plan.planes(first + 1, last - 1, move, BATCH)
    plan.planes(0, cells, finish, BATCH)


def unpack_kernel(plan, arrived, ocean, turned, strips, sems):
    sub, chunks = plan.sub, plan.chunks
    block = 4 * sub
    copies = [
        pltpu.make_async_copy(strips.at[yl], ocean.at[:, yl], sems.at[yl])
        for yl in range(plan.strips)
    ]
    for yl in range(plan.strips):
        by_chunk = [
            arrived[pl.ds(kc * plan.strips + yl, plan.nx // chunks, stride=plan.lead), :]
            for kc in range(chunks)
        ]
        for i in range(chunks):
            turned[yl, pl.ds(i, plan.nx // chunks, stride=chunks), :] = place(
                by_chunk, [i] * chunks, block
            )
        whole = turned[yl].T
        for kc in range(chunks):
            for f in range(4):
                at = (kc * 4 + f) * sub
                strips[yl, f, kc * sub : (kc + 1) * sub, :] = whole[at : at + sub]
        copies[yl].start()
    for copy in copies:
        copy.wait()


def on_device(plan, velocity, stress, ocean, zones, materials, slip, bathy):
    n, cells, sub, lanes, width = plan.n, plan.cells, plan.sub, plan.lanes, plan.width
    vmem = pl.BlockSpec(memory_space=pltpu.VMEM)
    smem = pl.BlockSpec(memory_space=pltpu.SMEM)
    hbm = pl.BlockSpec(memory_space=pltpu.HBM)

    def shape(*dims):
        return jax.ShapeDtypeStruct(dims, F32)

    def in_vmem(*dims):
        return pltpu.VMEM(dims, F32) if plan.unrolled else shape(*dims)

    def like(array):
        return jax.ShapeDtypeStruct(array.shape, array.dtype)

    def held(array):
        return pltpu.VMEM(array.shape, array.dtype)

    def call(kernel, name, out, ins, scratch, room=16, outs=None, **rest):
        room = room if plan.unrolled else 56
        return pl.pallas_call(
            functools.partial(kernel, plan),
            out_shape=out,
            in_specs=ins,
            out_specs=jax.tree.map(lambda _: vmem, out) if outs is None else outs,
            scratch_shapes=scratch,
            compiler_params=pltpu.CompilerParams(vmem_limit_bytes=room * 1024 * 1024),
            name=name,
            **rest,
        )

    def pinned(array):
        return pltpu.with_memory_space_constraint(array, pltpu.HBM)

    def near(array):
        return pltpu.with_memory_space_constraint(array, pltpu.VMEM) if plan.unrolled else array

    mates = [(i, i ^ 1) for i in range(n)]
    others = [(i, i + 1) for i in range(1, n - 1, 2)]
    others += [(target, source) for source, target in others]
    message, crust, border = call(
        pack_kernel,
        "pack",
        (
            shape(n * plan.rows, LANES),
            shape(10 * cells + 1, sub, lanes),
            shape(10 * cells - 6, sub, lanes),
        ),
        [hbm] * 6,
        [held(a) for a in (velocity, stress, zones, slip, ocean, bathy)]
        + [
            pltpu.VMEM((plan.strips, plan.nx, LANES), F32),
            pltpu.VMEM(
                ((plan.nx // plan.chunks + 2 * plan.halo_groups) * plan.lead, LANES), F32
            ),
            pltpu.VMEM((n * plan.strips, LANES), F32),
            pltpu.VMEM((n * plan.rows, LANES), F32),
            pltpu.SemaphoreType.DMA((7,)),
        ],
        outs=(hbm, vmem, vmem),
    )(*(pinned(a) for a in (velocity, stress, zones, slip, ocean, bathy)))
    arrived = lax.all_to_all(
        message.reshape(n // 2, 2 * plan.rows, LANES),
        "map",
        split_axis=0,
        concat_axis=0,
        axis_index_groups=[list(range(core, n, 2)) for core in range(2)],
        tiled=True,
    ).reshape(n * plan.rows, LANES)
    other = lax.ppermute(border, "map", others)
    mate = lax.ppermute(crust, "map", mates)
    columns = 2 * cells + 2 * HALO
    vel, strs, mats, material_rows = call(
        begin_kernel,
        "first_velocity",
        (
            shape(3, columns, sub, lanes),
            shape(6, columns, sub, lanes),
            shape(5, columns, sub, lanes),
            shape(3 * ZONES, lanes),
        ),
        [smem] + [vmem] * 2,
        [],
    )(materials, crust, mate)
    arrived, vel = lax.optimization_barrier((arrived, vel))
    swapped = lax.ppermute(arrived, "map", mates)
    planes_of = {
        "vel": shape(3, columns, sub, lanes),
        "stress": shape(6, columns, sub, lanes),
        "mats": shape(5, columns, sub, lanes),
        "oc": shape(4, columns + 2, sub, lanes),
        "mask": shape(columns + 2, sub, lanes),
        "loads": shape(columns, sub, lanes),
    }
    vel, strs, oc, water, bottom, loads = call(
        inner_kernel,
        "inner_substeps",
        tuple(planes_of[k] for k in ("vel", "stress", "oc", "mask", "mask", "loads")),
        [vmem] * 5,
        [
            pltpu.VMEM((lanes, LANES), F32),
            pltpu.VMEM((2, plan.depth, lanes), F32),
            pltpu.VMEM((SLOTS * slot_rows(plan), lanes), F32),
        ],
        input_output_aliases={3: 0, 4: 1},
    )(*(near(a) for a in (arrived, swapped, mats, vel, strs)))
    vel, strs, mats, oc, loads, back = call(
        outer_kernel,
        "outer_substeps",
        tuple(planes_of[k] for k in ("vel", "stress", "mats", "oc", "loads"))
        + (in_vmem(n * plan.back_rows, LANES),),
        [vmem] * 9,
        [
            pltpu.VMEM((plan.own_groups, lanes, LANES), F32),
            pltpu.VMEM((SLOTS * slot_rows(plan), lanes), F32),
        ],
        outs=(vmem,) * 6,
        input_output_aliases={4: 0, 5: 1, 6: 2, 7: 3, 8: 4},
    )(*(near(a) for a in (material_rows, other, water, bottom, vel, strs, mats, oc, loads)))
    returned = lax.all_to_all(
        back.reshape(n, plan.back_rows, LANES), "map", split_axis=0, concat_axis=0, tiled=True
    ).reshape(n * plan.back_rows, LANES)
    new_velocity, new_stress = call(
        end_kernel,
        "last_updates",
        (shape(*velocity.shape), shape(*stress.shape)),
        [vmem] * 4,
        [
            pltpu.VMEM((3, width, sub, lanes), F32),
            pltpu.VMEM((6, width, sub, lanes), F32),
        ],
    )(vel, strs, mats, loads)
    new_ocean = call(
        unpack_kernel,
        "ocean_strips",
        shape(*ocean.shape),
        [vmem],
        [
            pltpu.VMEM((plan.strips, plan.nx, LANES), F32),
            pltpu.VMEM((plan.strips, 4, plan.depth, plan.nx), F32),
            pltpu.SemaphoreType.DMA((plan.strips,)),
        ],
        outs=hbm,
    )(returned)
    return new_velocity, new_stress, new_ocean


def solution(mesh):
    n = mesh.shape["map"]

    def body(velocity, stress, ocean, zones, materials, slip, bathy):
        _, cells, depth, ny = velocity.shape
        plan = Plan(n, cells, depth, ny, ocean.shape[1])
        return on_device(plan, velocity, stress, ocean, zones, materials, slip, bathy)

    return jax.shard_map(
        body,
        mesh=mesh,
        in_specs=(
            P("parts", "map", None, None),
            P("parts", "map", None, None),
            P("parts", "map", None, None),
            P("map", "parts", None),
            P(),
            P("map", "parts"),
            P("map", "parts"),
        ),
        out_specs=(
            P("parts", "map", None, None),
            P("parts", "map", None, None),
            P("parts", "map", None, None),
        ),
        check_vma=False,
    )
```

```python
import functools

import jax
import jax.numpy as jnp
from jax import lax
from jax.experimental import pallas as pl
from jax.experimental.pallas import tpu as pltpu
from jax.sharding import PartitionSpec as P

STEPS = 4
ZONES = 8
DT = 0.25
HALF = 0.5 * DT
KBULK = 2.25
GRAV = 0.1
HALO = 2 * STEPS
LANES = 128
F32 = jnp.float32
VX, VY, VZ = range(3)
SXX, SYY, SZZ, SXY, SXZ, SYZ = range(6)
BUOY, LAMB, SHEAR, FAULT, FLOOR = range(5)


class Plan:
    def __init__(self, devices, cells, depth, ny, strips):
        self.n = devices
        self.cells = cells
        self.depth = depth
        self.ny = ny
        self.strips = strips
        self.chunks = max(1, LANES // ny)
        self.sub = depth // self.chunks
        self.lanes = self.chunks * ny
        self.width = cells + 2 * HALO
        self.own_groups = cells // self.chunks
        self.halo_groups = HALO // self.chunks
        self.sent_groups = self.own_groups + self.halo_groups
        self.lead = self.chunks * strips
        self.rows = self.lead * self.sent_groups
        self.back_rows = self.lead * self.own_groups
        self.nx = devices * cells
        self.block = 4 * self.sub
        self.unrolled = self.sub * self.lanes <= 1024
        assert devices % 2 == 0 and cells == HALO and self.block * self.chunks == LANES

    def planes(self, start, stop, body, batch=1):
        if self.unrolled:
            for j in range(start, stop, batch):
                body(j, min(batch, stop - j))
        else:
            def run(j, carry):
                body(j, 1)
                return carry

            lax.fori_loop(start, stop, run, 0)


BATCH = 8
SLOTS = 16


def slot_rows(plan):
    return BATCH * 2 * (plan.sub + 2)


def odd_device():
    return lax.rem(lax.axis_index("map"), 2)


def place(pieces, wanted, block):
    out = None
    for i, piece in enumerate(pieces):
        shift = (i - wanted[i]) * block % piece.shape[-1]
        moved = pltpu.roll(piece, shift, piece.ndim - 1) if shift else piece
        if out is None:
            out = moved
        else:
            lane = lax.broadcasted_iota(jnp.int32, moved.shape, moved.ndim - 1)
            out = jnp.where(lane >= i * block, moved, out)
    return out


def pack_kernel(
    plan, vel_ref, stress_ref, zones_ref, slip_ref, ocean_ref, bathy_ref,
    message_out, crust, border,
    vel, stress, zones, slip, ocean, bathy, turned, grouped, extra, message, sems,
):
    cells, sub, chunks, ny = plan.cells, plan.sub, plan.chunks, plan.ny
    n, strips, block, sent, rows = plan.n, plan.strips, plan.block, plan.sent_groups, plan.rows
    pairs = (
        (ocean_ref, ocean),
        (bathy_ref, bathy),
        (vel_ref, vel),
        (stress_ref, stress),
        (zones_ref, zones),
        (slip_ref, slip),
    )
    copies = [
        pltpu.make_async_copy(source, target, sems.at[i])
        for i, (source, target) in enumerate(pairs)
    ]
    for copy in copies:
        copy.start()
    copies[1].wait()
    depths = bathy[...].astype(F32)
    wide = lax.broadcasted_iota(jnp.int32, depths.shape, 1)
    for d in range(n):
        first = d * cells - HALO - 1
        moved = pltpu.roll(depths, -first % plan.nx, 1)
        moved = jnp.where((wide + first >= 0) & (wide + first < plan.nx), moved, 0.0)
        extra[d * strips : (d + 1) * strips, :] = moved[:, :LANES]
    copies[0].wait()
    count = plan.nx // chunks
    lead = plan.lead
    pad = plan.halo_groups * lead
    grouped[:pad, :] = jnp.zeros((pad, LANES), F32)
    grouped[pad + count * lead :, :] = jnp.zeros((pad, LANES), F32)
    for yl in range(strips):
        stacked = jnp.concatenate(
            [ocean[f, yl, kc * sub : (kc + 1) * sub, :] for kc in range(chunks) for f in range(4)],
            axis=0,
        )
        turned[yl] = stacked.T
        by_x = [turned[yl, pl.ds(i, count, stride=chunks), :] for i in range(chunks)]
        for kc in range(chunks):
            grouped[pl.ds(pad + kc * strips + yl, count, stride=lead), :] = place(
                by_x, [kc] * chunks, block
            )
    for d in range(n):
        start = (d * plan.own_groups + (d % 2) * plan.halo_groups) * lead
        message[d * rows : (d + 1) * rows, :] = grouped[start : start + rows, :]
    pairs = n // 2
    lane = lax.broadcasted_iota(jnp.int32, (pairs, LANES), 1)
    blank = jnp.zeros((1, LANES), F32)
    for odd in range(2):
        slot = (odd * (chunks - 1) * 4 + 2) * sub
        group = odd * (sent - 1)
        for yl in range(strips):
            if odd:
                column = turned[yl, pl.ds(2 * cells + HALO, pairs - 1, stride=2 * cells), :]
                column = jnp.concatenate([column, blank], axis=0)
            else:
                column = turned[yl, pl.ds(2 * cells - HALO - 1, pairs - 1, stride=2 * cells), :]
                column = jnp.concatenate([blank, column], axis=0)
            deep = extra[pl.ds(odd * strips + yl, pairs, stride=2 * strips), :]
            for kc in range(chunks):
                at = odd * rows + group * lead + kc * strips + yl
                old = message[pl.ds(at, pairs, stride=2 * rows), :]
                edge = pltpu.roll(column, (slot - kc * block) % LANES, 1)
                floor = pltpu.roll(deep, (slot + sub - kc * sub) % LANES, 1)
                new = jnp.where((lane >= slot) & (lane < slot + sub), edge, old)
                new = jnp.where((lane >= slot + sub) & (lane < slot + 2 * sub), floor, new)
                message[pl.ds(at, pairs, stride=2 * rows), :] = new
    out = pltpu.make_async_copy(message, message_out, sems.at[6])
    out.start()

    for copy in copies[2:]:
        copy.wait()

    def joined(ref, *at):
        parts = [ref[(*at, pl.ds(kc * sub, sub), slice(None))] for kc in range(chunks)]
        return jnp.concatenate(parts, axis=-1) if chunks > 1 else parts[0]

    for f in range(3):
        for x in range(cells):
            crust[f * cells + x] = joined(vel, f, x)
    for f in range(6):
        for x in range(cells):
            crust[(3 + f) * cells + x] = joined(stress, f, x)
    for x in range(cells):
        crust[9 * cells + x] = (joined(zones, x) + 1).astype(F32)
    fault_chunk = (plan.depth // 2) // sub
    pieces = [
        slip[...] if kc == fault_chunk else jnp.zeros((cells, ny), F32) for kc in range(chunks)
    ]
    fault = jnp.concatenate(pieces, axis=-1) if chunks > 1 else pieces[0]
    if sub > cells:
        fault = jnp.concatenate([fault, jnp.zeros((sub - cells, plan.lanes), F32)], axis=0)
    crust[10 * cells] = fault
    odd = odd_device()
    near = cells - 1
    for f in range(10):
        for i in range(near):
            border[f * near + i] = crust[f * cells + i + odd]
    for i, f in enumerate((SXX, SXY, SXZ)):
        border[10 * near + i] = crust[(3 + f) * cells + near * (1 - odd)]
    border[10 * near + 3] = fault
    out.wait()


class Shifts:
    def __init__(self, plan, memory=None):
        self.plan = plan
        self.memory = memory if plan.unrolled else None
        self.slot = 0
        shape = (plan.sub, plan.lanes)
        self.row = lax.broadcasted_iota(jnp.int32, shape, 0)
        self.lane = lax.broadcasted_iota(jnp.int32, shape, 1)
        self.y = lax.rem(self.lane, plan.ny)
        self.first_row = self.row == 0
        self.last_row = self.row == plan.sub - 1
        self.top = self.first_row & (self.lane < plan.ny)
        self.floor_cell = self.last_row & (self.lane >= plan.lanes - plan.ny)
        self.not_low_y = jnp.where(self.y == 0, 0.0, 1.0).astype(F32)
        self.not_high_y = jnp.where(self.y == plan.ny - 1, 0.0, 1.0).astype(F32)
        self.depth = (
            lax.div(self.lane, plan.ny) * plan.sub + self.row
        ).astype(F32)

    def by_lane(self, f, shift):
        return pltpu.roll(f, shift % self.plan.lanes, f.ndim - 1)

    def by_row(self, f, shift):
        return pltpu.roll(f, shift % self.plan.sub, f.ndim - 2)

    def dy(self, f):
        return self.by_lane(f, -1) * self.not_high_y - self.by_lane(f, 1) * self.not_low_y

    def below(self, f):
        plan = self.plan
        moved = self.by_row(f, -1)
        if plan.chunks > 1:
            moved = jnp.where(self.last_row, self.by_lane(moved, -plan.ny), moved)
        return jnp.where(self.floor_cell, 0.0, moved)

    def above(self, f, top):
        plan = self.plan
        moved = self.by_row(f, 1)
        if plan.chunks > 1:
            moved = jnp.where(self.first_row, self.by_lane(moved, plan.ny), moved)
        return jnp.where(self.top, top, moved)

    def block(self):
        start = self.slot * slot_rows(self.plan)
        self.slot = (self.slot + 1) % SLOTS
        return start

    def dz(self, f, top):
        if self.memory is None or f.ndim == 2:
            return self.below(f) - self.above(f, top * f if top else 0.0)
        plan, memory = self.plan, self.memory
        count, sub = f.shape[:2]
        start, size = self.block(), 2 * (sub + 2)
        for i in range(count):
            memory[pl.ds(start + i * size + 2, sub, stride=2), :] = f[i]
        lane = lax.broadcasted_iota(jnp.int32, (count, plan.lanes), 1)
        first = memory[pl.ds(start + 2, count, stride=size), :]
        last = memory[pl.ds(start + 2 * sub, count, stride=size), :]
        after = jnp.where(lane < plan.lanes - plan.ny, self.by_lane(first, -plan.ny), 0.0)
        before = jnp.where(lane >= plan.ny, self.by_lane(last, plan.ny), top * first)
        memory[pl.ds(start, count, stride=size), :] = before
        memory[pl.ds(start + 2 * (sub + 1), count, stride=size), :] = after
        return jnp.stack(
            [
                memory[pl.ds(start + i * size + 4, sub, stride=2), :]
                - memory[pl.ds(start + i * size, sub, stride=2), :]
                for i in range(count)
            ]
        )

    def spread_rows(self, start, rows):
        plan, memory = self.plan, self.memory
        count = rows.shape[0]
        memory[pl.ds(start, count), :] = rows
        return jnp.stack(
            [
                jnp.broadcast_to(memory[pl.ds(start + i, 1), :], (plan.sub, plan.lanes))
                for i in range(count)
            ]
        )

    def seafloor(self, vz):
        if self.memory is None or vz.ndim == 2:
            row = self.over_chunks(jnp.where(self.top, vz, 0.0))
            return jnp.broadcast_to(row[..., 0:1, :], vz.shape)
        memory, start = self.memory, self.block()
        count, sub, lanes = vz.shape
        for i in range(count):
            memory[pl.ds(start + i * sub, sub), :] = vz[i]
        rows = memory[pl.ds(start, count, stride=sub), :]
        lane = lax.broadcasted_iota(jnp.int32, rows.shape, 1)
        rows = self.over_chunks(jnp.where(lane < self.plan.ny, rows, 0.0))
        return self.spread_rows(start + BATCH * sub, rows)

    def on_top(self, f):
        if self.memory is None or f.ndim == 2:
            shift = self.plan.sub // 2
            while shift:
                f = f + self.by_row(f, shift)
                shift //= 2
            return jnp.where(self.top, self.over_chunks(f), 0.0)
        memory, start = self.memory, self.block()
        count, sub, lanes = f.shape
        for i in range(count):
            memory[pl.ds(start + i * sub, sub), :] = f[i]
        rows = memory[pl.ds(start, count, stride=sub), :]
        for k in range(1, sub):
            rows = rows + memory[pl.ds(start + k, count, stride=sub), :]
        rows = self.spread_rows(start + BATCH * sub, self.over_chunks(rows))
        return jnp.where(self.top, rows, 0.0)

    def over_chunks(self, f):
        shift = self.plan.ny
        while shift < self.plan.lanes:
            f = f + self.by_lane(f, shift)
            shift *= 2
        return f


def acceleration(sh, stress, j, count):
    at, before, after = (pl.ds(j + k, count) for k in (0, -1, 1))
    sxy, sxz = stress[SXY, at], stress[SXZ, at]
    ax = stress[SXX, after] - stress[SXX, before] + sh.dy(sxy) + sh.dz(sxz, 0.0)
    syz = stress[SYZ, at]
    ay = stress[SXY, after] - stress[SXY, before] + sh.dy(stress[SYY, at])
    ay = ay + sh.dz(syz, 0.0)
    szz = stress[SZZ, at]
    az = stress[SXZ, after] - stress[SXZ, before] + sh.dy(syz) + sh.dz(szz, 0.0)
    return ax, ay, az


def strained(sh, vel, stress, mats, j, count):
    at, before, after = (pl.ds(j + k, count) for k in (0, -1, 1))
    vx, vy, vz = vel[VX, at], vel[VY, at], vel[VZ, at]
    exx = vel[VX, after] - vel[VX, before]
    eyy = sh.dy(vy)
    ezz = sh.dz(vz, 1.0)
    mu = mats[SHEAR, at]
    mu2 = mu + mu
    common = mats[LAMB, at] * (exx + eyy + ezz)
    yield SXX, stress[SXX, at] + (common + mu2 * exx)
    yield SYY, stress[SYY, at] + (common + mu2 * eyy)
    yield SZZ, stress[SZZ, at] + (common + mu2 * ezz)
    exy = sh.dy(vx) + vel[VY, after] - vel[VY, before]
    yield SXY, stress[SXY, at] + mu * exy
    exz = sh.dz(vx, 1.0) + vel[VZ, after] - vel[VZ, before]
    yield SXZ, stress[SXZ, at] + (mu * exz + mats[FAULT, at])
    eyz = sh.dz(vy, 1.0) + sh.dy(vz)
    yield SYZ, stress[SYZ, at] + mu * eyz


def bring(plan, sh, material, state, ref, fields, x, count, column, first):
    vel, stress, mats = state
    to = pl.ds(column, count)

    def read(f):
        return ref[pl.ds(f * fields + x, count)]

    for f in range(3):
        vel[f, to] = read(f)
    for f in range(6):
        stress[f, to] = read(3 + f)
    zone = read(9)
    values = [jnp.zeros_like(zone) for _ in range(3)]
    for z in range(ZONES):
        here = zone == float(z + 1)
        values = [jnp.where(here, material(c, z), values[c]) for c in range(3)]
    for c in range(3):
        mats[c, to] = values[c] * HALF
    mats[FLOOR, to] = sh.seafloor(read(VZ))
    for i in range(count):
        slip = ref[ref.shape[0] - 1, pl.ds(first + x + i, 1), :]
        slip = jnp.broadcast_to(slip, (plan.sub, plan.lanes))
        mats[FAULT, column + i] = jnp.where(
            sh.row == (plan.depth // 2) % plan.sub, DT * slip, 0.0
        )


def begin_kernel(plan, table, own, mate, vel, stress, mats, rows):
    cells = plan.cells
    sh = Shifts(plan)
    odd = odd_device()
    state = (vel, stress, mats)
    starts = (HALO + cells * odd, HALO + cells * (1 - odd))
    for start, ref in zip(starts, (own, mate)):
        plan.planes(
            0,
            cells,
            lambda x, count, start=start, ref=ref: bring(
                plan, sh, lambda c, z: table[c, z], state, ref, cells, x, count, start + x, 0
            ),
            BATCH,
        )

    def move(j, count):
        at = pl.ds(j, count)
        b = mats[BUOY, at]
        for f, a in enumerate(acceleration(sh, stress, j, count)):
            vel[f, at] = vel[f, at] + b * a

    plan.planes(HALO + 1, HALO + 2 * cells - 1, move, BATCH)
    for c in range(3):
        for z in range(ZONES):
            at = c * ZONES + z
            rows[at : at + 1, :] = jnp.full((1, plan.lanes), table[c, z], F32)


class Updates:
    def __init__(self, plan, sh, vel, stress, mats, oc, water, bottom):
        self.plan, self.sh = plan, sh
        self.vel, self.stress, self.mats = vel, stress, mats
        self.oc, self.water, self.bottom = oc, water, bottom

    def flow_x(self, j, count):
        oc = self.oc
        before, at, after = (pl.ds(j + k, count) for k in range(3))
        oc[1, at] = self.water[at] * (oc[1, at] - HALF * (oc[0, after] - oc[0, before]))

    def flow(self, j, count):
        oc, sh = self.oc, self.sh
        at = pl.ds(j + 1, count)
        p = oc[0, at]
        wet = self.water[at]
        rise = sh.dz(p, -1.0) + self.bottom[at] * p
        oc[3, at] = wet * (oc[3, at] - (HALF * rise + (DT * GRAV) * p))
        oc[2, at] = wet * (oc[2, at] - HALF * sh.dy(p))

    def press(self, j, count, floor):
        oc, sh = self.oc, self.sh
        before, at, after = (pl.ds(j + k, count) for k in range(3))
        w = oc[3, at]
        rise = sh.dz(w, 1.0)
        if floor is not None:
            rise = rise + self.bottom[at] * floor(pl.ds(j, count))
        total = oc[1, after] - oc[1, before] + sh.dy(oc[2, at]) + rise
        oc[0, at] = self.water[at] * (oc[0, at] - (HALF * KBULK) * total)

    def add_floor(self, j, count):
        at = pl.ds(j + 1, count)
        floor = self.first_floor(pl.ds(j, count))
        self.oc[0, at] = self.oc[0, at] - (HALF * KBULK) * (self.bottom[at] * floor)

    def first_floor(self, at):
        return self.mats[FLOOR, at]

    def floor(self, at):
        return self.sh.seafloor(self.vel[VZ, at])

    def load(self, j, count):
        at = pl.ds(j + 1, count)
        return self.sh.on_top(self.bottom[at] * self.oc[0, at])

    def add_load(self, j, count):
        at = pl.ds(j, count)
        self.vel[VZ, at] = self.vel[VZ, at] + self.mats[BUOY, at] * self.load(j, count)

    def move(self, j, count):
        vel = self.vel
        at = pl.ds(j, count)
        ax, ay, az = acceleration(self.sh, self.stress, j, count)
        b = self.mats[BUOY, at]
        vel[VX, at] = vel[VX, at] + b * ax
        vel[VY, at] = vel[VY, at] + b * ay
        vel[VZ, at] = vel[VZ, at] + b * (az + self.load(j, count))

    def strain(self, j, count):
        for f, value in strained(self.sh, self.vel, self.stress, self.mats, j, count):
            self.stress[f, pl.ds(j, count)] = value

    def run(self, spans, inner, send=None):
        def planes(t, inset, update):
            self.plan.planes(*spans(t, inset), update, BATCH)

        def flows(t):
            planes(t, 0, self.flow_x)
            planes(t, 1, self.flow)

        if inner:
            columns = self.vel.shape[1]
            first, last = spans(0, 1)
            self.plan.planes(0, columns, self.flow_x, BATCH)
            self.plan.planes(1, columns - 1, self.flow, BATCH)
            planes(0, 1, functools.partial(self.press, floor=self.first_floor))
            later = functools.partial(self.press, floor=None)
            self.plan.planes(1, first, later, BATCH)
            self.plan.planes(last, columns - 1, later, BATCH)
        else:
            planes(0, 1, self.add_floor)
        for t in range(STEPS - 1):
            flows(t + 1)
            planes(t, 1, self.add_load if inner and t == 0 else self.move)
            if t < STEPS - 2:
                planes(t, 2, self.strain)
            planes(t + 1, 1, functools.partial(self.press, floor=self.floor))
        if send is not None:
            send()


def inner_kernel(
    plan, arrived, swapped, mats, vel_in, stress_in, vel, stress, oc, water, bottom,
    gather, depths, memory,
):
    sub, chunks, n, strips = plan.sub, plan.chunks, plan.n, plan.strips
    cells, sent = plan.cells, plan.sent_groups
    sh = Shifts(plan, memory)
    odd = odd_device()
    half = n // 2
    columns = 2 * cells + 2 * HALO

    def turn(owner, group):
        for core, ref in ((odd, arrived), (1 - odd, swapped)):
            for kc in range(chunks):
                for yl in range(strips):
                    at = owner * plan.rows + group * plan.lead + kc * strips + yl
                    to = kc * plan.ny + core * strips + yl
                    gather[pl.ds(to, half, stride=2 * strips), :] = ref[
                        pl.ds(at, half, stride=2 * plan.rows), :
                    ]
        return gather[...].T

    deeps = []
    for owner in range(2):
        for group in range(sent):
            turned = turn(owner, group)
            for i in range(chunks):
                for f in range(4):
                    at = (i * 4 + f) * sub
                    column = 1 + owner * (cells + HALO) + group * chunks + i
                    oc[f, column] = turned[at : at + sub]
            if owner == 0 and group == 0:
                oc[0, 0] = turned[2 * sub : 3 * sub]
                deeps.append(turned[3 * sub : 4 * sub])
            if owner == 1 and group == sent - 1:
                oc[0, columns + 1] = turned[LANES - 2 * sub : LANES - sub]
                deeps.append(turned[LANES - sub :])
    for i, deep in enumerate(deeps):
        for kc in range(chunks):
            mine = (sh.lane >= kc * plan.ny) & (sh.lane < (kc + 1) * plan.ny)
            depths[i, kc * sub : (kc + 1) * sub, :] = sh.over_chunks(jnp.where(mine, deep, 0.0))

    def mask(owner, j, _):
        low = jnp.broadcast_to(depths[owner, pl.ds(j - owner * cells, 1), :], (sub, plan.lanes))
        wet = jnp.where(sh.depth < low, 1.0, 0.0).astype(F32)
        water[j] = wet
        bottom[j] = jnp.where(sh.depth == low - 1.0, 1.0, 0.0).astype(F32)
        oc[0, j] = oc[0, j] * wet

    def mask_x(j, _):
        oc[1, j] = oc[1, j] * water[j]

    def mask_yw(j, _):
        oc[2, j] = oc[2, j] * water[j]
        oc[3, j] = oc[3, j] * water[j]

    plan.planes(0, plan.width + 2, lambda j, _: mask(0, j, _))
    plan.planes(plan.width + 2, columns + 2, lambda j, _: mask(1, j, _))
    plan.planes(1, columns + 1, mask_x)
    plan.planes(2, columns, mask_yw)

    def bring_in(j, _):
        for f in range(3):
            vel[f, j] = vel_in[f, j]
        for f in range(6):
            stress[f, j] = stress_in[f, j]

    if not plan.unrolled:
        plan.planes(HALO, HALO + 2 * cells, bring_in)
    updates = Updates(plan, sh, vel, stress, mats, oc, water, bottom)
    updates.run(lambda t, inset: (HALO + 2 * t + inset, HALO + 2 * cells - 2 * t - inset), True)


def outer_kernel(
    plan, materials, border, water, bottom, vel_in, stress_in, mats_in, oc_in,
    vel, stress, mats, oc, rows, gather, memory,
):
    sub, chunks, n, strips, cells = plan.sub, plan.chunks, plan.n, plan.strips, plan.cells
    near = cells - 1
    sh = Shifts(plan, memory)
    odd = odd_device()
    if not plan.unrolled:
        for here, there in (
            (vel, vel_in), (stress, stress_in), (mats, mats_in), (oc, oc_in)
        ):
            here[...] = there[...]
    updates = Updates(plan, sh, vel, stress, mats, oc, water, bottom)

    def material(c, z):
        row = materials[pl.ds(c * ZONES + z, 1), :]
        return jnp.broadcast_to(row, (sub, plan.lanes))

    def side(core):
        low, far = ((1, 0), (HALO + 2 * cells, 2 * HALO + 2 * cells - 1))[core]
        state = (vel, stress, mats)
        plan.planes(
            0,
            near,
            lambda x, count: bring(
                plan, sh, material, state, border, near, x, count, low + x, 1 - core
            ),
            BATCH,
        )
        for i, f in enumerate((SXX, SXY, SXZ)):
            stress[f, far] = border[10 * near + i]

        def spans(t, inset):
            if core == 0:
                return 2 * t + inset, 2 * t + inset + HALO
            last = 2 * HALO + 2 * cells - 2 * t - inset
            return last - HALO, last

        def send():
            for group in range(plan.own_groups):
                stacked = jnp.concatenate(
                    [
                        oc[f, 1 + HALO + core * cells + group * chunks + i]
                        for i in range(chunks)
                        for f in range(4)
                    ],
                    axis=0,
                )
                gather[group] = stacked.T
                for kc in range(chunks):
                    for yl in range(strips):
                        at = group * plan.lead + kc * strips + yl
                        rows[pl.ds(at, n, stride=plan.back_rows), :] = gather[
                            group, pl.ds(kc * plan.ny + yl, n, stride=strips), :
                        ]

        updates.run(spans, False, send)

    for core in range(2):
        pl.when(odd == core)(functools.partial(side, core))


def end_kernel(
    plan, vel_all, stress_all, mats_all, oc_all, bottom_all, vel_out, stress_out, vel, stress
):
    cells, sub, chunks, ny = plan.cells, plan.sub, plan.chunks, plan.ny
    sh = Shifts(plan)
    first, last = 2 * (STEPS - 1), plan.width - 2 * (STEPS - 1)
    window = pl.ds(cells * odd_device(), plan.width)
    vel_in, stress_in = vel_all.at[:, window], stress_all.at[:, window]
    mats = mats_all.at[:, window]
    window = pl.ds(cells * odd_device(), plan.width + 2)
    pressure, bottom = oc_all.at[0, window], bottom_all.at[window]

    def put(out, f, x, count, planes):
        for kc in range(chunks):
            out[f, pl.ds(x, count), kc * sub : (kc + 1) * sub, :] = planes[
                :, :, kc * ny : (kc + 1) * ny
            ]

    def strain(j, count):
        for f, value in strained(sh, vel_in, stress_in, mats, j, count):
            stress[f, pl.ds(j, count)] = value

    def move(j, count):
        at = pl.ds(j, count)
        ax, ay, az = acceleration(sh, stress, j, count)
        b = mats[BUOY, at]
        wet = pl.ds(j + 1, count)
        load = sh.on_top(bottom[wet] * pressure[wet])
        for f, a in enumerate((ax, ay, az + load)):
            vel[f, at] = vel_in[f, at] + b * a

    def finish(x, count):
        for f in range(3):
            put(vel_out, f, x, count, vel[f, pl.ds(x + HALO, count)])
        for f, value in strained(sh, vel, stress, mats, x + HALO, count):
            put(stress_out, f, x, count, value)

    plan.planes(first, last, strain, BATCH)
    plan.planes(first + 1, last - 1, move, BATCH)
    plan.planes(0, cells, finish, BATCH)


def unpack_kernel(plan, arrived, ocean, turned, strips, sems):
    sub, chunks = plan.sub, plan.chunks
    block = 4 * sub
    copies = [
        pltpu.make_async_copy(strips.at[yl], ocean.at[:, yl], sems.at[yl])
        for yl in range(plan.strips)
    ]
    for yl in range(plan.strips):
        by_chunk = [
            arrived[pl.ds(kc * plan.strips + yl, plan.nx // chunks, stride=plan.lead), :]
            for kc in range(chunks)
        ]
        for i in range(chunks):
            turned[yl, pl.ds(i, plan.nx // chunks, stride=chunks), :] = place(
                by_chunk, [i] * chunks, block
            )
        whole = turned[yl].T
        for kc in range(chunks):
            for f in range(4):
                at = (kc * 4 + f) * sub
                strips[yl, f, kc * sub : (kc + 1) * sub, :] = whole[at : at + sub]
        copies[yl].start()
    for copy in copies:
        copy.wait()


def on_device(plan, velocity, stress, ocean, zones, materials, slip, bathy):
    n, cells, sub, lanes, width = plan.n, plan.cells, plan.sub, plan.lanes, plan.width
    vmem = pl.BlockSpec(memory_space=pltpu.VMEM)
    smem = pl.BlockSpec(memory_space=pltpu.SMEM)
    hbm = pl.BlockSpec(memory_space=pltpu.HBM)

    def shape(*dims):
        return jax.ShapeDtypeStruct(dims, F32)

    def in_vmem(*dims):
        return pltpu.VMEM(dims, F32) if plan.unrolled else shape(*dims)

    def like(array):
        return jax.ShapeDtypeStruct(array.shape, array.dtype)

    def held(array):
        return pltpu.VMEM(array.shape, array.dtype)

    def call(kernel, name, out, ins, scratch, room=16, outs=None, **rest):
        room = room if plan.unrolled else 56
        return pl.pallas_call(
            functools.partial(kernel, plan),
            out_shape=out,
            in_specs=ins,
            out_specs=jax.tree.map(lambda _: vmem, out) if outs is None else outs,
            scratch_shapes=scratch,
            compiler_params=pltpu.CompilerParams(vmem_limit_bytes=room * 1024 * 1024),
            name=name,
            **rest,
        )

    def pinned(array):
        return pltpu.with_memory_space_constraint(array, pltpu.HBM)

    def near(array):
        return pltpu.with_memory_space_constraint(array, pltpu.VMEM) if plan.unrolled else array

    mates = [(i, i ^ 1) for i in range(n)]
    others = [(i, i + 1) for i in range(1, n - 1, 2)]
    others += [(target, source) for source, target in others]
    message, crust, border = call(
        pack_kernel,
        "pack",
        (
            shape(n * plan.rows, LANES),
            shape(10 * cells + 1, sub, lanes),
            shape(10 * cells - 6, sub, lanes),
        ),
        [hbm] * 6,
        [held(a) for a in (velocity, stress, zones, slip, ocean, bathy)]
        + [
            pltpu.VMEM((plan.strips, plan.nx, LANES), F32),
            pltpu.VMEM(
                ((plan.nx // plan.chunks + 2 * plan.halo_groups) * plan.lead, LANES), F32
            ),
            pltpu.VMEM((n * plan.strips, LANES), F32),
            pltpu.VMEM((n * plan.rows, LANES), F32),
            pltpu.SemaphoreType.DMA((7,)),
        ],
        outs=(hbm, vmem, vmem),
    )(*(pinned(a) for a in (velocity, stress, zones, slip, ocean, bathy)))
    arrived = lax.all_to_all(
        message.reshape(n // 2, 2 * plan.rows, LANES),
        "map",
        split_axis=0,
        concat_axis=0,
        axis_index_groups=[list(range(core, n, 2)) for core in range(2)],
        tiled=True,
    ).reshape(n * plan.rows, LANES)
    other = lax.ppermute(border, "map", others)
    mate = lax.ppermute(crust, "map", mates)
    columns = 2 * cells + 2 * HALO
    vel, strs, mats, material_rows = call(
        begin_kernel,
        "first_velocity",
        (
            shape(3, columns, sub, lanes),
            shape(6, columns, sub, lanes),
            shape(5, columns, sub, lanes),
            shape(3 * ZONES, lanes),
        ),
        [smem] + [vmem] * 2,
        [],
    )(materials, crust, mate)
    arrived, vel = lax.optimization_barrier((arrived, vel))
    swapped = lax.ppermute(arrived, "map", mates)
    planes_of = {
        "vel": shape(3, columns, sub, lanes),
        "stress": shape(6, columns, sub, lanes),
        "mats": shape(5, columns, sub, lanes),
        "oc": shape(4, columns + 2, sub, lanes),
        "mask": shape(columns + 2, sub, lanes),
    }
    vel, strs, oc, water, bottom = call(
        inner_kernel,
        "inner_substeps",
        tuple(planes_of[k] for k in ("vel", "stress", "oc", "mask", "mask")),
        [vmem] * 5,
        [
            pltpu.VMEM((lanes, LANES), F32),
            pltpu.VMEM((2, plan.depth, lanes), F32),
            pltpu.VMEM((SLOTS * slot_rows(plan), lanes), F32),
        ],
        input_output_aliases={3: 0, 4: 1},
    )(*(near(a) for a in (arrived, swapped, mats, vel, strs)))
    vel, strs, mats, oc, back = call(
        outer_kernel,
        "outer_substeps",
        tuple(planes_of[k] for k in ("vel", "stress", "mats", "oc"))
        + (in_vmem(n * plan.back_rows, LANES),),
        [vmem] * 8,
        [
            pltpu.VMEM((plan.own_groups, lanes, LANES), F32),
            pltpu.VMEM((SLOTS * slot_rows(plan), lanes), F32),
        ],
        outs=(vmem,) * 5,
        input_output_aliases={4: 0, 5: 1, 6: 2, 7: 3},
    )(*(near(a) for a in (material_rows, other, water, bottom, vel, strs, mats, oc)))
    returned = lax.all_to_all(
        back.reshape(n, plan.back_rows, LANES), "map", split_axis=0, concat_axis=0, tiled=True
    ).reshape(n * plan.back_rows, LANES)
    new_velocity, new_stress = call(
        end_kernel,
        "last_updates",
        (shape(*velocity.shape), shape(*stress.shape)),
        [vmem] * 5,
        [
            pltpu.VMEM((3, width, sub, lanes), F32),
            pltpu.VMEM((6, width, sub, lanes), F32),
        ],
    )(vel, strs, mats, oc, bottom)
    new_ocean = call(
        unpack_kernel,
        "ocean_strips",
        shape(*ocean.shape),
        [vmem],
        [
            pltpu.VMEM((plan.strips, plan.nx, LANES), F32),
            pltpu.VMEM((plan.strips, 4, plan.depth, plan.nx), F32),
            pltpu.SemaphoreType.DMA((plan.strips,)),
        ],
        outs=hbm,
    )(returned)
    return new_velocity, new_stress, new_ocean


def solution(mesh):
    n = mesh.shape["map"]

    def body(velocity, stress, ocean, zones, materials, slip, bathy):
        _, cells, depth, ny = velocity.shape
        plan = Plan(n, cells, depth, ny, ocean.shape[1])
        return on_device(plan, velocity, stress, ocean, zones, materials, slip, bathy)

    return jax.shard_map(
        body,
        mesh=mesh,
        in_specs=(
            P("parts", "map", None, None),
            P("parts", "map", None, None),
            P("parts", "map", None, None),
            P("map", "parts", None),
            P(),
            P("map", "parts"),
            P("map", "parts"),
        ),
        out_specs=(
            P("parts", "map", None, None),
            P("parts", "map", None, None),
            P("parts", "map", None, None),
        ),
        check_vma=False,
    )
```

```python
import functools

import jax
import jax.numpy as jnp
from jax import lax
from jax.experimental import pallas as pl
from jax.experimental.pallas import tpu as pltpu
from jax.sharding import PartitionSpec as P

STEPS = 4
ZONES = 8
DT = 0.25
HALF = 0.5 * DT
KBULK = 2.25
GRAV = 0.1
HALO = 2 * STEPS
LANES = 128
F32 = jnp.float32
VX, VY, VZ = range(3)
SXX, SYY, SZZ, SXY, SXZ, SYZ = range(6)
BUOY, LAMB, SHEAR, FAULT, FLOOR = range(5)


class Plan:
    def __init__(self, devices, cells, depth, ny, strips):
        self.n = devices
        self.cells = cells
        self.depth = depth
        self.ny = ny
        self.strips = strips
        self.chunks = max(1, LANES // ny)
        self.sub = depth // self.chunks
        self.lanes = self.chunks * ny
        self.width = cells + 2 * HALO
        self.own_groups = cells // self.chunks
        self.halo_groups = HALO // self.chunks
        self.sent_groups = self.own_groups + self.halo_groups
        self.lead = self.chunks * strips
        self.rows = self.lead * self.sent_groups
        self.back_rows = self.lead * self.own_groups
        self.nx = devices * cells
        self.block = 4 * self.sub
        self.unrolled = self.sub * self.lanes <= 1024
        assert devices % 2 == 0 and cells == HALO and self.block * self.chunks == LANES

    def planes(self, start, stop, body, batch=1):
        if self.unrolled:
            for j in range(start, stop, batch):
                body(j, min(batch, stop - j))
        else:
            def run(j, carry):
                body(j, 1)
                return carry

            lax.fori_loop(start, stop, run, 0)


BATCH = 8
SLOTS = 16


def slot_rows(plan):
    return BATCH * 2 * (plan.sub + 2)


def odd_device():
    return lax.rem(lax.axis_index("map"), 2)


def place(pieces, wanted, block):
    out = None
    for i, piece in enumerate(pieces):
        shift = (i - wanted[i]) * block % piece.shape[-1]
        moved = pltpu.roll(piece, shift, piece.ndim - 1) if shift else piece
        if out is None:
            out = moved
        else:
            lane = lax.broadcasted_iota(jnp.int32, moved.shape, moved.ndim - 1)
            out = jnp.where(lane >= i * block, moved, out)
    return out


def pack_kernel(
    plan, vel_ref, stress_ref, zones_ref, slip_ref, ocean_ref, bathy_ref,
    message_out, crust, border,
    vel, stress, zones, slip, ocean, bathy, turned, grouped, extra, message, sems,
):
    cells, sub, chunks, ny = plan.cells, plan.sub, plan.chunks, plan.ny
    n, strips, block, sent, rows = plan.n, plan.strips, plan.block, plan.sent_groups, plan.rows
    pairs = (
        (ocean_ref, ocean),
        (bathy_ref, bathy),
        (vel_ref, vel),
        (stress_ref, stress),
        (zones_ref, zones),
        (slip_ref, slip),
    )
    copies = [
        pltpu.make_async_copy(source, target, sems.at[i])
        for i, (source, target) in enumerate(pairs)
    ]
    for copy in copies:
        copy.start()
    copies[1].wait()
    depths = bathy[...].astype(F32)
    wide = lax.broadcasted_iota(jnp.int32, depths.shape, 1)
    for d in range(n):
        first = d * cells - HALO - 1
        moved = pltpu.roll(depths, -first % plan.nx, 1)
        moved = jnp.where((wide + first >= 0) & (wide + first < plan.nx), moved, 0.0)
        extra[d * strips : (d + 1) * strips, :] = moved[:, :LANES]
    copies[0].wait()
    count = plan.nx // chunks
    lead = plan.lead
    pad = plan.halo_groups * lead
    grouped[:pad, :] = jnp.zeros((pad, LANES), F32)
    grouped[pad + count * lead :, :] = jnp.zeros((pad, LANES), F32)
    for yl in range(strips):
        stacked = jnp.concatenate(
            [ocean[f, yl, kc * sub : (kc + 1) * sub, :] for kc in range(chunks) for f in range(4)],
            axis=0,
        )
        turned[yl] = stacked.T
        by_x = [turned[yl, pl.ds(i, count, stride=chunks), :] for i in range(chunks)]
        for kc in range(chunks):
            grouped[pl.ds(pad + kc * strips + yl, count, stride=lead), :] = place(
                by_x, [kc] * chunks, block
            )
    pairs = n // 2
    lane = lax.broadcasted_iota(jnp.int32, (pairs, LANES), 1)
    blank = jnp.zeros((1, LANES), F32)
    slots = {}
    for odd in range(2):
        slot = (odd * (chunks - 1) * 4 + 2) * sub
        for yl in range(strips):
            if odd:
                column = turned[yl, pl.ds(2 * cells + HALO, pairs - 1, stride=2 * cells), :]
                column = jnp.concatenate([column, blank], axis=0)
            else:
                column = turned[yl, pl.ds(2 * cells - HALO - 1, pairs - 1, stride=2 * cells), :]
                column = jnp.concatenate([blank, column], axis=0)
            deep = extra[pl.ds(odd * strips + yl, pairs, stride=2 * strips), :]
            for kc in range(chunks):
                edge = pltpu.roll(column, (slot - kc * block) % LANES, 1)
                floor = pltpu.roll(deep, (slot + sub - kc * sub) % LANES, 1)
                slots[odd, kc, yl] = jnp.where(lane < slot + sub, edge, floor)
    outs = []
    for part in range(2):
        for d in range(part * pairs, (part + 1) * pairs):
            start = (d * plan.own_groups + (d % 2) * plan.halo_groups) * lead
            message[d * rows : (d + 1) * rows, :] = grouped[start : start + rows, :]
        some = pl.ds(part * pairs * rows, pairs * rows)
        mine = slice(part * pairs // 2, (part + 1) * pairs // 2)
        for (odd, kc, yl), new in slots.items():
            slot = (odd * (chunks - 1) * 4 + 2) * sub
            at = part * pairs * rows + odd * rows + odd * (sent - 1) * lead + kc * strips + yl
            to = pl.ds(at, pairs // 2, stride=2 * rows)
            inside = (lane[mine] >= slot) & (lane[mine] < slot + 2 * sub)
            message[to, :] = jnp.where(inside, new[mine], message[to, :])
        outs.append(
            pltpu.make_async_copy(message.at[some], message_out.at[some], sems.at[6 + part])
        )
        outs[-1].start()

    for copy in copies[2:]:
        copy.wait()

    def joined(ref, *at):
        parts = [ref[(*at, pl.ds(kc * sub, sub), slice(None))] for kc in range(chunks)]
        return jnp.concatenate(parts, axis=-1) if chunks > 1 else parts[0]

    for f in range(3):
        for x in range(cells):
            crust[f * cells + x] = joined(vel, f, x)
    for f in range(6):
        for x in range(cells):
            crust[(3 + f) * cells + x] = joined(stress, f, x)
    for x in range(cells):
        crust[9 * cells + x] = (joined(zones, x) + 1).astype(F32)
    fault_chunk = (plan.depth // 2) // sub
    pieces = [
        slip[...] if kc == fault_chunk else jnp.zeros((cells, ny), F32) for kc in range(chunks)
    ]
    fault = jnp.concatenate(pieces, axis=-1) if chunks > 1 else pieces[0]
    if sub > cells:
        fault = jnp.concatenate([fault, jnp.zeros((sub - cells, plan.lanes), F32)], axis=0)
    crust[10 * cells] = fault
    odd = odd_device()
    near = cells - 1
    for f in range(10):
        for i in range(near):
            border[f * near + i] = crust[f * cells + i + odd]
    for i, f in enumerate((SXX, SXY, SXZ)):
        border[10 * near + i] = crust[(3 + f) * cells + near * (1 - odd)]
    border[10 * near + 3] = fault
    for out in outs:
        out.wait()


class Shifts:
    def __init__(self, plan, memory=None):
        self.plan = plan
        self.memory = memory if plan.unrolled else None
        self.slot = 0
        shape = (plan.sub, plan.lanes)
        self.row = lax.broadcasted_iota(jnp.int32, shape, 0)
        self.lane = lax.broadcasted_iota(jnp.int32, shape, 1)
        self.y = lax.rem(self.lane, plan.ny)
        self.first_row = self.row == 0
        self.last_row = self.row == plan.sub - 1
        self.top = self.first_row & (self.lane < plan.ny)
        self.floor_cell = self.last_row & (self.lane >= plan.lanes - plan.ny)
        self.not_low_y = jnp.where(self.y == 0, 0.0, 1.0).astype(F32)
        self.not_high_y = jnp.where(self.y == plan.ny - 1, 0.0, 1.0).astype(F32)
        self.depth = (
            lax.div(self.lane, plan.ny) * plan.sub + self.row
        ).astype(F32)

    def by_lane(self, f, shift):
        return pltpu.roll(f, shift % self.plan.lanes, f.ndim - 1)

    def by_row(self, f, shift):
        return pltpu.roll(f, shift % self.plan.sub, f.ndim - 2)

    def dy(self, f):
        return self.by_lane(f, -1) * self.not_high_y - self.by_lane(f, 1) * self.not_low_y

    def below(self, f):
        plan = self.plan
        moved = self.by_row(f, -1)
        if plan.chunks > 1:
            moved = jnp.where(self.last_row, self.by_lane(moved, -plan.ny), moved)
        return jnp.where(self.floor_cell, 0.0, moved)

    def above(self, f, top):
        plan = self.plan
        moved = self.by_row(f, 1)
        if plan.chunks > 1:
            moved = jnp.where(self.first_row, self.by_lane(moved, plan.ny), moved)
        return jnp.where(self.top, top, moved)

    def block(self):
        start = self.slot * slot_rows(self.plan)
        self.slot = (self.slot + 1) % SLOTS
        return start

    def dz(self, f, top):
        if self.memory is None or f.ndim == 2:
            return self.below(f) - self.above(f, top * f if top else 0.0)
        plan, memory = self.plan, self.memory
        count, sub = f.shape[:2]
        start, size = self.block(), 2 * (sub + 2)
        for i in range(count):
            memory[pl.ds(start + i * size + 2, sub, stride=2), :] = f[i]
        lane = lax.broadcasted_iota(jnp.int32, (count, plan.lanes), 1)
        first = memory[pl.ds(start + 2, count, stride=size), :]
        last = memory[pl.ds(start + 2 * sub, count, stride=size), :]
        after = jnp.where(lane < plan.lanes - plan.ny, self.by_lane(first, -plan.ny), 0.0)
        before = jnp.where(lane >= plan.ny, self.by_lane(last, plan.ny), top * first)
        memory[pl.ds(start, count, stride=size), :] = before
        memory[pl.ds(start + 2 * (sub + 1), count, stride=size), :] = after
        return jnp.stack(
            [
                memory[pl.ds(start + i * size + 4, sub, stride=2), :]
                - memory[pl.ds(start + i * size, sub, stride=2), :]
                for i in range(count)
            ]
        )

    def spread_rows(self, start, rows):
        plan, memory = self.plan, self.memory
        count = rows.shape[0]
        memory[pl.ds(start, count), :] = rows
        return jnp.stack(
            [
                jnp.broadcast_to(memory[pl.ds(start + i, 1), :], (plan.sub, plan.lanes))
                for i in range(count)
            ]
        )

    def seafloor(self, vz):
        if self.memory is None or vz.ndim == 2:
            row = self.over_chunks(jnp.where(self.top, vz, 0.0))
            return jnp.broadcast_to(row[..., 0:1, :], vz.shape)
        memory, start = self.memory, self.block()
        count, sub, lanes = vz.shape
        for i in range(count):
            memory[pl.ds(start + i * sub, sub), :] = vz[i]
        rows = memory[pl.ds(start, count, stride=sub), :]
        lane = lax.broadcasted_iota(jnp.int32, rows.shape, 1)
        rows = self.over_chunks(jnp.where(lane < self.plan.ny, rows, 0.0))
        return self.spread_rows(start + BATCH * sub, rows)

    def on_top(self, f):
        if self.memory is None or f.ndim == 2:
            shift = self.plan.sub // 2
            while shift:
                f = f + self.by_row(f, shift)
                shift //= 2
            return jnp.where(self.top, self.over_chunks(f), 0.0)
        memory, start = self.memory, self.block()
        count, sub, lanes = f.shape
        for i in range(count):
            memory[pl.ds(start + i * sub, sub), :] = f[i]
        rows = memory[pl.ds(start, count, stride=sub), :]
        for k in range(1, sub):
            rows = rows + memory[pl.ds(start + k, count, stride=sub), :]
        rows = self.spread_rows(start + BATCH * sub, self.over_chunks(rows))
        return jnp.where(self.top, rows, 0.0)

    def over_chunks(self, f):
        shift = self.plan.ny
        while shift < self.plan.lanes:
            f = f + self.by_lane(f, shift)
            shift *= 2
        return f


def acceleration(sh, stress, j, count):
    at, before, after = (pl.ds(j + k, count) for k in (0, -1, 1))
    sxy, sxz = stress[SXY, at], stress[SXZ, at]
    ax = stress[SXX, after] - stress[SXX, before] + sh.dy(sxy) + sh.dz(sxz, 0.0)
    syz = stress[SYZ, at]
    ay = stress[SXY, after] - stress[SXY, before] + sh.dy(stress[SYY, at])
    ay = ay + sh.dz(syz, 0.0)
    szz = stress[SZZ, at]
    az = stress[SXZ, after] - stress[SXZ, before] + sh.dy(syz) + sh.dz(szz, 0.0)
    return ax, ay, az


def strained(sh, vel, stress, mats, j, count):
    at, before, after = (pl.ds(j + k, count) for k in (0, -1, 1))
    vx, vy, vz = vel[VX, at], vel[VY, at], vel[VZ, at]
    exx = vel[VX, after] - vel[VX, before]
    eyy = sh.dy(vy)
    ezz = sh.dz(vz, 1.0)
    mu = mats[SHEAR, at]
    mu2 = mu + mu
    common = mats[LAMB, at] * (exx + eyy + ezz)
    yield SXX, stress[SXX, at] + (common + mu2 * exx)
    yield SYY, stress[SYY, at] + (common + mu2 * eyy)
    yield SZZ, stress[SZZ, at] + (common + mu2 * ezz)
    exy = sh.dy(vx) + vel[VY, after] - vel[VY, before]
    yield SXY, stress[SXY, at] + mu * exy
    exz = sh.dz(vx, 1.0) + vel[VZ, after] - vel[VZ, before]
    yield SXZ, stress[SXZ, at] + (mu * exz + mats[FAULT, at])
    eyz = sh.dz(vy, 1.0) + sh.dy(vz)
    yield SYZ, stress[SYZ, at] + mu * eyz


def bring(plan, sh, material, state, ref, fields, x, count, column, first):
    vel, stress, mats = state
    to = pl.ds(column, count)

    def read(f):
        return ref[pl.ds(f * fields + x, count)]

    mats[FLOOR, to] = sh.seafloor(read(VZ))
    for f in range(3):
        vel[f, to] = read(f)
    for f in range(6):
        stress[f, to] = read(3 + f)
    zone = read(9)
    values = [jnp.zeros_like(zone) for _ in range(3)]
    for z in range(ZONES):
        here = zone == float(z + 1)
        values = [jnp.where(here, material(c, z), values[c]) for c in range(3)]
    for c in range(3):
        mats[c, to] = values[c] * HALF
    for i in range(count):
        slip = ref[ref.shape[0] - 1, pl.ds(first + x + i, 1), :]
        slip = jnp.broadcast_to(slip, (plan.sub, plan.lanes))
        mats[FAULT, column + i] = jnp.where(
            sh.row == (plan.depth // 2) % plan.sub, DT * slip, 0.0
        )


def begin_kernel(plan, table, own, mate, vel, stress, mats, rows):
    cells = plan.cells
    sh = Shifts(plan)
    odd = odd_device()
    state = (vel, stress, mats)
    starts = (HALO + cells * odd, HALO + cells * (1 - odd))
    for start, ref in zip(starts, (own, mate)):
        plan.planes(
            0,
            cells,
            lambda x, count, start=start, ref=ref: bring(
                plan, sh, lambda c, z: table[c, z], state, ref, cells, x, count, start + x, 0
            ),
            BATCH,
        )

    def move(j, count):
        at = pl.ds(j, count)
        b = mats[BUOY, at]
        for f, a in enumerate(acceleration(sh, stress, j, count)):
            vel[f, at] = vel[f, at] + b * a

    plan.planes(HALO + 1, HALO + 2 * cells - 1, move, BATCH)
    for c in range(3):
        for z in range(ZONES):
            at = c * ZONES + z
            rows[at : at + 1, :] = jnp.full((1, plan.lanes), table[c, z], F32)


class Updates:
    def __init__(self, plan, sh, vel, stress, mats, oc, water, bottom):
        self.plan, self.sh = plan, sh
        self.vel, self.stress, self.mats = vel, stress, mats
        self.oc, self.water, self.bottom = oc, water, bottom

    def flow_x(self, j, count):
        oc = self.oc
        before, at, after = (pl.ds(j + k, count) for k in range(3))
        oc[1, at] = self.water[at] * (oc[1, at] - HALF * (oc[0, after] - oc[0, before]))

    def flow(self, j, count):
        oc, sh = self.oc, self.sh
        at = pl.ds(j + 1, count)
        p = oc[0, at]
        wet = self.water[at]
        rise = sh.dz(p, -1.0) + self.bottom[at] * p
        oc[3, at] = wet * (oc[3, at] - (HALF * rise + (DT * GRAV) * p))
        oc[2, at] = wet * (oc[2, at] - HALF * sh.dy(p))

    def press(self, j, count, floor):
        oc, sh = self.oc, self.sh
        before, at, after = (pl.ds(j + k, count) for k in range(3))
        w = oc[3, at]
        rise = sh.dz(w, 1.0)
        if floor is not None:
            rise = rise + self.bottom[at] * floor(pl.ds(j, count))
        total = oc[1, after] - oc[1, before] + sh.dy(oc[2, at]) + rise
        oc[0, at] = self.water[at] * (oc[0, at] - (HALF * KBULK) * total)

    def add_floor(self, j, count):
        at = pl.ds(j + 1, count)
        floor = self.first_floor(pl.ds(j, count))
        self.oc[0, at] = self.oc[0, at] - (HALF * KBULK) * (self.bottom[at] * floor)

    def first_floor(self, at):
        return self.mats[FLOOR, at]

    def floor(self, at):
        return self.sh.seafloor(self.vel[VZ, at])

    def load(self, j, count):
        at = pl.ds(j + 1, count)
        return self.sh.on_top(self.bottom[at] * self.oc[0, at])

    def add_load(self, j, count):
        at = pl.ds(j, count)
        self.vel[VZ, at] = self.vel[VZ, at] + self.mats[BUOY, at] * self.load(j, count)

    def move(self, j, count):
        vel = self.vel
        at = pl.ds(j, count)
        ax, ay, az = acceleration(self.sh, self.stress, j, count)
        b = self.mats[BUOY, at]
        vel[VX, at] = vel[VX, at] + b * ax
        vel[VY, at] = vel[VY, at] + b * ay
        vel[VZ, at] = vel[VZ, at] + b * (az + self.load(j, count))

    def strain(self, j, count):
        for f, value in strained(self.sh, self.vel, self.stress, self.mats, j, count):
            self.stress[f, pl.ds(j, count)] = value

    def run(self, spans, inner, send=None):
        def planes(t, inset, update):
            self.plan.planes(*spans(t, inset), update, BATCH)

        def flows(t):
            planes(t, 0, self.flow_x)
            planes(t, 1, self.flow)

        if inner:
            columns = self.vel.shape[1]
            first, last = spans(0, 1)
            self.plan.planes(0, columns, self.flow_x, BATCH)
            self.plan.planes(1, columns - 1, self.flow, BATCH)
            planes(0, 1, functools.partial(self.press, floor=self.first_floor))
            later = functools.partial(self.press, floor=None)
            self.plan.planes(1, first, later, BATCH)
            self.plan.planes(last, columns - 1, later, BATCH)
        else:
            planes(0, 1, self.add_floor)
        for t in range(STEPS - 1):
            flows(t + 1)
            planes(t, 1, self.add_load if inner and t == 0 else self.move)
            if t < STEPS - 2:
                planes(t, 2, self.strain)
            planes(t + 1, 1, functools.partial(self.press, floor=self.floor))
        if send is not None:
            send()


def inner_kernel(
    plan, arrived, swapped, mats, vel_in, stress_in, vel, stress, oc, water, bottom,
    gather, depths, memory,
):
    sub, chunks, n, strips = plan.sub, plan.chunks, plan.n, plan.strips
    cells, sent = plan.cells, plan.sent_groups
    sh = Shifts(plan, memory)
    odd = odd_device()
    half = n // 2
    columns = 2 * cells + 2 * HALO

    def turn(owner, group):
        for core, ref in ((odd, arrived), (1 - odd, swapped)):
            for kc in range(chunks):
                for yl in range(strips):
                    at = owner * plan.rows + group * plan.lead + kc * strips + yl
                    to = kc * plan.ny + core * strips + yl
                    gather[pl.ds(to, half, stride=2 * strips), :] = ref[
                        pl.ds(at, half, stride=2 * plan.rows), :
                    ]
        return gather[...].T

    deeps = []
    for owner in range(2):
        for group in range(sent):
            turned = turn(owner, group)
            for i in range(chunks):
                for f in range(4):
                    at = (i * 4 + f) * sub
                    column = 1 + owner * (cells + HALO) + group * chunks + i
                    oc[f, column] = turned[at : at + sub]
            if owner == 0 and group == 0:
                oc[0, 0] = turned[2 * sub : 3 * sub]
                deeps.append(turned[3 * sub : 4 * sub])
            if owner == 1 and group == sent - 1:
                oc[0, columns + 1] = turned[LANES - 2 * sub : LANES - sub]
                deeps.append(turned[LANES - sub :])
    for i, deep in enumerate(deeps):
        for kc in range(chunks):
            mine = (sh.lane >= kc * plan.ny) & (sh.lane < (kc + 1) * plan.ny)
            depths[i, kc * sub : (kc + 1) * sub, :] = sh.over_chunks(jnp.where(mine, deep, 0.0))

    def mask(owner, j, _):
        low = jnp.broadcast_to(depths[owner, pl.ds(j - owner * cells, 1), :], (sub, plan.lanes))
        wet = jnp.where(sh.depth < low, 1.0, 0.0).astype(F32)
        water[j] = wet
        bottom[j] = jnp.where(sh.depth == low - 1.0, 1.0, 0.0).astype(F32)
        oc[0, j] = oc[0, j] * wet

    def mask_x(j, _):
        oc[1, j] = oc[1, j] * water[j]

    def mask_yw(j, _):
        oc[2, j] = oc[2, j] * water[j]
        oc[3, j] = oc[3, j] * water[j]

    plan.planes(0, plan.width + 2, lambda j, _: mask(0, j, _))
    plan.planes(plan.width + 2, columns + 2, lambda j, _: mask(1, j, _))
    plan.planes(1, columns + 1, mask_x)
    plan.planes(2, columns, mask_yw)

    def bring_in(j, _):
        for f in range(3):
            vel[f, j] = vel_in[f, j]
        for f in range(6):
            stress[f, j] = stress_in[f, j]

    if not plan.unrolled:
        plan.planes(HALO, HALO + 2 * cells, bring_in)
    updates = Updates(plan, sh, vel, stress, mats, oc, water, bottom)
    updates.run(lambda t, inset: (HALO + 2 * t + inset, HALO + 2 * cells - 2 * t - inset), True)


def outer_kernel(
    plan, materials, border, water, bottom, vel_in, stress_in, mats_in, oc_in,
    vel, stress, mats, oc, rows, gather, memory,
):
    sub, chunks, n, strips, cells = plan.sub, plan.chunks, plan.n, plan.strips, plan.cells
    near = cells - 1
    sh = Shifts(plan, memory)
    odd = odd_device()
    if not plan.unrolled:
        for here, there in (
            (vel, vel_in), (stress, stress_in), (mats, mats_in), (oc, oc_in)
        ):
            here[...] = there[...]
    updates = Updates(plan, sh, vel, stress, mats, oc, water, bottom)

    def material(c, z):
        row = materials[pl.ds(c * ZONES + z, 1), :]
        return jnp.broadcast_to(row, (sub, plan.lanes))

    def side(core):
        low, far = ((1, 0), (HALO + 2 * cells, 2 * HALO + 2 * cells - 1))[core]
        state = (vel, stress, mats)
        plan.planes(
            0,
            near,
            lambda x, count: bring(
                plan, sh, material, state, border, near, x, count, low + x, 1 - core
            ),
            BATCH,
        )
        for i, f in enumerate((SXX, SXY, SXZ)):
            stress[f, far] = border[10 * near + i]

        def spans(t, inset):
            if core == 0:
                return 2 * t + inset, 2 * t + inset + HALO
            last = 2 * HALO + 2 * cells - 2 * t - inset
            return last - HALO, last

        def send():
            for group in range(plan.own_groups):
                stacked = jnp.concatenate(
                    [
                        oc[f, 1 + HALO + core * cells + group * chunks + i]
                        for i in range(chunks)
                        for f in range(4)
                    ],
                    axis=0,
                )
                gather[group] = stacked.T
                for kc in range(chunks):
                    for yl in range(strips):
                        at = group * plan.lead + kc * strips + yl
                        rows[pl.ds(at, n, stride=plan.back_rows), :] = gather[
                            group, pl.ds(kc * plan.ny + yl, n, stride=strips), :
                        ]

        updates.run(spans, False, send)

    for core in range(2):
        pl.when(odd == core)(functools.partial(side, core))


def end_kernel(
    plan, vel_all, stress_all, mats_all, oc_all, bottom_all, vel_out, stress_out, vel, stress
):
    cells, sub, chunks, ny = plan.cells, plan.sub, plan.chunks, plan.ny
    sh = Shifts(plan)
    first, last = 2 * (STEPS - 1), plan.width - 2 * (STEPS - 1)
    window = pl.ds(cells * odd_device(), plan.width)
    vel_in, stress_in = vel_all.at[:, window], stress_all.at[:, window]
    mats = mats_all.at[:, window]
    window = pl.ds(cells * odd_device(), plan.width + 2)
    pressure, bottom = oc_all.at[0, window], bottom_all.at[window]

    def put(out, f, x, count, planes):
        for kc in range(chunks):
            out[f, pl.ds(x, count), kc * sub : (kc + 1) * sub, :] = planes[
                :, :, kc * ny : (kc + 1) * ny
            ]

    def strain(j, count):
        for f, value in strained(sh, vel_in, stress_in, mats, j, count):
            stress[f, pl.ds(j, count)] = value

    def move(j, count):
        at = pl.ds(j, count)
        ax, ay, az = acceleration(sh, stress, j, count)
        b = mats[BUOY, at]
        wet = pl.ds(j + 1, count)
        load = sh.on_top(bottom[wet] * pressure[wet])
        for f, a in enumerate((ax, ay, az + load)):
            vel[f, at] = vel_in[f, at] + b * a

    def finish(x, count):
        for f in range(3):
            put(vel_out, f, x, count, vel[f, pl.ds(x + HALO, count)])
        for f, value in strained(sh, vel, stress, mats, x + HALO, count):
            put(stress_out, f, x, count, value)

    plan.planes(first, last, strain, BATCH)
    plan.planes(first + 1, last - 1, move, BATCH)
    plan.planes(0, cells, finish, BATCH)


def unpack_kernel(plan, arrived, ocean, turned, strips, sems):
    sub, chunks = plan.sub, plan.chunks
    block = 4 * sub
    copies = [
        pltpu.make_async_copy(strips.at[yl], ocean.at[:, yl], sems.at[yl])
        for yl in range(plan.strips)
    ]
    for yl in range(plan.strips):
        by_chunk = [
            arrived[pl.ds(kc * plan.strips + yl, plan.nx // chunks, stride=plan.lead), :]
            for kc in range(chunks)
        ]
        for i in range(chunks):
            turned[yl, pl.ds(i, plan.nx // chunks, stride=chunks), :] = place(
                by_chunk, [i] * chunks, block
            )
        whole = turned[yl].T
        for kc in range(chunks):
            for f in range(4):
                at = (kc * 4 + f) * sub
                strips[yl, f, kc * sub : (kc + 1) * sub, :] = whole[at : at + sub]
        copies[yl].start()
    for copy in copies:
        copy.wait()


def on_device(plan, velocity, stress, ocean, zones, materials, slip, bathy):
    n, cells, sub, lanes, width = plan.n, plan.cells, plan.sub, plan.lanes, plan.width
    vmem = pl.BlockSpec(memory_space=pltpu.VMEM)
    smem = pl.BlockSpec(memory_space=pltpu.SMEM)
    hbm = pl.BlockSpec(memory_space=pltpu.HBM)

    def shape(*dims):
        return jax.ShapeDtypeStruct(dims, F32)

    def in_vmem(*dims):
        return pltpu.VMEM(dims, F32) if plan.unrolled else shape(*dims)

    def like(array):
        return jax.ShapeDtypeStruct(array.shape, array.dtype)

    def held(array):
        return pltpu.VMEM(array.shape, array.dtype)

    def call(kernel, name, out, ins, scratch, room=16, outs=None, **rest):
        room = room if plan.unrolled else 56
        return pl.pallas_call(
            functools.partial(kernel, plan),
            out_shape=out,
            in_specs=ins,
            out_specs=jax.tree.map(lambda _: vmem, out) if outs is None else outs,
            scratch_shapes=scratch,
            compiler_params=pltpu.CompilerParams(vmem_limit_bytes=room * 1024 * 1024),
            name=name,
            **rest,
        )

    def pinned(array):
        return pltpu.with_memory_space_constraint(array, pltpu.HBM)

    def near(array):
        return pltpu.with_memory_space_constraint(array, pltpu.VMEM) if plan.unrolled else array

    mates = [(i, i ^ 1) for i in range(n)]
    others = [(i, i + 1) for i in range(1, n - 1, 2)]
    others += [(target, source) for source, target in others]
    message, crust, border = call(
        pack_kernel,
        "pack",
        (
            shape(n * plan.rows, LANES),
            shape(10 * cells + 1, sub, lanes),
            shape(10 * cells - 6, sub, lanes),
        ),
        [hbm] * 6,
        [held(a) for a in (velocity, stress, zones, slip, ocean, bathy)]
        + [
            pltpu.VMEM((plan.strips, plan.nx, LANES), F32),
            pltpu.VMEM(
                ((plan.nx // plan.chunks + 2 * plan.halo_groups) * plan.lead, LANES), F32
            ),
            pltpu.VMEM((n * plan.strips, LANES), F32),
            pltpu.VMEM((n * plan.rows, LANES), F32),
            pltpu.SemaphoreType.DMA((8,)),
        ],
        outs=(hbm, vmem, vmem),
    )(*(pinned(a) for a in (velocity, stress, zones, slip, ocean, bathy)))
    arrived = lax.all_to_all(
        message.reshape(n // 2, 2 * plan.rows, LANES),
        "map",
        split_axis=0,
        concat_axis=0,
        axis_index_groups=[list(range(core, n, 2)) for core in range(2)],
        tiled=True,
    ).reshape(n * plan.rows, LANES)
    other = lax.ppermute(border, "map", others)
    mate = lax.ppermute(crust, "map", mates)
    columns = 2 * cells + 2 * HALO
    vel, strs, mats, material_rows = call(
        begin_kernel,
        "first_velocity",
        (
            shape(3, columns, sub, lanes),
            shape(6, columns, sub, lanes),
            shape(5, columns, sub, lanes),
            shape(3 * ZONES, lanes),
        ),
        [smem] + [vmem] * 2,
        [],
    )(materials, crust, mate)
    arrived, vel = lax.optimization_barrier((arrived, vel))
    swapped = lax.ppermute(arrived, "map", mates)
    planes_of = {
        "vel": shape(3, columns, sub, lanes),
        "stress": shape(6, columns, sub, lanes),
        "mats": shape(5, columns, sub, lanes),
        "oc": shape(4, columns + 2, sub, lanes),
        "mask": shape(columns + 2, sub, lanes),
    }
    vel, strs, oc, water, bottom = call(
        inner_kernel,
        "inner_substeps",
        tuple(planes_of[k] for k in ("vel", "stress", "oc", "mask", "mask")),
        [vmem] * 5,
        [
            pltpu.VMEM((lanes, LANES), F32),
            pltpu.VMEM((2, plan.depth, lanes), F32),
            pltpu.VMEM((SLOTS * slot_rows(plan), lanes), F32),
        ],
        input_output_aliases={3: 0, 4: 1},
    )(*(near(a) for a in (arrived, swapped, mats, vel, strs)))
    vel, strs, mats, oc, back = call(
        outer_kernel,
        "outer_substeps",
        tuple(planes_of[k] for k in ("vel", "stress", "mats", "oc"))
        + (in_vmem(n * plan.back_rows, LANES),),
        [vmem] * 8,
        [
            pltpu.VMEM((plan.own_groups, lanes, LANES), F32),
            pltpu.VMEM((SLOTS * slot_rows(plan), lanes), F32),
        ],
        outs=(vmem,) * 5,
        input_output_aliases={4: 0, 5: 1, 6: 2, 7: 3},
    )(*(near(a) for a in (material_rows, other, water, bottom, vel, strs, mats, oc)))
    returned = lax.all_to_all(
        back.reshape(n, plan.back_rows, LANES), "map", split_axis=0, concat_axis=0, tiled=True
    ).reshape(n * plan.back_rows, LANES)
    new_velocity, new_stress = call(
        end_kernel,
        "last_updates",
        (shape(*velocity.shape), shape(*stress.shape)),
        [vmem] * 5,
        [
            pltpu.VMEM((3, width, sub, lanes), F32),
            pltpu.VMEM((6, width, sub, lanes), F32),
        ],
    )(vel, strs, mats, oc, bottom)
    new_ocean = call(
        unpack_kernel,
        "ocean_strips",
        shape(*ocean.shape),
        [vmem],
        [
            pltpu.VMEM((plan.strips, plan.nx, LANES), F32),
            pltpu.VMEM((plan.strips, 4, plan.depth, plan.nx), F32),
            pltpu.SemaphoreType.DMA((plan.strips,)),
        ],
        outs=hbm,
    )(returned)
    return new_velocity, new_stress, new_ocean


def solution(mesh):
    n = mesh.shape["map"]

    def body(velocity, stress, ocean, zones, materials, slip, bathy):
        _, cells, depth, ny = velocity.shape
        plan = Plan(n, cells, depth, ny, ocean.shape[1])
        return on_device(plan, velocity, stress, ocean, zones, materials, slip, bathy)

    return jax.shard_map(
        body,
        mesh=mesh,
        in_specs=(
            P("parts", "map", None, None),
            P("parts", "map", None, None),
            P("parts", "map", None, None),
            P("map", "parts", None),
            P(),
            P("map", "parts"),
            P("map", "parts"),
        ),
        out_specs=(
            P("parts", "map", None, None),
            P("parts", "map", None, None),
            P("parts", "map", None, None),
        ),
        check_vma=False,
    )
```

```python
import functools

import jax
import jax.numpy as jnp
from jax import lax
from jax.experimental import pallas as pl
from jax.experimental.pallas import tpu as pltpu
from jax.sharding import PartitionSpec as P

STEPS = 4
ZONES = 8
DT = 0.25
HALF = 0.5 * DT
KBULK = 2.25
GRAV = 0.1
HALO = 2 * STEPS
LANES = 128
F32 = jnp.float32
VX, VY, VZ = range(3)
SXX, SYY, SZZ, SXY, SXZ, SYZ = range(6)
BUOY, LAMB, SHEAR, FAULT, FLOOR = range(5)


class Plan:
    def __init__(self, devices, cells, depth, ny, strips):
        self.n = devices
        self.cells = cells
        self.depth = depth
        self.ny = ny
        self.strips = strips
        self.chunks = max(1, LANES // ny)
        self.sub = depth // self.chunks
        self.lanes = self.chunks * ny
        self.width = cells + 2 * HALO
        self.own_groups = cells // self.chunks
        self.halo_groups = HALO // self.chunks
        self.sent_groups = self.own_groups + self.halo_groups
        self.lead = self.chunks * strips
        self.rows = self.lead * self.sent_groups
        self.back_rows = self.lead * self.own_groups
        self.nx = devices * cells
        self.block = 4 * self.sub
        self.unrolled = self.sub * self.lanes <= 1024
        assert devices % 2 == 0 and cells == HALO and self.block * self.chunks == LANES

    def planes(self, start, stop, body, batch=1):
        if self.unrolled:
            for j in range(start, stop, batch):
                body(j, min(batch, stop - j))
        else:
            def run(j, carry):
                body(j, 1)
                return carry

            lax.fori_loop(start, stop, run, 0)


BATCH = 8
SLOTS = 16


def slot_rows(plan):
    return BATCH * 2 * (plan.sub + 2)


def odd_device():
    return lax.rem(lax.axis_index("map"), 2)


def place(pieces, wanted, block):
    out = None
    for i, piece in enumerate(pieces):
        shift = (i - wanted[i]) * block % piece.shape[-1]
        moved = pltpu.roll(piece, shift, piece.ndim - 1) if shift else piece
        if out is None:
            out = moved
        else:
            lane = lax.broadcasted_iota(jnp.int32, moved.shape, moved.ndim - 1)
            out = jnp.where(lane >= i * block, moved, out)
    return out


def pack_kernel(
    plan, vel_ref, stress_ref, zones_ref, slip_ref, ocean_ref, bathy_ref,
    message_out, crust, border,
    vel, stress, zones, slip, ocean, bathy, turned, grouped, extra, message, sems,
):
    cells, sub, chunks, ny = plan.cells, plan.sub, plan.chunks, plan.ny
    n, strips, block, sent, rows = plan.n, plan.strips, plan.block, plan.sent_groups, plan.rows
    pairs = (
        (ocean_ref, ocean),
        (bathy_ref, bathy),
        (vel_ref, vel),
        (stress_ref, stress),
        (zones_ref, zones),
        (slip_ref, slip),
    )
    copies = [
        pltpu.make_async_copy(source, target, sems.at[i])
        for i, (source, target) in enumerate(pairs)
    ]
    for copy in copies:
        copy.start()
    copies[1].wait()
    depths = bathy[...].astype(F32)
    wide = lax.broadcasted_iota(jnp.int32, depths.shape, 1)
    for d in range(n):
        first = d * cells - HALO - 1
        moved = pltpu.roll(depths, -first % plan.nx, 1)
        moved = jnp.where((wide + first >= 0) & (wide + first < plan.nx), moved, 0.0)
        extra[d * strips : (d + 1) * strips, :] = moved[:, :LANES]
    copies[0].wait()
    count = plan.nx // chunks
    lead = plan.lead
    pad = plan.halo_groups * lead
    grouped[:pad, :] = jnp.zeros((pad, LANES), F32)
    grouped[pad + count * lead :, :] = jnp.zeros((pad, LANES), F32)
    for yl in range(strips):
        stacked = jnp.concatenate(
            [ocean[f, yl, kc * sub : (kc + 1) * sub, :] for kc in range(chunks) for f in range(4)],
            axis=0,
        )
        turned[yl] = stacked.T
        by_x = [turned[yl, pl.ds(i, count, stride=chunks), :] for i in range(chunks)]
        for kc in range(chunks):
            grouped[pl.ds(pad + kc * strips + yl, count, stride=lead), :] = place(
                by_x, [kc] * chunks, block
            )
    for d in range(n):
        start = (d * plan.own_groups + (d % 2) * plan.halo_groups) * lead
        message[d * rows : (d + 1) * rows, :] = grouped[start : start + rows, :]
    pairs = n // 2
    lane = lax.broadcasted_iota(jnp.int32, (pairs, LANES), 1)
    blank = jnp.zeros((1, LANES), F32)
    for odd in range(2):
        slot = (odd * (chunks - 1) * 4 + 2) * sub
        group = odd * (sent - 1)
        for yl in range(strips):
            if odd:
                column = turned[yl, pl.ds(2 * cells + HALO, pairs - 1, stride=2 * cells), :]
                column = jnp.concatenate([column, blank], axis=0)
            else:
                column = turned[yl, pl.ds(2 * cells - HALO - 1, pairs - 1, stride=2 * cells), :]
                column = jnp.concatenate([blank, column], axis=0)
            deep = extra[pl.ds(odd * strips + yl, pairs, stride=2 * strips), :]
            for kc in range(chunks):
                at = odd * rows + group * lead + kc * strips + yl
                old = message[pl.ds(at, pairs, stride=2 * rows), :]
                edge = pltpu.roll(column, (slot - kc * block) % LANES, 1)
                floor = pltpu.roll(deep, (slot + sub - kc * sub) % LANES, 1)
                new = jnp.where((lane >= slot) & (lane < slot + sub), edge, old)
                new = jnp.where((lane >= slot + sub) & (lane < slot + 2 * sub), floor, new)
                message[pl.ds(at, pairs, stride=2 * rows), :] = new
    out = pltpu.make_async_copy(message, message_out, sems.at[6])
    out.start()

    for copy in copies[2:]:
        copy.wait()

    def joined(ref, *at):
        parts = [ref[(*at, pl.ds(kc * sub, sub), slice(None))] for kc in range(chunks)]
        return jnp.concatenate(parts, axis=-1) if chunks > 1 else parts[0]

    for f in range(3):
        for x in range(cells):
            crust[f * cells + x] = joined(vel, f, x)
    for f in range(6):
        for x in range(cells):
            crust[(3 + f) * cells + x] = joined(stress, f, x)
    for x in range(cells):
        crust[9 * cells + x] = (joined(zones, x) + 1).astype(F32)
    fault_chunk = (plan.depth // 2) // sub
    pieces = [
        slip[...] if kc == fault_chunk else jnp.zeros((cells, ny), F32) for kc in range(chunks)
    ]
    fault = jnp.concatenate(pieces, axis=-1) if chunks > 1 else pieces[0]
    if sub > cells:
        fault = jnp.concatenate([fault, jnp.zeros((sub - cells, plan.lanes), F32)], axis=0)
    crust[10 * cells] = fault
    odd = odd_device()
    near = cells - 1
    for f in range(10):
        for i in range(near):
            border[f * near + i] = crust[f * cells + i + odd]
    for i, f in enumerate((SXX, SXY, SXZ)):
        border[10 * near + i] = crust[(3 + f) * cells + near * (1 - odd)]
    border[10 * near + 3] = fault
    out.wait()


class Shifts:
    def __init__(self, plan, memory=None):
        self.plan = plan
        self.memory = memory if plan.unrolled else None
        self.slot = 0
        shape = (plan.sub, plan.lanes)
        self.row = lax.broadcasted_iota(jnp.int32, shape, 0)
        self.lane = lax.broadcasted_iota(jnp.int32, shape, 1)
        self.y = lax.rem(self.lane, plan.ny)
        self.first_row = self.row == 0
        self.last_row = self.row == plan.sub - 1
        self.top = self.first_row & (self.lane < plan.ny)
        self.floor_cell = self.last_row & (self.lane >= plan.lanes - plan.ny)
        self.not_low_y = jnp.where(self.y == 0, 0.0, 1.0).astype(F32)
        self.not_high_y = jnp.where(self.y == plan.ny - 1, 0.0, 1.0).astype(F32)
        self.depth = (
            lax.div(self.lane, plan.ny) * plan.sub + self.row
        ).astype(F32)

    def by_lane(self, f, shift):
        return pltpu.roll(f, shift % self.plan.lanes, f.ndim - 1)

    def by_row(self, f, shift):
        return pltpu.roll(f, shift % self.plan.sub, f.ndim - 2)

    def dy(self, f):
        return self.by_lane(f, -1) * self.not_high_y - self.by_lane(f, 1) * self.not_low_y

    def below(self, f):
        plan = self.plan
        moved = self.by_row(f, -1)
        if plan.chunks > 1:
            moved = jnp.where(self.last_row, self.by_lane(moved, -plan.ny), moved)
        return jnp.where(self.floor_cell, 0.0, moved)

    def above(self, f, top):
        plan = self.plan
        moved = self.by_row(f, 1)
        if plan.chunks > 1:
            moved = jnp.where(self.first_row, self.by_lane(moved, plan.ny), moved)
        return jnp.where(self.top, top, moved)

    def block(self):
        start = self.slot * slot_rows(self.plan)
        self.slot = (self.slot + 1) % SLOTS
        return start

    def dz(self, f, top):
        if self.memory is None or f.ndim == 2:
            return self.below(f) - self.above(f, top * f if top else 0.0)
        plan, memory = self.plan, self.memory
        count, sub = f.shape[:2]
        start, size = self.block(), 2 * (sub + 2)
        for i in range(count):
            memory[pl.ds(start + i * size + 2, sub, stride=2), :] = f[i]
        lane = lax.broadcasted_iota(jnp.int32, (count, plan.lanes), 1)
        first = memory[pl.ds(start + 2, count, stride=size), :]
        last = memory[pl.ds(start + 2 * sub, count, stride=size), :]
        after = jnp.where(lane < plan.lanes - plan.ny, self.by_lane(first, -plan.ny), 0.0)
        before = jnp.where(lane >= plan.ny, self.by_lane(last, plan.ny), top * first)
        memory[pl.ds(start, count, stride=size), :] = before
        memory[pl.ds(start + 2 * (sub + 1), count, stride=size), :] = after
        return jnp.stack(
            [
                memory[pl.ds(start + i * size + 4, sub, stride=2), :]
                - memory[pl.ds(start + i * size, sub, stride=2), :]
                for i in range(count)
            ]
        )

    def spread_rows(self, start, rows):
        plan, memory = self.plan, self.memory
        count = rows.shape[0]
        memory[pl.ds(start, count), :] = rows
        return jnp.stack(
            [
                jnp.broadcast_to(memory[pl.ds(start + i, 1), :], (plan.sub, plan.lanes))
                for i in range(count)
            ]
        )

    def seafloor(self, vz):
        if self.memory is None or vz.ndim == 2:
            row = self.over_chunks(jnp.where(self.top, vz, 0.0))
            return jnp.broadcast_to(row[..., 0:1, :], vz.shape)
        memory, start = self.memory, self.block()
        count, sub, lanes = vz.shape
        for i in range(count):
            memory[pl.ds(start + i * sub, sub), :] = vz[i]
        rows = memory[pl.ds(start, count, stride=sub), :]
        lane = lax.broadcasted_iota(jnp.int32, rows.shape, 1)
        rows = self.over_chunks(jnp.where(lane < self.plan.ny, rows, 0.0))
        return self.spread_rows(start + BATCH * sub, rows)

    def on_top(self, f):
        if self.memory is None or f.ndim == 2:
            shift = self.plan.sub // 2
            while shift:
                f = f + self.by_row(f, shift)
                shift //= 2
            return jnp.where(self.top, self.over_chunks(f), 0.0)
        memory, start = self.memory, self.block()
        count, sub, lanes = f.shape
        for i in range(count):
            memory[pl.ds(start + i * sub, sub), :] = f[i]
        rows = memory[pl.ds(start, count, stride=sub), :]
        for k in range(1, sub):
            rows = rows + memory[pl.ds(start + k, count, stride=sub), :]
        rows = self.spread_rows(start + BATCH * sub, self.over_chunks(rows))
        return jnp.where(self.top, rows, 0.0)

    def over_chunks(self, f):
        shift = self.plan.ny
        while shift < self.plan.lanes:
            f = f + self.by_lane(f, shift)
            shift *= 2
        return f


def acceleration(sh, stress, j, count):
    at, before, after = (pl.ds(j + k, count) for k in (0, -1, 1))
    sxy, sxz = stress[SXY, at], stress[SXZ, at]
    ax = stress[SXX, after] - stress[SXX, before] + sh.dy(sxy) + sh.dz(sxz, 0.0)
    syz = stress[SYZ, at]
    ay = stress[SXY, after] - stress[SXY, before] + sh.dy(stress[SYY, at])
    ay = ay + sh.dz(syz, 0.0)
    szz = stress[SZZ, at]
    az = stress[SXZ, after] - stress[SXZ, before] + sh.dy(syz) + sh.dz(szz, 0.0)
    return ax, ay, az


def strained(sh, vel, stress, mats, j, count):
    at, before, after = (pl.ds(j + k, count) for k in (0, -1, 1))
    vx, vy, vz = vel[VX, at], vel[VY, at], vel[VZ, at]
    exx = vel[VX, after] - vel[VX, before]
    eyy = sh.dy(vy)
    ezz = sh.dz(vz, 1.0)
    mu = mats[SHEAR, at]
    mu2 = mu + mu
    common = mats[LAMB, at] * (exx + eyy + ezz)
    yield SXX, stress[SXX, at] + (common + mu2 * exx)
    yield SYY, stress[SYY, at] + (common + mu2 * eyy)
    yield SZZ, stress[SZZ, at] + (common + mu2 * ezz)
    exy = sh.dy(vx) + vel[VY, after] - vel[VY, before]
    yield SXY, stress[SXY, at] + mu * exy
    exz = sh.dz(vx, 1.0) + vel[VZ, after] - vel[VZ, before]
    yield SXZ, stress[SXZ, at] + (mu * exz + mats[FAULT, at])
    eyz = sh.dz(vy, 1.0) + sh.dy(vz)
    yield SYZ, stress[SYZ, at] + mu * eyz


def bring(plan, sh, material, state, ref, fields, x, count, column, first):
    vel, stress, mats = state
    to = pl.ds(column, count)

    def read(f):
        return ref[pl.ds(f * fields + x, count)]

    for f in range(3):
        vel[f, to] = read(f)
    for f in range(6):
        stress[f, to] = read(3 + f)
    zone = read(9)
    values = [jnp.zeros_like(zone) for _ in range(3)]
    for z in range(ZONES):
        here = zone == float(z + 1)
        values = [jnp.where(here, material(c, z), values[c]) for c in range(3)]
    for c in range(3):
        mats[c, to] = values[c] * HALF
    mats[FLOOR, to] = sh.seafloor(read(VZ))
    for i in range(count):
        slip = ref[ref.shape[0] - 1, pl.ds(first + x + i, 1), :]
        slip = jnp.broadcast_to(slip, (plan.sub, plan.lanes))
        mats[FAULT, column + i] = jnp.where(
            sh.row == (plan.depth // 2) % plan.sub, DT * slip, 0.0
        )


def begin_kernel(plan, table, own, mate, vel, stress, mats, rows):
    cells = plan.cells
    sh = Shifts(plan)
    odd = odd_device()
    state = (vel, stress, mats)
    starts = (HALO + cells * odd, HALO + cells * (1 - odd))
    for start, ref in zip(starts, (own, mate)):
        plan.planes(
            0,
            cells,
            lambda x, count, start=start, ref=ref: bring(
                plan, sh, lambda c, z: table[c, z], state, ref, cells, x, count, start + x, 0
            ),
            BATCH,
        )

    def move(j, count):
        at = pl.ds(j, count)
        b = mats[BUOY, at]
        for f, a in enumerate(acceleration(sh, stress, j, count)):
            vel[f, at] = vel[f, at] + b * a

    plan.planes(HALO + 1, HALO + 2 * cells - 1, move, BATCH)
    for c in range(3):
        for z in range(ZONES):
            at = c * ZONES + z
            rows[at : at + 1, :] = jnp.full((1, plan.lanes), table[c, z], F32)


class Updates:
    def __init__(self, plan, sh, vel, stress, mats, oc, water, bottom):
        self.plan, self.sh = plan, sh
        self.vel, self.stress, self.mats = vel, stress, mats
        self.oc, self.water, self.bottom = oc, water, bottom

    def flow_x(self, j, count):
        oc = self.oc
        before, at, after = (pl.ds(j + k, count) for k in range(3))
        oc[1, at] = self.water[at] * (oc[1, at] - HALF * (oc[0, after] - oc[0, before]))

    def flow(self, j, count):
        oc, sh = self.oc, self.sh
        at = pl.ds(j + 1, count)
        p = oc[0, at]
        wet = self.water[at]
        rise = sh.dz(p, -1.0) + self.bottom[at] * p
        oc[3, at] = wet * (oc[3, at] - (HALF * rise + (DT * GRAV) * p))
        oc[2, at] = wet * (oc[2, at] - HALF * sh.dy(p))

    def press(self, j, count, floor):
        oc, sh = self.oc, self.sh
        before, at, after = (pl.ds(j + k, count) for k in range(3))
        w = oc[3, at]
        rise = sh.dz(w, 1.0)
        if floor is not None:
            rise = rise + self.bottom[at] * floor(pl.ds(j, count))
        total = oc[1, after] - oc[1, before] + sh.dy(oc[2, at]) + rise
        oc[0, at] = self.water[at] * (oc[0, at] - (HALF * KBULK) * total)

    def add_floor(self, j, count):
        at = pl.ds(j + 1, count)
        floor = self.first_floor(pl.ds(j, count))
        self.oc[0, at] = self.oc[0, at] - (HALF * KBULK) * (self.bottom[at] * floor)

    def first_floor(self, at):
        return self.mats[FLOOR, at]

    def floor(self, at):
        return self.sh.seafloor(self.vel[VZ, at])

    def load(self, j, count):
        at = pl.ds(j + 1, count)
        return self.sh.on_top(self.bottom[at] * self.oc[0, at])

    def add_load(self, j, count):
        at = pl.ds(j, count)
        self.vel[VZ, at] = self.vel[VZ, at] + self.mats[BUOY, at] * self.load(j, count)

    def move(self, j, count):
        vel = self.vel
        at = pl.ds(j, count)
        ax, ay, az = acceleration(self.sh, self.stress, j, count)
        b = self.mats[BUOY, at]
        vel[VX, at] = vel[VX, at] + b * ax
        vel[VY, at] = vel[VY, at] + b * ay
        vel[VZ, at] = vel[VZ, at] + b * (az + self.load(j, count))

    def move_z(self, j, count):
        at = pl.ds(j, count)
        _, _, az = acceleration(self.sh, self.stress, j, count)
        vz = self.vel[VZ, at] + self.mats[BUOY, at] * (az + self.load(j, count))
        self.vel[VZ, at] = vz

    def strain(self, j, count):
        for f, value in strained(self.sh, self.vel, self.stress, self.mats, j, count):
            self.stress[f, pl.ds(j, count)] = value

    def run(self, spans, inner, send=None):
        def planes(t, inset, update):
            self.plan.planes(*spans(t, inset), update, BATCH)

        def flows(t):
            planes(t, 0, self.flow_x)
            planes(t, 1, self.flow)

        if inner:
            columns = self.vel.shape[1]
            first, last = spans(0, 1)
            self.plan.planes(0, columns, self.flow_x, BATCH)
            self.plan.planes(1, columns - 1, self.flow, BATCH)
            planes(0, 1, functools.partial(self.press, floor=self.first_floor))
            later = functools.partial(self.press, floor=None)
            self.plan.planes(1, first, later, BATCH)
            self.plan.planes(last, columns - 1, later, BATCH)
        else:
            planes(0, 1, self.add_floor)
        for t in range(STEPS - 1):
            flows(t + 1)
            move = self.add_load if inner and t == 0 else self.move
            if not inner and t == STEPS - 2:
                move = self.move_z
            planes(t, 1, move)
            if t < STEPS - 2:
                planes(t, 2, self.strain)
            planes(t + 1, 1, functools.partial(self.press, floor=self.floor))
        if send is not None:
            send()


def inner_kernel(
    plan, arrived, swapped, mats, vel_in, stress_in, vel, stress, oc, water, bottom,
    gather, depths, memory,
):
    sub, chunks, n, strips = plan.sub, plan.chunks, plan.n, plan.strips
    cells, sent = plan.cells, plan.sent_groups
    sh = Shifts(plan, memory)
    odd = odd_device()
    half = n // 2
    columns = 2 * cells + 2 * HALO

    def turn(owner, group):
        for core, ref in ((odd, arrived), (1 - odd, swapped)):
            for kc in range(chunks):
                for yl in range(strips):
                    at = owner * plan.rows + group * plan.lead + kc * strips + yl
                    to = kc * plan.ny + core * strips + yl
                    gather[pl.ds(to, half, stride=2 * strips), :] = ref[
                        pl.ds(at, half, stride=2 * plan.rows), :
                    ]
        return gather[...].T

    deeps = []
    for owner in range(2):
        for group in range(sent):
            turned = turn(owner, group)
            for i in range(chunks):
                for f in range(4):
                    at = (i * 4 + f) * sub
                    column = 1 + owner * (cells + HALO) + group * chunks + i
                    oc[f, column] = turned[at : at + sub]
            if owner == 0 and group == 0:
                oc[0, 0] = turned[2 * sub : 3 * sub]
                deeps.append(turned[3 * sub : 4 * sub])
            if owner == 1 and group == sent - 1:
                oc[0, columns + 1] = turned[LANES - 2 * sub : LANES - sub]
                deeps.append(turned[LANES - sub :])
    for i, deep in enumerate(deeps):
        for kc in range(chunks):
            mine = (sh.lane >= kc * plan.ny) & (sh.lane < (kc + 1) * plan.ny)
            depths[i, kc * sub : (kc + 1) * sub, :] = sh.over_chunks(jnp.where(mine, deep, 0.0))

    def mask(owner, j, _):
        low = jnp.broadcast_to(depths[owner, pl.ds(j - owner * cells, 1), :], (sub, plan.lanes))
        wet = jnp.where(sh.depth < low, 1.0, 0.0).astype(F32)
        water[j] = wet
        bottom[j] = jnp.where(sh.depth == low - 1.0, 1.0, 0.0).astype(F32)
        oc[0, j] = oc[0, j] * wet

    def mask_x(j, _):
        oc[1, j] = oc[1, j] * water[j]

    def mask_yw(j, _):
        oc[2, j] = oc[2, j] * water[j]
        oc[3, j] = oc[3, j] * water[j]

    plan.planes(0, plan.width + 2, lambda j, _: mask(0, j, _))
    plan.planes(plan.width + 2, columns + 2, lambda j, _: mask(1, j, _))
    plan.planes(1, columns + 1, mask_x)
    plan.planes(2, columns, mask_yw)

    def bring_in(j, _):
        for f in range(3):
            vel[f, j] = vel_in[f, j]
        for f in range(6):
            stress[f, j] = stress_in[f, j]

    if not plan.unrolled:
        plan.planes(HALO, HALO + 2 * cells, bring_in)
    updates = Updates(plan, sh, vel, stress, mats, oc, water, bottom)
    updates.run(lambda t, inset: (HALO + 2 * t + inset, HALO + 2 * cells - 2 * t - inset), True)


def outer_kernel(
    plan, materials, border, water, bottom, vel_in, stress_in, mats_in, oc_in,
    vel, stress, mats, oc, rows, gather, memory,
):
    sub, chunks, n, strips, cells = plan.sub, plan.chunks, plan.n, plan.strips, plan.cells
    near = cells - 1
    sh = Shifts(plan, memory)
    odd = odd_device()
    if not plan.unrolled:
        for here, there in (
            (vel, vel_in), (stress, stress_in), (mats, mats_in), (oc, oc_in)
        ):
            here[...] = there[...]
    updates = Updates(plan, sh, vel, stress, mats, oc, water, bottom)

    def material(c, z):
        row = materials[pl.ds(c * ZONES + z, 1), :]
        return jnp.broadcast_to(row, (sub, plan.lanes))

    def side(core):
        low, far = ((1, 0), (HALO + 2 * cells, 2 * HALO + 2 * cells - 1))[core]
        state = (vel, stress, mats)
        plan.planes(
            0,
            near,
            lambda x, count: bring(
                plan, sh, material, state, border, near, x, count, low + x, 1 - core
            ),
            BATCH,
        )
        for i, f in enumerate((SXX, SXY, SXZ)):
            stress[f, far] = border[10 * near + i]

        def spans(t, inset):
            if core == 0:
                return 2 * t + inset, 2 * t + inset + HALO
            last = 2 * HALO + 2 * cells - 2 * t - inset
            return last - HALO, last

        def send():
            for group in range(plan.own_groups):
                stacked = jnp.concatenate(
                    [
                        oc[f, 1 + HALO + core * cells + group * chunks + i]
                        for i in range(chunks)
                        for f in range(4)
                    ],
                    axis=0,
                )
                gather[group] = stacked.T
                for kc in range(chunks):
                    for yl in range(strips):
                        at = group * plan.lead + kc * strips + yl
                        rows[pl.ds(at, n, stride=plan.back_rows), :] = gather[
                            group, pl.ds(kc * plan.ny + yl, n, stride=strips), :
                        ]

        updates.run(spans, False, send)

    for core in range(2):
        pl.when(odd == core)(functools.partial(side, core))


def end_kernel(
    plan, vel_all, stress_all, mats_all, oc_all, bottom_all, vel_out, stress_out, vel, stress
):
    cells, sub, chunks, ny = plan.cells, plan.sub, plan.chunks, plan.ny
    sh = Shifts(plan)
    first, last = 2 * (STEPS - 1), plan.width - 2 * (STEPS - 1)
    window = pl.ds(cells * odd_device(), plan.width)
    vel_in, stress_in = vel_all.at[:, window], stress_all.at[:, window]
    mats = mats_all.at[:, window]
    window = pl.ds(cells * odd_device(), plan.width + 2)
    pressure, bottom = oc_all.at[0, window], bottom_all.at[window]

    def put(out, f, x, count, planes):
        for kc in range(chunks):
            out[f, pl.ds(x, count), kc * sub : (kc + 1) * sub, :] = planes[
                :, :, kc * ny : (kc + 1) * ny
            ]

    def hold(j, count):
        for f in range(3):
            vel[f, pl.ds(j, count)] = vel_in[f, pl.ds(j, count)]

    def catch_up(x, count):
        j = first - 1 + (last - first - 6) * odd_device() + x
        at = pl.ds(j, count)
        ax, ay, _ = acceleration(sh, stress_in, j, count)
        vel[VX, at] = vel[VX, at] + mats[BUOY, at] * ax
        vel[VY, at] = vel[VY, at] + mats[BUOY, at] * ay

    def strain(j, count):
        for f, value in strained(sh, vel, stress_in, mats, j, count):
            stress[f, pl.ds(j, count)] = value

    def move(j, count):
        at = pl.ds(j, count)
        ax, ay, az = acceleration(sh, stress, j, count)
        b = mats[BUOY, at]
        wet = pl.ds(j + 1, count)
        load = sh.on_top(bottom[wet] * pressure[wet])
        for f, a in enumerate((ax, ay, az + load)):
            vel[f, at] = vel[f, at] + b * a

    def finish(x, count):
        for f in range(3):
            put(vel_out, f, x, count, vel[f, pl.ds(x + HALO, count)])
        for f, value in strained(sh, vel, stress, mats, x + HALO, count):
            put(stress_out, f, x, count, value)

    plan.planes(first - 1, last + 1, hold, BATCH)
    plan.planes(0, HALO, catch_up, BATCH)
    plan.planes(first, last, strain, BATCH)
    plan.planes(first + 1, last - 1, move, BATCH)
    plan.planes(0, cells, finish, BATCH)


def unpack_kernel(plan, arrived, ocean, turned, strips, sems):
    sub, chunks = plan.sub, plan.chunks
    block = 4 * sub
    copies = [
        pltpu.make_async_copy(strips.at[yl], ocean.at[:, yl], sems.at[yl])
        for yl in range(plan.strips)
    ]
    for yl in range(plan.strips):
        by_chunk = [
            arrived[pl.ds(kc * plan.strips + yl, plan.nx // chunks, stride=plan.lead), :]
            for kc in range(chunks)
        ]
        for i in range(chunks):
            turned[yl, pl.ds(i, plan.nx // chunks, stride=chunks), :] = place(
                by_chunk, [i] * chunks, block
            )
        whole = turned[yl].T
        for kc in range(chunks):
            for f in range(4):
                at = (kc * 4 + f) * sub
                strips[yl, f, kc * sub : (kc + 1) * sub, :] = whole[at : at + sub]
        copies[yl].start()
    for copy in copies:
        copy.wait()


def on_device(plan, velocity, stress, ocean, zones, materials, slip, bathy):
    n, cells, sub, lanes, width = plan.n, plan.cells, plan.sub, plan.lanes, plan.width
    vmem = pl.BlockSpec(memory_space=pltpu.VMEM)
    smem = pl.BlockSpec(memory_space=pltpu.SMEM)
    hbm = pl.BlockSpec(memory_space=pltpu.HBM)

    def shape(*dims):
        return jax.ShapeDtypeStruct(dims, F32)

    def in_vmem(*dims):
        return pltpu.VMEM(dims, F32) if plan.unrolled else shape(*dims)

    def like(array):
        return jax.ShapeDtypeStruct(array.shape, array.dtype)

    def held(array):
        return pltpu.VMEM(array.shape, array.dtype)

    def call(kernel, name, out, ins, scratch, room=16, outs=None, **rest):
        room = room if plan.unrolled else 56
        return pl.pallas_call(
            functools.partial(kernel, plan),
            out_shape=out,
            in_specs=ins,
            out_specs=jax.tree.map(lambda _: vmem, out) if outs is None else outs,
            scratch_shapes=scratch,
            compiler_params=pltpu.CompilerParams(vmem_limit_bytes=room * 1024 * 1024),
            name=name,
            **rest,
        )

    def pinned(array):
        return pltpu.with_memory_space_constraint(array, pltpu.HBM)

    def near(array):
        return pltpu.with_memory_space_constraint(array, pltpu.VMEM) if plan.unrolled else array

    mates = [(i, i ^ 1) for i in range(n)]
    others = [(i, i + 1) for i in range(1, n - 1, 2)]
    others += [(target, source) for source, target in others]
    message, crust, border = call(
        pack_kernel,
        "pack",
        (
            shape(n * plan.rows, LANES),
            shape(10 * cells + 1, sub, lanes),
            shape(10 * cells - 6, sub, lanes),
        ),
        [hbm] * 6,
        [held(a) for a in (velocity, stress, zones, slip, ocean, bathy)]
        + [
            pltpu.VMEM((plan.strips, plan.nx, LANES), F32),
            pltpu.VMEM(
                ((plan.nx // plan.chunks + 2 * plan.halo_groups) * plan.lead, LANES), F32
            ),
            pltpu.VMEM((n * plan.strips, LANES), F32),
            pltpu.VMEM((n * plan.rows, LANES), F32),
            pltpu.SemaphoreType.DMA((7,)),
        ],
        outs=(hbm, vmem, vmem),
    )(*(pinned(a) for a in (velocity, stress, zones, slip, ocean, bathy)))
    arrived = lax.all_to_all(
        message.reshape(n // 2, 2 * plan.rows, LANES),
        "map",
        split_axis=0,
        concat_axis=0,
        axis_index_groups=[list(range(core, n, 2)) for core in range(2)],
        tiled=True,
    ).reshape(n * plan.rows, LANES)
    other = lax.ppermute(border, "map", others)
    mate = lax.ppermute(crust, "map", mates)
    columns = 2 * cells + 2 * HALO
    vel, strs, mats, material_rows = call(
        begin_kernel,
        "first_velocity",
        (
            shape(3, columns, sub, lanes),
            shape(6, columns, sub, lanes),
            shape(5, columns, sub, lanes),
            shape(3 * ZONES, lanes),
        ),
        [smem] + [vmem] * 2,
        [],
    )(materials, crust, mate)
    arrived, vel = lax.optimization_barrier((arrived, vel))
    swapped = lax.ppermute(arrived, "map", mates)
    planes_of = {
        "vel": shape(3, columns, sub, lanes),
        "stress": shape(6, columns, sub, lanes),
        "mats": shape(5, columns, sub, lanes),
        "oc": shape(4, columns + 2, sub, lanes),
        "mask": shape(columns + 2, sub, lanes),
    }
    vel, strs, oc, water, bottom = call(
        inner_kernel,
        "inner_substeps",
        tuple(planes_of[k] for k in ("vel", "stress", "oc", "mask", "mask")),
        [vmem] * 5,
        [
            pltpu.VMEM((lanes, LANES), F32),
            pltpu.VMEM((2, plan.depth, lanes), F32),
            pltpu.VMEM((SLOTS * slot_rows(plan), lanes), F32),
        ],
        input_output_aliases={3: 0, 4: 1},
    )(*(near(a) for a in (arrived, swapped, mats, vel, strs)))
    vel, strs, mats, oc, back = call(
        outer_kernel,
        "outer_substeps",
        tuple(planes_of[k] for k in ("vel", "stress", "mats", "oc"))
        + (in_vmem(n * plan.back_rows, LANES),),
        [vmem] * 8,
        [
            pltpu.VMEM((plan.own_groups, lanes, LANES), F32),
            pltpu.VMEM((SLOTS * slot_rows(plan), lanes), F32),
        ],
        outs=(vmem,) * 5,
        input_output_aliases={4: 0, 5: 1, 6: 2, 7: 3},
    )(*(near(a) for a in (material_rows, other, water, bottom, vel, strs, mats, oc)))
    returned = lax.all_to_all(
        back.reshape(n, plan.back_rows, LANES), "map", split_axis=0, concat_axis=0, tiled=True
    ).reshape(n * plan.back_rows, LANES)
    new_velocity, new_stress = call(
        end_kernel,
        "last_updates",
        (shape(*velocity.shape), shape(*stress.shape)),
        [vmem] * 5,
        [
            pltpu.VMEM((3, width, sub, lanes), F32),
            pltpu.VMEM((6, width, sub, lanes), F32),
        ],
    )(vel, strs, mats, oc, bottom)
    new_ocean = call(
        unpack_kernel,
        "ocean_strips",
        shape(*ocean.shape),
        [vmem],
        [
            pltpu.VMEM((plan.strips, plan.nx, LANES), F32),
            pltpu.VMEM((plan.strips, 4, plan.depth, plan.nx), F32),
            pltpu.SemaphoreType.DMA((plan.strips,)),
        ],
        outs=hbm,
    )(returned)
    return new_velocity, new_stress, new_ocean


def solution(mesh):
    n = mesh.shape["map"]

    def body(velocity, stress, ocean, zones, materials, slip, bathy):
        _, cells, depth, ny = velocity.shape
        plan = Plan(n, cells, depth, ny, ocean.shape[1])
        return on_device(plan, velocity, stress, ocean, zones, materials, slip, bathy)

    return jax.shard_map(
        body,
        mesh=mesh,
        in_specs=(
            P("parts", "map", None, None),
            P("parts", "map", None, None),
            P("parts", "map", None, None),
            P("map", "parts", None),
            P(),
            P("map", "parts"),
            P("map", "parts"),
        ),
        out_specs=(
            P("parts", "map", None, None),
            P("parts", "map", None, None),
            P("parts", "map", None, None),
        ),
        check_vma=False,
    )
```
